32 devices in a mesh: seq: 4 (over y, core), ctx: 2 (over x), exp: 4 (over z).
Axes of the slice: x: 2, y: 2, z: 4, core: 2. Of those that a mesh axis runs over, the one named last changes fastest.
Arguments:
- residual_in: bfloat16 [16, 1024, 2048], P(('seq', 'exp'), 'ctx'), may hold values from -24 to 24
- segments: int32 [16, 1024], P(('seq', 'exp')), may hold values from 0 to 515, as said below
- routes: int32 [16, 1024, 8], P(('seq', 'exp'), 'ctx'), may hold values from 0 to 15, all different within a row; in each aligned block of 512 rows (0 to 511, 512 to 1023, ..., all dimensions but the last counted through in order) at most 288 rows name the same one
- gates: float32 [16, 1024, 8], P(('seq', 'exp'), 'ctx'), may hold values from 0.005 to 0.7
- attn_gain: bfloat16 [2048], P(('seq', 'ctx', 'exp')), may hold values from 0.5 to 1.5
- q_proj: bfloat16 [2048, 4096], P(('seq', 'ctx', 'exp')), may hold values from -0.125 to 0.125
- key_projection: bfloat16 [2048, 512], P(('seq', 'ctx', 'exp')), may hold values from -0.125 to 0.125
- value_projection: bfloat16 [2048, 512], P(('seq', 'ctx', 'exp')), may hold values from -0.125 to 0.125
- q_gain: bfloat16 [128], P(('seq', 'ctx', 'exp')), may hold values from 0.5 to 1.5
- k_gain: bfloat16 [128], P(('seq', 'ctx', 'exp')), may hold values from 0.5 to 1.5
- o_proj: bfloat16 [4096, 2048], P(('seq', 'ctx', 'exp')), may hold values from -0.5 to 0.5
- mlp_gain: bfloat16 [2048], P(('seq', 'ctx', 'exp')), may hold values from 0.5 to 1.5
- gate_proj: bfloat16 [16, 2048, 768], P('exp', ('seq', 'ctx')), may hold values from -0.125 to 0.125
- up_proj: bfloat16 [16, 2048, 768], P('exp', ('seq', 'ctx')), may hold values from -0.125 to 0.125
- down_proj: bfloat16 [16, 768, 2048], P('exp', ('seq', 'ctx')), may hold values from -0.875 to 0.875
- out_grad: bfloat16 [16, 1024, 2048], P(('seq', 'exp'), 'ctx'), may hold values from -6 to 6
Outputs:
- residual_out: bfloat16 [16, 1024, 2048], P(('seq', 'exp'), 'ctx')
- residual_grad: bfloat16 [16, 1024, 2048], P(('seq', 'exp'), 'ctx')
- attn_gain_grad: float32 [2048], P(('seq', 'ctx', 'exp'))
- q_proj_grad: float32 [2048, 4096], P(('seq', 'ctx', 'exp'))
- k_proj_grad: float32 [2048, 512], P(('seq', 'ctx', 'exp'))
- v_proj_grad: float32 [2048, 512], P(('seq', 'ctx', 'exp'))
- q_gain_grad: float32 [128], P(('seq', 'ctx', 'exp'))
- k_gain_grad: float32 [128], P(('seq', 'ctx', 'exp'))
- o_proj_grad: float32 [4096, 2048], P(('seq', 'ctx', 'exp'))
- mlp_gain_grad: float32 [2048], P(('seq', 'ctx', 'exp'))
- gate_proj_grad: float32 [16, 2048, 768], P('exp', ('seq', 'ctx'))
- up_proj_grad: float32 [16, 2048, 768], P('exp', ('seq', 'ctx'))
- down_proj_grad: float32 [16, 768, 2048], P('exp', ('seq', 'ctx'))
- rms_stats: float32 [3], replicated
The draws below stay inside these ranges and needn't reach their ends.
Inputs may be any that keep to these rules, and one draw needn't show every extreme that they name: `segments`: along a sequence the numbers never fall; 0 marks unused slots, which come only at the end, one or more in every sequence; the last used document of every sequence has the number 512 + 3; in every sequence one document begins among the first 512 positions and ends among the last 512. `routes`: A token names 8 different experts. In the tokens of one device (aligned blocks of 512 tokens) no expert is named more than 288 times, a bound that some block reaches.
All inputs are finite; a program needn't handle non-finite values.
Results may differ from the reference program's by a relative error of at most 0.015.
Values may be sent and summed in bfloat16 or wider, within the bound.
A program may use at most 576 MiB of HBM per device.

```python
import math
import jax
import jax.numpy as jnp
import numpy as np
from jax import lax

MODEL_DIM = 2048
QUERY_HEADS = 32
KEY_VALUE_HEADS = 4
HEAD_DIM = 128
FF = 768
TOP = 8
PACKED_LENGTH = 1024
TOK_DEV = 512
SEQS = 16
EXPERTS = 16
CAP = 288


def draw_residual_in(key, part):
    key = jax.random.fold_in(key, 11)
    key_entries, key_rough = jax.random.split(key)
    seq_index = jnp.arange(SEQS, dtype=jnp.float32) / (SEQS - 1)
    entries = jnp.clip(jax.random.normal(key_entries, (SEQS, PACKED_LENGTH, MODEL_DIM), jnp.float32), -6.0, 6.0)
    row_rough = jnp.exp(jax.random.uniform(key_rough, (SEQS, PACKED_LENGTH, 1), jnp.float32, -0.35, 0.35))
    seq_scale = 0.55 * jnp.exp(seq_index * math.log(3.0))
    return (entries * row_rough * seq_scale[:, None, None]).astype(jnp.bfloat16)


def draw_gates(key, part):
    key = jax.random.fold_in(key, 37)
    seq_frac = (jnp.arange(SEQS, dtype=jnp.float32) / (SEQS - 1))[:, None, None]
    pos_frac = (jnp.arange(PACKED_LENGTH, dtype=jnp.float32) / (PACKED_LENGTH - 1))[None, :, None]
    base = jnp.exp(jax.random.uniform(key, (SEQS, PACKED_LENGTH, TOP), jnp.float32, math.log(0.03), math.log(0.15)))
    spread = math.log(3.0)
    return (base * jnp.exp(spread * (seq_frac + pos_frac - 1.0))).astype(jnp.float32)


def draw_segments(key, part):
    key = jax.random.fold_in(key, 23)
    key_lead, key_pad, key_after, key_breaks = jax.random.split(key, 4)
    half_tok = TOK_DEV // 2
    lead_len = jax.random.randint(key_lead, (SEQS, 1), 1, half_tok)
    tail_pad = jax.random.randint(key_pad, (SEQS, 1), 1, half_tok)
    after_len = jax.random.randint(key_after, (SEQS, 1), 1, half_tok)
    position = jnp.arange(PACKED_LENGTH, dtype=jnp.int32)[None, :]
    finish = PACKED_LENGTH - tail_pad - after_len
    used_len = PACKED_LENGTH - tail_pad
    breaks = jax.random.randint(key_breaks, (SEQS, PACKED_LENGTH), 0, 24) == 0
    starts = (position == 0) | (position == lead_len) | (position == finish) | breaks & ((position < lead_len) | (position > finish))
    number = jnp.cumsum(starts.astype(jnp.int32), axis=1).astype(jnp.int32)
    used = position < used_len
    last_number = jnp.max(jnp.where(used, number, 0), axis=1, keepdims=True).astype(jnp.int32)
    number = (number + (TOK_DEV + 3) - last_number).astype(jnp.int32)
    return jnp.where(used, number, 0).astype(jnp.int32)


def shard_levels(stream_key, dims, shards, low, top_value):
    loudness, own = 1.0, jax.random.fold_in(stream_key, 6)
    for dim, blocks in shards:
        heights = jnp.exp(jax.random.uniform(jax.random.fold_in(own, dim), (blocks,), jnp.float32, low / len(shards), top_value / len(shards)))
        loudness = loudness * jnp.repeat(heights, dims[dim] // blocks).reshape([-1 if axis == dim else 1 for axis in range(len(dims))])
    return loudness


def deal_out(rng, own, number, rows, amount, top, limit, skew):
    sequence = jax.random.permutation(rng, amount)
    crowded, ordinary = portions_of(amount, rows * top, limit, skew, True), portions_of(amount, rows * top, limit, skew, False)
    places = jnp.arange(amount)

    def named(tallies, rotation):
        used = int((tallies > 0).sum())
        fixed = max(1, used // 4)
        moved = fixed + (places - fixed + rotation * (used - fixed)) % max(1, amount - fixed)
        return jnp.zeros((amount,), jnp.int32).at[sequence[jnp.where(places < fixed, places, moved)]].set(jnp.asarray(tallies, jnp.int32))

    tallies = jnp.where(number % 4 == 0, named(crowded, number // 4), named(ordinary, number - number // 4 - 1))
    mixed = jax.random.permutation(jax.random.fold_in(own, 3), amount)
    donor, receiver = mixed[0:amount // 2 * 2:2], mixed[1:amount // 2 * 2:2]
    margin = jnp.minimum(tallies[donor] - 1, limit - tallies[receiver]) // 2
    margin = jnp.where((donor == sequence[0]) | (receiver == sequence[0]) | (tallies[receiver] == 0), 0, jnp.maximum(margin, 0))
    moved = jax.random.randint(jax.random.fold_in(own, 4), (amount // 2,), 0, 1 << 20) % (margin + 1)
    tallies = tallies.at[donor].add(-moved).at[receiver].add(moved)
    labels = jnp.searchsorted(jnp.cumsum(tallies), jnp.arange(rows * top), side="right").astype(jnp.int32)
    listing = labels.reshape(top, rows).T
    listing = listing[jax.random.permutation(jax.random.fold_in(own, 1), rows)]
    rotation = jax.random.randint(jax.random.fold_in(own, 2), (rows, 1), 0, top)
    return jnp.take_along_axis(listing, (jnp.arange(top)[None, :] + rotation) % top, axis=1)


def portions_of(amount, total, reach, skew, full):
    loads = [(1 << 20) // math.isqrt(grade ** skew) + 1 for grade in range(1, amount + 1)]
    largest = reach if full else min(reach, max(-(-total // amount), total * loads[0] // sum(loads)))
    least = 1 if total - largest >= amount - 1 else 0
    given, spare = [largest] + [least] * (amount - 1), total - largest - least * (amount - 1)
    while spare > 0:
        candidates = [i for i in range(1, amount) if given[i] < largest] or [i for i in range(1, amount) if given[i] < reach]
        mass, left = sum([loads[i] for i in candidates]), spare
        for i in candidates:
            extra = min(reach - given[i], max(1, left * loads[i] // mass), spare)
            given[i] = given[i] + extra
            spare = spare - extra
    return np.array(given)


def scatter_about(rng, extent, width, limit, shards=(), kind=jnp.bfloat16):
    result = width * jax.random.normal(rng, extent, jnp.float32)
    if shards:
        result = result * shard_levels(rng, extent, shards, -0.22, 0.18)
    return jnp.clip(result, -limit, limit).astype(kind)


def setup_inputs(seed: int = 0) -> dict:
    streams_of = jax.random.split(jax.random.key(seed), 17)
    residual_in = draw_residual_in(jax.random.fold_in(streams_of[16], 71), 0)
    segments = draw_segments(jax.random.fold_in(streams_of[16], 71), 0)
    routes_keys = jax.random.split(jax.random.fold_in(streams_of[2], 1), SEQS * PACKED_LENGTH // TOK_DEV)
    routes_turns = jax.random.permutation(jax.random.fold_in(streams_of[2], 3), SEQS * PACKED_LENGTH // TOK_DEV)
    routes = jax.vmap(lambda own, number: deal_out(jax.random.fold_in(streams_of[2], 2), own, number, TOK_DEV, EXPERTS, TOP, CAP, 1))(routes_keys, routes_turns).reshape((SEQS, PACKED_LENGTH, TOP))
    gates = draw_gates(jax.random.fold_in(streams_of[16], 71), 0)
    attn_gain = jnp.clip(1.0 + 0.1 * jax.random.normal(streams_of[4], (MODEL_DIM,), jnp.float32), 0.5, 1.5).astype(jnp.bfloat16)
    q_proj = scatter_about(streams_of[5], (MODEL_DIM, QUERY_HEADS * HEAD_DIM), MODEL_DIM ** -0.5, 0.125, ((0, 32),))
    key_projection = scatter_about(streams_of[6], (MODEL_DIM, KEY_VALUE_HEADS * HEAD_DIM), MODEL_DIM ** -0.5, 0.125, ((0, 32),))
    value_projection = scatter_about(streams_of[7], (MODEL_DIM, KEY_VALUE_HEADS * HEAD_DIM), MODEL_DIM ** -0.5, 0.125, ((0, 32),))
    q_gain = jnp.clip(1.0 + 0.1 * jax.random.normal(streams_of[8], (HEAD_DIM,), jnp.float32), 0.5, 1.5).astype(jnp.bfloat16)
    k_gain = jnp.clip(1.0 + 0.1 * jax.random.normal(streams_of[9], (HEAD_DIM,), jnp.float32), 0.5, 1.5).astype(jnp.bfloat16)
    o_proj = scatter_about(streams_of[10], (QUERY_HEADS * HEAD_DIM, MODEL_DIM), (QUERY_HEADS * HEAD_DIM // 32) ** -0.5, 0.5, ((0, 32),))
    mlp_gain = jnp.clip(1.0 + 0.1 * jax.random.normal(streams_of[11], (MODEL_DIM,), jnp.float32), 0.5, 1.5).astype(jnp.bfloat16)
    gate_proj = scatter_about(streams_of[12], (EXPERTS, MODEL_DIM, FF), MODEL_DIM ** -0.5, 0.125, ((0, 4), (1, 8)))
    up_proj = scatter_about(streams_of[13], (EXPERTS, MODEL_DIM, FF), MODEL_DIM ** -0.5, 0.125, ((0, 4), (1, 8)))
    down_proj = scatter_about(streams_of[14], (EXPERTS, FF, MODEL_DIM), (FF // 16) ** -0.5, 0.875, ((0, 4), (1, 8)))
    out_grad = scatter_about(streams_of[15], (SEQS, PACKED_LENGTH, MODEL_DIM), 1.0, 6.0, ((0, 16), (1, 2)))
    return dict(residual_in=residual_in, segments=segments, routes=routes, gates=gates, attn_gain=attn_gain, q_proj=q_proj, key_projection=key_projection, value_projection=value_projection, q_gain=q_gain, k_gain=k_gain, o_proj=o_proj, mlp_gain=mlp_gain, gate_proj=gate_proj, up_proj=up_proj, down_proj=down_proj, out_grad=out_grad)


EPS = 1e-06
ROPE_BASE = 1000000.0
MASKED = -1e+30
HIGHEST = lax.Precision.HIGHEST

@jax.custom_vjp
def reduced_input(v):
    return lax.optimization_barrier(v.astype(jnp.bfloat16)).astype(jnp.float32)

@jax.custom_vjp
def reduced_gradient(v):
    return v

def low_keep(v):
    return (reduced_input(v), None)

def low_pass(kept, grad):
    return (grad,)

def back_keep(v):
    return (v, None)

def back_low(kept, grad):
    return (reduced_input(grad),)
reduced_input.defvjp(low_keep, low_pass)
reduced_gradient.defvjp(back_keep, back_low)

def matrix_product(first_op, second_op):
    return jnp.dot(first_op, second_op, precision=HIGHEST, preferred_element_type=jnp.float32)

def rms_norm(source, gain_vec):
    return source * lax.rsqrt(lax.optimization_barrier(jnp.mean(source * source, axis=-1, keepdims=True)) + EPS) * gain_vec

def rope_tables(positions):
    half_dim = HEAD_DIM // 2
    inverse = ROPE_BASE ** (-jnp.arange(half_dim, dtype=jnp.float32) * 2.0 / HEAD_DIM)
    angles = positions.astype(jnp.float32)[:, None] * inverse[None, :]
    cosine_table = jnp.cos(angles)
    sine_values = jnp.sin(angles)
    return (jnp.concatenate([cosine_table, cosine_table], -1), jnp.concatenate([sine_values, sine_values], -1))

def rotate(vectors, cosine_table, sine_values):
    half_dim = vectors.shape[-1] // 2
    turned = jnp.concatenate([-vectors[..., half_dim:], vectors[..., :half_dim]], -1)
    return vectors * cosine_table[:, None, :] + turned * sine_values[:, None, :]

def head_group(packed, allowed):
    query_group, key_head, value_head = packed
    scores = jnp.einsum('qgd,kd->gqk', query_group, key_head, precision=HIGHEST) * HEAD_DIM ** (-0.5)
    scores = jnp.where(allowed[None], reduced_gradient(scores), MASKED)
    probs_low = reduced_input(jax.nn.softmax(scores, axis=-1))
    return jnp.einsum('gqk,kd->qgd', probs_low, value_head, precision=HIGHEST)

def expert_rows(packed, source):
    row_ids, w_gate, w_up, w_down = packed
    taken_rows = reduced_gradient(source[row_ids])
    gate_act = reduced_gradient(matrix_product(taken_rows, w_gate))
    up_act = reduced_gradient(matrix_product(taken_rows, w_up))
    product = reduced_input(jax.nn.silu(gate_act) * up_act)
    return reduced_gradient(reduced_input(matrix_product(product, w_down)))

def dispatch_tables(route_ids, gate_vals):
    blocks = PACKED_LENGTH // TOK_DEV
    hit_counts = (route_ids[:, :, None] == jnp.arange(EXPERTS, dtype=jnp.int32)[None, None, :]).astype(jnp.int32).sum(1).astype(jnp.int32)
    hit_counts = hit_counts.reshape(blocks, TOK_DEV, EXPERTS)
    earlier = (jnp.cumsum(hit_counts, axis=1).astype(jnp.int32) - hit_counts).reshape(PACKED_LENGTH, EXPERTS)
    slot_ids = jnp.take_along_axis(earlier, route_ids, axis=1).astype(jnp.int32)
    block_ids = (jnp.arange(PACKED_LENGTH, dtype=jnp.int32) // TOK_DEV)[:, None]
    row_ids = (block_ids * CAP + slot_ids).astype(jnp.int32)
    token_ids = jnp.broadcast_to(jnp.arange(PACKED_LENGTH, dtype=jnp.int32)[:, None], route_ids.shape)
    slot_token = jnp.full((EXPERTS, blocks * CAP), PACKED_LENGTH, jnp.int32).at[route_ids, row_ids].set(token_ids)
    slot_gate = jnp.zeros((EXPERTS, blocks * CAP), jnp.float32).at[route_ids, row_ids].set(gate_vals)
    return (slot_token, slot_gate)

def sequence_layer(inputs, params):
    hidden, seg_ids, route_ids, gate_vals = inputs
    gain_attn, w_query, key_weight, value_weight, gain_query, gain_key, w_out, gain_mlp, w_gate, w_up, w_down = params
    positions = jnp.arange(PACKED_LENGTH, dtype=jnp.int32)
    cosine_table, sine_values = rope_tables(positions)
    normalized_input = reduced_input(rms_norm(hidden, gain_attn))
    q_raw = reduced_gradient(matrix_product(normalized_input, w_query)).reshape(PACKED_LENGTH, QUERY_HEADS, HEAD_DIM)
    unrotated_keys = reduced_gradient(matrix_product(normalized_input, key_weight)).reshape(PACKED_LENGTH, KEY_VALUE_HEADS, HEAD_DIM)
    value_rows = reduced_gradient(reduced_input(matrix_product(normalized_input, value_weight))).reshape(PACKED_LENGTH, KEY_VALUE_HEADS, HEAD_DIM)
    query_rows = reduced_input(rotate(rms_norm(q_raw, gain_query), cosine_table, sine_values))
    key_rows = reduced_input(rotate(rms_norm(unrotated_keys, gain_key), cosine_table, sine_values))
    allowed = (seg_ids[:, None] == seg_ids[None, :]) & (positions[:, None] >= positions[None, :])
    grouped_rows = query_rows.reshape(PACKED_LENGTH, KEY_VALUE_HEADS, QUERY_HEADS // KEY_VALUE_HEADS, HEAD_DIM).transpose(1, 0, 2, 3)
    attend = jax.checkpoint(head_group)
    mixed_heads = lax.map(lambda packed: attend(packed, allowed), (grouped_rows, key_rows.transpose(1, 0, 2), value_rows.transpose(1, 0, 2)))
    mixed_heads = mixed_heads.transpose(1, 0, 2, 3).reshape(PACKED_LENGTH, QUERY_HEADS * HEAD_DIM)
    valid_rows = (seg_ids > 0).astype(jnp.float32)[:, None]
    mixed_heads = reduced_gradient(reduced_input(mixed_heads * valid_rows))
    attn_out = reduced_gradient(matrix_product(mixed_heads, w_out))
    middle = hidden + attn_out
    normed_mlp = reduced_input(rms_norm(middle, gain_mlp))
    slot_token, slot_gate = dispatch_tables(route_ids, gate_vals)
    source = jnp.concatenate([normed_mlp, jnp.zeros((1, MODEL_DIM), jnp.float32)], 0)
    run_expert = jax.checkpoint(expert_rows)
    results = lax.map(lambda packed: run_expert(packed, source), (slot_token, w_gate, w_up, w_down))
    weighted = results * slot_gate[:, :, None]
    expert_out = jnp.zeros((PACKED_LENGTH + 1, MODEL_DIM), jnp.float32).at[slot_token.reshape(-1)].add(weighted.reshape(-1, MODEL_DIM))[:PACKED_LENGTH]
    return (middle + expert_out, attn_out, expert_out)

def reference(residual_in, segments, routes, gates, attn_gain, q_proj, key_projection, value_projection, q_gain, k_gain, o_proj, mlp_gain, gate_proj, up_proj, down_proj, out_grad):
    hidden = residual_in.astype(jnp.float32)
    params = tuple((weight.astype(jnp.float32) for weight in (attn_gain, q_proj, key_projection, value_projection, q_gain, k_gain, o_proj, mlp_gain, gate_proj, up_proj, down_proj)))
    layer_step = jax.checkpoint(sequence_layer)

    def forward(hidden_in, param_set):
        outputs = lax.map(lambda packed: layer_step(packed, param_set), (hidden_in, segments, routes, gates))
        return (outputs[0], (outputs[1], outputs[2]))
    final_out, pullback, aux_out = jax.vjp(forward, hidden, params, has_aux=True)
    attn_all, expert_all = aux_out
    grad_hidden, grad_params = pullback(out_grad.astype(jnp.float32))
    valid_rows = (segments > 0).astype(jnp.float32)[:, :, None]
    valid_count = jnp.sum(valid_rows) * MODEL_DIM
    rms_stats = jnp.sqrt(jnp.stack([jnp.sum(hidden * hidden * valid_rows), jnp.sum(attn_all * attn_all * valid_rows), jnp.sum(expert_all * expert_all * valid_rows)]) / valid_count)
    return (final_out.astype(jnp.bfloat16), grad_hidden.astype(jnp.bfloat16), grad_params[0], grad_params[1], grad_params[2], grad_params[3], grad_params[4], grad_params[5], grad_params[6], grad_params[7], grad_params[8], grad_params[9], grad_params[10], rms_stats)
```

```python
import jax
import jax.numpy as jnp
from jax import lax
from jax.sharding import PartitionSpec as P

QUERY_HEADS = 32
KEY_VALUE_HEADS = 4
HEAD_DIM = 128


EPS = 1e-06
ROPE_BASE = 1000000.0
MASKED = -1e30


def contract_rows(first_op, second_op):
    return lax.dot_general(
        first_op, second_op, (((0,), (0,)), ((), ())), preferred_element_type=jnp.float32
    )


def contract_cols(first_op, second_op):
    return lax.dot_general(
        first_op, second_op, (((1,), (1,)), ((), ())), preferred_element_type=jnp.float32
    )


def rope_tables(positions):
    half_dim = HEAD_DIM // 2
    inverse = ROPE_BASE ** (-jnp.arange(half_dim, dtype=jnp.float32) * 2.0 / HEAD_DIM)
    angles = positions.astype(jnp.float32)[:, None] * inverse[None, :]
    cosine_table = jnp.cos(angles)
    sine_values = jnp.sin(angles)
    return (
        jnp.concatenate([cosine_table, cosine_table], -1),
        jnp.concatenate([sine_values, sine_values], -1),
    )


def rotate(vectors, cosine_table, sine_values):
    half_dim = vectors.shape[-1] // 2
    turned = jnp.concatenate([-vectors[..., half_dim:], vectors[..., :half_dim]], -1)
    return vectors * cosine_table[:, None, :] + turned * sine_values[:, None, :]


def inverse_rotation(gradient, cosine_table, sine_values):
    half_dim = gradient.shape[-1] // 2
    scaled = gradient * sine_values[:, None, :]
    return gradient * cosine_table[:, None, :] + jnp.concatenate(
        [scaled[..., half_dim:], -scaled[..., :half_dim]], -1
    )


def norm_back(gradient, source, inverse, gain_vec):
    scaled = gradient * gain_vec
    return inverse * scaled - source * inverse**3 * jnp.mean(
        scaled * source, axis=-1, keepdims=True
    )


def pick(core, first, second):
    return jnp.where(core == 0, first, second)


def column_halves(weight, core):
    width = weight.shape[1] // KEY_VALUE_HEADS
    parts = [weight[:, i * width : (i + 1) * width] for i in range(KEY_VALUE_HEADS)]
    mine = [pick(core, parts[i], parts[i + 1]) for i in range(0, KEY_VALUE_HEADS, 2)]
    other = [pick(core, parts[i + 1], parts[i]) for i in range(0, KEY_VALUE_HEADS, 2)]
    return mine, other


def on_device(
    residual_in,
    segments,
    routes,
    gates,
    attn_gain,
    q_proj,
    key_projection,
    value_projection,
    q_gain,
    k_gain,
    o_proj,
    mlp_gain,
    gate_proj,
    up_proj,
    down_proj,
    out_grad,
):
    bf16, f32 = jnp.bfloat16, jnp.float32
    n_seq, n_ctx, n_exp = lax.axis_size("seq"), lax.axis_size("ctx"), lax.axis_size("exp")
    n_y = n_seq // 2
    devices = n_seq * n_ctx * n_exp
    core = lax.axis_index("seq") % 2
    span_index = lax.axis_index("ctx")
    z_index = lax.axis_index("exp")
    group_all = [
        [(s * n_ctx + x) * n_exp + z for s in range(c, n_seq, 2) for x in range(n_ctx) for z in range(n_exp)]
        for c in range(2)
    ]
    group_plane = [[s * n_ctx + x for s in range(c, n_seq, 2) for x in range(n_ctx)] for c in range(2)]

    def swap(value):
        return lax.ppermute(value, "seq", [(i, i ^ 1) for i in range(n_seq)])

    def across(value, step):
        return lax.ppermute(value, "exp", [(i, i ^ step) for i in range(n_exp)])

    token_count = residual_in.shape[1]
    model_width = residual_in.shape[2]
    sequence_length = segments.shape[1]
    route_count = routes.shape[2]
    local_experts = gate_proj.shape[0]
    expert_count = local_experts * n_exp
    half_experts = local_experts // 2
    capacity = token_count * route_count * 9 // (expert_count * 8)
    slots = -(-capacity // 16) * 16
    groups = KEY_VALUE_HEADS // 2
    heads = QUERY_HEADS // 2
    heads_per_group = QUERY_HEADS // KEY_VALUE_HEADS
    score_scale = HEAD_DIM ** (-0.5)
    rows = q_proj.shape[0]
    gain_rows = q_gain.shape[0]
    q_width, kv_width = heads * HEAD_DIM, groups * HEAD_DIM
    width = q_width + 2 * kv_width

    extra = jnp.zeros((rows, 128), bf16)
    extra = extra.at[0, :rows].set(attn_gain).at[0, rows : 2 * rows].set(mlp_gain)
    extra = extra.at[1, :gain_rows].set(q_gain).at[1, gain_rows : 2 * gain_rows].set(k_gain)
    mine_cols, other_cols = [], []
    for weight in (q_proj, key_projection, value_projection):
        mine, other = column_halves(weight, core)
        mine_cols += mine
        other_cols += other
    mine_block = jnp.concatenate(mine_cols + [extra], 1)
    theirs = swap(jnp.concatenate(other_cols + [extra], 1))
    pair = jnp.stack([pick(core, mine_block, theirs), pick(core, theirs, mine_block)])
    w_gathered = lax.all_gather(
        pair, ("seq", "ctx", "exp"), axis=0, tiled=False, axis_index_groups=group_all
    )
    w_rows = w_gathered.reshape(n_y, n_ctx * n_exp, 2, rows, width + 128).transpose(0, 2, 1, 3, 4)
    w_qkv = w_rows[..., :width].reshape(model_width, width)
    w_extra = w_rows[..., width:].reshape(devices, rows, 128)[:, :2]
    gain_attn = w_extra[:, 0, :rows].reshape(model_width).astype(f32)
    gain_mlp_f = w_extra[:, 0, rows : 2 * rows].reshape(model_width).astype(f32)
    gain_query_f = w_extra[:, 1, :gain_rows].reshape(HEAD_DIM).astype(f32)
    gain_key_f = w_extra[:, 1, gain_rows : 2 * gain_rows].reshape(HEAD_DIM).astype(f32)
    w_out = lax.all_gather(
        o_proj, ("seq", "ctx", "exp"), axis=0, tiled=True, axis_index_groups=group_all
    )

    def gather_expert(weight):
        mine = pick(core, weight[:half_experts], weight[half_experts:])
        theirs = swap(pick(core, weight[half_experts:], weight[:half_experts]))
        both = jnp.stack([pick(core, mine, theirs), pick(core, theirs, mine)])
        full = lax.all_gather(
            both, ("seq", "ctx"), axis=0, tiled=False, axis_index_groups=group_plane
        )
        full = full.reshape((n_y, n_ctx, 2) + mine.shape).transpose(3, 0, 2, 1, 4, 5)
        return full.reshape(half_experts, -1, weight.shape[2])

    w_gate, w_up, w_down = gather_expert(gate_proj), gather_expert(up_proj), gather_expert(down_proj)

    route_ids = routes[0]
    route_hit = route_ids[:, :, None] == jnp.arange(expert_count, dtype=jnp.int32)[None, None, :]
    hit_counts = route_hit.astype(jnp.int32).sum(1)
    earlier = jnp.cumsum(hit_counts, axis=0) - hit_counts
    slot_of = jnp.where(hit_counts > 0, earlier, -1).astype(f32)
    gate_of = jnp.sum(jnp.where(route_hit, gates[0][:, :, None], 0.0), axis=1)
    table = jnp.concatenate([slot_of.T, gate_of.T], 0)
    table_own = lax.all_gather(table, "exp", axis=0, tiled=False)
    table_sib = swap(table_own)
    tables = jnp.stack([table_own, table_sib], 1).reshape(
        n_exp, 2, 2, n_exp, 2, half_experts, token_count
    )
    tables = lax.dynamic_index_in_dim(tables, z_index, 3, keepdims=False)
    tables = lax.dynamic_index_in_dim(tables, core, 3, keepdims=False)

    cot_chunks = []
    for step in range(n_exp):
        own = out_grad[0] if step == 0 else across(out_grad[0], step)
        cot_chunks.append(jnp.stack([own, swap(own)]))

    hidden = residual_in[0].astype(f32)
    seg_two = jnp.stack([segments[0], swap(segments)[0]])
    seg_here = lax.dynamic_slice_in_dim(seg_two, span_index * token_count, token_count, 1)
    valid_two = (seg_here > 0).astype(f32).reshape(2 * token_count, 1)
    valid_rows = valid_two[:token_count]
    positions = span_index * token_count + jnp.arange(token_count, dtype=jnp.int32)
    cos_one, sin_one = rope_tables(positions)
    cosine_table, sine_values = jnp.concatenate([cos_one] * 2, 0), jnp.concatenate([sin_one] * 2, 0)
    inv_attn = lax.rsqrt(jnp.mean(hidden * hidden, axis=-1, keepdims=True) + EPS)
    normed_own = (hidden * inv_attn * gain_attn).astype(bf16)
    normed_two = jnp.concatenate([normed_own, swap(normed_own)], 0)
    kv_raw = jnp.dot(normed_two, w_qkv[:, q_width:], preferred_element_type=f32)
    k_raw = kv_raw[:, :kv_width].reshape(-1, groups, HEAD_DIM)
    value_rows = kv_raw[:, kv_width:].astype(bf16)
    inv_key = lax.rsqrt(jnp.mean(k_raw * k_raw, axis=-1, keepdims=True) + EPS)
    key_rows = rotate(k_raw * inv_key * gain_key_f, cosine_table, sine_values).astype(bf16)
    kv_here = jnp.concatenate([key_rows.reshape(-1, kv_width), value_rows], 1).reshape(
        2, token_count, 2 * kv_width
    )
    if n_ctx == 2:
        kv_there = lax.ppermute(kv_here, "ctx", [(0, 1), (1, 0)])
        kv_full = jnp.concatenate(
            [pick(span_index, kv_here, kv_there), pick(span_index, kv_there, kv_here)], 1
        )
    else:
        kv_full = lax.all_gather(kv_here, "ctx", axis=1, tiled=True)
    q_raw = jnp.dot(normed_two, w_qkv[:, :q_width], preferred_element_type=f32).reshape(
        -1, heads, HEAD_DIM
    )
    inv_query = lax.rsqrt(jnp.mean(q_raw * q_raw, axis=-1, keepdims=True) + EPS)
    query_rows = rotate(q_raw * inv_query * gain_query_f, cosine_table, sine_values).astype(bf16)
    grouped_queries = query_rows.reshape(2, token_count, groups, heads_per_group, HEAD_DIM)
    key_heads = kv_full[..., :kv_width].reshape(2, sequence_length, groups, HEAD_DIM)
    value_heads = kv_full[..., kv_width:].reshape(2, sequence_length, groups, HEAD_DIM)
    key_pos = jnp.arange(sequence_length, dtype=jnp.int32)
    allowed = (seg_here[:, :, None] == seg_two[:, None, :]) & (
        positions[None, :, None] >= key_pos[None, None, :]
    )

    def head_scores(s, g):
        raw_scores = (
            jnp.einsum(
                "qgd,kd->gqk", grouped_queries[s, :, g], key_heads[s, :, g], preferred_element_type=f32
            )
            * score_scale
        )
        return jnp.where(allowed[s][None], raw_scores, MASKED)

    mixed_parts, log_totals = [], {}
    for s in range(2):
        for g in range(groups):
            scores = head_scores(s, g)
            row_peak = jnp.max(scores, axis=-1, keepdims=True)
            exp_scores = jnp.exp(scores - row_peak)
            row_total = jnp.sum(exp_scores, axis=-1, keepdims=True)
            probs_low = (exp_scores / row_total).astype(bf16)
            mixed_parts.append(
                jnp.einsum("gqk,kd->qgd", probs_low, value_heads[s, :, g], preferred_element_type=f32)
            )
            log_totals[s, g] = row_peak + jnp.log(row_total)
    mixed_heads = jnp.stack(mixed_parts).reshape(2, groups, token_count, heads_per_group * HEAD_DIM)
    mixed_heads = mixed_heads.transpose(0, 2, 1, 3).reshape(2 * token_count, q_width)
    mixed_low = (mixed_heads * valid_two).astype(bf16)
    attn_partial = jnp.dot(mixed_low, w_out, preferred_element_type=f32)
    attn_out = attn_partial[:token_count] + swap(attn_partial[token_count:])
    middle = hidden + attn_out
    inv_mlp = lax.rsqrt(jnp.mean(middle * middle, axis=-1, keepdims=True) + EPS)
    normed_mlp = (middle * inv_mlp * gain_mlp_f).astype(bf16)

    row_chunks, val_chunks, product_chunks, gg_chunks, gu_chunks = [], [], [], [], []
    grad_total, out_total = None, None
    for step in range(n_exp):
        own = normed_mlp if step == 0 else across(normed_mlp, step)
        tokens = jnp.stack([own, swap(own)])
        table_here = lax.dynamic_index_in_dim(tables, z_index ^ step, 0, keepdims=False)
        slot_here, gate_here = table_here[:, 0], table_here[:, 1]
        hits = slot_here[:, :, None, :] == jnp.arange(slots, dtype=f32)[None, None, :, None]
        one_hot = hits.astype(bf16)
        gate_row = jnp.sum(jnp.where(hits, gate_here[:, :, None, :], 0.0), -1, keepdims=True)
        x_rows = jnp.einsum("sert,std->serd", one_hot, tokens, preferred_element_type=f32).astype(bf16)
        cot_rows = jnp.einsum("sert,std->serd", one_hot, cot_chunks[step], preferred_element_type=f32)
        grad_val = (gate_row * cot_rows).astype(bf16)
        gate_part = jnp.einsum("serd,edf->serf", x_rows, w_gate, preferred_element_type=f32)
        up_part = jnp.einsum("serd,edf->serf", x_rows, w_up, preferred_element_type=f32)
        sigmoid_gate = jax.nn.sigmoid(gate_part)
        silu_gate = gate_part * sigmoid_gate
        product = (silu_gate * up_part).astype(bf16)
        expert_val = jnp.einsum("serf,efd->serd", product, w_down, preferred_element_type=f32)
        weighted = (gate_row * expert_val).astype(bf16)
        grad_product = jnp.einsum("serd,efd->serf", grad_val, w_down, preferred_element_type=f32)
        grad_gate = (
            grad_product * up_part * sigmoid_gate * (1.0 + gate_part * (1.0 - sigmoid_gate))
        ).astype(bf16)
        grad_up = (grad_product * silu_gate).astype(bf16)
        grad_rows = (
            jnp.einsum("serf,edf->serd", grad_gate, w_gate, preferred_element_type=f32)
            + jnp.einsum("serf,edf->serd", grad_up, w_up, preferred_element_type=f32)
        ).astype(bf16)
        grad_part = jnp.einsum("sert,serd->std", one_hot, grad_rows, preferred_element_type=f32)
        out_part = jnp.einsum("sert,serd->std", one_hot, weighted, preferred_element_type=f32)
        grad_part = grad_part[0] + swap(grad_part[1].astype(bf16)).astype(f32)
        out_part = out_part[0] + swap(out_part[1].astype(bf16)).astype(f32)
        if step:
            grad_part = across(grad_part.astype(bf16), step).astype(f32)
            out_part = across(out_part.astype(bf16), step).astype(f32)
        grad_total = grad_part if grad_total is None else grad_total + grad_part
        out_total = out_part if out_total is None else out_total + out_part
        row_chunks.append(x_rows)
        val_chunks.append(grad_val)
        product_chunks.append(product)
        gg_chunks.append(grad_gate)
        gu_chunks.append(grad_up)
    grad_normed_mlp, expert_out = grad_total, out_total
    final_out = middle + expert_out

    stats = jnp.zeros((8, 128), f32)
    for index, value in enumerate(
        (
            jnp.sum(hidden * hidden * valid_rows),
            jnp.sum(attn_out * attn_out * valid_rows),
            jnp.sum(expert_out * expert_out * valid_rows),
            jnp.sum(valid_rows),
        )
    ):
        stats = stats.at[0, index].set(value)
    for axis, count in (("seq", n_seq), ("ctx", n_ctx), ("exp", n_exp)):
        hop = 1
        while hop < count:
            stats = stats + lax.ppermute(stats, axis, [(i, i ^ hop) for i in range(count)])
            hop *= 2
    rms_stats = jnp.sqrt(stats[0, :3] / (stats[0, 3] * model_width))

    x_all, val_all, product_all, gg_all, gu_all = (
        jnp.stack(chunks) for chunks in (row_chunks, val_chunks, product_chunks, gg_chunks, gu_chunks)
    )

    def scatter_expert(grad):
        depth = grad.shape[1] // (n_seq * n_ctx)
        blocks = grad.astype(bf16).reshape(half_experts, n_y, 2, n_ctx, depth, grad.shape[2])
        blocks = blocks.transpose(1, 3, 2, 0, 4, 5).reshape(
            n_y * n_ctx, 2, half_experts, depth, grad.shape[2]
        )
        part = lax.psum_scatter(
            blocks,
            ("seq", "ctx"),
            scatter_dimension=0,
            tiled=True,
            axis_index_groups=group_plane,
        )[0]
        mine = pick(core, part[0], part[1])
        theirs = swap(pick(core, part[1], part[0]))
        return jnp.concatenate([pick(core, mine, theirs), pick(core, theirs, mine)], 0).astype(f32)

    down_grad = scatter_expert(
        jnp.einsum("cserf,cserd->efd", product_all, val_all, preferred_element_type=f32)
    )
    gate_grad = scatter_expert(
        jnp.einsum("cserd,cserf->edf", x_all, gg_all, preferred_element_type=f32)
    )
    up_grad = scatter_expert(
        jnp.einsum("cserd,cserf->edf", x_all, gu_all, preferred_element_type=f32)
    )

    cotangent = out_grad[0].astype(f32)
    mlp_gain_grad = jnp.sum(grad_normed_mlp * middle * inv_mlp, axis=0)
    grad_middle = cotangent + norm_back(grad_normed_mlp, middle, inv_mlp, gain_mlp_f)
    grad_attn_own = grad_middle.astype(bf16)
    grad_attn = jnp.concatenate([grad_attn_own, swap(grad_attn_own)], 0)
    o_grad_part = contract_rows(mixed_low, grad_attn).astype(bf16)
    o_proj_grad = lax.psum_scatter(
        o_grad_part,
        ("seq", "ctx", "exp"),
        scatter_dimension=0,
        tiled=True,
        axis_index_groups=group_all,
    ).astype(f32)
    mixture_gradient = contract_cols(grad_attn, w_out).astype(bf16) * valid_two.astype(bf16)
    group_gradient = mixture_gradient.reshape(
        2, token_count, groups, heads_per_group, HEAD_DIM
    )
    grad_q_parts, key_parts, value_parts = [], [], []
    for s in range(2):
        for g in range(groups):
            probs = jnp.exp(head_scores(s, g) - log_totals[s, g])
            grad_head = group_gradient[s, :, g]
            grad_probs = jnp.einsum(
                "qgd,kd->gqk", grad_head, value_heads[s, :, g], preferred_element_type=f32
            )
            inner_sum = jnp.sum(probs * grad_probs, axis=-1, keepdims=True)
            grad_scores = (probs * (grad_probs - inner_sum)).astype(bf16)
            grad_q_parts.append(
                jnp.einsum(
                    "gqk,kd->qgd", grad_scores, key_heads[s, :, g], preferred_element_type=f32
                )
                * score_scale
            )
            key_parts.append(
                jnp.einsum(
                    "gqk,qgd->kd", grad_scores, grouped_queries[s, :, g], preferred_element_type=f32
                )
                * score_scale
            )
            value_parts.append(
                jnp.einsum("gqk,qgd->kd", probs.astype(bf16), grad_head, preferred_element_type=f32)
            )
    grad_queries = (
        jnp.stack(grad_q_parts)
        .reshape(2, groups, token_count, heads_per_group, HEAD_DIM)
        .transpose(0, 2, 1, 3, 4)
        .reshape(2 * token_count, heads, HEAD_DIM)
    )
    kv_grad = jnp.concatenate(
        [
            jnp.stack([jnp.concatenate(parts[s * groups : (s + 1) * groups], 1) for s in range(2)])
            for parts in (key_parts, value_parts)
        ],
        2,
    )
    if n_ctx == 2:
        first, second = kv_grad[:, :token_count], kv_grad[:, token_count:]
        received = lax.ppermute(
            pick(span_index, second, first).astype(bf16), "ctx", [(0, 1), (1, 0)]
        )
        kv_grad_here = pick(span_index, first, second) + received.astype(f32)
    else:
        kv_grad_here = lax.psum_scatter(
            kv_grad.astype(bf16), "ctx", scatter_dimension=1, tiled=True
        ).astype(f32)
    kv_grad_here = kv_grad_here.reshape(2 * token_count, 2 * kv_width)
    grad_qn = inverse_rotation(grad_queries, cosine_table, sine_values)
    q_gain_grad = jnp.sum(grad_qn * q_raw * inv_query, axis=(0, 1))
    grad_q_raw = norm_back(grad_qn, q_raw, inv_query, gain_query_f).astype(bf16)
    grad_kn = inverse_rotation(
        kv_grad_here[:, :kv_width].reshape(-1, groups, HEAD_DIM), cosine_table, sine_values
    )
    k_gain_grad = jnp.sum(grad_kn * k_raw * inv_key, axis=(0, 1))
    grad_k_raw = norm_back(grad_kn, k_raw, inv_key, gain_key_f).astype(bf16)
    grad_qkv = jnp.concatenate(
        [
            grad_q_raw.reshape(-1, q_width),
            grad_k_raw.reshape(-1, kv_width),
            kv_grad_here[:, kv_width:].astype(bf16),
        ],
        1,
    )
    normed_partial = contract_cols(grad_qkv, w_qkv)
    grad_normed = normed_partial[:token_count] + swap(normed_partial[token_count:])
    attn_gain_grad = jnp.sum(grad_normed * hidden * inv_attn, axis=0)
    grad_hidden = grad_middle + norm_back(grad_normed, hidden, inv_attn, gain_attn)

    extra_grad = jnp.zeros((devices, rows, 128), f32)
    extra_grad = extra_grad.at[:, 0, :rows].set(attn_gain_grad.reshape(devices, rows))
    extra_grad = extra_grad.at[:, 0, rows : 2 * rows].set(mlp_gain_grad.reshape(devices, rows))
    extra_grad = extra_grad.at[:, 1, :gain_rows].set(q_gain_grad.reshape(devices, gain_rows))
    extra_grad = extra_grad.at[:, 1, gain_rows : 2 * gain_rows].set(
        k_gain_grad.reshape(devices, gain_rows)
    )
    w_grad = jnp.concatenate(
        [
            contract_rows(normed_two, grad_qkv).astype(bf16),
            extra_grad.reshape(model_width, 128).astype(bf16),
        ],
        1,
    )
    w_grad = (
        w_grad.reshape(n_y, 2, n_ctx * n_exp, rows, width + 128)
        .transpose(0, 2, 1, 3, 4)
        .reshape(devices // 2, 2, rows, width + 128)
    )
    w_grad = lax.psum_scatter(
        w_grad,
        ("seq", "ctx", "exp"),
        scatter_dimension=0,
        tiled=True,
        axis_index_groups=group_all,
    )[0]
    grad_mine = pick(core, w_grad[0], w_grad[1])
    grad_theirs = swap(pick(core, w_grad[1], w_grad[0]))
    even = pick(core, grad_mine, grad_theirs).astype(f32)
    odd = pick(core, grad_theirs, grad_mine).astype(f32)

    def columns(start, size):
        step = size // groups
        parts = []
        for g in range(groups):
            parts += [half[:, start + g * step : start + (g + 1) * step] for half in (even, odd)]
        return jnp.concatenate(parts, 1)

    extra_total = even[:, width:] + odd[:, width:]
    return (
        final_out.astype(bf16)[None],
        grad_hidden.astype(bf16)[None],
        extra_total[0, :rows],
        columns(0, q_width),
        columns(q_width, kv_width),
        columns(q_width + kv_width, kv_width),
        extra_total[1, :gain_rows],
        extra_total[1, gain_rows : 2 * gain_rows],
        o_proj_grad,
        extra_total[0, rows : 2 * rows],
        gate_grad,
        up_grad,
        down_grad,
        rms_stats,
    )


def solution(mesh):
    in_specs = (
        P(("seq", "exp"), "ctx", None),
        P(("seq", "exp"), None),
        P(("seq", "exp"), "ctx", None),
        P(("seq", "exp"), "ctx", None),
        P(("seq", "ctx", "exp")),
        P(("seq", "ctx", "exp"), None),
        P(("seq", "ctx", "exp"), None),
        P(("seq", "ctx", "exp"), None),
        P(("seq", "ctx", "exp")),
        P(("seq", "ctx", "exp")),
        P(("seq", "ctx", "exp"), None),
        P(("seq", "ctx", "exp")),
        P("exp", ("seq", "ctx"), None),
        P("exp", ("seq", "ctx"), None),
        P("exp", ("seq", "ctx"), None),
        P(("seq", "exp"), "ctx", None),
    )
    out_specs = (
        P(("seq", "exp"), "ctx", None),
        P(("seq", "exp"), "ctx", None),
        P(("seq", "ctx", "exp")),
        P(("seq", "ctx", "exp"), None),
        P(("seq", "ctx", "exp"), None),
        P(("seq", "ctx", "exp"), None),
        P(("seq", "ctx", "exp")),
        P(("seq", "ctx", "exp")),
        P(("seq", "ctx", "exp"), None),
        P(("seq", "ctx", "exp")),
        P("exp", ("seq", "ctx"), None),
        P("exp", ("seq", "ctx"), None),
        P("exp", ("seq", "ctx"), None),
        P(),
    )
    return jax.shard_map(
        on_device, mesh=mesh, in_specs=in_specs, out_specs=out_specs, check_vma=False
    )
```

```python
import functools

import jax
import jax.numpy as jnp
from jax import lax
from jax.experimental import pallas as pl
from jax.experimental.pallas import tpu as pltpu
from jax.sharding import PartitionSpec as P

QUERY_HEADS = 32
KEY_VALUE_HEADS = 4
HEAD_DIM = 128


EPS = 1e-06
ROPE_BASE = 1000000.0
MASKED = -1e30


def contract_rows(first_op, second_op):
    return lax.dot_general(
        first_op, second_op, (((0,), (0,)), ((), ())), preferred_element_type=jnp.float32
    )


def contract_cols(first_op, second_op):
    return lax.dot_general(
        first_op, second_op, (((1,), (1,)), ((), ())), preferred_element_type=jnp.float32
    )


def rope_tables(positions):
    half_dim = HEAD_DIM // 2
    inverse = ROPE_BASE ** (-jnp.arange(half_dim, dtype=jnp.float32) * 2.0 / HEAD_DIM)
    angles = positions.astype(jnp.float32)[:, None] * inverse[None, :]
    cosine_table = jnp.cos(angles)
    sine_values = jnp.sin(angles)
    return (
        jnp.concatenate([cosine_table, cosine_table], -1),
        jnp.concatenate([sine_values, sine_values], -1),
    )


def inverse_rotation(gradient, cosine_table, sine_values):
    half_dim = gradient.shape[-1] // 2
    scaled = gradient * sine_values[:, None, :]
    return gradient * cosine_table[:, None, :] + jnp.concatenate(
        [scaled[..., half_dim:], -scaled[..., :half_dim]], -1
    )


def norm_back(gradient, source, inverse, gain_vec):
    scaled = gradient * gain_vec
    return inverse * scaled - source * inverse**3 * jnp.mean(
        scaled * source, axis=-1, keepdims=True
    )


def neighbours(n_exp):
    seq, x, z = lax.axis_index("seq"), lax.axis_index("ctx"), lax.axis_index("exp")
    y, core = seq // 2, seq % 2
    ids = {
        "core": {"seq": 2 * y + 1 - core},
        "x": {"ctx": 1 - x},
        "y": {"seq": 2 * (1 - y) + core},
        "up": {"exp": z + 1},
        "down": {"exp": z - 1},
    }
    return x, y, z, core, ids


def greet(z, n_exp, ids, names):
    barrier = pltpu.get_barrier_semaphore()
    count = 0
    for name in names:
        if name in ("up", "down"):
            there = (z < n_exp - 1) if name == "up" else (z > 0)

            @pl.when(there)
            def _():
                pl.semaphore_signal(
                    barrier, inc=1, device_id=ids[name], device_id_type=pl.DeviceIdType.MESH
                )

            count = count + there.astype(jnp.int32)
        else:
            pl.semaphore_signal(
                barrier, inc=1, device_id=ids[name], device_id_type=pl.DeviceIdType.MESH
            )
            count = count + 1
    pl.semaphore_wait(barrier, count)


def gather_kernel(n_exp, mine_ref, other_ref, full_ref, local_sem, core_sems, z_sems, x_sems, y_sems, xf_sems, yf_sems):
    x, y, z, core, ids = neighbours(n_exp)
    greet(z, n_exp, ids, ("core", "x", "y", "up", "down"))
    here, beside, across = 2 * y + x, 2 * y + 1 - x, 2 * (1 - y) + x

    def remote(part, sems, slot, name):
        return pltpu.make_async_remote_copy(
            src_ref=part,
            dst_ref=part,
            send_sem=sems.at[0, slot],
            recv_sem=sems.at[1, slot],
            device_id=ids[name],
            device_id_type=pl.DeviceIdType.MESH,
        )

    local = pltpu.make_async_copy(mine_ref, full_ref.at[here, z, core], local_sem)
    local.start()
    to_core = pltpu.make_async_remote_copy(
        src_ref=other_ref,
        dst_ref=full_ref.at[here, z, core],
        send_sem=core_sems.at[0],
        recv_sem=core_sems.at[1],
        device_id=ids["core"],
        device_id_type=pl.DeviceIdType.MESH,
    )
    to_core.start()
    to_core.wait()
    local.wait()

    def source(label):
        hop = (label + 1) // 2
        if label == 0:
            return z, None
        return (z - hop, z >= hop) if label % 2 else (z + hop, z + hop < n_exp)

    labels = range(2 * n_exp - 1)

    def guarded(condition, action):
        if condition is None:
            action()
        else:
            pl.when(condition)(action)

    def z_copy(label, name):
        part, _ = source(label)
        slot = label + 1 if label % 2 else label + 1
        if label == 0:
            slot = 0 if name == "up" else 1
        else:
            slot = label + 1
        return remote(full_ref.at[here, part], z_sems, slot, name)

    def z_sends(label):
        part, there = source(label)
        for name in ("up", "down") if label == 0 else (("up",) if label % 2 else ("down",)):
            room = (z < n_exp - 1) if name == "up" else (z > 0)
            yield name, room if there is None else there & room

    def z_arrival(label):
        hop = (label + 1) // 2
        name = "up" if label % 2 else "down"
        slot = (label - 1) if hop > 1 else (0 if name == "up" else 1)
        part, _ = source(label)
        remote(full_ref.at[here, part], z_sems, slot, name).wait_recv()

    def spread(label):
        part, there = source(label)

        def action():
            remote(full_ref.at[here, part], x_sems, label, "x").start()
            remote(full_ref.at[here, part], y_sems, label, "y").start()

        guarded(there, action)
        for name, condition in z_sends(label):
            pl.when(condition)(lambda name=name: z_copy(label, name).start())

    def turn(label):
        part, there = source(label)

        def action():
            remote(full_ref.at[beside, part], x_sems, label, "x").wait_recv()
            remote(full_ref.at[beside, part, 0], xf_sems, label, "y").start()
            remote(full_ref.at[across, part], y_sems, label, "y").wait_recv()
            remote(full_ref.at[across, part, 1], yf_sems, label, "x").start()

        guarded(there, action)

    spread(0)
    for hop in range(1, n_exp):
        for label in (2 * hop - 1, 2 * hop):
            part, there = source(label)

            def action(label=label):
                z_arrival(label)

            pl.when(there)(action)
            spread(label)
        for label in (0,) if hop == 1 else (2 * hop - 3, 2 * hop - 2):
            turn(label)
    for label in (2 * n_exp - 3, 2 * n_exp - 2):
        turn(label)
    opposite = 2 * (1 - y) + 1 - x
    for label in labels:
        part, there = source(label)

        def action(label=label, part=part):
            remote(full_ref.at[here, part], x_sems, label, "x").wait_send()
            remote(full_ref.at[here, part], y_sems, label, "y").wait_send()
            remote(full_ref.at[beside, part, 0], xf_sems, label, "y").wait_send()
            remote(full_ref.at[across, part, 1], yf_sems, label, "x").wait_send()
            remote(full_ref.at[opposite, part, 0], xf_sems, label, "y").wait_recv()
            remote(full_ref.at[opposite, part, 1], yf_sems, label, "x").wait_recv()

        guarded(there, action)
        for name, condition in z_sends(label):
            pl.when(condition)(lambda label=label, name=name: z_copy(label, name).wait_send())


def gather_chips(mine, other, n_exp):
    labels = 2 * n_exp - 1
    any_spec = pl.BlockSpec(memory_space=pl.ANY)
    vmem_spec = pl.BlockSpec(memory_space=pltpu.VMEM)
    pair = lambda count: pltpu.SemaphoreType.DMA((2, count))
    return pl.pallas_call(
        functools.partial(gather_kernel, n_exp),
        in_specs=[vmem_spec, vmem_spec],
        out_specs=any_spec,
        out_shape=jax.ShapeDtypeStruct((4, n_exp, 2) + mine.shape, mine.dtype),
        scratch_shapes=[
            pltpu.SemaphoreType.DMA,
            pltpu.SemaphoreType.DMA((2,)),
            pair(2 * n_exp),
            pair(labels),
            pair(labels),
            pair(labels),
            pair(labels),
        ],
        compiler_params=pltpu.CompilerParams(collective_id=1, has_side_effects=True),
        name="gather_chips",
    )(mine, other)


def exchange_kernel(n_exp, token_ref, table_ref, tokens_ref, tables_ref, z_sems, core_sems):
    x, y, z, core, ids = neighbours(n_exp)
    greet(z, n_exp, ids, ("core", "up", "down"))
    sources, results = (token_ref, table_ref), (tokens_ref, tables_ref)

    def remote(which, label, sems, slot, name):
        there = results[which].at[source(label)[0], core]
        return pltpu.make_async_remote_copy(
            src_ref=sources[which] if label == 0 else there,
            dst_ref=there,
            send_sem=sems.at[0, which, slot],
            recv_sem=sems.at[1, which, slot],
            device_id=ids[name],
            device_id_type=pl.DeviceIdType.MESH,
        )

    def source(label):
        hop = (label + 1) // 2
        if label == 0:
            return z, None
        return (z - hop, z >= hop) if label % 2 else (z + hop, z + hop < n_exp)

    def guarded(condition, action):
        if condition is None:
            action()
        else:
            pl.when(condition)(action)

    def each(label, sems, slot, name, method):
        for which in range(2):
            getattr(remote(which, label, sems, slot, name), method)()

    def z_sends(label, method):
        part, there = source(label)
        for name in ("up", "down") if label == 0 else (("up",) if label % 2 else ("down",)):
            room = (z < n_exp - 1) if name == "up" else (z > 0)
            slot = (0 if name == "up" else 1) if label == 0 else label + 1
            condition = room if there is None else there & room
            pl.when(condition)(lambda name=name, slot=slot: each(label, z_sems, slot, name, method))

    z_sends(0, "start")
    each(0, core_sems, 0, "core", "start")
    for hop in range(1, n_exp):
        for label in (2 * hop - 1, 2 * hop):
            part, there = source(label)
            name = "up" if label % 2 else "down"
            slot = (label - 1) if hop > 1 else (0 if name == "up" else 1)
            guarded(there, lambda: each(label, z_sems, slot, name, "wait_recv"))
            z_sends(label, "start")
            guarded(there, lambda: each(label, core_sems, label, "core", "start"))
    for label in range(2 * n_exp - 1):
        part, there = source(label)
        z_sends(label, "wait_send")
        guarded(there, lambda: each(label, core_sems, label, "core", "wait"))


def exchange_column(tokens, table, n_exp):
    any_spec = pl.BlockSpec(memory_space=pl.ANY)
    labels = 2 * n_exp - 1
    return pl.pallas_call(
        functools.partial(exchange_kernel, n_exp),
        in_specs=[any_spec] * 2,
        out_specs=[any_spec] * 2,
        out_shape=[
            jax.ShapeDtypeStruct((n_exp, 2) + a.shape, a.dtype) for a in (tokens, table)
        ],
        scratch_shapes=[
            pltpu.SemaphoreType.DMA((2, 2, 2 * n_exp)),
            pltpu.SemaphoreType.DMA((2, 2, labels)),
        ],
        compiler_params=pltpu.CompilerParams(collective_id=3, has_side_effects=True),
        cost_estimate=pl.CostEstimate(
            flops=0, bytes_accessed=16 * n_exp * tokens.size, transcendentals=0
        ),
        name="exchange_column",
    )(tokens, table)


def scatter_kernel(
    n_exp,
    normed_ref,
    grad_ref,
    kv_grad_ref,
    extra_ref,
    after_ref,
    mine_ref,
    theirs_ref,
    turned,
    part,
    from_x,
    from_y,
    second_x,
    second_y,
    total,
    from_z,
    from_core,
    x_sems,
    y_sems,
    x2_sems,
    y2_sems,
    z_sems,
    core_sems,
):
    bf16, f32 = jnp.bfloat16, jnp.float32
    x, y, z, core, ids = neighbours(n_exp)
    barrier = pltpu.get_barrier_semaphore()
    columns = [{"exp": (z + k) % n_exp} for k in range(1, n_exp)]
    for there in [ids["core"], ids["x"], ids["y"]] + columns:
        pl.semaphore_signal(barrier, inc=1, device_id=there, device_id_type=pl.DeviceIdType.MESH)
    pl.semaphore_wait(barrier, 2 + n_exp)

    def remote(source, target, sems, slot, there):
        return pltpu.make_async_remote_copy(
            src_ref=source,
            dst_ref=target,
            send_sem=sems.at[0, slot],
            recv_sem=sems.at[1, slot],
            device_id=there,
            device_id_type=pl.DeviceIdType.MESH,
        )

    rows = mine_ref.shape[0]
    q_width, width = grad_ref.shape[1], grad_ref.shape[1] + kv_grad_ref.shape[1]
    turned[...] = normed_ref[...].T
    steps = range(n_exp)

    def first_copies(k):
        return [
            remote(part.at[k, 1 - x, :, 0], from_x.at[k], x_sems, k, ids["x"]),
            remote(part.at[k, :, 1 - y, 1], from_y.at[k], y_sems, k, ids["y"]),
        ]

    def second_copies(k):
        return [
            remote(part.at[k, x, 1 - y, 0], second_x.at[k], x2_sems, k, ids["y"]),
            remote(part.at[k, 1 - x, y, 1], second_y.at[k], y2_sems, k, ids["x"]),
        ]

    def z_copy(k):
        return remote(
            total.at[k], from_z.at[k], z_sems, k, {"exp": (z + k + 1) % n_exp}
        )

    for k in steps:
        place = (z + k + 1) % n_exp
        blocks = []
        for px in range(2):
            for py in range(2):
                for c in range(2):
                    start = (((py * 2 + c) * 2 + px) * n_exp + place) * rows
                    blocks.append(turned[pl.ds(pl.multiple_of(start, rows), rows), :])
        block = jnp.concatenate(blocks, 0)
        grad = dot_plain(block, grad_ref[...]).astype(bf16)
        kv_grad = dot_plain(block, kv_grad_ref[...]).astype(bf16)
        i = 0
        for px in range(2):
            for py in range(2):
                for c in range(2):
                    part[k, px, py, c, :, :q_width] = grad[i * rows : (i + 1) * rows]
                    part[k, px, py, c, :, q_width:width] = kv_grad[i * rows : (i + 1) * rows]
                    part[k, px, py, c, :, width:] = extra_ref[py, c, px, place]
                    i += 1
        for copy in first_copies(k):
            copy.start()

    def second(k):
        along_x, along_y = first_copies(k)
        along_x.wait_recv()
        for py in range(2):
            part[k, x, py, 0] = (part[k, x, py, 0].astype(f32) + from_x[k, py].astype(f32)).astype(bf16)
        along_y.wait_recv()
        for px in range(2):
            part[k, px, y, 1] = (part[k, px, y, 1].astype(f32) + from_y[k, px].astype(f32)).astype(bf16)
        for copy in second_copies(k):
            copy.start()

    def third(k):
        along_y, along_x = second_copies(k)
        along_y.wait_recv()
        total[k, 0] = (part[k, x, y, 0].astype(f32) + second_x[k].astype(f32)).astype(bf16)
        along_x.wait_recv()
        total[k, 1] = (part[k, x, y, 1].astype(f32) + second_y[k].astype(f32)).astype(bf16)
        if k < n_exp - 1:
            z_copy(k).start()

    second(0)
    for k in range(1, n_exp):
        second(k)
        third(k - 1)
    third(n_exp - 1)
    result = total[n_exp - 1].astype(f32)
    for k in range(n_exp - 1):
        z_copy(k).wait_recv()
        result = result + from_z[k].astype(f32)
    total[n_exp - 1] = result.astype(bf16)
    to_core = remote(total.at[n_exp - 1, 1 - core], from_core, core_sems, 0, ids["core"])
    to_core.start()
    for k in steps:
        for copy in first_copies(k) + second_copies(k) + ([z_copy(k)] if k < n_exp - 1 else []):
            copy.wait_send()
    to_core.wait()
    mine_ref[...] = total[n_exp - 1, core].astype(f32)
    theirs_ref[...] = from_core[...].astype(f32)


def dense_grad_scatter(normed, grad, kv_grad, extra, after, n_exp):
    bf16 = jnp.bfloat16
    rows, model = extra.shape[4], normed.shape[1]
    width = grad.shape[1] + kv_grad.shape[1] + extra.shape[5]
    block = (rows, width)
    vmem = lambda *lead: pltpu.VMEM(lead + block, bf16)
    pair = lambda count: pltpu.SemaphoreType.DMA((2, count))
    spec = pl.BlockSpec(memory_space=pltpu.VMEM)
    return pl.pallas_call(
        functools.partial(scatter_kernel, n_exp),
        in_specs=[spec] * 4 + [pl.BlockSpec(memory_space=pl.ANY)],
        out_specs=[spec] * 2,
        out_shape=[jax.ShapeDtypeStruct(block, jnp.float32)] * 2,
        scratch_shapes=[
            pltpu.VMEM((model, normed.shape[0]), bf16),
            vmem(n_exp, 2, 2, 2),
            vmem(n_exp, 2),
            vmem(n_exp, 2),
            vmem(n_exp),
            vmem(n_exp),
            vmem(n_exp, 2),
            vmem(n_exp, 2),
            vmem(),
            pair(n_exp),
            pair(n_exp),
            pair(n_exp),
            pair(n_exp),
            pair(n_exp),
            pair(1),
        ],
        compiler_params=pltpu.CompilerParams(
            collective_id=2, has_side_effects=True, vmem_limit_bytes=60 * MIB
        ),
        cost_estimate=pl.CostEstimate(
            flops=2 * normed.shape[0] * model * width, bytes_accessed=16 * MIB, transcendentals=0
        ),
        name="dense_grad_scatter",
    )(normed, grad, kv_grad, extra, after)


def pick(core, first, second):
    return jnp.where(core == 0, first, second)


def column_halves(weight, core):
    width = weight.shape[1] // KEY_VALUE_HEADS
    parts = [weight[:, i * width : (i + 1) * width] for i in range(KEY_VALUE_HEADS)]
    mine = [pick(core, parts[i], parts[i + 1]) for i in range(0, KEY_VALUE_HEADS, 2)]
    other = [pick(core, parts[i + 1], parts[i]) for i in range(0, KEY_VALUE_HEADS, 2)]
    return mine, other


LOG2E = 1.4426950408889634
MIB = 1 << 20


def rotate_rows(vectors, cosine_table, signed_sine):
    return vectors * cosine_table + pltpu.roll(vectors, HEAD_DIM // 2, 1) * signed_sine


def rotate_rows_back(gradient, cosine_table, signed_sine):
    return gradient * cosine_table - pltpu.roll(gradient, HEAD_DIM // 2, 1) * signed_sine


def dot_cols(first, second):
    return lax.dot_general(
        first, second, (((1,), (1,)), ((), ())), preferred_element_type=jnp.float32
    )


def dot_plain(first, second):
    return jnp.dot(first, second, preferred_element_type=jnp.float32)


def projection_kernel(
    n_y, n_xz, normed_ref, weight_ref, gain_ref, cos_ref, sin_ref, raw_ref, low_ref, ordered_ref, *, plain
):
    pieces = [
        weight_ref[y * n_xz + i, c] for y in range(n_y) for c in range(2) for i in range(n_xz)
    ]
    weight = jnp.concatenate(pieces, 0)
    ordered_ref[...] = weight
    raw = dot_plain(normed_ref[...], weight)
    raw_ref[...] = raw
    tokens = cos_ref.shape[0]

    def normed_store():
        for h in range(2):
            columns = slice(h * HEAD_DIM, (h + 1) * HEAD_DIM)
            head = raw[:, columns]
            inverse = lax.rsqrt(jnp.mean(head * head, axis=-1, keepdims=True) + EPS)
            scaled = head * inverse * gain_ref[...]
            for s in range(2):
                part = slice(s * tokens, (s + 1) * tokens)
                low_ref[part, columns] = rotate_rows(
                    scaled[part], cos_ref[...], sin_ref[...]
                ).astype(jnp.bfloat16)

    if plain is None:
        normed_store()
    else:
        pl.when(pl.program_id(0) != plain)(normed_store)

        @pl.when(pl.program_id(0) == plain)
        def _():
            low_ref[...] = raw.astype(jnp.bfloat16)


def project(normed, gathered, first_block, blocks, gain, cos, sin, n_y, plain=None):
    total, model = normed.shape
    n_yxz, _, rows, _ = gathered.shape
    width = 2 * HEAD_DIM
    fixed = lambda j: (0, 0)
    moving = lambda j: (0, j)
    return pl.pallas_call(
        functools.partial(projection_kernel, n_y, n_yxz // n_y, plain=plain),
        grid=(blocks,),
        in_specs=[
            pl.BlockSpec((total, model), fixed),
            pl.BlockSpec((n_yxz, 2, rows, width), lambda j: (0, 0, 0, j + first_block)),
            pl.BlockSpec((1, HEAD_DIM), fixed),
            pl.BlockSpec(cos.shape, fixed),
            pl.BlockSpec(sin.shape, fixed),
        ],
        out_specs=[
            pl.BlockSpec((total, width), moving),
            pl.BlockSpec((total, width), moving),
            pl.BlockSpec((model, width), moving),
        ],
        out_shape=[
            jax.ShapeDtypeStruct((total, blocks * width), jnp.float32),
            jax.ShapeDtypeStruct((total, blocks * width), jnp.bfloat16),
            jax.ShapeDtypeStruct((model, blocks * width), jnp.bfloat16),
        ],
        compiler_params=pltpu.CompilerParams(vmem_limit_bytes=56 * MIB),
        cost_estimate=pl.CostEstimate(
            flops=2 * total * model * blocks * width,
            bytes_accessed=total * model * 2 + blocks * width * (model * 4 + total * 6),
            transcendentals=0,
        ),
        name="project",
    )(normed, gathered, gain, cos, sin)


def mask_bias(seg_key, info):
    keys, tokens = seg_key.shape[0], info.shape[1]
    key_pos = lax.broadcasted_iota(jnp.int32, (keys, tokens), 0)
    allowed = (seg_key == info[0:1]) & (key_pos <= info[1:2])
    return jnp.where(allowed, 0.0, MASKED)


def key_tile(keys):
    return min(keys, 256)


def attention_kernel(info_ref, seg_ref, q_ref, k_ref, v_ref, mixed_ref, recip_ref, bias_ref, vt_ref):
    keys = k_ref.shape[1]
    tile = key_tile(keys)

    @pl.when((pl.program_id(1) == 0) & (pl.program_id(2) == 0))
    def _():
        bias_ref[...] = mask_bias(seg_ref[0], info_ref[0])

    @pl.when(pl.program_id(2) == 0)
    def _():
        vt_ref[...] = v_ref[0].astype(jnp.float32).T.astype(jnp.bfloat16)

    queries = q_ref[...]
    total, mixed = None, None
    for start in range(0, keys, tile):
        part = slice(start, start + tile)
        scores = dot_cols(k_ref[0, part], queries) * (HEAD_DIM**-0.5 * LOG2E) + bias_ref[part]
        weights = jnp.exp2(scores)
        tile_total = jnp.sum(weights, axis=0, keepdims=True)
        tile_mixed = dot_plain(vt_ref[:, part], weights.astype(jnp.bfloat16))
        total = tile_total if total is None else total + tile_total
        mixed = tile_mixed if mixed is None else mixed + tile_mixed
    recip = 1.0 / total
    recip_ref[0] = recip
    valid = (info_ref[0, 0:1] > 0).astype(jnp.float32)
    mixed_ref[...] = (mixed * (recip * valid)).T.astype(jnp.bfloat16)


def attention_specs(tokens, keys, groups, per_group):
    head = pl.BlockSpec((tokens, HEAD_DIM), lambda s, g, h: (s, g * per_group + h))
    return dict(
        info=pl.BlockSpec((1, 8, tokens), lambda s, g, h: (s, 0, 0)),
        seg=pl.BlockSpec((1, keys, 1), lambda s, g, h: (s, 0, 0)),
        head=head,
        key=pl.BlockSpec((1, keys, HEAD_DIM), lambda s, g, h: (s, 0, g)),
        value=pl.BlockSpec((1, keys, HEAD_DIM), lambda s, g, h: (s, 0, groups + g)),
        recip=pl.BlockSpec((1, 1, tokens), lambda s, g, h: ((s * groups + g) * per_group + h, 0, 0)),
    )


def attend(info, seg_keys, queries, kv_full, groups, per_group):
    tokens, keys = info.shape[2], seg_keys.shape[1]
    specs = attention_specs(tokens, keys, groups, per_group)
    steps = 2 * groups * per_group
    return pl.pallas_call(
        attention_kernel,
        grid=(2, groups, per_group),
        in_specs=[specs["info"], specs["seg"], specs["head"], specs["key"], specs["value"]],
        out_specs=[specs["head"], specs["recip"]],
        out_shape=[
            jax.ShapeDtypeStruct(queries.shape, jnp.bfloat16),
            jax.ShapeDtypeStruct((steps, 1, tokens), jnp.float32),
        ],
        scratch_shapes=[
            pltpu.VMEM((keys, tokens), jnp.float32),
            pltpu.VMEM((HEAD_DIM, keys), jnp.bfloat16),
        ],
        compiler_params=pltpu.CompilerParams(vmem_limit_bytes=48 * MIB),
        cost_estimate=pl.CostEstimate(
            flops=steps * 8 * tokens * keys * HEAD_DIM,
            bytes_accessed=queries.size * 4 + kv_full.size * 2,
            transcendentals=steps * tokens * keys,
        ),
        name="attend",
    )(info, seg_keys, queries, kv_full, kv_full)


def attention_back_kernel(
    info_ref,
    seg_ref,
    q_ref,
    k_ref,
    v_ref,
    mixed_ref,
    grad_ref,
    recip_ref,
    raw_ref,
    gain_ref,
    cos_ref,
    sin_ref,
    raw_grad_ref,
    key_grad_ref,
    value_grad_ref,
    gain_grad_ref,
    bias_ref,
    kt_ref,
):
    keys = k_ref.shape[1]
    tile = key_tile(keys)
    scale = HEAD_DIM**-0.5
    first = (pl.program_id(1) == 0) & (pl.program_id(2) == 0)

    @pl.when(first)
    def _():
        bias_ref[...] = mask_bias(seg_ref[0], info_ref[0])

    @pl.when(first & (pl.program_id(0) == 0))
    def _():
        gain_grad_ref[...] = jnp.zeros_like(gain_grad_ref)

    @pl.when(pl.program_id(2) == 0)
    def _():
        kt_ref[...] = k_ref[0].astype(jnp.float32).T.astype(jnp.bfloat16)
        key_grad_ref[...] = jnp.zeros_like(key_grad_ref)
        value_grad_ref[...] = jnp.zeros_like(value_grad_ref)

    queries, grad = q_ref[...], grad_ref[...]
    recip = recip_ref[0]
    overlap = grad.astype(jnp.float32) * mixed_ref[...].astype(jnp.float32)
    inner = jnp.sum(overlap.T, axis=0, keepdims=True)
    query_grad = None
    for start in range(0, keys, tile):
        part = slice(start, start + tile)
        scores = dot_cols(k_ref[0, part], queries) * (scale * LOG2E) + bias_ref[part]
        probs = jnp.exp2(scores) * recip
        grad_probs = dot_cols(v_ref[0, part], grad)
        grad_scores = (probs * (grad_probs - inner)).astype(jnp.bfloat16)
        value_grad_ref[0, part] += dot_plain(probs.astype(jnp.bfloat16), grad)
        key_grad_ref[0, part] += dot_plain(grad_scores, queries) * scale
        tile_grad = dot_plain(kt_ref[:, part], grad_scores)
        query_grad = tile_grad if query_grad is None else query_grad + tile_grad
    turned = rotate_rows_back((query_grad * scale).T, cos_ref[...], sin_ref[...])
    raw = raw_ref[...]
    inverse = lax.rsqrt(jnp.mean(raw * raw, axis=-1, keepdims=True) + EPS)
    unit = raw * inverse
    gain_grad_ref[0:1] += jnp.sum(turned * unit, axis=0, keepdims=True)
    scaled = turned * gain_ref[...]
    raw_grad_ref[...] = (
        inverse * (scaled - unit * jnp.mean(scaled * unit, axis=-1, keepdims=True))
    ).astype(jnp.bfloat16)


def attend_back(
    info, seg_keys, queries, kv_full, mixed, grad_mixed, recip, raw, gain, cos, sin, groups, per_group
):
    tokens, keys = info.shape[2], seg_keys.shape[1]
    specs = attention_specs(tokens, keys, groups, per_group)
    steps = 2 * groups * per_group
    fixed = lambda s, g, h: (0, 0)
    key_grad = jax.ShapeDtypeStruct((2, keys, groups * HEAD_DIM), jnp.float32)
    return pl.pallas_call(
        attention_back_kernel,
        grid=(2, groups, per_group),
        in_specs=[specs["info"], specs["seg"], specs["head"], specs["key"], specs["value"]]
        + [specs["head"], specs["head"], specs["recip"], specs["head"]]
        + [pl.BlockSpec(a.shape, fixed) for a in (gain, cos, sin)],
        out_specs=[specs["head"], specs["key"], specs["key"], pl.BlockSpec((8, HEAD_DIM), fixed)],
        out_shape=[
            jax.ShapeDtypeStruct(queries.shape, jnp.bfloat16),
            key_grad,
            key_grad,
            jax.ShapeDtypeStruct((8, HEAD_DIM), jnp.float32),
        ],
        scratch_shapes=[
            pltpu.VMEM((keys, tokens), jnp.float32),
            pltpu.VMEM((HEAD_DIM, keys), jnp.bfloat16),
        ],
        compiler_params=pltpu.CompilerParams(vmem_limit_bytes=48 * MIB),
        cost_estimate=pl.CostEstimate(
            flops=steps * 20 * tokens * keys * HEAD_DIM,
            bytes_accessed=queries.size * 12 + kv_full.size * 6,
            transcendentals=steps * tokens * keys,
        ),
        name="attend_back",
    )(
        info, seg_keys, queries, kv_full, kv_full, mixed, grad_mixed, recip, raw, gain, cos, sin
    )


def expert_kernel(
    here,
    place_ref,
    table_ref,
    own_ref,
    tokens_ref,
    own_cot_ref,
    sib_cot_ref,
    gate_w_ref,
    up_w_ref,
    down_w_ref,
    *refs,
):
    (x_ref, val_ref, product_ref, gate_grad_ref, up_grad_ref, out_ref, grad_ref) = refs[-12:-5]
    token_scr, cot_scr, out_scr, grad_scr, sems = refs[-5:]
    bf16 = jnp.bfloat16
    e, s = pl.program_id(0), pl.program_id(1)
    slots, tokens = x_ref.shape[1], token_scr.shape[1]
    chip, core = place_ref[0], place_ref[1]
    owner = jnp.where(s == 0, core, 1 - core)

    def copies(which):
        held_by = core if which == 0 else 1 - core
        tokens_from = own_ref if here and which == 0 else tokens_ref.at[chip, held_by]
        sources = (tokens_from, (own_cot_ref, sib_cot_ref)[which])
        return [
            pltpu.make_async_copy(source, scratch.at[which], sems.at[which, i])
            for i, (source, scratch) in enumerate(zip(sources, (token_scr, cot_scr)))
        ]

    @pl.when((e == 0) & (s == 0))
    def _():
        for which in range(2):
            for copy in copies(which):
                copy.start()
        for copy in copies(0):
            copy.wait()

    @pl.when((e == 0) & (s == 1))
    def _():
        for copy in copies(1):
            copy.wait()

    slot_ids = lax.broadcasted_iota(jnp.int32, (slots, tokens), 0).astype(jnp.float32)

    def hits_of(expert):
        return table_ref[chip, owner, pl.ds(place_ref[2] + expert, 1)] == slot_ids

    hits = hits_of(e)
    one_hot = hits.astype(jnp.float32).astype(bf16)
    gate_row = jnp.sum(jnp.where(hits, table_ref[chip, owner, pl.ds(place_ref[3] + e, 1)], 0.0), axis=1, keepdims=True)
    x_rows = dot_plain(one_hot, token_scr[s]).astype(bf16)
    x_ref[0] = x_rows
    grad_val = (gate_row * dot_plain(one_hot, cot_scr[s])).astype(bf16)
    val_ref[0] = grad_val
    gate_act = dot_plain(x_rows, gate_w_ref[0])
    up_act = dot_plain(x_rows, up_w_ref[0])
    sigmoid = 1.0 / (1.0 + jnp.exp(-gate_act))
    silu = gate_act * sigmoid
    product = (silu * up_act).astype(bf16)
    product_ref[0] = product
    grad_product = dot_cols(grad_val, down_w_ref[0])
    grad_gate = (grad_product * up_act * (sigmoid * (1.0 + gate_act * (1.0 - sigmoid)))).astype(bf16)
    grad_up = (grad_product * silu).astype(bf16)
    gate_grad_ref[0] = grad_gate
    up_grad_ref[0] = grad_up
    grad_rows = (dot_cols(grad_gate, gate_w_ref[0]) + dot_cols(grad_up, up_w_ref[0])).astype(bf16)
    weighted = (gate_row * dot_plain(product, down_w_ref[0])).astype(bf16)

    @pl.when(e == 0)
    def _():
        out_scr[s] = weighted
        grad_scr[s] = grad_rows

    @pl.when(e == 1)
    def _():
        before = hits_of(0).astype(jnp.float32).astype(bf16)
        for result, held, rows in ((grad_ref, grad_scr, grad_rows), (out_ref, out_scr, weighted)):
            combined = lax.dot_general(
                jnp.concatenate([before, one_hot], 0),
                jnp.concatenate([held[s], rows], 0),
                (((0,), (0,)), ((), ())),
                preferred_element_type=jnp.float32,
            )
            result[0] = combined.astype(bf16)


def run_experts(step, chips, place, tables, tokens, cots, weights, held):
    bf16 = jnp.bfloat16
    token_count, model = cots[0].shape
    w_gate, w_up, w_down = weights
    slots, ff = held["slots"], w_gate.shape[2]
    at_expert = lambda e, s: (e, 0, 0)
    row_spec = lambda width: pl.BlockSpec((1, slots, width), lambda e, s: (e, 2 * step + s, 0))
    any_spec = pl.BlockSpec(memory_space=pl.ANY)
    widths = (model, model, ff, ff, ff)
    earlier = held.get("rows", [])
    part_spec = pl.BlockSpec((1, token_count, model), lambda e, s: (e * s, 0, 0))
    part_shape = jax.ShapeDtypeStruct((2, token_count, model), bf16)
    results = pl.pallas_call(
        functools.partial(expert_kernel, tokens[0] is not None),
        grid=(2, 2),
        in_specs=[
            pl.BlockSpec(memory_space=pltpu.SMEM),
            pl.BlockSpec(tables.shape, lambda e, s: (0, 0, 0, 0)),
        ]
        + [any_spec] * 4
        + [
            pl.BlockSpec((1, model, ff), at_expert),
            pl.BlockSpec((1, model, ff), at_expert),
            pl.BlockSpec((1, ff, model), at_expert),
        ]
        + [any_spec] * len(earlier),
        out_specs=[row_spec(width) for width in widths] + [part_spec, part_spec],
        out_shape=[
            jax.ShapeDtypeStruct((2, 2 * chips * slots, width), bf16) for width in widths
        ]
        + [part_shape, part_shape],
        scratch_shapes=[
            pltpu.VMEM((2, token_count, model), bf16),
            pltpu.VMEM((2, token_count, model), bf16),
            pltpu.VMEM((2, slots, model), bf16),
            pltpu.VMEM((2, slots, model), bf16),
            pltpu.SemaphoreType.DMA((2, 2)),
        ],
        input_output_aliases={9 + i: i for i in range(len(earlier))},
        compiler_params=pltpu.CompilerParams(vmem_limit_bytes=62 * MIB),
        cost_estimate=pl.CostEstimate(
            flops=4 * (12 * slots * model * ff + 8 * slots * token_count * model),
            bytes_accessed=3 * w_gate.size * 2 + 4 * slots * (2 * model + 3 * ff) * 2 + 16 * token_count * model,
            transcendentals=4 * slots * ff,
        ),
        name="experts",
    )(place, tables, tokens[1] if tokens[0] is None else tokens[0], tokens[1], *cots, w_gate, w_up, w_down, *earlier)
    held["rows"] = results[:5]
    return results[5], results[6]


def weight_grad_kernel(
    n_y, n_ctx, after_ref, x_ref, val_ref, product_ref, gg_ref, gu_ref, gate_ref, up_ref, down_ref, pt_ref, ggt_ref, gut_ref
):
    bf16 = jnp.bfloat16

    @pl.when(pl.program_id(1) == 0)
    def _():
        for source, turned in ((product_ref, pt_ref), (gg_ref, ggt_ref), (gu_ref, gut_ref)):
            turned[...] = source[0].T

    for turned, result in ((ggt_ref, gate_ref), (gut_ref, up_ref)):
        grad = dot_plain(turned[...], x_ref[0]).astype(bf16)
        depth = result.shape[-1]
        for i in range(result.shape[1]):
            result[0, i, 0, 0] = grad[:, i * depth : (i + 1) * depth]
    grad = dot_plain(pt_ref[...], val_ref[0]).astype(bf16)
    depth = down_ref.shape[4]
    for y in range(n_y):
        for c in range(2):
            for x in range(n_ctx):
                start = ((y * 2 + c) * n_ctx + x) * depth
                down_ref[y, x, c, 0] = grad[start : start + depth]


def expert_weight_grads(rows, after, n_y, n_ctx):
    bf16 = jnp.bfloat16
    x_all, val_all, product_all, gg_all, gu_all = rows
    _, total, model = x_all.shape
    ff = gg_all.shape[2]
    shards = 2 * n_y * n_ctx
    col, depth, down_depth = 256, model // shards, ff // shards
    k = max(1, col // depth)
    wide = pl.BlockSpec((1, total, col), lambda e, n: (e, 0, n))
    whole = pl.BlockSpec((1, total, ff), lambda e, n: (e, 0, 0))

    def place(e, n):
        shard = n * k
        return (shard // (2 * n_ctx), shard % n_ctx // k, shard // n_ctx % 2, e, 0, 0)

    up_spec = pl.BlockSpec((1, k, 1, 1, ff, depth), place)
    up_shape = jax.ShapeDtypeStruct((n_y, n_ctx, 2, 2, ff, depth), bf16)
    return pl.pallas_call(
        functools.partial(weight_grad_kernel, n_y, n_ctx),
        grid=(2, model // col),
        in_specs=[pl.BlockSpec(memory_space=pl.ANY), wide, wide, whole, whole, whole],
        out_specs=[
            up_spec,
            up_spec,
            pl.BlockSpec((n_y, n_ctx, 2, 1, down_depth, col), lambda e, n: (0, 0, 0, e, 0, n)),
        ],
        out_shape=[
            up_shape,
            up_shape,
            jax.ShapeDtypeStruct((n_y, n_ctx, 2, 2, down_depth, model), bf16),
        ],
        scratch_shapes=[pltpu.VMEM((ff, total), bf16)] * 3,
        compiler_params=pltpu.CompilerParams(vmem_limit_bytes=60 * MIB),
        cost_estimate=pl.CostEstimate(
            flops=2 * 6 * total * model * ff,
            bytes_accessed=2 * (2 * total * (2 * model + 3 * ff) + 6 * model * ff),
            transcendentals=0,
        ),
        name="expert_weight_grads",
    )(after, x_all, val_all, product_all, gg_all, gu_all)


def on_device(
    residual_in,
    segments,
    routes,
    gates,
    attn_gain,
    q_proj,
    key_projection,
    value_projection,
    q_gain,
    k_gain,
    o_proj,
    mlp_gain,
    gate_proj,
    up_proj,
    down_proj,
    out_grad,
):
    bf16, f32 = jnp.bfloat16, jnp.float32
    n_seq, n_ctx, n_exp = lax.axis_size("seq"), lax.axis_size("ctx"), lax.axis_size("exp")
    n_y = n_seq // 2
    devices = n_seq * n_ctx * n_exp
    core = lax.axis_index("seq") % 2
    span_index = lax.axis_index("ctx")
    z_index = lax.axis_index("exp")
    group_all = [
        [(s * n_ctx + x) * n_exp + z for s in range(c, n_seq, 2) for x in range(n_ctx) for z in range(n_exp)]
        for c in range(2)
    ]
    group_plane = [[s * n_ctx + x for s in range(c, n_seq, 2) for x in range(n_ctx)] for c in range(2)]

    def swap(value):
        return lax.ppermute(value, "seq", [(i, i ^ 1) for i in range(n_seq)])

    def across(value, step):
        return lax.ppermute(value, "exp", [(i, i ^ step) for i in range(n_exp)])

    token_count = residual_in.shape[1]
    model_width = residual_in.shape[2]
    sequence_length = segments.shape[1]
    route_count = routes.shape[2]
    local_experts = gate_proj.shape[0]
    expert_count = local_experts * n_exp
    half_experts = local_experts // 2
    capacity = token_count * route_count * 9 // (expert_count * 8)
    slots = -(-capacity // 16) * 16
    groups = KEY_VALUE_HEADS // 2
    heads = QUERY_HEADS // 2
    heads_per_group = QUERY_HEADS // KEY_VALUE_HEADS
    score_scale = HEAD_DIM ** (-0.5)
    rows = q_proj.shape[0]
    gain_rows = q_gain.shape[0]
    q_width, kv_width = heads * HEAD_DIM, groups * HEAD_DIM
    width = q_width + 2 * kv_width

    extra = jnp.zeros((rows, 128), bf16)
    extra = extra.at[0, :rows].set(attn_gain).at[0, rows : 2 * rows].set(mlp_gain)
    extra = extra.at[1, :gain_rows].set(q_gain).at[1, gain_rows : 2 * gain_rows].set(k_gain)
    mine_cols, other_cols = [], []
    for weight in (q_proj, key_projection, value_projection):
        mine, other = column_halves(weight, core)
        mine_cols += mine
        other_cols += other
    mine_block = jnp.concatenate(mine_cols + [extra], 1)
    other_block = jnp.concatenate(other_cols + [extra], 1)
    chips = n_y * n_ctx
    own_links = n_y == 2 and n_ctx == 2
    if own_links:
        w_gathered = gather_chips(mine_block, other_block, n_exp)
        w_gathered = w_gathered.reshape(chips * n_exp, 2, rows, width + 128)
    else:
        theirs = swap(other_block)
        pair = jnp.stack([pick(core, mine_block, theirs), pick(core, theirs, mine_block)])
        w_gathered = lax.all_gather(
            pair, ("seq", "ctx", "exp"), axis=0, tiled=False, axis_index_groups=group_all
        )
    w_extra = w_gathered[:, :, :2, width:].reshape(n_y, n_ctx * n_exp, 2, 2, 128)
    w_extra = w_extra.transpose(0, 2, 1, 3, 4).reshape(devices, 2, 128).astype(f32)
    gain_attn = w_extra[:, 0, :rows].reshape(model_width)
    gain_mlp_f = w_extra[:, 0, rows : 2 * rows].reshape(model_width)
    gain_query_f = w_extra[:, 1, :gain_rows].reshape(1, HEAD_DIM)
    gain_key_f = w_extra[:, 1, gain_rows : 2 * gain_rows].reshape(1, HEAD_DIM)
    w_out = lax.all_gather(
        o_proj, ("seq", "ctx", "exp"), axis=0, tiled=True, axis_index_groups=group_all
    )

    def gather_expert(weight):
        mine = pick(core, weight[:half_experts], weight[half_experts:])
        theirs = swap(pick(core, weight[half_experts:], weight[:half_experts]))
        both = jnp.stack([pick(core, mine, theirs), pick(core, theirs, mine)])
        both = lax.optimization_barrier((both, normed_own))[0]
        full = lax.all_gather(
            both, ("seq", "ctx"), axis=0, tiled=False, axis_index_groups=group_plane
        )
        full = full.reshape((n_y, n_ctx, 2) + mine.shape).transpose(3, 0, 2, 1, 4, 5)
        return full.reshape(half_experts, -1, weight.shape[2])

    route_ids = routes[0]
    route_hit = route_ids[:, :, None] == jnp.arange(expert_count, dtype=jnp.int32)[None, None, :]
    hit_counts = route_hit.astype(jnp.int32).sum(1)
    earlier = jnp.cumsum(hit_counts, axis=0) - hit_counts
    slot_of = jnp.where(hit_counts > 0, earlier, -1).astype(f32)
    gate_of = jnp.sum(jnp.where(route_hit, gates[0][:, :, None], 0.0), axis=1)
    table = jnp.concatenate([slot_of.T, gate_of.T], 0)
    hidden = residual_in[0].astype(f32)
    seg_two = jnp.stack([segments[0], swap(segments)[0]])
    seg_here = lax.dynamic_slice_in_dim(seg_two, span_index * token_count, token_count, 1)
    valid_two = (seg_here > 0).astype(f32).reshape(2 * token_count, 1)
    valid_rows = valid_two[:token_count]
    positions = span_index * token_count + jnp.arange(token_count, dtype=jnp.int32)
    cos_one, sin_one = rope_tables(positions)
    half_dim = HEAD_DIM // 2
    signed_sine = jnp.concatenate([-sin_one[:, :half_dim], sin_one[:, half_dim:]], 1)
    info = jnp.zeros((2, 8, token_count), jnp.int32)
    info = info.at[:, 0].set(seg_here).at[:, 1].set(positions[None])
    seg_keys = seg_two[:, :, None]
    inv_attn = lax.rsqrt(jnp.mean(hidden * hidden, axis=-1, keepdims=True) + EPS)
    normed_own = (hidden * inv_attn * gain_attn).astype(bf16)
    w_gate, w_up, w_down = gather_expert(gate_proj), gather_expert(up_proj), gather_expert(down_proj)

    ring_up = [(i, i + 1) for i in range(n_exp - 1)]
    ring_down = [(i + 1, i) for i in range(n_exp - 1)]
    cot_up = cot_down = lax.optimization_barrier((out_grad[0], normed_own))[0]
    cot_from = {0: cot_up}
    cot_steps = []
    for hop in range(1, n_exp):
        cot_up = lax.ppermute(cot_up, "exp", ring_up)
        cot_down = lax.ppermute(cot_down, "exp", ring_down)
        cot_from[-hop], cot_from[hop] = cot_up, cot_down
        cot_steps.append(cot_up[:8, :128].astype(f32) + cot_down[:8, :128].astype(f32))
    normed_two = jnp.concatenate([normed_own, swap(normed_own)], 0)
    q_blocks = q_width // (2 * HEAD_DIM)
    kv_raw, kv_low, w_kv = project(
        normed_two, w_gathered, q_blocks, 2, gain_key_f, cos_one, signed_sine, n_y, plain=1
    )
    kv_here = kv_low.reshape(2, token_count, 2 * kv_width)
    if n_ctx == 2:
        kv_there = lax.ppermute(kv_here, "ctx", [(0, 1), (1, 0)])
        kv_full = jnp.concatenate(
            [pick(span_index, kv_here, kv_there), pick(span_index, kv_there, kv_here)], 1
        )
    else:
        kv_full = lax.all_gather(kv_here, "ctx", axis=1, tiled=True)
    q_raw, query_rows, w_query = project(
        normed_two, w_gathered, 0, q_blocks, gain_query_f, cos_one, signed_sine, n_y
    )
    info = lax.optimization_barrier((info, cot_steps[0]))[0]
    mixed_low, recip = attend(info, seg_keys, query_rows, kv_full, groups, heads_per_group)
    mixed_low = lax.optimization_barrier((mixed_low, cot_steps[1]))[0]
    attn_partial = jnp.dot(mixed_low, w_out, preferred_element_type=f32)
    attn_out = attn_partial[:token_count] + swap(attn_partial[token_count:])
    middle = hidden + attn_out
    inv_mlp = lax.rsqrt(jnp.mean(middle * middle, axis=-1, keepdims=True) + EPS)
    normed_mlp = (middle * inv_mlp * gain_mlp_f).astype(bf16)

    tokens_all, tables_all = exchange_column(normed_mlp, table, n_exp)
    tables_all = lax.dynamic_update_slice(
        tables_all, table[None, None], (z_index, core, jnp.int32(0), jnp.int32(0))
    )
    grad_parts, out_parts = [], []
    held = {"slots": slots}
    first_row = z_index * local_experts + core * half_experts
    for step in range(n_exp):
        there = z_index ^ step
        own_cot = cot_from[0]
        if step:
            offsets = sorted({(i ^ step) - i for i in range(n_exp)})
            own_cot = cot_from[offsets[0]]
            for offset in offsets[1:]:
                own_cot = jnp.where(there - z_index == offset, cot_from[offset], own_cot)
        place = jnp.stack([there, core, first_row, expert_count + first_row]).astype(jnp.int32)
        if step == 3:
            place = lax.optimization_barrier((place, grad_parts[1]))[0]
        out_part, grad_part = run_experts(
            step,
            n_exp,
            place,
            tables_all,
            (normed_mlp if step == 0 else None, tokens_all),
            (own_cot, swap(own_cot)),
            (w_gate, w_up, w_down),
            held,
        )
        grad_part = grad_part[0].astype(f32) + swap(grad_part[1]).astype(f32)
        if step:
            grad_part = across(grad_part.astype(bf16), step)
        grad_parts.append(grad_part)
        out_parts.append(out_part)
    grad_total = grad_parts[0]
    for part in grad_parts[1:]:
        grad_total = grad_total + part.astype(f32)
    out_total = None
    for step, part in enumerate(out_parts):
        part = part[0].astype(f32) + swap(part[1]).astype(f32)
        if step:
            part = lax.optimization_barrier((part.astype(bf16), grad_parts[-1]))[0]
            part = across(part, step).astype(f32)
        out_total = part if out_total is None else out_total + part
    grad_normed_mlp, expert_out = grad_total, out_total
    final_out = middle + expert_out

    stats = jnp.zeros((8, 128), f32)
    for index, value in enumerate(
        (
            jnp.sum(hidden * hidden * valid_rows),
            jnp.sum(attn_out * attn_out * valid_rows),
            jnp.sum(expert_out * expert_out * valid_rows),
            jnp.sum(valid_rows),
        )
    ):
        stats = stats.at[0, index].set(value)
    for axis, count in (("seq", n_seq), ("ctx", n_ctx), ("exp", n_exp)):
        hop = 1
        while hop < count:
            stats = stats + lax.ppermute(stats, axis, [(i, i ^ hop) for i in range(count)])
            hop *= 2
    rms_stats = jnp.sqrt(stats[0, :3] / (stats[0, 3] * model_width))

    gate_blocks, up_blocks, down_blocks = expert_weight_grads(
        held["rows"], lax.optimization_barrier((place, grad_parts[2]))[0], n_y, n_ctx
    )

    def scatter_plane(blocks):
        return lax.psum_scatter(
            blocks.reshape((n_y * n_ctx,) + blocks.shape[2:]),
            ("seq", "ctx"),
            scatter_dimension=0,
            tiled=True,
            axis_index_groups=group_plane,
        )[0]

    def all_experts(part):
        mine = pick(core, part[0], part[1])
        theirs = swap(pick(core, part[1], part[0]))
        return jnp.concatenate([pick(core, mine, theirs), pick(core, theirs, mine)], 0).astype(f32)

    gate_part = scatter_plane(gate_blocks)
    up_blocks, gate_part = lax.optimization_barrier((up_blocks, gate_part))
    up_part = scatter_plane(up_blocks)
    down_blocks, up_part = lax.optimization_barrier((down_blocks, up_part))
    down_part = scatter_plane(down_blocks)

    cotangent = out_grad[0].astype(f32)
    mlp_gain_grad = jnp.sum(grad_normed_mlp * middle * inv_mlp, axis=0)
    grad_middle = cotangent + norm_back(grad_normed_mlp, middle, inv_mlp, gain_mlp_f)
    grad_attn_own = grad_middle.astype(bf16)
    grad_attn = jnp.concatenate([grad_attn_own, swap(grad_attn_own)], 0)
    o_grad_part = contract_rows(mixed_low, grad_attn).astype(bf16)
    o_grad_part, down_part = lax.optimization_barrier((o_grad_part, down_part))
    o_proj_grad = lax.psum_scatter(
        scatter_plane(o_grad_part.reshape(n_y, n_ctx, n_exp, -1, model_width)),
        "exp",
        scatter_dimension=0,
        tiled=True,
    )[0].astype(f32)
    mixture_gradient = contract_cols(grad_attn, w_out).astype(bf16) * valid_two.astype(bf16)
    grad_q_raw, key_grad, value_grad, q_gain_rows = attend_back(
        info,
        seg_keys,
        query_rows,
        kv_full,
        mixed_low,
        mixture_gradient,
        recip,
        q_raw,
        gain_query_f,
        cos_one,
        signed_sine,
        groups,
        heads_per_group,
    )
    q_gain_grad = q_gain_rows[0]
    kv_grad = jnp.concatenate([key_grad, value_grad], 2)
    if n_ctx == 2:
        first, second = kv_grad[:, :token_count], kv_grad[:, token_count:]
        received = lax.ppermute(
            pick(span_index, second, first).astype(bf16), "ctx", [(0, 1), (1, 0)]
        )
        kv_grad_here = pick(span_index, first, second) + received.astype(f32)
    else:
        kv_grad_here = lax.psum_scatter(
            kv_grad.astype(bf16), "ctx", scatter_dimension=1, tiled=True
        ).astype(f32)
    kv_grad_here = kv_grad_here.reshape(2 * token_count, 2 * kv_width)
    cosine_table, sine_values = jnp.concatenate([cos_one] * 2, 0), jnp.concatenate([sin_one] * 2, 0)
    k_raw = kv_raw[:, :kv_width].reshape(-1, groups, HEAD_DIM)
    inv_key = lax.rsqrt(jnp.mean(k_raw * k_raw, axis=-1, keepdims=True) + EPS)
    grad_kn = inverse_rotation(
        kv_grad_here[:, :kv_width].reshape(-1, groups, HEAD_DIM), cosine_table, sine_values
    )
    k_gain_grad = jnp.sum(grad_kn * k_raw * inv_key, axis=(0, 1))
    grad_k_raw = norm_back(grad_kn, k_raw, inv_key, gain_key_f).astype(bf16)
    grad_kv = jnp.concatenate(
        [grad_k_raw.reshape(-1, kv_width), kv_grad_here[:, kv_width:].astype(bf16)], 1
    )
    normed_partial = contract_cols(grad_q_raw, w_query) + contract_cols(grad_kv, w_kv)
    grad_normed = normed_partial[:token_count] + swap(normed_partial[token_count:])
    attn_gain_grad = jnp.sum(grad_normed * hidden * inv_attn, axis=0)
    grad_hidden = grad_middle + norm_back(grad_normed, hidden, inv_attn, gain_attn)

    extra_grad = jnp.zeros((devices, rows, 128), f32)
    extra_grad = extra_grad.at[:, 0, :rows].set(attn_gain_grad.reshape(devices, rows))
    extra_grad = extra_grad.at[:, 0, rows : 2 * rows].set(mlp_gain_grad.reshape(devices, rows))
    extra_grad = extra_grad.at[:, 1, :gain_rows].set(q_gain_grad.reshape(devices, gain_rows))
    extra_grad = extra_grad.at[:, 1, gain_rows : 2 * gain_rows].set(
        k_gain_grad.reshape(devices, gain_rows)
    )
    extra_grad = extra_grad.astype(bf16)
    if own_links:
        grad_mine, grad_theirs = dense_grad_scatter(
            normed_two,
            grad_q_raw,
            grad_kv,
            extra_grad.reshape(n_y, 2, n_ctx, n_exp, rows, 128),
            stats,
            n_exp,
        )
    else:
        w_grad = jnp.concatenate(
            [
                contract_rows(normed_two, grad_q_raw).astype(bf16),
                contract_rows(normed_two, grad_kv).astype(bf16),
                extra_grad.reshape(model_width, 128),
            ],
            1,
        )
        w_grad = w_grad.reshape(n_y, 2, n_ctx, n_exp, rows, width + 128).transpose(0, 2, 3, 1, 4, 5)
        w_grad, o_proj_grad = lax.optimization_barrier((w_grad, o_proj_grad))
        w_grad = lax.psum_scatter(
            scatter_plane(w_grad), "exp", scatter_dimension=0, tiled=True
        )[0]
        grad_mine = pick(core, w_grad[0], w_grad[1])
        grad_theirs = swap(pick(core, w_grad[1], w_grad[0]))
    gate_grad = all_experts(gate_part).transpose(0, 2, 1)
    up_grad = all_experts(up_part).transpose(0, 2, 1)
    down_grad = all_experts(down_part)
    even = pick(core, grad_mine, grad_theirs).astype(f32)
    odd = pick(core, grad_theirs, grad_mine).astype(f32)

    def columns(start, size):
        step = size // groups
        parts = []
        for g in range(groups):
            parts += [half[:, start + g * step : start + (g + 1) * step] for half in (even, odd)]
        return jnp.concatenate(parts, 1)

    extra_total = even[:, width:] + odd[:, width:]
    return (
        final_out.astype(bf16)[None],
        grad_hidden.astype(bf16)[None],
        extra_total[0, :rows],
        columns(0, q_width),
        columns(q_width, kv_width),
        columns(q_width + kv_width, kv_width),
        extra_total[1, :gain_rows],
        extra_total[1, gain_rows : 2 * gain_rows],
        o_proj_grad,
        extra_total[0, rows : 2 * rows],
        gate_grad,
        up_grad,
        down_grad,
        rms_stats,
    )


def solution(mesh):
    in_specs = (
        P(("seq", "exp"), "ctx", None),
        P(("seq", "exp"), None),
        P(("seq", "exp"), "ctx", None),
        P(("seq", "exp"), "ctx", None),
        P(("seq", "ctx", "exp")),
        P(("seq", "ctx", "exp"), None),
        P(("seq", "ctx", "exp"), None),
        P(("seq", "ctx", "exp"), None),
        P(("seq", "ctx", "exp")),
        P(("seq", "ctx", "exp")),
        P(("seq", "ctx", "exp"), None),
        P(("seq", "ctx", "exp")),
        P("exp", ("seq", "ctx"), None),
        P("exp", ("seq", "ctx"), None),
        P("exp", ("seq", "ctx"), None),
        P(("seq", "exp"), "ctx", None),
    )
    out_specs = (
        P(("seq", "exp"), "ctx", None),
        P(("seq", "exp"), "ctx", None),
        P(("seq", "ctx", "exp")),
        P(("seq", "ctx", "exp"), None),
        P(("seq", "ctx", "exp"), None),
        P(("seq", "ctx", "exp"), None),
        P(("seq", "ctx", "exp")),
        P(("seq", "ctx", "exp")),
        P(("seq", "ctx", "exp"), None),
        P(("seq", "ctx", "exp")),
        P("exp", ("seq", "ctx"), None),
        P("exp", ("seq", "ctx"), None),
        P("exp", ("seq", "ctx"), None),
        P(),
    )
    return jax.shard_map(
        on_device, mesh=mesh, in_specs=in_specs, out_specs=out_specs, check_vma=False
    )
```

```python
import functools

import jax
import jax.numpy as jnp
from jax import lax
from jax.experimental import pallas as pl
from jax.experimental.pallas import tpu as pltpu
from jax.sharding import PartitionSpec as P

QUERY_HEADS = 32
KEY_VALUE_HEADS = 4
HEAD_DIM = 128


EPS = 1e-06
ROPE_BASE = 1000000.0
MASKED = -1e30
MESH = pl.DeviceIdType.MESH
SEQ = "seq"
CTX = "ctx"
EXP = "exp"
CORE = "core"
X = "x"
Y = "y"
UP = "up"
DOWN = "down"
START = "start"
WAIT = "wait"
WAIT_SEND = "wait_send"
WAIT_RECV = "wait_recv"
INFO = "info"
SEG = "seg"
HEAD = "head"
KEY = "key"
VALUE = "value"
RECIP = "recip"


def contract_rows(first_op, second_op):
    return lax.dot_general(
        first_op, second_op, (((0,), (0,)), ((), ())), preferred_element_type=jnp.float32
    )


def contract_cols(first_op, second_op):
    return lax.dot_general(
        first_op, second_op, (((1,), (1,)), ((), ())), preferred_element_type=jnp.float32
    )


def rope_tables(positions):
    half_dim = HEAD_DIM // 2
    inverse = ROPE_BASE ** (-jnp.arange(half_dim, dtype=jnp.float32) * 2.0 / HEAD_DIM)
    angles = positions.astype(jnp.float32)[:, None] * inverse[None, :]
    cosine_table = jnp.cos(angles)
    sine_values = jnp.sin(angles)
    return (
        jnp.concatenate([cosine_table, cosine_table], -1),
        jnp.concatenate([sine_values, sine_values], -1),
    )


def inverse_rotation(gradient, cosine_table, sine_values):
    half_dim = gradient.shape[-1] // 2
    scaled = gradient * sine_values[:, None, :]
    return gradient * cosine_table[:, None, :] + jnp.concatenate(
        [scaled[..., half_dim:], -scaled[..., :half_dim]], -1
    )


def norm_back(gradient, source, inverse, gain_vec):
    scaled = gradient * gain_vec
    return inverse * scaled - source * inverse**3 * jnp.mean(
        scaled * source, axis=-1, keepdims=True
    )


def neighbours(n_exp):
    seq, x, z = lax.axis_index(SEQ), lax.axis_index(CTX), lax.axis_index(EXP)
    y, core = seq // 2, seq % 2
    ids = {
        CORE: {SEQ: 2 * y + 1 - core},
        X: {CTX: 1 - x},
        Y: {SEQ: 2 * (1 - y) + core},
        UP: {EXP: z + 1},
        DOWN: {EXP: z - 1},
    }
    return x, y, z, core, ids


def greet(z, n_exp, ids, names):
    barrier = pltpu.get_barrier_semaphore()
    count = 0
    for name in names:
        if name in (UP, DOWN):
            there = (z < n_exp - 1) if name == UP else (z > 0)

            @pl.when(there)
            def _():
                pl.semaphore_signal(
                    barrier, inc=1, device_id=ids[name], device_id_type=MESH
                )

            count = count + there.astype(jnp.int32)
        else:
            pl.semaphore_signal(
                barrier, inc=1, device_id=ids[name], device_id_type=MESH
            )
            count = count + 1
    pl.semaphore_wait(barrier, count)


def xor_chip(z, step, n_exp):
    result, bit = 0, 1
    while bit < n_exp:
        result = result + bit * ((z // bit % 2 + step // bit % 2) % 2)
        bit *= 2
    return result


class Plane:
    def __init__(self, n_exp, fulls, sems):
        x, y, _, _, self.ids = neighbours(n_exp)
        self.here, self.beside, self.across = 2 * y + x, 2 * y + 1 - x, 2 * (1 - y) + x
        self.fulls, self.sems = fulls, sems

    def each(self, method, far):
        near = ((self.here,), X), ((self.here,), Y)
        cases = (((self.beside, 0), Y), ((self.across, 1), X)) if far else near
        for which, full in enumerate(self.fulls):
            for lane, (place, name) in enumerate(cases):
                part = full.at[place]
                copy = pltpu.make_async_remote_copy(
                    src_ref=part,
                    dst_ref=part,
                    send_sem=self.sems.at[0, which, lane],
                    recv_sem=self.sems.at[1, which, lane],
                    device_id=self.ids[name],
                    device_id_type=MESH,
                )
                getattr(copy, method)()


def plane_sems(arrays):
    return pltpu.SemaphoreType.DMA((2, arrays, 2))


class Column:
    def __init__(self, n_exp, everyone, sems, own=None):
        self.x, self.y, self.z, self.core, self.ids = neighbours(n_exp)
        self.n_exp, self.everyone, self.sems, self.own = n_exp, everyone, sems, own

    def copies(self, lane, part, first):
        for which, result in enumerate(self.everyone):
            there = result.at[part, self.core]
            yield pltpu.make_async_remote_copy(
                src_ref=self.own[which] if first else there,
                dst_ref=there,
                send_sem=self.sems.at[0, which, lane, part],
                recv_sem=self.sems.at[1, which, lane, part],
                device_id=self.ids[(UP, DOWN, CORE)[lane]],
                device_id_type=MESH,
            )

    def each(self, method, cases, first=False):
        for lane, part, there in cases:

            @pl.when(there)
            def _(lane=lane, part=part):
                for copy in self.copies(lane, part, first):
                    getattr(copy, method)()

    def sends(self, hop, method):
        z, n = self.z, self.n_exp
        cases = (
            (0, z - hop + 1, (z >= hop - 1) & (z < n - 1)),
            (1, z + hop - 1, (z + hop - 1 < n) & (z > 0)),
        )
        self.each(method, cases, first=isinstance(hop, int) and hop == 1)

    def arrivals(self, hop):
        z, n = self.z, self.n_exp
        self.each(WAIT_RECV, ((0, z - hop, z >= hop), (1, z + hop, z + hop < n)))

    def passes(self, hop, method):
        z, n = self.z, self.n_exp
        self.each(method, ((2, z - hop, z >= hop), (2, z + hop, z + hop < n)))

    def pass_own(self, method):
        for copy in self.copies(2, self.z, True):
            getattr(copy, method)()


def column_sems(arrays, n_exp):
    return pltpu.SemaphoreType.DMA((2, arrays, 3, n_exp))


def sent_rows(chip_ref, into_ref, job, sems, i, n_exp):
    slot, into, step, start, stop = job
    rows = pl.ds(start, stop - start)
    return pltpu.make_async_remote_copy(
        src_ref=chip_ref.at[slot, rows],
        dst_ref=into_ref.at[into, rows],
        send_sem=sems.at[0, i],
        recv_sem=sems.at[1, i],
        device_id={EXP: xor_chip(lax.axis_index(EXP), step, n_exp)},
        device_id_type=MESH,
    )


def greet_slots(slots, n_exp):
    barrier = pltpu.get_barrier_semaphore()
    for slot in slots:
        pl.semaphore_signal(
            barrier,
            inc=1,
            device_id={EXP: xor_chip(lax.axis_index(EXP), slot, n_exp)},
            device_id_type=MESH,
        )
    pl.semaphore_wait(barrier, len(slots))


def gather_kernel(
    n_exp,
    mine_ref,
    other_ref,
    gate_ref,
    other_gate_ref,
    up_ref,
    other_up_ref,
    down_ref,
    other_down_ref,
    out_ref,
    cot_ref,
    table_ref,
    full_ref,
    out_full_ref,
    gate_full_ref,
    up_full_ref,
    down_pair_ref,
    cots_ref,
    tables_ref,
    local_sems,
    core_sems,
    z_sems,
    x_sems,
    y_sems,
    xf_sems,
    yf_sems,
    column_sem,
):
    column = Column(n_exp, (cots_ref, tables_ref), column_sem, (cot_ref, table_ref))
    x, y, z, core, ids = neighbours(n_exp)
    greet(z, n_exp, ids, (CORE, X, Y, UP, DOWN))
    here, beside, across = 2 * y + x, 2 * y + 1 - x, 2 * (1 - y) + x

    fulls = (full_ref, out_full_ref)

    def act(method, place, sems, slot, name):
        for which, full in enumerate(fulls):
            part = full.at[place]
            copy = pltpu.make_async_remote_copy(
                src_ref=part,
                dst_ref=part,
                send_sem=sems.at[0, which, slot],
                recv_sem=sems.at[1, which, slot],
                device_id=ids[name],
                device_id_type=MESH,
            )
            getattr(copy, method)()

    places = (
        full_ref.at[here, z, core],
        gate_full_ref.at[here, core],
        up_full_ref.at[here, core],
        down_pair_ref.at[core],
    )
    kept = [
        pltpu.make_async_copy(source, place, local_sems.at[i])
        for i, (source, place) in enumerate(zip((mine_ref, gate_ref, up_ref, down_ref), places))
    ]
    kept.insert(1, pltpu.make_async_copy(out_ref, out_full_ref.at[here, z], local_sems.at[4]))
    to_core = [
        pltpu.make_async_remote_copy(
            src_ref=source,
            dst_ref=place,
            send_sem=core_sems.at[0, i],
            recv_sem=core_sems.at[1, i],
            device_id=ids[CORE],
            device_id_type=MESH,
        )
        for i, (source, place) in enumerate(zip((other_ref, other_gate_ref, other_up_ref, other_down_ref), places))
    ]
    for copy in kept + to_core:
        copy.start()
    to_core[0].wait()
    kept[0].wait()
    kept[1].wait()
    column.pass_own(START)

    def source(label):
        hop = (label + 1) // 2
        if label == 0:
            return z, None
        return (z - hop, z >= hop) if label % 2 else (z + hop, z + hop < n_exp)

    labels = range(2 * n_exp - 1)

    def guarded(condition, action):
        if condition is None:
            action()
        else:
            pl.when(condition)(action)

    def z_slot(label, name):
        return label + 1 if label else (0 if name == UP else 1)

    def z_sends(label, method):
        part, there = source(label)
        for name in (UP, DOWN) if label == 0 else ((UP,) if label % 2 else (DOWN,)):
            room = (z < n_exp - 1) if name == UP else (z > 0)
            condition = room if there is None else there & room
            pl.when(condition)(
                lambda name=name: act(method, (here, part), z_sems, z_slot(label, name), name)
            )

    def z_arrival(label):
        hop = (label + 1) // 2
        name = UP if label % 2 else DOWN
        part, there = source(label)
        slot = z_slot(label - 2 if hop > 1 else 0, name)
        pl.when(there)(lambda: act(WAIT_RECV, (here, part), z_sems, slot, name))

    def spread(label):
        part, there = source(label)
        z_sends(label, START)

        def action():
            act(START, (here, part), x_sems, label, X)
            act(START, (here, part), y_sems, label, Y)

        guarded(there, action)

    def turn(label):
        part, there = source(label)

        def action():
            act(WAIT_RECV, (beside, part), x_sems, label, X)
            act(START, (beside, part, 0), xf_sems, label, Y)
            act(WAIT_RECV, (across, part), y_sems, label, Y)
            act(START, (across, part, 1), yf_sems, label, X)

        guarded(there, action)

    spread(0)
    for hop in range(1, n_exp):
        for label in (2 * hop - 1, 2 * hop):
            z_arrival(label)
            spread(label)
        if hop == n_exp - 1:
            column.sends(1, START)
        for label in (0,) if hop == 1 else (2 * hop - 3, 2 * hop - 2):
            turn(label)
    for label in (2 * n_exp - 3, 2 * n_exp - 2):
        turn(label)
    opposite = 2 * (1 - y) + 1 - x
    for label in labels:
        part, there = source(label)

        def action(label=label, part=part):
            act(WAIT_SEND, (here, part), x_sems, label, X)
            act(WAIT_SEND, (here, part), y_sems, label, Y)
            act(WAIT_SEND, (beside, part, 0), xf_sems, label, Y)
            act(WAIT_SEND, (across, part, 1), yf_sems, label, X)
            act(WAIT_RECV, (opposite, part, 0), xf_sems, label, Y)
            act(WAIT_RECV, (opposite, part, 1), yf_sems, label, X)

        guarded(there, action)
        z_sends(label, WAIT_SEND)
    column.arrivals(1)
    column.sends(1, WAIT_SEND)
    column.pass_own(WAIT)
    for copy in kept[2:] + to_core[1:]:
        copy.wait()


def gather_chips(mine, other, halves, out, cot, table, n_exp):
    labels = 2 * n_exp - 1
    any_spec = pl.BlockSpec(memory_space=pl.ANY)
    vmem_spec = pl.BlockSpec(memory_space=pltpu.VMEM)
    pair = lambda count: pltpu.SemaphoreType.DMA((2, 2, count))
    return pl.pallas_call(
        functools.partial(gather_kernel, n_exp),
        in_specs=[vmem_spec] * 9 + [any_spec, any_spec],
        out_specs=[any_spec] * 7,
        out_shape=[
            jax.ShapeDtypeStruct((4, n_exp, 2) + mine.shape, mine.dtype),
            jax.ShapeDtypeStruct((4, n_exp) + out.shape, out.dtype),
        ]
        + [jax.ShapeDtypeStruct((4, 2) + a.shape, a.dtype) for a in halves[:4:2]]
        + [jax.ShapeDtypeStruct((2,) + halves[4].shape, halves[4].dtype)]
        + [jax.ShapeDtypeStruct((n_exp, 2) + a.shape, a.dtype) for a in (cot, table)],
        scratch_shapes=[
            pltpu.SemaphoreType.DMA((5,)),
            pltpu.SemaphoreType.DMA((2, 4)),
            pair(2 * n_exp),
            pair(labels),
            pair(labels),
            pair(labels),
            pair(labels),
            column_sems(2, n_exp),
        ],
        compiler_params=pltpu.CompilerParams(
            collective_id=1, has_side_effects=True, vmem_limit_bytes=32 * MIB
        ),
    )(mine, other, *halves, out, cot, table)


def exchange_kernel(n_exp, first_ref, second_ref, firsts_ref, seconds_ref, sems):
    column = Column(n_exp, (firsts_ref, seconds_ref), sems, (first_ref, second_ref))
    greet(column.z, n_exp, column.ids, (CORE, UP, DOWN))
    column.sends(1, START)
    column.pass_own(START)
    for hop in range(1, n_exp):
        column.arrivals(hop)
        if hop < n_exp - 1:
            column.sends(hop + 1, START)
        column.passes(hop, START)
    column.pass_own(WAIT)
    for hop in range(1, n_exp):
        column.sends(hop, WAIT_SEND)
        column.passes(hop, WAIT)


def exchange_column(tokens, table, n_exp):
    any_spec = pl.BlockSpec(memory_space=pl.ANY)
    return pl.pallas_call(
        functools.partial(exchange_kernel, n_exp),
        in_specs=[any_spec] * 2,
        out_specs=[any_spec] * 2,
        out_shape=[
            jax.ShapeDtypeStruct((n_exp, 2) + a.shape, a.dtype) for a in (tokens, table)
        ],
        scratch_shapes=[column_sems(2, n_exp)],
        compiler_params=pltpu.CompilerParams(collective_id=3, has_side_effects=True),
        cost_estimate=pl.CostEstimate(
            flops=0, bytes_accessed=16 * n_exp * tokens.size, transcendentals=0
        ),
    )(tokens, table)


def scatter_kernel(
    n_exp,
    normed_ref,
    grad_ref,
    kv_grad_ref,
    extra_ref,
    mine_ref,
    theirs_ref,
    turned,
    part,
    from_x,
    from_y,
    second_x,
    second_y,
    total,
    from_z,
    from_core,
    x_sems,
    y_sems,
    x2_sems,
    y2_sems,
    z_sems,
    core_sems,
):
    bf16, f32 = jnp.bfloat16, jnp.float32
    x, y, z, core, ids = neighbours(n_exp)
    barrier = pltpu.get_barrier_semaphore()
    columns = [{EXP: (z + k) % n_exp} for k in range(1, n_exp)]
    for there in [ids[CORE], ids[X], ids[Y]] + columns:
        pl.semaphore_signal(barrier, inc=1, device_id=there, device_id_type=MESH)
    pl.semaphore_wait(barrier, 2 + n_exp)

    def remote(source, target, sems, slot, there):
        return pltpu.make_async_remote_copy(
            src_ref=source,
            dst_ref=target,
            send_sem=sems.at[0, slot],
            recv_sem=sems.at[1, slot],
            device_id=there,
            device_id_type=MESH,
        )

    rows = mine_ref.shape[0]
    q_width, width = grad_ref.shape[1], grad_ref.shape[1] + kv_grad_ref.shape[1]
    turned[...] = normed_ref[...].T
    steps = range(n_exp)

    def first_copies(k):
        return [
            remote(part.at[k, 1 - x, :, 0], from_x.at[k], x_sems, k, ids[X]),
            remote(part.at[k, :, 1 - y, 1], from_y.at[k], y_sems, k, ids[Y]),
        ]

    def second_copies(k):
        return [
            remote(part.at[k, x, 1 - y, 0], second_x.at[k], x2_sems, k, ids[Y]),
            remote(part.at[k, 1 - x, y, 1], second_y.at[k], y2_sems, k, ids[X]),
        ]

    def z_copy(k):
        return remote(
            total.at[k], from_z.at[k], z_sems, k, {EXP: (z + k + 1) % n_exp}
        )

    def produce(k):
        place = (z + k + 1) % n_exp
        blocks = []
        for px in range(2):
            for py in range(2):
                for c in range(2):
                    start = (((py * 2 + c) * 2 + px) * n_exp + place) * rows
                    blocks.append(turned[pl.ds(pl.multiple_of(start, rows), rows), :])
        block = jnp.concatenate(blocks, 0)
        grad = dot_plain(block, grad_ref[...]).astype(bf16)
        kv_grad = dot_plain(block, kv_grad_ref[...]).astype(bf16)
        i = 0
        for px in range(2):
            for py in range(2):
                for c in range(2):
                    part[k, px, py, c, :, :q_width] = grad[i * rows : (i + 1) * rows]
                    part[k, px, py, c, :, q_width:width] = kv_grad[i * rows : (i + 1) * rows]
                    part[k, px, py, c, :, width:] = extra_ref[py, c, px, place]
                    i += 1

    def launch(k):
        for copy in first_copies(k):
            copy.start()

    for k in steps:
        produce(k)
        if k < 2:
            launch(k)

    def second(k):
        along_x, along_y = first_copies(k)
        along_x.wait_recv()
        for py in range(2):
            part[k, x, py, 0] = (part[k, x, py, 0].astype(f32) + from_x[k, py].astype(f32)).astype(bf16)
        along_y.wait_recv()
        for px in range(2):
            part[k, px, y, 1] = (part[k, px, y, 1].astype(f32) + from_y[k, px].astype(f32)).astype(bf16)
        for copy in second_copies(k):
            copy.start()

    def third(k):
        along_y, along_x = second_copies(k)
        along_y.wait_recv()
        total[k, 0] = (part[k, x, y, 0].astype(f32) + second_x[k].astype(f32)).astype(bf16)
        along_x.wait_recv()
        total[k, 1] = (part[k, x, y, 1].astype(f32) + second_y[k].astype(f32)).astype(bf16)
        if k < n_exp - 1:
            z_copy(k).start()

    for k in steps:
        second(k)
        if k + 2 < n_exp:
            launch(k + 2)
        if k:
            third(k - 1)
    third(n_exp - 1)
    result = total[n_exp - 1].astype(f32)
    for k in range(n_exp - 1):
        z_copy(k).wait_recv()
        result = result + from_z[k].astype(f32)
    total[n_exp - 1] = result.astype(bf16)
    to_core = remote(total.at[n_exp - 1, 1 - core], from_core, core_sems, 0, ids[CORE])
    to_core.start()
    for k in steps:
        for copy in first_copies(k) + second_copies(k) + ([z_copy(k)] if k < n_exp - 1 else []):
            copy.wait_send()
    to_core.wait()
    mine_ref[...] = total[n_exp - 1, core].astype(f32)
    theirs_ref[...] = from_core[...].astype(f32)


def dense_grad_scatter(normed, grad, kv_grad, extra, n_exp):
    bf16 = jnp.bfloat16
    rows, model = extra.shape[4], normed.shape[1]
    width = grad.shape[1] + kv_grad.shape[1] + extra.shape[5]
    block = (rows, width)
    vmem = lambda *lead: pltpu.VMEM(lead + block, bf16)
    pair = lambda count: pltpu.SemaphoreType.DMA((2, count))
    spec = pl.BlockSpec(memory_space=pltpu.VMEM)
    return pl.pallas_call(
        functools.partial(scatter_kernel, n_exp),
        in_specs=[spec] * 4,
        out_specs=[spec] * 2,
        out_shape=[jax.ShapeDtypeStruct(block, jnp.float32)] * 2,
        scratch_shapes=[
            pltpu.VMEM((model, normed.shape[0]), bf16),
            vmem(n_exp, 2, 2, 2),
            vmem(n_exp, 2),
            vmem(n_exp, 2),
            vmem(n_exp),
            vmem(n_exp),
            vmem(n_exp, 2),
            vmem(n_exp, 2),
            vmem(),
            pair(n_exp),
            pair(n_exp),
            pair(n_exp),
            pair(n_exp),
            pair(n_exp),
            pair(1),
        ],
        compiler_params=pltpu.CompilerParams(
            collective_id=2, has_side_effects=True, vmem_limit_bytes=60 * MIB
        ),
        cost_estimate=pl.CostEstimate(
            flops=2 * normed.shape[0] * model * width, bytes_accessed=16 * MIB, transcendentals=0
        ),
    )(normed, grad, kv_grad, extra)


def back_kernel(
    n_exp,
    jobs,
    query_grad_ref,
    key_grad_ref,
    value_grad_ref,
    raw_ref,
    w_query_ref,
    w_kv_ref,
    gain_ref,
    cos_ref,
    sin_ref,
    hidden_ref,
    row_gain_ref,
    middle_grad_ref,
    chip_ref,
    into_in_ref,
    kv_grad_ref,
    hidden_grad_ref,
    row_gain_grad_ref,
    gain_grad_ref,
    into_ref,
    kv_send,
    kv_got,
    sib_part,
    own_part,
    part_got,
    x_sems,
    core_sems,
    job_sems,
):
    bf16, f32 = jnp.bfloat16, jnp.float32
    x, _, z, _, ids = neighbours(n_exp)
    tokens, model = hidden_ref.shape
    keys_width = raw_ref.shape[1] // 2
    barrier = pltpu.get_barrier_semaphore()
    slots = sorted({job[2] for job in jobs})
    greeted = [ids[CORE], ids[X]] + [{EXP: xor_chip(z, slot, n_exp)} for slot in slots]
    for there in greeted:
        pl.semaphore_signal(barrier, inc=1, device_id=there, device_id_type=MESH)
    here, there = (pl.ds(pl.multiple_of(i * tokens, tokens), tokens) for i in (x, 1 - x))
    for s in range(2):
        kv_send[s, :, :keys_width] = key_grad_ref[s, there].astype(bf16)
        kv_send[s, :, keys_width:] = value_grad_ref[s, there].astype(bf16)
    pl.semaphore_wait(barrier, len(greeted))
    to_x = pltpu.make_async_remote_copy(
        src_ref=kv_send,
        dst_ref=kv_got,
        send_sem=x_sems.at[0],
        recv_sem=x_sems.at[1],
        device_id=ids[X],
        device_id_type=MESH,
    )
    to_x.start()
    sent = [sent_rows(chip_ref, into_ref, job, job_sems, i, n_exp) for i, job in enumerate(jobs)]
    for copy in sent:
        copy.start()
    tile = 256
    parts = ((1, sib_part), (0, own_part))

    def query_product(s, part):
        rows = query_grad_ref[s * tokens : (s + 1) * tokens]
        for start in range(0, model, tile):
            part[:, start : start + tile] = dot_cols(rows, w_query_ref[start : start + tile])

    for s, part in parts:
        query_product(s, part)
    to_x.wait()
    gain_grad = None
    for s in range(2):
        rows = slice(s * tokens, (s + 1) * tokens)
        for start in range(0, keys_width, HEAD_DIM):
            columns = slice(start, start + HEAD_DIM)
            grad = key_grad_ref[s, here, columns] + kv_got[s, :, columns].astype(f32)
            turned = rotate_rows_back(grad, cos_ref[...], sin_ref[...])
            raw = raw_ref[rows, columns]
            inverse = lax.rsqrt(jnp.mean(raw * raw, axis=-1, keepdims=True) + EPS)
            unit = raw * inverse
            total = jnp.sum(turned * unit, axis=0, keepdims=True)
            gain_grad = total if gain_grad is None else gain_grad + total
            scaled = turned * gain_ref[...]
            kv_grad_ref[rows, columns] = (
                inverse * (scaled - unit * jnp.mean(scaled * unit, axis=-1, keepdims=True))
            ).astype(bf16)
        value_grad = value_grad_ref[s, here] + kv_got[s, :, keys_width:].astype(f32)
        kv_grad_ref[rows, keys_width:] = value_grad.astype(bf16)
    gain_grad_ref[0:1] = gain_grad

    def kv_product(s, part):
        rows = kv_grad_ref[s * tokens : (s + 1) * tokens]
        for start in range(0, model, tile):
            part[:, start : start + tile] += dot_cols(rows, w_kv_ref[start : start + tile])

    kv_product(*parts[0])
    to_core = pltpu.make_async_remote_copy(
        src_ref=sib_part,
        dst_ref=part_got,
        send_sem=core_sems.at[0],
        recv_sem=core_sems.at[1],
        device_id=ids[CORE],
        device_id_type=MESH,
    )
    to_core.start()
    kv_product(*parts[1])
    to_core.wait()
    row_gain_grad_ref[...] = jnp.zeros_like(row_gain_grad_ref)
    count = min(tokens, 64)

    @pl.loop(0, tokens // count)
    def _(i):
        rows = pl.ds(pl.multiple_of(i * count, count), count)
        grad = own_part[rows] + part_got[rows]
        hidden = hidden_ref[rows].astype(f32)
        inverse = lax.rsqrt(jnp.mean(hidden * hidden, axis=-1, keepdims=True) + EPS)
        unit = hidden * inverse
        row_gain_grad_ref[...] += jnp.sum(grad * unit, axis=0, keepdims=True)
        scaled = grad * row_gain_ref[...]
        back = inverse * (scaled - unit * jnp.mean(scaled * unit, axis=-1, keepdims=True))
        hidden_grad_ref[rows] = (middle_grad_ref[rows] + back).astype(bf16)

    for copy in sent:
        copy.wait()


def back_to_input(
    query_grad, key_grad, value_grad, raw, w_query, w_kv, gain, cos, sin, hidden, row_gain, middle_grad,
    chip, into, jobs, n_exp
):
    bf16, f32 = jnp.bfloat16, jnp.float32
    tokens, model = hidden.shape
    total, kv_width = raw.shape
    vmem, any_spec = pl.BlockSpec(memory_space=pltpu.VMEM), pl.BlockSpec(memory_space=pl.ANY)
    return pl.pallas_call(
        functools.partial(back_kernel, n_exp, jobs),
        in_specs=[vmem] * 12 + [any_spec] * 2,
        out_specs=[vmem] * 4 + [any_spec],
        out_shape=[
            jax.ShapeDtypeStruct((total, kv_width), bf16),
            jax.ShapeDtypeStruct((tokens, model), bf16),
            jax.ShapeDtypeStruct((1, model), f32),
            jax.ShapeDtypeStruct((8, HEAD_DIM), f32),
            jax.ShapeDtypeStruct(into.shape, into.dtype),
        ],
        scratch_shapes=[
            pltpu.VMEM((2, tokens, kv_width), bf16),
            pltpu.VMEM((2, tokens, kv_width), bf16),
            pltpu.VMEM((tokens, model), f32),
            pltpu.VMEM((tokens, model), f32),
            pltpu.VMEM((tokens, model), f32),
            pltpu.SemaphoreType.DMA((2,)),
            pltpu.SemaphoreType.DMA((2,)),
            pltpu.SemaphoreType.DMA((2, len(jobs))),
        ],
        input_output_aliases={13: 4},
        compiler_params=pltpu.CompilerParams(
            vmem_limit_bytes=60 * MIB, collective_id=11, has_side_effects=True
        ),
        cost_estimate=pl.CostEstimate(
            flops=2 * total * model * (query_grad.shape[1] + kv_width),
            bytes_accessed=48 * MIB,
            transcendentals=0,
        ),
    )(
        query_grad, key_grad, value_grad, raw, w_query, w_kv, gain, cos, sin, hidden, row_gain,
        middle_grad, chip, into
    )


def out_back_kernel(
    n_exp, jobs, mixed_ref, grad_ref, weight_ref, valid_ref, chip_ref, into_in, weight_grad_ref, mixed_grad_ref, into_ref, sems
):
    bf16 = jnp.bfloat16
    sent = [sent_rows(chip_ref, into_ref, job, sems, i, n_exp) for i, job in enumerate(jobs)]
    step = pl.program_id(0)

    @pl.when(step == 0)
    def _():
        greet_slots(sorted({job[2] for job in jobs}), n_exp)
        for copy in sent:
            copy.start()

    weight_grad_ref[...] = dot_plain(mixed_ref[...].T, grad_ref[...]).astype(bf16)
    mixed_grad = dot_cols(grad_ref[...], weight_ref[...]).astype(bf16)
    mixed_grad_ref[...] = mixed_grad * valid_ref[...].astype(bf16)

    @pl.when(step == pl.num_programs(0) - 1)
    def _():
        for copy in sent:
            copy.wait()


def out_back(mixed, grad, weight, valid, chip, into, jobs, n_exp):
    bf16 = jnp.bfloat16
    total, width = mixed.shape
    model = grad.shape[1]
    block = 2 * HEAD_DIM
    any_spec = pl.BlockSpec(memory_space=pl.ANY)
    columns = pl.BlockSpec((total, block), lambda j: (0, j))
    rows = pl.BlockSpec((block, model), lambda j: (j, 0))
    return pl.pallas_call(
        functools.partial(out_back_kernel, n_exp, jobs),
        grid=(width // block,),
        in_specs=[
            columns,
            pl.BlockSpec(grad.shape, lambda j: (0, 0)),
            rows,
            pl.BlockSpec(valid.shape, lambda j: (0, 0)),
            any_spec,
            any_spec,
        ],
        out_specs=[rows, columns, any_spec],
        out_shape=[
            jax.ShapeDtypeStruct((width, model), bf16),
            jax.ShapeDtypeStruct((total, width), bf16),
            jax.ShapeDtypeStruct(into.shape, bf16),
        ],
        input_output_aliases={5: 2},
        scratch_shapes=[pltpu.SemaphoreType.DMA((2, len(jobs)))],
        compiler_params=pltpu.CompilerParams(
            vmem_limit_bytes=40 * MIB, collective_id=12, has_side_effects=True
        ),
        cost_estimate=pl.CostEstimate(
            flops=4 * total * model * width, bytes_accessed=24 * MIB, transcendentals=0
        ),
    )(mixed, grad, weight, valid, chip, into)


def pick(core, first, second):
    return jnp.where(core == 0, first, second)


def column_halves(weight, core):
    width = weight.shape[1] // KEY_VALUE_HEADS
    parts = [weight[:, i * width : (i + 1) * width] for i in range(KEY_VALUE_HEADS)]
    mine = [pick(core, parts[i], parts[i + 1]) for i in range(0, KEY_VALUE_HEADS, 2)]
    other = [pick(core, parts[i + 1], parts[i]) for i in range(0, KEY_VALUE_HEADS, 2)]
    return mine, other


LOG2E = 1.4426950408889634
MIB = 1 << 20


def rotate_rows(vectors, cosine_table, signed_sine):
    return vectors * cosine_table + pltpu.roll(vectors, HEAD_DIM // 2, 1) * signed_sine


def rotate_rows_back(gradient, cosine_table, signed_sine):
    return gradient * cosine_table - pltpu.roll(gradient, HEAD_DIM // 2, 1) * signed_sine


def dot_cols(first, second):
    return lax.dot_general(
        first, second, (((1,), (1,)), ((), ())), preferred_element_type=jnp.float32
    )


def dot_plain(first, second):
    return jnp.dot(first, second, preferred_element_type=jnp.float32)


def ordered_weight(n_y, weight_ref, ordered_ref):
    n_xz = weight_ref.shape[0] // n_y
    weight = jnp.concatenate(
        [weight_ref[y * n_xz + i, c] for y in range(n_y) for c in range(2) for i in range(n_xz)], 0
    )
    ordered_ref[...] = weight
    return weight


def store_rotated(raw, gain, cos_ref, sin_ref, low_ref):
    tokens = cos_ref.shape[0]
    for h in range(2):
        columns = slice(h * HEAD_DIM, (h + 1) * HEAD_DIM)
        head = raw[:, columns]
        inverse = lax.rsqrt(jnp.mean(head * head, axis=-1, keepdims=True) + EPS)
        scaled = head * inverse * gain
        for s in range(2):
            part = slice(s * tokens, (s + 1) * tokens)
            low_ref[part, columns] = rotate_rows(scaled[part], cos_ref[...], sin_ref[...]).astype(
                jnp.bfloat16
            )


def key_value_kernel(
    n_y,
    own_ref,
    sib_ref,
    row_gain_ref,
    weight_ref,
    gain_ref,
    cos_ref,
    sin_ref,
    raw_ref,
    low_ref,
    ordered_ref,
    normed_ref,
):
    tokens = own_ref.shape[0]

    @pl.when(pl.program_id(0) == 0)
    def _():
        for s, source in enumerate((own_ref, sib_ref)):
            hidden = source[...].astype(jnp.float32)
            inverse = lax.rsqrt(jnp.mean(hidden * hidden, axis=-1, keepdims=True) + EPS)
            normed_ref[s * tokens : (s + 1) * tokens] = (hidden * inverse * row_gain_ref[...]).astype(
                jnp.bfloat16
            )

    raw = dot_plain(normed_ref[...], ordered_weight(n_y, weight_ref, ordered_ref))
    raw_ref[...] = raw

    @pl.when(pl.program_id(0) == 0)
    def _():
        store_rotated(raw, gain_ref[...], cos_ref, sin_ref, low_ref)

    @pl.when(pl.program_id(0) == 1)
    def _():
        low_ref[...] = raw.astype(jnp.bfloat16)


def query_kernel(n_y, n_exp, normed_ref, weight_ref, gain_ref, cos_ref, sin_ref, *refs):
    if n_exp:
        raw_ref, low_ref, ordered_ref, gate_full_ref, up_full_ref, cots_ref, tables_ref = refs[4:11]
        plane = Plane(n_exp, (gate_full_ref, up_full_ref), refs[11])
        column = Column(n_exp, (cots_ref, tables_ref), refs[12])

        @pl.when(pl.program_id(0) == 0)
        def _():
            greet(column.z, n_exp, plane.ids, (CORE, X, Y, UP, DOWN))
            plane.each(START, False)
            column.sends(2, START)
            column.passes(1, START)
    else:
        raw_ref, low_ref, ordered_ref = refs
    raw = dot_plain(normed_ref[...], ordered_weight(n_y, weight_ref, ordered_ref))
    raw_ref[...] = raw
    store_rotated(raw, gain_ref[...], cos_ref, sin_ref, low_ref)
    if n_exp:

        @pl.when(pl.program_id(0) == pl.num_programs(0) - 1)
        def _():
            plane.each(WAIT, False)
            column.arrivals(2)
            column.sends(2, WAIT_SEND)
            column.passes(1, WAIT)


def projection_specs(normed_shape, gathered, first_block, blocks, cos):
    total, model = normed_shape
    n_yxz, _, rows, _ = gathered.shape
    width = 2 * HEAD_DIM
    fixed = lambda j: (0, 0)
    moving = lambda j: (0, j)
    weight = pl.BlockSpec((n_yxz, 2, rows, width), lambda j: (0, 0, 0, j + first_block))
    tail = [pl.BlockSpec((1, HEAD_DIM), fixed), pl.BlockSpec(cos.shape, fixed), pl.BlockSpec(cos.shape, fixed)]
    out_specs = [pl.BlockSpec((total, width), moving)] * 2 + [pl.BlockSpec((model, width), moving)]
    out_shape = [
        jax.ShapeDtypeStruct((total, blocks * width), jnp.float32),
        jax.ShapeDtypeStruct((total, blocks * width), jnp.bfloat16),
        jax.ShapeDtypeStruct((model, blocks * width), jnp.bfloat16),
    ]
    cost = pl.CostEstimate(
        flops=2 * total * model * blocks * width,
        bytes_accessed=total * model * 2 + blocks * width * (model * 4 + total * 6),
        transcendentals=0,
    )
    return weight, tail, out_specs, out_shape, cost


def project_keys(own, sib, row_gain, gathered, first_block, gain, cos, sin, n_y):
    tokens, model = own.shape
    normed_shape = (2 * tokens, model)
    weight, tail, out_specs, out_shape, cost = projection_specs(normed_shape, gathered, first_block, 2, cos)
    fixed = lambda j: (0, 0)
    return pl.pallas_call(
        functools.partial(key_value_kernel, n_y),
        grid=(2,),
        in_specs=[pl.BlockSpec(own.shape, fixed)] * 2
        + [pl.BlockSpec((1, model), fixed), weight]
        + tail,
        out_specs=out_specs + [pl.BlockSpec(normed_shape, fixed)],
        out_shape=out_shape + [jax.ShapeDtypeStruct(normed_shape, jnp.bfloat16)],
        compiler_params=pltpu.CompilerParams(vmem_limit_bytes=56 * MIB),
        cost_estimate=cost,
    )(own, sib, row_gain, gathered, gain, cos, sin)


def project_queries(normed, gathered, blocks, gain, cos, sin, n_y, n_exp, moving):
    weight, tail, out_specs, out_shape, cost = projection_specs(normed.shape, gathered, 0, blocks, cos)
    any_specs = [pl.BlockSpec(memory_space=pl.ANY)] * len(moving)
    return pl.pallas_call(
        functools.partial(query_kernel, n_y, n_exp if moving else 0),
        grid=(blocks,),
        in_specs=[pl.BlockSpec(normed.shape, lambda j: (0, 0)), weight] + tail + any_specs,
        out_specs=out_specs + any_specs,
        out_shape=out_shape + [jax.ShapeDtypeStruct(a.shape, a.dtype) for a in moving],
        scratch_shapes=[plane_sems(2), column_sems(2, n_exp)] if moving else [],
        input_output_aliases={5 + i: 3 + i for i in range(len(moving))},
        compiler_params=pltpu.CompilerParams(
            vmem_limit_bytes=56 * MIB,
            collective_id=4 if moving else None,
            has_side_effects=bool(moving),
        ),
        cost_estimate=cost,
    )(normed, gathered, gain, cos, sin, *moving)


def mask_bias(seg_key, info):
    keys, tokens = seg_key.shape[0], info.shape[1]
    key_pos = lax.broadcasted_iota(jnp.int32, (keys, tokens), 0)
    allowed = (seg_key == info[0:1]) & (key_pos <= info[1:2])
    return jnp.where(allowed, 0.0, MASKED)


def key_tile(keys):
    return min(keys, 256)


def attention_kernel(hops, info_ref, seg_ref, q_ref, k_ref, v_ref, *refs):
    if hops:
        mixed_ref, recip_ref, gate_ref, up_ref, cots_ref, tables_ref = refs[4:10]
        bias_ref, vt_ref, plane_sem, sems = refs[10:]
        column = Column(hops, (cots_ref, tables_ref), sems)
        plane = Plane(hops, (gate_ref, up_ref), plane_sem)
        places = [pl.program_id(i) for i in range(3)]
        ends = [pl.num_programs(i) - 1 for i in range(3)]

        @pl.when((places[0] == 0) & (places[1] == 0) & (places[2] == 0))
        def _():
            greet(column.z, hops, column.ids, (CORE, X, Y, UP, DOWN))
            plane.each(START, True)
            column.sends(hops - 1, START)
            column.passes(hops - 2, START)
    else:
        mixed_ref, recip_ref, bias_ref, vt_ref = refs
    keys = k_ref.shape[1]
    tile = key_tile(keys)

    @pl.when((pl.program_id(1) == 0) & (pl.program_id(2) == 0))
    def _():
        bias_ref[...] = mask_bias(seg_ref[0], info_ref[0])

    @pl.when(pl.program_id(2) == 0)
    def _():
        vt_ref[...] = v_ref[0].astype(jnp.float32).T.astype(jnp.bfloat16)

    queries = q_ref[...]
    total, mixed = None, None
    for start in range(0, keys, tile):
        part = slice(start, start + tile)
        scores = dot_cols(k_ref[0, part], queries) * (HEAD_DIM**-0.5 * LOG2E) + bias_ref[part]
        weights = jnp.exp2(scores)
        tile_total = jnp.sum(weights, axis=0, keepdims=True)
        tile_mixed = dot_plain(vt_ref[:, part], weights.astype(jnp.bfloat16))
        total = tile_total if total is None else total + tile_total
        mixed = tile_mixed if mixed is None else mixed + tile_mixed
    recip = 1.0 / total
    recip_ref[0] = recip
    valid = (info_ref[0, 0:1] > 0).astype(jnp.float32)
    mixed_ref[...] = (mixed * (recip * valid)).T.astype(jnp.bfloat16)
    if hops:

        @pl.when((places[0] == ends[0]) & (places[1] == ends[1]) & (places[2] == ends[2]))
        def _():
            plane.each(WAIT, True)
            column.arrivals(hops - 1)
            column.passes(hops - 1, START)
            column.sends(hops - 1, WAIT_SEND)
            column.passes(hops - 2, WAIT)
            column.passes(hops - 1, WAIT)


def attention_specs(tokens, keys, groups, per_group):
    head = pl.BlockSpec((tokens, HEAD_DIM), lambda s, g, h: (s, g * per_group + h))
    return dict(
        info=pl.BlockSpec((1, 8, tokens), lambda s, g, h: (s, 0, 0)),
        seg=pl.BlockSpec((1, keys, 1), lambda s, g, h: (s, 0, 0)),
        head=head,
        key=pl.BlockSpec((1, keys, HEAD_DIM), lambda s, g, h: (s, 0, g)),
        value=pl.BlockSpec((1, keys, HEAD_DIM), lambda s, g, h: (s, 0, groups + g)),
        recip=pl.BlockSpec((1, 1, tokens), lambda s, g, h: ((s * groups + g) * per_group + h, 0, 0)),
    )


def attend(info, seg_keys, queries, kv_full, groups, per_group, n_exp, moving):
    tokens, keys = info.shape[2], seg_keys.shape[1]
    specs = attention_specs(tokens, keys, groups, per_group)
    steps = 2 * groups * per_group
    return pl.pallas_call(
        functools.partial(attention_kernel, n_exp if moving else 0),
        grid=(2, groups, per_group),
        in_specs=[specs[INFO], specs[SEG], specs[HEAD], specs[KEY], specs[VALUE]]
        + [pl.BlockSpec(memory_space=pl.ANY)] * len(moving),
        out_specs=[specs[HEAD], specs[RECIP]]
        + [pl.BlockSpec(memory_space=pl.ANY)] * len(moving),
        out_shape=[
            jax.ShapeDtypeStruct(queries.shape, jnp.bfloat16),
            jax.ShapeDtypeStruct((steps, 1, tokens), jnp.float32),
        ]
        + [jax.ShapeDtypeStruct(a.shape, a.dtype) for a in moving],
        scratch_shapes=[
            pltpu.VMEM((keys, tokens), jnp.float32),
            pltpu.VMEM((HEAD_DIM, keys), jnp.bfloat16),
        ]
        + ([plane_sems(2), column_sems(2, n_exp)] if moving else []),
        input_output_aliases={5 + i: 2 + i for i in range(len(moving))},
        compiler_params=pltpu.CompilerParams(
            vmem_limit_bytes=48 * MIB,
            collective_id=5 if moving else None,
            has_side_effects=bool(moving),
        ),
        cost_estimate=pl.CostEstimate(
            flops=steps * 8 * tokens * keys * HEAD_DIM,
            bytes_accessed=queries.size * 4 + kv_full.size * 2,
            transcendentals=steps * tokens * keys,
        ),
    )(info, seg_keys, queries, kv_full, kv_full, *moving)


def attention_back_kernel(
    info_ref,
    seg_ref,
    q_ref,
    k_ref,
    v_ref,
    mixed_ref,
    grad_ref,
    recip_ref,
    raw_ref,
    gain_ref,
    cos_ref,
    sin_ref,
    chip_ref,
    into_in_ref,
    raw_grad_ref,
    key_grad_ref,
    value_grad_ref,
    gain_grad_ref,
    into_ref,
    bias_ref,
    kt_ref,
    job_sems,
    *,
    n_exp,
    jobs,
):
    sent = [sent_rows(chip_ref, into_ref, job, job_sems, i, n_exp) for i, job in enumerate(jobs)]
    places = [pl.program_id(i) for i in range(3)]
    ends = [pl.num_programs(i) - 1 for i in range(3)]

    @pl.when((places[0] == 0) & (places[1] == 0) & (places[2] == 0))
    def _():
        greet_slots(sorted({job[2] for job in jobs}), n_exp)
        for copy in sent:
            copy.start()

    keys = k_ref.shape[1]
    tile = key_tile(keys)
    scale = HEAD_DIM**-0.5
    first = (pl.program_id(1) == 0) & (pl.program_id(2) == 0)

    @pl.when(first)
    def _():
        bias_ref[...] = mask_bias(seg_ref[0], info_ref[0])

    @pl.when(first & (pl.program_id(0) == 0))
    def _():
        gain_grad_ref[...] = jnp.zeros_like(gain_grad_ref)

    @pl.when(pl.program_id(2) == 0)
    def _():
        kt_ref[...] = k_ref[0].astype(jnp.float32).T.astype(jnp.bfloat16)
        key_grad_ref[...] = jnp.zeros_like(key_grad_ref)
        value_grad_ref[...] = jnp.zeros_like(value_grad_ref)

    queries, grad = q_ref[...], grad_ref[...]
    recip = recip_ref[0]
    overlap = grad.astype(jnp.float32) * mixed_ref[...].astype(jnp.float32)
    inner = jnp.sum(overlap.T, axis=0, keepdims=True)
    query_grad = None
    for start in range(0, keys, tile):
        part = slice(start, start + tile)
        scores = dot_cols(k_ref[0, part], queries) * (scale * LOG2E) + bias_ref[part]
        probs = jnp.exp2(scores) * recip
        grad_probs = dot_cols(v_ref[0, part], grad)
        grad_scores = (probs * (grad_probs - inner)).astype(jnp.bfloat16)
        value_grad_ref[0, part] += dot_plain(probs.astype(jnp.bfloat16), grad)
        key_grad_ref[0, part] += dot_plain(grad_scores, queries) * scale
        tile_grad = dot_plain(kt_ref[:, part], grad_scores)
        query_grad = tile_grad if query_grad is None else query_grad + tile_grad
    turned = rotate_rows_back((query_grad * scale).T, cos_ref[...], sin_ref[...])
    raw = raw_ref[...]
    inverse = lax.rsqrt(jnp.mean(raw * raw, axis=-1, keepdims=True) + EPS)
    unit = raw * inverse
    gain_grad_ref[0:1] += jnp.sum(turned * unit, axis=0, keepdims=True)
    scaled = turned * gain_ref[...]
    raw_grad_ref[...] = (
        inverse * (scaled - unit * jnp.mean(scaled * unit, axis=-1, keepdims=True))
    ).astype(jnp.bfloat16)

    @pl.when((places[0] == ends[0]) & (places[1] == ends[1]) & (places[2] == ends[2]))
    def _():
        for copy in sent:
            copy.wait()


def attend_back(
    info,
    seg_keys,
    queries,
    kv_full,
    mixed,
    grad_mixed,
    recip,
    raw,
    gain,
    cos,
    sin,
    groups,
    per_group,
    chip,
    into,
    jobs,
    n_exp,
):
    tokens, keys = info.shape[2], seg_keys.shape[1]
    specs = attention_specs(tokens, keys, groups, per_group)
    steps = 2 * groups * per_group
    fixed = lambda s, g, h: (0, 0)
    key_grad = jax.ShapeDtypeStruct((2, keys, groups * HEAD_DIM), jnp.float32)
    return pl.pallas_call(
        functools.partial(attention_back_kernel, n_exp=n_exp, jobs=jobs),
        grid=(2, groups, per_group),
        in_specs=[specs[INFO], specs[SEG], specs[HEAD], specs[KEY], specs[VALUE]]
        + [specs[HEAD], specs[HEAD], specs[RECIP], specs[HEAD]]
        + [pl.BlockSpec(a.shape, fixed) for a in (gain, cos, sin)]
        + [pl.BlockSpec(memory_space=pl.ANY)] * 2,
        out_specs=[specs[HEAD], specs[KEY], specs[KEY], pl.BlockSpec((8, HEAD_DIM), fixed)]
        + [pl.BlockSpec(memory_space=pl.ANY)],
        out_shape=[
            jax.ShapeDtypeStruct(queries.shape, jnp.bfloat16),
            key_grad,
            key_grad,
            jax.ShapeDtypeStruct((8, HEAD_DIM), jnp.float32),
            jax.ShapeDtypeStruct(into.shape, into.dtype),
        ],
        scratch_shapes=[
            pltpu.VMEM((keys, tokens), jnp.float32),
            pltpu.VMEM((HEAD_DIM, keys), jnp.bfloat16),
            pltpu.SemaphoreType.DMA((2, len(jobs))),
        ],
        input_output_aliases={13: 4},
        compiler_params=pltpu.CompilerParams(
            vmem_limit_bytes=48 * MIB, collective_id=6, has_side_effects=True
        ),
        cost_estimate=pl.CostEstimate(
            flops=steps * 20 * tokens * keys * HEAD_DIM,
            bytes_accessed=queries.size * 12 + kv_full.size * 6,
            transcendentals=steps * tokens * keys,
        ),
    )(
        info, seg_keys, queries, kv_full, kv_full, mixed, grad_mixed, recip, raw, gain, cos, sin, chip, into
    )


def moe_kernel(
    n_exp,
    n_y,
    local_experts,
    table_ref,
    own_ref,
    own_cot_ref,
    cots_ref,
    gate_any,
    up_any,
    down_any,
    x_ref,
    val_ref,
    product_ref,
    gate_grad_ref,
    up_grad_ref,
    tokens_ref,
    partial_ref,
    grad_chip_ref,
    out_chip_ref,
    grad_into_ref,
    out_into_ref,
    gate_w,
    up_w,
    down_w,
    token_scr,
    cot_scr,
    held,
    send,
    got,
    weight_sems,
    load_sems,
    token_sems,
    core_sems,
    local_sems,
    grad_sems,
):
    bf16, f32 = jnp.bfloat16, jnp.float32
    column = Column(n_exp, (tokens_ref,), token_sems, (own_ref,))
    z, core = column.z, column.core
    c, q = pl.program_id(0), pl.program_id(1)
    e, s = q // 2, (q % 3 + 1) // 2
    owner = core + s * (1 - 2 * core)
    chip = xor_chip(z, c, n_exp)
    slots, tokens = x_ref.shape[1], token_scr.shape[1]

    def weight_copies(expert):
        for which, (source, target) in enumerate(
            ((gate_any, gate_w), (up_any, up_w), (down_any, down_w))
        ):
            chips, cores, _, depth, _ = source.shape
            n_x = chips // n_y
            for p in range(chips):
                for k in range(cores):
                    start = ((p // n_x * cores + k) * n_x + p % n_x) * depth
                    yield pltpu.make_async_copy(
                        source.at[p, k, expert],
                        target.at[expert, pl.ds(start, depth)],
                        weight_sems.at[which, expert, p * cores + k],
                    )

    def load(which, sources, methods):
        copies = [
            pltpu.make_async_copy(source, scratch.at[which], load_sems.at[which, i])
            for i, (source, scratch) in enumerate(zip(sources, (token_scr, cot_scr)))
        ]
        for method in methods:
            for copy in copies:
                getattr(copy, method)()

    def fetch(i):
        return pltpu.make_async_copy(partial_ref.at[c, i], got.at[i], local_sems.at[i])

    def store(chunk, i):
        target = (grad_chip_ref, out_chip_ref)[i].at[chunk]
        return pltpu.make_async_copy(got.at[i], target, local_sems.at[2 + i])

    other_parts = (tokens_ref.at[chip, 1 - core], cots_ref.at[chip, 1 - core])

    def core_copy(chunk, i):
        return pltpu.make_async_remote_copy(
            src_ref=send.at[i],
            dst_ref=partial_ref.at[chunk, i],
            send_sem=core_sems.at[0, chunk, i],
            recv_sem=core_sems.at[1, chunk, i],
            device_id=column.ids[CORE],
            device_id_type=MESH,
        )

    def grad_copy(chunk):
        return pltpu.make_async_remote_copy(
            src_ref=grad_chip_ref.at[chunk],
            dst_ref=grad_into_ref.at[chunk],
            send_sem=grad_sems.at[0, chunk],
            recv_sem=grad_sems.at[1, chunk],
            device_id={EXP: xor_chip(z, chunk, n_exp)},
            device_id_type=MESH,
        )

    @pl.when((c == 0) & (q == 0))
    def _():
        barrier = pltpu.get_barrier_semaphore()
        greeted = [column.ids[CORE]] + [{EXP: xor_chip(z, k, n_exp)} for k in range(1, n_exp)]
        for there in greeted:
            pl.semaphore_signal(barrier, inc=1, device_id=there, device_id_type=MESH)
        pl.semaphore_wait(barrier, n_exp)
        column.sends(1, START)
        column.pass_own(START)
        for expert in range(2):
            for copy in weight_copies(expert):
                copy.start()
        load(0, (own_ref, own_cot_ref), (START, WAIT))
        for copy in weight_copies(0):
            copy.wait()

    @pl.when((c > 0) & (q == 0))
    def _():
        column.arrivals(c)
        pl.when(c < n_exp - 1)(lambda: column.sends(c + 1, START))
        column.passes(c, START)
        load(0, (tokens_ref.at[chip, core], cots_ref.at[chip, core]), (START,))
        for i in range(2):
            store(c - 1, i).wait()
        pl.when(c == n_exp - 1)(lambda: grad_copy(1).start())
        pl.when(c > 2)(lambda: grad_copy(c - 1).start())
        load(0, (tokens_ref.at[chip, core], cots_ref.at[chip, core]), (WAIT,))

    @pl.when(q == 1)
    def _():
        for copy in column.copies(2, chip, False):
            copy.wait_recv()
        load(1, other_parts, (START, WAIT))

    @pl.when((c == 0) & (q == 2))
    def _():
        for copy in weight_copies(1):
            copy.wait()

    slot_ids = lax.broadcasted_iota(jnp.int32, (slots, tokens), 0).astype(f32)
    expert_rows = table_ref.shape[2] // 2
    first_row = z * local_experts + core * 2

    def hits_of(expert):
        return table_ref[chip, owner, pl.ds(first_row + expert, 1)] == slot_ids

    hits = hits_of(e)
    one_hot = hits.astype(f32).astype(bf16)
    gates = table_ref[chip, owner, pl.ds(expert_rows + first_row + e, 1)]
    gate_row = jnp.sum(jnp.where(hits, gates, 0.0), axis=1, keepdims=True)
    x_rows = dot_plain(one_hot, token_scr[s]).astype(bf16)
    x_ref[0] = x_rows
    grad_val = (gate_row * dot_plain(one_hot, cot_scr[s])).astype(bf16)
    val_ref[0] = grad_val
    gate_act = dot_plain(x_rows, gate_w[e])
    up_act = dot_plain(x_rows, up_w[e])
    sigmoid = 1.0 / (1.0 + jnp.exp(-gate_act))
    silu = gate_act * sigmoid
    product = (silu * up_act).astype(bf16)
    product_ref[0] = product
    grad_product = dot_cols(grad_val, down_w[e])
    grad_gate = (grad_product * up_act * (sigmoid * (1.0 + gate_act * (1.0 - sigmoid)))).astype(bf16)
    grad_up = (grad_product * silu).astype(bf16)
    gate_grad_ref[0] = grad_gate
    up_grad_ref[0] = grad_up
    grad_rows = (dot_cols(grad_gate, gate_w[e]) + dot_cols(grad_up, up_w[e])).astype(bf16)
    weighted = (gate_row * dot_plain(product, down_w[e])).astype(bf16)

    @pl.when(e == 0)
    def _():
        held[s, 0] = grad_rows
        held[s, 1] = weighted

    def combined(i, rows):
        before = hits_of(0).astype(f32).astype(bf16)
        return lax.dot_general(
            jnp.concatenate([before, one_hot], 0),
            jnp.concatenate([held[s, i], rows], 0),
            (((0,), (0,)), ((), ())),
            preferred_element_type=f32,
        )

    @pl.when(q == 2)
    def _():
        for i, rows in enumerate((grad_rows, weighted)):
            pl.when(c > 0)(lambda i=i: core_copy(c - 1, i).wait_send())
            send[i] = combined(i, rows).astype(bf16)
            core_copy(c, i).start()

    @pl.when(q == 3)
    def _():
        for i, rows in enumerate((grad_rows, weighted)):
            own = combined(i, rows)
            core_copy(c, i).wait_recv()
            fetch(i).start()
            fetch(i).wait()
            got[i] = (own + got[i].astype(f32)).astype(bf16)
            store(c, i).start()

    @pl.when((c == n_exp - 1) & (q == 3))
    def _():
        column.pass_own(WAIT_SEND)
        for hop in range(1, n_exp):
            column.sends(hop, WAIT_SEND)
            column.passes(hop, WAIT_SEND)
        for i in range(2):
            core_copy(n_exp - 1, i).wait_send()
            store(n_exp - 1, i).wait()
        for chunk in range(1, n_exp - 1):
            grad_copy(chunk).wait()


def run_experts(tables, own, own_cot, cots, weights, n_y, local_experts, slots, n_exp):
    bf16 = jnp.bfloat16
    tokens, model = own.shape
    ff = weights[0].shape[4]
    pieces = weights[0].shape[0] * weights[0].shape[1]
    any_spec = pl.BlockSpec(memory_space=pl.ANY)
    row_spec = lambda width: pl.BlockSpec(
        (1, slots, width), lambda c, q: (q // 2, 2 * c + (q % 3 + 1) // 2, 0)
    )
    widths = (model, model, ff, ff, ff)
    chip_shape = jax.ShapeDtypeStruct((n_exp, tokens, model), bf16)
    results = pl.pallas_call(
        functools.partial(moe_kernel, n_exp, n_y, local_experts),
        grid=(n_exp, 4),
        in_specs=[pl.BlockSpec(tables.shape, lambda c, q: (0, 0, 0, 0))] + [any_spec] * 6,
        out_specs=[row_spec(width) for width in widths] + [any_spec] * 6,
        out_shape=[jax.ShapeDtypeStruct((2, 2 * n_exp * slots, width), bf16) for width in widths]
        + [
            jax.ShapeDtypeStruct(cots.shape, bf16),
            jax.ShapeDtypeStruct((n_exp, 2, tokens, model), bf16),
            chip_shape,
            chip_shape,
            chip_shape,
            chip_shape,
        ],
        scratch_shapes=[
            pltpu.VMEM((2, model, ff), bf16),
            pltpu.VMEM((2, model, ff), bf16),
            pltpu.VMEM((2, ff, model), bf16),
            pltpu.VMEM((2, tokens, model), bf16),
            pltpu.VMEM((2, tokens, model), bf16),
            pltpu.VMEM((2, 2, slots, model), bf16),
            pltpu.VMEM((2, tokens, model), bf16),
            pltpu.VMEM((2, tokens, model), bf16),
            pltpu.SemaphoreType.DMA((3, 2, pieces)),
            pltpu.SemaphoreType.DMA((2, 2)),
            column_sems(1, n_exp),
            pltpu.SemaphoreType.DMA((2, n_exp, 2)),
            pltpu.SemaphoreType.DMA((4,)),
            pltpu.SemaphoreType.DMA((2, n_exp)),
        ],
        compiler_params=pltpu.CompilerParams(
            vmem_limit_bytes=63 * MIB, collective_id=7, has_side_effects=True
        ),
        cost_estimate=pl.CostEstimate(
            flops=4 * n_exp * (12 * slots * model * ff + 8 * slots * tokens * model),
            bytes_accessed=24 * model * ff + 4 * n_exp * slots * (2 * model + 3 * ff) * 2,
            transcendentals=4 * n_exp * slots * ff,
        ),
    )(tables, own, own_cot, cots, *weights)
    return results[:5], *results[7:]


def weight_grad_kernel(
    n_y,
    n_ctx,
    n_exp,
    merged,
    x_ref,
    val_ref,
    product_ref,
    gg_ref,
    gu_ref,
    chip_ref,
    into_in_ref,
    out_chip_ref,
    *refs,
):
    bf16 = jnp.bfloat16
    results, (into_ref, out_into_ref, pt_ref, ggt_ref, gut_ref, job_sems) = refs[:-6], refs[-6:]
    e, n = pl.program_id(0), pl.program_id(1)
    last, rows = n_exp - 1, chip_ref.shape[1]
    sent = [
        sent_rows(chip_ref, into_ref, (last, last, last, 0, rows), job_sems, 0, n_exp),
        sent_rows(out_chip_ref, out_into_ref, (last, last, 1, 0, rows), job_sems, 1, n_exp),
    ]

    @pl.when((e == 0) & (n == 0))
    def _():
        greet_slots([1, last], n_exp)
        for copy in sent:
            copy.start()

    @pl.when(n == 0)
    def _():
        for source, turned in ((product_ref, pt_ref), (gg_ref, ggt_ref), (gu_ref, gut_ref)):
            turned[...] = source[0].T

    gate, up = (dot_plain(turned[...], x_ref[0]).astype(bf16) for turned in (ggt_ref, gut_ref))
    down = dot_plain(pt_ref[...], val_ref[0]).astype(bf16)
    if merged:
        (result,) = results
        depth = result.shape[-2] // (2 * n_y * n_ctx)
        y, c, x = n // (2 * n_ctx), n // n_ctx % 2, n % n_ctx
        result[y, x, c, 0, 0] = gate
        result[y, x, c, 1, 0] = up
        rows = pl.ds(pl.multiple_of(n * depth, depth), depth)
        for shard in range(2 * n_y * n_ctx):
            place = (shard // (2 * n_ctx), shard % n_ctx, shard // n_ctx % 2, 2, 0, rows)
            result[place] = down[shard * depth : (shard + 1) * depth]
    else:
        for grad, result in zip((gate, up), results):
            depth = result.shape[-1]
            for i in range(result.shape[1]):
                result[0, i, 0, 0] = grad[:, i * depth : (i + 1) * depth]
        depth = results[2].shape[4]
        for shard in range(2 * n_y * n_ctx):
            place = (shard // (2 * n_ctx), shard % n_ctx, shard // n_ctx % 2, 0)
            results[2][place] = down[shard * depth : (shard + 1) * depth]

    @pl.when((e == 1) & (n == pl.num_programs(1) - 1))
    def _():
        for copy in sent:
            copy.wait()


def expert_weight_grads(rows, chip, into, out_chip, n_y, n_ctx, n_exp, merged):
    bf16 = jnp.bfloat16
    x_all, val_all, product_all, gg_all, gu_all = rows
    _, total, model = x_all.shape
    ff = gg_all.shape[2]
    shards = 2 * n_y * n_ctx
    col, depth, down_depth = 256, model // shards, ff // shards
    wide = pl.BlockSpec((1, total, col), lambda e, n: (e, 0, n))
    whole = pl.BlockSpec((1, total, ff), lambda e, n: (e, 0, 0))
    any_spec = pl.BlockSpec(memory_space=pl.ANY)
    if merged:
        out_specs = [
            pl.BlockSpec((n_y, n_ctx, 2, 3, 1, ff, depth), lambda e, n: (0, 0, 0, 0, e, 0, 0))
        ]
        out_shape = [jax.ShapeDtypeStruct((n_y, n_ctx, 2, 3, 2, ff, depth), bf16)]
    else:
        k = col // depth

        def place(e, n):
            shard = n * k
            return (shard // (2 * n_ctx), shard % n_ctx // k, shard // n_ctx % 2, e, 0, 0)

        out_specs = [pl.BlockSpec((1, k, 1, 1, ff, depth), place)] * 2
        out_specs.append(
            pl.BlockSpec((n_y, n_ctx, 2, 1, down_depth, col), lambda e, n: (0, 0, 0, e, 0, n))
        )
        out_shape = [jax.ShapeDtypeStruct((n_y, n_ctx, 2, 2, ff, depth), bf16)] * 2
        out_shape.append(jax.ShapeDtypeStruct((n_y, n_ctx, 2, 2, down_depth, model), bf16))
    *blocks, into, out_into = pl.pallas_call(
        functools.partial(weight_grad_kernel, n_y, n_ctx, n_exp, merged),
        grid=(2, model // col),
        in_specs=[wide, wide, whole, whole, whole] + [any_spec] * 3,
        out_specs=out_specs + [any_spec] * 2,
        out_shape=out_shape + [jax.ShapeDtypeStruct(a.shape, a.dtype) for a in (into, out_chip)],
        scratch_shapes=[pltpu.VMEM((ff, total), bf16)] * 3 + [pltpu.SemaphoreType.DMA((2, 2))],
        input_output_aliases={6: len(out_shape)},
        compiler_params=pltpu.CompilerParams(
            vmem_limit_bytes=63 * MIB, collective_id=8, has_side_effects=True
        ),
        cost_estimate=pl.CostEstimate(
            flops=2 * 6 * total * model * ff,
            bytes_accessed=2 * (2 * total * (2 * model + 3 * ff) + 6 * model * ff),
            transcendentals=0,
        ),
    )(x_all, val_all, product_all, gg_all, gu_all, chip, into, out_chip)
    return blocks, into, out_into


def part_grad_kernel(n_y, n_ctx, n_exp, jobs, wide_ref, *refs):
    bf16 = jnp.bfloat16
    sources, refs = (refs[:2], refs[2:]) if len(refs) == 12 else (refs[:1], refs[1:])
    chip_ref, _, out_chip_ref, _, result, into_ref, out_into_ref = refs[:7]
    turned_refs, job_sems = refs[7:-1], refs[-1]
    e, n = pl.program_id(0), pl.program_id(1)
    pairs = ((chip_ref, into_ref), (out_chip_ref, out_into_ref))
    sent = [
        sent_rows(*pairs[which], job, job_sems, i, n_exp) for i, (which, job) in enumerate(jobs)
    ]

    @pl.when((e == 0) & (n == 0))
    def _():
        greet_slots(sorted({job[2] for _, job in jobs}), n_exp)
        for copy in sent:
            copy.start()

    @pl.when(n == 0)
    def _():
        for source, turned in zip(sources, turned_refs):
            turned[...] = source[0].T

    grads = [dot_plain(turned[...], wide_ref[0]).astype(bf16) for turned in turned_refs]
    shards = 2 * n_y * n_ctx
    depth = result.shape[-2] // shards
    if len(grads) == 2:
        y, c, x = n // (2 * n_ctx), n // n_ctx % 2, n % n_ctx
        for i, grad in enumerate(grads):
            result[y, x, c, i, 0] = grad
    else:
        rows = pl.ds(pl.multiple_of(n * depth, depth), depth)
        for shard in range(shards):
            place = (shard // (2 * n_ctx), shard % n_ctx, shard // n_ctx % 2, 0, 0, rows)
            result[place] = grads[0][shard * depth : (shard + 1) * depth]

    @pl.when((e == 1) & (n == pl.num_programs(1) - 1))
    def _():
        for copy in sent:
            copy.wait()


def part_weight_grads(wide, sources, chip, into, out_chip, out_into, jobs, collective, n_y, n_ctx, n_exp):
    bf16 = jnp.bfloat16
    _, total, model = wide.shape
    ff, kinds, col = sources[0].shape[2], len(sources), 256
    whole = pl.BlockSpec((1, total, ff), lambda e, n: (e, 0, 0))
    any_spec = pl.BlockSpec(memory_space=pl.ANY)
    return pl.pallas_call(
        functools.partial(part_grad_kernel, n_y, n_ctx, n_exp, jobs),
        grid=(2, model // col),
        in_specs=[pl.BlockSpec((1, total, col), lambda e, n: (e, 0, n))]
        + [whole] * kinds
        + [any_spec] * 4,
        out_specs=[
            pl.BlockSpec((n_y, n_ctx, 2, kinds, 1, ff, col), lambda e, n: (0, 0, 0, 0, e, 0, 0))
        ]
        + [any_spec] * 2,
        out_shape=[jax.ShapeDtypeStruct((n_y, n_ctx, 2, kinds, 2, ff, col), bf16)]
        + [jax.ShapeDtypeStruct(a.shape, a.dtype) for a in (into, out_into)],
        scratch_shapes=[pltpu.VMEM((ff, total), bf16)] * kinds
        + [pltpu.SemaphoreType.DMA((2, len(jobs)))],
        input_output_aliases={kinds + 2: 1, kinds + 4: 2},
        compiler_params=pltpu.CompilerParams(
            vmem_limit_bytes=60 * MIB, collective_id=collective, has_side_effects=True
        ),
        cost_estimate=pl.CostEstimate(
            flops=4 * kinds * total * model * ff,
            bytes_accessed=4 * (total * (model + kinds * ff) + kinds * model * ff),
            transcendentals=0,
        ),
    )(wide, *sources, chip, into, out_chip, out_into)


def sum_kernel(plan, value_ref, total_ref, held, arrived, sems):
    partners = [{axis: xor_chip(lax.axis_index(axis), hop, size)} for axis, size, hop in plan]
    barrier = pltpu.get_barrier_semaphore()
    for there in partners:
        pl.semaphore_signal(barrier, inc=1, device_id=there, device_id_type=MESH)
    pl.semaphore_wait(barrier, len(plan))
    held[0] = value_ref[...]
    for i, there in enumerate(partners):
        copy = pltpu.make_async_remote_copy(
            src_ref=held.at[i],
            dst_ref=arrived.at[i],
            send_sem=sems.at[0, i],
            recv_sem=sems.at[1, i],
            device_id=there,
            device_id_type=MESH,
        )
        copy.start()
        copy.wait()
        held[i + 1] = held[i] + arrived[i]
    total_ref[...] = held[len(plan)]


def sum_devices(value, axes):
    plan = [(axis, size, 1 << i) for axis, size in axes for i in range(size.bit_length() - 1)]
    spec = pl.BlockSpec(memory_space=pltpu.VMEM)
    return pl.pallas_call(
        functools.partial(sum_kernel, plan),
        in_specs=[spec],
        out_specs=spec,
        out_shape=jax.ShapeDtypeStruct(value.shape, value.dtype),
        scratch_shapes=[
            pltpu.VMEM((len(plan) + 1,) + value.shape, value.dtype),
            pltpu.VMEM((len(plan),) + value.shape, value.dtype),
            pltpu.SemaphoreType.DMA((2, len(plan))),
        ],
        compiler_params=pltpu.CompilerParams(collective_id=9, has_side_effects=True),
    )(value)


def on_device(
    residual_in,
    segments,
    routes,
    gates,
    attn_gain,
    q_proj,
    key_projection,
    value_projection,
    q_gain,
    k_gain,
    o_proj,
    mlp_gain,
    gate_proj,
    up_proj,
    down_proj,
    out_grad,
):
    bf16, f32 = jnp.bfloat16, jnp.float32
    n_seq, n_ctx, n_exp = lax.axis_size(SEQ), lax.axis_size(CTX), lax.axis_size(EXP)
    n_y = n_seq // 2
    devices = n_seq * n_ctx * n_exp
    core = lax.axis_index(SEQ) % 2
    span_index = lax.axis_index(CTX)
    z_index = lax.axis_index(EXP)
    group_all = [
        [(s * n_ctx + x) * n_exp + z for s in range(c, n_seq, 2) for x in range(n_ctx) for z in range(n_exp)]
        for c in range(2)
    ]
    group_plane = [[s * n_ctx + x for s in range(c, n_seq, 2) for x in range(n_ctx)] for c in range(2)]

    def swap(value):
        return lax.ppermute(value, SEQ, [(i, i ^ 1) for i in range(n_seq)])

    def across(value, step):
        return lax.ppermute(value, EXP, [(i, i ^ step) for i in range(n_exp)])

    token_count = residual_in.shape[1]
    model_width = residual_in.shape[2]
    sequence_length = segments.shape[1]
    route_count = routes.shape[2]
    local_experts = gate_proj.shape[0]
    expert_count = local_experts * n_exp
    half_experts = local_experts // 2
    capacity = token_count * route_count * 9 // (expert_count * 8)
    slots = -(-capacity // 16) * 16
    groups = KEY_VALUE_HEADS // 2
    heads = QUERY_HEADS // 2
    heads_per_group = QUERY_HEADS // KEY_VALUE_HEADS
    score_scale = HEAD_DIM ** (-0.5)
    rows = q_proj.shape[0]
    gain_rows = q_gain.shape[0]
    q_width, kv_width = heads * HEAD_DIM, groups * HEAD_DIM
    width = q_width + 2 * kv_width

    route_ids = routes[0]
    route_hit = route_ids[:, :, None] == jnp.arange(expert_count, dtype=jnp.int32)[None, None, :]
    hit_counts = route_hit.astype(jnp.int32).sum(1)
    earlier = jnp.cumsum(hit_counts, axis=0) - hit_counts
    slot_of = jnp.where(hit_counts > 0, earlier, -1).astype(f32)
    gate_of = jnp.sum(jnp.where(route_hit, gates[0][:, :, None], 0.0), axis=1)
    table = jnp.concatenate([slot_of.T, gate_of.T], 0)
    def gain_block(model_parts, head_parts, dtype):
        lead = model_parts[0].shape[:-1]
        fill = lambda size: jnp.zeros(lead + (1, size), dtype)
        first = jnp.concatenate([p[..., None, :] for p in model_parts] + [fill(128 - 2 * rows)], -1)
        second = jnp.concatenate(
            [p[..., None, :] for p in head_parts] + [fill(128 - 2 * gain_rows)], -1
        )
        return jnp.concatenate([first, second, jnp.zeros(lead + (rows - 2, 128), dtype)], -2)

    extra = gain_block([attn_gain, mlp_gain], [q_gain, k_gain], bf16)
    mine_cols, other_cols = [], []
    for weight in (q_proj, key_projection, value_projection):
        mine, other = column_halves(weight, core)
        mine_cols += mine
        other_cols += other
    mine_block = jnp.concatenate(mine_cols + [extra], 1)
    other_block = jnp.concatenate(other_cols + [extra], 1)
    chips = n_y * n_ctx
    own_links = n_y == 2 and n_ctx == 2 and n_exp == 4
    if own_links:
        halves = []
        for weight in (gate_proj, up_proj, down_proj):
            low, high = weight[:half_experts], weight[half_experts:]
            halves += [pick(core, low, high), pick(core, high, low)]
        w_gathered, w_out, gate_full, up_full, down_pair, cots_all, tables_all = gather_chips(
            mine_block,
            other_block,
            halves,
            o_proj.reshape(2, -1, model_width),
            out_grad[0],
            table,
            n_exp,
        )
        w_out = w_out.reshape(q_width, model_width)
        w_gathered = w_gathered.reshape(chips * n_exp, 2, rows, width + 128)
    else:
        theirs = swap(other_block)
        pair = jnp.stack([pick(core, mine_block, theirs), pick(core, theirs, mine_block)])
        w_gathered = lax.all_gather(
            pair, (SEQ, CTX, EXP), axis=0, tiled=False, axis_index_groups=group_all
        )
        cots_all, tables_all = exchange_column(out_grad[0], table, n_exp)
    w_extra = w_gathered[:, :, :2, width:].reshape(n_y, n_ctx * n_exp, 2, 2, 128)
    w_extra = w_extra.transpose(0, 2, 1, 3, 4).reshape(devices, 2, 128).astype(f32)
    gain_attn = w_extra[:, 0, :rows].reshape(model_width)
    gain_mlp_f = w_extra[:, 0, rows : 2 * rows].reshape(model_width)
    gain_query_f = w_extra[:, 1, :gain_rows].reshape(1, HEAD_DIM)
    gain_key_f = w_extra[:, 1, gain_rows : 2 * gain_rows].reshape(1, HEAD_DIM)

    if not own_links:
        w_out = lax.all_gather(
            o_proj, (SEQ, CTX, EXP), axis=0, tiled=True, axis_index_groups=group_all
        )

    def gather_expert(weight, after):
        if own_links:
            both = weight
        else:
            mine = pick(core, weight[:half_experts], weight[half_experts:])
            theirs = swap(pick(core, weight[half_experts:], weight[:half_experts]))
            both = jnp.stack([pick(core, mine, theirs), pick(core, theirs, mine)])
        both = lax.optimization_barrier((both, after))[0]
        full = lax.all_gather(
            both, (SEQ, CTX), axis=0, tiled=False, axis_index_groups=group_plane
        )
        full = full.reshape((n_y * n_ctx,) + both.shape)
        if own_links:
            return full
        full = full.reshape((n_y, n_ctx) + both.shape).transpose(3, 0, 2, 1, 4, 5)
        return full.reshape(1, 1, half_experts, -1, weight.shape[2])

    hidden = residual_in[0].astype(f32)
    seg_two = jnp.stack([segments[0], swap(segments)[0]])
    seg_here = lax.dynamic_slice_in_dim(seg_two, span_index * token_count, token_count, 1)
    valid_two = (seg_here > 0).astype(f32).reshape(2 * token_count, 1)
    valid_rows = valid_two[:token_count]
    positions = span_index * token_count + jnp.arange(token_count, dtype=jnp.int32)
    cos_one, sin_one = rope_tables(positions)
    half_dim = HEAD_DIM // 2
    signed_sine = jnp.concatenate([-sin_one[:, :half_dim], sin_one[:, half_dim:]], 1)
    info = jnp.zeros((2, 8, token_count), jnp.int32)
    info = info.at[:, 0].set(seg_here).at[:, 1].set(positions[None])
    seg_keys = seg_two[:, :, None]
    inv_attn = lax.rsqrt(jnp.mean(hidden * hidden, axis=-1, keepdims=True) + EPS)
    q_blocks = q_width // (2 * HEAD_DIM)
    kv_raw, kv_low, w_kv, normed_two = project_keys(
        residual_in[0],
        swap(residual_in[0]),
        gain_attn[None],
        w_gathered,
        q_blocks,
        gain_key_f,
        cos_one,
        signed_sine,
        n_y,
    )
    kv_here = kv_low.reshape(2, token_count, 2 * kv_width)
    if n_ctx == 2:
        kv_there = lax.ppermute(kv_here, CTX, [(0, 1), (1, 0)])
        kv_full = jnp.concatenate(
            [pick(span_index, kv_here, kv_there), pick(span_index, kv_there, kv_here)], 1
        )
    else:
        kv_full = lax.all_gather(kv_here, CTX, axis=1, tiled=True)
    moving = (gate_full, up_full, cots_all, tables_all) if own_links else ()
    q_raw, query_rows, w_query, *moving = project_queries(
        normed_two, w_gathered, q_blocks, gain_query_f, cos_one, signed_sine, n_y, n_exp, moving
    )
    mixed_low, recip, *moving = attend(
        info, seg_keys, query_rows, kv_full, groups, heads_per_group, n_exp, moving
    )
    if own_links:
        gate_full, up_full, cots_all, tables_all = moving
    else:
        gate_full, up_full = gather_expert(gate_proj, gain_attn), gather_expert(up_proj, gain_attn)
    down_full = gather_expert(
        down_pair if own_links else down_proj, query_rows if own_links else gain_attn
    )
    tables_all = lax.dynamic_update_slice(
        tables_all, table[None, None], (z_index, core, jnp.int32(0), jnp.int32(0))
    )
    attn_partial = jnp.dot(mixed_low, w_out, preferred_element_type=f32)
    attn_out = attn_partial[:token_count] + swap(attn_partial[token_count:])
    middle = hidden + attn_out
    inv_mlp = lax.rsqrt(jnp.mean(middle * middle, axis=-1, keepdims=True) + EPS)
    normed_mlp = (middle * inv_mlp * gain_mlp_f).astype(bf16)

    rows_all, grad_chip, out_chip, grad_into, out_into = run_experts(
        tables_all,
        normed_mlp,
        out_grad[0],
        cots_all,
        (gate_full, up_full, down_full),
        n_y if own_links else 1,
        local_experts,
        slots,
        n_exp,
    )

    if own_links:
        x_rows, val_rows, product_rows, gate_rows, up_rows = rows_all
        last, first_rows = n_exp - 1, 5 * token_count // 16
        blocks = []
        for i, (wide, sources) in enumerate(
            ((val_rows, (product_rows,)), (x_rows, (gate_rows, up_rows)))
        ):
            span = ((0, first_rows), (first_rows, token_count))[i]
            jobs = [(0, (last, last, last, *span)), (1, (last, last, 1, *span))]
            block, grad_into, out_into = part_weight_grads(
                wide, sources, grad_chip, grad_into, out_chip, out_into, jobs, 13 + i, n_y, n_ctx, n_exp
            )
            blocks.append(block)
    else:
        weight_blocks, grad_into, out_into = expert_weight_grads(
            rows_all, grad_chip, grad_into, out_chip, n_y, n_ctx, n_exp, merged=False
        )
    out_far = (out_chip[2:3].astype(f32) + out_into[3:4].astype(f32)).astype(bf16)

    def scatter_plane(blocks):
        return lax.psum_scatter(
            blocks.reshape((n_y * n_ctx,) + blocks.shape[2:]),
            (SEQ, CTX),
            scatter_dimension=0,
            tiled=True,
            axis_index_groups=group_plane,
        )[0]

    def all_experts(part):
        mine = pick(core, part[0], part[1])
        theirs = swap(pick(core, part[1], part[0]))
        axis = mine.ndim - 3
        both = [pick(core, mine, theirs), pick(core, theirs, mine)]
        return jnp.concatenate(both, axis).astype(f32)

    if own_links:
        parts = []
        for block in blocks:
            part = scatter_plane(block.reshape(n_y, n_ctx, -1, block.shape[-1]))
            parts.append(lax.optimization_barrier(part).reshape(block.shape[2:]))
    else:
        parts = [scatter_plane(weight_blocks[0])]
        for blocks in weight_blocks[1:]:
            blocks, parts[-1] = lax.optimization_barrier((blocks, parts[-1]))
            parts.append(scatter_plane(blocks))

    grad_normed_mlp = grad_chip[0].astype(f32)
    for step in range(1, n_exp):
        grad_normed_mlp = grad_normed_mlp + grad_into[step].astype(f32)
    cotangent = out_grad[0].astype(f32)
    mlp_gain_grad = jnp.sum(grad_normed_mlp * middle * inv_mlp, axis=0)
    grad_middle = cotangent + norm_back(grad_normed_mlp, middle, inv_mlp, gain_mlp_f)
    grad_attn_own = grad_middle.astype(bf16)
    grad_attn = jnp.concatenate([grad_attn_own, swap(grad_attn_own)], 0)
    part_rows = token_count // 4
    out_jobs, back_jobs = [(0, 2, 2, 0, part_rows)], [(0, 2, 2, part_rows, token_count)]
    last_jobs = [(1, 1, 1, 0, token_count)]
    o_grad_part, mixture_gradient, out_into = out_back(
        mixed_low, grad_attn, w_out, valid_two, out_far, out_into, out_jobs, n_exp
    )
    o_grad_plane = scatter_plane(o_grad_part.reshape(n_y, n_ctx, n_exp, -1, model_width))
    grad_q_raw, key_grad, value_grad, q_gain_rows, out_into = attend_back(
        info,
        seg_keys,
        query_rows,
        kv_full,
        mixed_low,
        mixture_gradient,
        recip,
        q_raw,
        gain_query_f,
        cos_one,
        signed_sine,
        groups,
        heads_per_group,
        out_far,
        out_into,
        back_jobs,
        n_exp,
    )
    q_gain_grad = q_gain_rows[0]
    if own_links:
        grad_kv, grad_hidden, attn_gain_grad, k_gain_rows, out_into = back_to_input(
            grad_q_raw,
            key_grad,
            value_grad,
            kv_raw,
            w_query,
            w_kv,
            gain_key_f,
            cos_one,
            signed_sine,
            residual_in[0],
            gain_attn[None],
            grad_middle,
            out_chip,
            out_into,
            last_jobs,
            n_exp,
        )
        k_gain_grad = k_gain_rows[0]
    else:
        kv_grad = jnp.concatenate([key_grad, value_grad], 2)
        query_part = contract_cols(grad_q_raw, w_query)
        kv_grad_here = lax.psum_scatter(
            kv_grad.astype(bf16), CTX, scatter_dimension=1, tiled=True
        ).astype(f32)
        kv_grad_here = kv_grad_here.reshape(2 * token_count, 2 * kv_width)
        cosine_table, sine_values = jnp.concatenate([cos_one] * 2, 0), jnp.concatenate([sin_one] * 2, 0)
        k_raw = kv_raw[:, :kv_width].reshape(-1, groups, HEAD_DIM)
        inv_key = lax.rsqrt(jnp.mean(k_raw * k_raw, axis=-1, keepdims=True) + EPS)
        grad_kn = inverse_rotation(
            kv_grad_here[:, :kv_width].reshape(-1, groups, HEAD_DIM), cosine_table, sine_values
        )
        k_gain_grad = jnp.sum(grad_kn * k_raw * inv_key, axis=(0, 1))
        grad_k_raw = norm_back(grad_kn, k_raw, inv_key, gain_key_f).astype(bf16)
        grad_kv = jnp.concatenate(
            [grad_k_raw.reshape(-1, kv_width), kv_grad_here[:, kv_width:].astype(bf16)], 1
        )
        normed_partial = query_part + contract_cols(grad_kv, w_kv)
        grad_normed = normed_partial[:token_count] + swap(normed_partial[token_count:])
        attn_gain_grad = jnp.sum(grad_normed * hidden * inv_attn, axis=0)
        grad_hidden = grad_middle + norm_back(grad_normed, hidden, inv_attn, gain_attn)

    extra_grad = gain_block(
        [attn_gain_grad.reshape(devices, rows), mlp_gain_grad.reshape(devices, rows)],
        [q_gain_grad.reshape(devices, gain_rows), k_gain_grad.reshape(devices, gain_rows)],
        f32,
    ).astype(bf16)
    if not own_links:
        near = across(out_chip[1], 1)
        out_into = lax.dynamic_update_slice(out_into, near[None], (1, 0, 0))
    expert_out = out_chip[0].astype(f32)
    for step in (1, 2):
        expert_out = expert_out + out_into[step].astype(f32)
    final_out = (middle + expert_out).astype(bf16)
    sums = [
        jnp.sum(value * value * valid_rows, keepdims=True) for value in (hidden, attn_out, expert_out)
    ]
    sums.append(jnp.sum(valid_rows, keepdims=True))
    stats = jnp.pad(jnp.concatenate(sums, 1), ((0, 7), (0, 124)))
    stats = sum_devices(stats, ((SEQ, n_seq), (CTX, n_ctx), (EXP, n_exp)))
    if own_links:
        extra_grad, o_grad_plane, parts, stats, final_out = lax.optimization_barrier(
            (extra_grad, o_grad_plane, parts, stats, final_out)
        )
    o_proj_grad = lax.psum_scatter(o_grad_plane, EXP, scatter_dimension=0, tiled=True)
    o_proj_grad = o_proj_grad[0].astype(f32)
    if own_links:
        grad_mine, grad_theirs = dense_grad_scatter(
            normed_two,
            grad_q_raw,
            grad_kv,
            extra_grad.reshape(n_y, 2, n_ctx, n_exp, rows, 128),
            n_exp,
        )
    else:
        w_grad = jnp.concatenate(
            [
                contract_rows(normed_two, grad_q_raw).astype(bf16),
                contract_rows(normed_two, grad_kv).astype(bf16),
                extra_grad.reshape(model_width, 128),
            ],
            1,
        )
        w_grad = w_grad.reshape(n_y, 2, n_ctx, n_exp, rows, width + 128).transpose(0, 2, 3, 1, 4, 5)
        w_grad = lax.psum_scatter(
            scatter_plane(w_grad), EXP, scatter_dimension=0, tiled=True
        )[0]
        grad_mine = pick(core, w_grad[0], w_grad[1])
        grad_theirs = swap(pick(core, w_grad[1], w_grad[0]))
    rms_stats = jnp.sqrt(stats[0, :3] / (stats[0, 3] * model_width))
    if own_links:
        part = all_experts(jnp.concatenate(parts[::-1], 1))
        gate_grad, up_grad = part[0].transpose(0, 2, 1), part[1].transpose(0, 2, 1)
        depth = part.shape[-1]
        down_grad = part[2].reshape(local_experts, model_width // depth, -1, depth)
        down_grad = down_grad.transpose(0, 2, 1, 3).reshape(local_experts, -1, model_width)
    else:
        gate_grad, up_grad = (all_experts(p).transpose(0, 2, 1) for p in parts[:2])
        down_grad = all_experts(parts[2])
    even = pick(core, grad_mine, grad_theirs).astype(f32)
    odd = pick(core, grad_theirs, grad_mine).astype(f32)

    def columns(start, size):
        step = size // groups
        parts = []
        for g in range(groups):
            parts += [half[:, start + g * step : start + (g + 1) * step] for half in (even, odd)]
        return jnp.concatenate(parts, 1)

    extra_total = even[:, width:] + odd[:, width:]
    return (
        final_out[None],
        grad_hidden.astype(bf16)[None],
        extra_total[0, :rows],
        columns(0, q_width),
        columns(q_width, kv_width),
        columns(q_width + kv_width, kv_width),
        extra_total[1, :gain_rows],
        extra_total[1, gain_rows : 2 * gain_rows],
        o_proj_grad,
        extra_total[0, rows : 2 * rows],
        gate_grad,
        up_grad,
        down_grad,
        rms_stats,
    )


def solution(mesh):
    in_specs = (
        P((SEQ, EXP), CTX, None),
        P((SEQ, EXP), None),
        P((SEQ, EXP), CTX, None),
        P((SEQ, EXP), CTX, None),
        P((SEQ, CTX, EXP)),
        P((SEQ, CTX, EXP), None),
        P((SEQ, CTX, EXP), None),
        P((SEQ, CTX, EXP), None),
        P((SEQ, CTX, EXP)),
        P((SEQ, CTX, EXP)),
        P((SEQ, CTX, EXP), None),
        P((SEQ, CTX, EXP)),
        P(EXP, (SEQ, CTX), None),
        P(EXP, (SEQ, CTX), None),
        P(EXP, (SEQ, CTX), None),
        P((SEQ, EXP), CTX, None),
    )
    out_specs = (
        P((SEQ, EXP), CTX, None),
        P((SEQ, EXP), CTX, None),
        P((SEQ, CTX, EXP)),
        P((SEQ, CTX, EXP), None),
        P((SEQ, CTX, EXP), None),
        P((SEQ, CTX, EXP), None),
        P((SEQ, CTX, EXP)),
        P((SEQ, CTX, EXP)),
        P((SEQ, CTX, EXP), None),
        P((SEQ, CTX, EXP)),
        P(EXP, (SEQ, CTX), None),
        P(EXP, (SEQ, CTX), None),
        P(EXP, (SEQ, CTX), None),
        P(),
    )
    return jax.shard_map(
        on_device, mesh=mesh, in_specs=in_specs, out_specs=out_specs, check_vma=False
    )
```

```python
import functools

import jax
import jax.numpy as jnp
from jax import lax
from jax.experimental import pallas as pl
from jax.experimental.pallas import tpu as pltpu
from jax.sharding import PartitionSpec as P

QUERY_HEADS = 32
KEY_VALUE_HEADS = 4
HEAD_DIM = 128


EPS = 1e-06
ROPE_BASE = 1000000.0
MASKED = -1e30
MESH = pl.DeviceIdType.MESH
SEQ = "seq"
CTX = "ctx"
EXP = "exp"
CORE = "core"
X = "x"
Y = "y"
UP = "up"
DOWN = "down"
START = "start"
WAIT = "wait"
WAIT_SEND = "wait_send"
WAIT_RECV = "wait_recv"
INFO = "info"
SEG = "seg"
HEAD = "head"
KEY = "key"
VALUE = "value"
RECIP = "recip"


def contract_rows(first_op, second_op):
    return lax.dot_general(
        first_op, second_op, (((0,), (0,)), ((), ())), preferred_element_type=jnp.float32
    )


def contract_cols(first_op, second_op):
    return lax.dot_general(
        first_op, second_op, (((1,), (1,)), ((), ())), preferred_element_type=jnp.float32
    )


def rope_tables(positions):
    half_dim = HEAD_DIM // 2
    inverse = ROPE_BASE ** (-jnp.arange(half_dim, dtype=jnp.float32) * 2.0 / HEAD_DIM)
    angles = positions.astype(jnp.float32)[:, None] * inverse[None, :]
    cosine_table = jnp.cos(angles)
    sine_values = jnp.sin(angles)
    return (
        jnp.concatenate([cosine_table, cosine_table], -1),
        jnp.concatenate([sine_values, sine_values], -1),
    )


def inverse_rotation(gradient, cosine_table, sine_values):
    half_dim = gradient.shape[-1] // 2
    scaled = gradient * sine_values[:, None, :]
    return gradient * cosine_table[:, None, :] + jnp.concatenate(
        [scaled[..., half_dim:], -scaled[..., :half_dim]], -1
    )


def norm_back(gradient, source, inverse, gain_vec):
    scaled = gradient * gain_vec
    return inverse * scaled - source * inverse**3 * jnp.mean(
        scaled * source, axis=-1, keepdims=True
    )


def neighbours(n_exp):
    seq, x, z = lax.axis_index(SEQ), lax.axis_index(CTX), lax.axis_index(EXP)
    y, core = seq // 2, seq % 2
    ids = {
        CORE: {SEQ: 2 * y + 1 - core},
        X: {CTX: 1 - x},
        Y: {SEQ: 2 * (1 - y) + core},
        UP: {EXP: z + 1},
        DOWN: {EXP: z - 1},
    }
    return x, y, z, core, ids


def greet(z, n_exp, ids, names):
    barrier = pltpu.get_barrier_semaphore()
    count = 0
    for name in names:
        if name in (UP, DOWN):
            there = (z < n_exp - 1) if name == UP else (z > 0)

            @pl.when(there)
            def _():
                pl.semaphore_signal(
                    barrier, inc=1, device_id=ids[name], device_id_type=MESH
                )

            count = count + there.astype(jnp.int32)
        else:
            pl.semaphore_signal(
                barrier, inc=1, device_id=ids[name], device_id_type=MESH
            )
            count = count + 1
    pl.semaphore_wait(barrier, count)


def xor_chip(z, step, n_exp):
    result, bit = 0, 1
    while bit < n_exp:
        result = result + bit * ((z // bit % 2 + step // bit % 2) % 2)
        bit *= 2
    return result


class Plane:
    def __init__(self, n_exp, fulls, sems):
        x, y, _, _, self.ids = neighbours(n_exp)
        self.here, self.beside, self.across = 2 * y + x, 2 * y + 1 - x, 2 * (1 - y) + x
        self.fulls, self.sems = fulls, sems

    def each(self, method, far):
        near = ((self.here,), X), ((self.here,), Y)
        cases = (((self.beside, 0), Y), ((self.across, 1), X)) if far else near
        for which, full in enumerate(self.fulls):
            for lane, (place, name) in enumerate(cases):
                part = full.at[place]
                copy = pltpu.make_async_remote_copy(
                    src_ref=part,
                    dst_ref=part,
                    send_sem=self.sems.at[0, which, lane],
                    recv_sem=self.sems.at[1, which, lane],
                    device_id=self.ids[name],
                    device_id_type=MESH,
                )
                getattr(copy, method)()


def plane_sems(arrays):
    return pltpu.SemaphoreType.DMA((2, arrays, 2))


class Column:
    def __init__(self, n_exp, everyone, sems, own=None):
        self.x, self.y, self.z, self.core, self.ids = neighbours(n_exp)
        self.n_exp, self.everyone, self.sems, self.own = n_exp, everyone, sems, own

    def copies(self, lane, part, first):
        for which, result in enumerate(self.everyone):
            there = result.at[part, self.core]
            yield pltpu.make_async_remote_copy(
                src_ref=self.own[which] if first else there,
                dst_ref=there,
                send_sem=self.sems.at[0, which, lane, part],
                recv_sem=self.sems.at[1, which, lane, part],
                device_id=self.ids[(UP, DOWN, CORE)[lane]],
                device_id_type=MESH,
            )

    def each(self, method, cases, first=False):
        for lane, part, there in cases:

            @pl.when(there)
            def _(lane=lane, part=part):
                for copy in self.copies(lane, part, first):
                    getattr(copy, method)()

    def sends(self, hop, method):
        z, n = self.z, self.n_exp
        cases = (
            (0, z - hop + 1, (z >= hop - 1) & (z < n - 1)),
            (1, z + hop - 1, (z + hop - 1 < n) & (z > 0)),
        )
        self.each(method, cases, first=isinstance(hop, int) and hop == 1)

    def arrivals(self, hop):
        z, n = self.z, self.n_exp
        self.each(WAIT_RECV, ((0, z - hop, z >= hop), (1, z + hop, z + hop < n)))

    def passes(self, hop, method):
        z, n = self.z, self.n_exp
        self.each(method, ((2, z - hop, z >= hop), (2, z + hop, z + hop < n)))

    def pass_own(self, method):
        for copy in self.copies(2, self.z, True):
            getattr(copy, method)()


def column_sems(arrays, n_exp):
    return pltpu.SemaphoreType.DMA((2, arrays, 3, n_exp))


def sent_rows(chip_ref, into_ref, job, sems, i, n_exp):
    slot, into, step, start, stop = job
    rows = pl.ds(start, stop - start)
    return pltpu.make_async_remote_copy(
        src_ref=chip_ref.at[slot, rows],
        dst_ref=into_ref.at[into, rows],
        send_sem=sems.at[0, i],
        recv_sem=sems.at[1, i],
        device_id={EXP: xor_chip(lax.axis_index(EXP), step, n_exp)},
        device_id_type=MESH,
    )


def greet_slots(slots, n_exp):
    barrier = pltpu.get_barrier_semaphore()
    for slot in slots:
        pl.semaphore_signal(
            barrier,
            inc=1,
            device_id={EXP: xor_chip(lax.axis_index(EXP), slot, n_exp)},
            device_id_type=MESH,
        )
    pl.semaphore_wait(barrier, len(slots))


def store_table(routes_ref, gates_ref, table_ref):
    f32, bf16 = jnp.float32, jnp.bfloat16
    experts, tokens = table_ref.shape[0] // 2, table_ref.shape[1]
    expert_ids = lax.broadcasted_iota(jnp.int32, (experts, tokens), 0)
    hits, gates = jnp.zeros((experts, tokens), f32), jnp.zeros((experts, tokens), f32)
    for k in range(routes_ref.shape[0]):
        named = routes_ref[k : k + 1] == expert_ids
        hits = hits + named.astype(f32)
        gates = gates + jnp.where(named, gates_ref[k : k + 1], 0.0)
    row = lax.broadcasted_iota(jnp.int32, (tokens, tokens), 0)
    before = (row < lax.broadcasted_iota(jnp.int32, (tokens, tokens), 1)).astype(f32).astype(bf16)
    table_ref[:experts] = jnp.where(hits > 0.0, dot_plain(hits.astype(bf16), before), -1.0)
    table_ref[experts:] = gates


def gather_kernel(
    n_exp,
    mine_ref,
    other_ref,
    gate_ref,
    other_gate_ref,
    up_ref,
    other_up_ref,
    down_ref,
    other_down_ref,
    out_ref,
    routes_ref,
    gates_ref,
    cot_ref,
    full_ref,
    out_full_ref,
    gate_full_ref,
    up_full_ref,
    down_pair_ref,
    cots_ref,
    tables_ref,
    local_sems,
    core_sems,
    z_sems,
    x_sems,
    y_sems,
    xf_sems,
    yf_sems,
    column_sem,
    first_sems,
    line_sems,
    table_ref,
):
    column = Column(n_exp, (cots_ref, tables_ref), column_sem, (cot_ref, table_ref))
    x, y, z, core, ids = neighbours(n_exp)
    greet(z, n_exp, ids, (CORE, X, Y, UP, DOWN))
    here, beside, across = 2 * y + x, 2 * y + 1 - x, 2 * (1 - y) + x

    fulls = (full_ref, out_full_ref)

    def act(method, place, sems, slot, name):
        for which, full in enumerate(fulls):
            if which and len(place) == 2:
                place = (*place, pl.ds(0, 2))
            part = full.at[place]
            copy = pltpu.make_async_remote_copy(
                src_ref=part,
                dst_ref=part,
                send_sem=sems.at[0, which, slot],
                recv_sem=sems.at[1, which, slot],
                device_id=ids[name],
                device_id_type=MESH,
            )
            getattr(copy, method)()

    def moved(method, place, sems, slot, name):
        part = out_full_ref.at[place]
        copy = pltpu.make_async_remote_copy(
            src_ref=part,
            dst_ref=part,
            send_sem=sems.at[(0, *slot)],
            recv_sem=sems.at[(1, *slot)],
            device_id=ids[name],
            device_id_type=MESH,
        )
        getattr(copy, method)()

    def first_near(method):
        for slot, name in enumerate((X, Y)):
            moved(method, (here, z, pl.ds(2, 2)), first_sems, (slot,), name)

    def first_far(method):
        moved(method, (beside, z, 2), first_sems, (2,), Y)
        moved(method, (across, z, 3), first_sems, (3,), X)

    def line(hop, method):
        for lane, name, part, there in (
            (0, UP, z - hop + 1, (z >= hop - 1) & (z < n_exp - 1)),
            (1, DOWN, z + hop - 1, (z + hop - 1 < n_exp) & (z > 0)),
        ):
            pl.when(there)(
                lambda lane=lane, name=name, part=part: moved(
                    method, (slice(None), part, pl.ds(2, 2)), line_sems, (lane, part), name
                )
            )

    def line_arrivals(hop):
        for lane, name, part, there in (
            (0, UP, z - hop, z >= hop),
            (1, DOWN, z + hop, z + hop < n_exp),
        ):
            pl.when(there)(
                lambda lane=lane, name=name, part=part: moved(
                    WAIT_RECV, (slice(None), part, pl.ds(2, 2)), line_sems, (lane, part), name
                )
            )

    places = (
        full_ref.at[here, z, core],
        gate_full_ref.at[here, core],
        up_full_ref.at[here, core],
        down_pair_ref.at[core],
    )
    kept = [
        pltpu.make_async_copy(source, place, local_sems.at[i])
        for i, (source, place) in enumerate(zip((mine_ref, gate_ref, up_ref, down_ref), places))
    ]
    kept.insert(1, pltpu.make_async_copy(out_ref, out_full_ref.at[here, z], local_sems.at[4]))
    to_core = [
        pltpu.make_async_remote_copy(
            src_ref=source,
            dst_ref=place,
            send_sem=core_sems.at[0, i],
            recv_sem=core_sems.at[1, i],
            device_id=ids[CORE],
            device_id_type=MESH,
        )
        for i, (source, place) in enumerate(zip((other_ref, other_gate_ref, other_up_ref, other_down_ref), places))
    ]
    for copy in kept + to_core:
        copy.start()
    store_table(routes_ref, gates_ref, table_ref)
    kept_table = pltpu.make_async_copy(table_ref, tables_ref.at[z, core], local_sems.at[5])
    kept_table.start()
    kept.append(kept_table)
    to_core[0].wait()
    kept[0].wait()
    kept[1].wait()
    column.pass_own(START)

    def source(label):
        hop = (label + 1) // 2
        if label == 0:
            return z, None
        return (z - hop, z >= hop) if label % 2 else (z + hop, z + hop < n_exp)

    labels = range(2 * n_exp - 1)

    def guarded(condition, action):
        if condition is None:
            action()
        else:
            pl.when(condition)(action)

    def z_slot(label, name):
        return label + 1 if label else (0 if name == UP else 1)

    def z_sends(label, method):
        part, there = source(label)
        for name in (UP, DOWN) if label == 0 else ((UP,) if label % 2 else (DOWN,)):
            room = (z < n_exp - 1) if name == UP else (z > 0)
            condition = room if there is None else there & room
            pl.when(condition)(
                lambda name=name: act(method, (here, part), z_sems, z_slot(label, name), name)
            )

    def z_arrival(label):
        hop = (label + 1) // 2
        name = UP if label % 2 else DOWN
        part, there = source(label)
        slot = z_slot(label - 2 if hop > 1 else 0, name)
        pl.when(there)(lambda: act(WAIT_RECV, (here, part), z_sems, slot, name))

    def spread(label):
        part, there = source(label)
        z_sends(label, START)

        def action():
            act(START, (here, part), x_sems, label, X)
            act(START, (here, part), y_sems, label, Y)

        guarded(there, action)

    def turn(label):
        part, there = source(label)

        def action():
            act(WAIT_RECV, (beside, part), x_sems, label, X)
            act(START, (beside, part, 0), xf_sems, label, Y)
            act(WAIT_RECV, (across, part), y_sems, label, Y)
            act(START, (across, part, 1), yf_sems, label, X)

        guarded(there, action)

    first_near(START)
    spread(0)
    for hop in range(1, n_exp):
        for label in (2 * hop - 1, 2 * hop):
            z_arrival(label)
            spread(label)
        if hop == 1:
            first_near(WAIT_RECV)
            first_far(START)
        if hop == n_exp - 1:
            first_far(WAIT_RECV)
            line(1, START)
        for label in (0,) if hop == 1 else (2 * hop - 3, 2 * hop - 2):
            turn(label)
    line_arrivals(1)
    line(2, START)
    for label in (2 * n_exp - 3, 2 * n_exp - 2):
        turn(label)
    for hop in range(2, n_exp):
        line_arrivals(hop)
        if hop < n_exp - 1:
            line(hop + 1, START)
    first_near(WAIT_SEND)
    first_far(WAIT_SEND)
    for hop in range(1, n_exp):
        line(hop, WAIT_SEND)
    opposite = 2 * (1 - y) + 1 - x
    for label in labels:
        part, there = source(label)

        def action(label=label, part=part):
            act(WAIT_SEND, (here, part), x_sems, label, X)
            act(WAIT_SEND, (here, part), y_sems, label, Y)
            act(WAIT_SEND, (beside, part, 0), xf_sems, label, Y)
            act(WAIT_SEND, (across, part, 1), yf_sems, label, X)
            act(WAIT_RECV, (opposite, part, 0), xf_sems, label, Y)
            act(WAIT_RECV, (opposite, part, 1), yf_sems, label, X)

        guarded(there, action)
        z_sends(label, WAIT_SEND)
    column.pass_own(WAIT)
    for copy in kept[2:] + to_core[1:]:
        copy.wait()


def gather_chips(mine, other, halves, out, routes, gates, cot, experts, n_exp):
    labels = 2 * n_exp - 1
    any_spec = pl.BlockSpec(memory_space=pl.ANY)
    vmem_spec = pl.BlockSpec(memory_space=pltpu.VMEM)
    pair = lambda count: pltpu.SemaphoreType.DMA((2, 2, count))
    return pl.pallas_call(
        functools.partial(gather_kernel, n_exp),
        in_specs=[vmem_spec] * 11 + [any_spec],
        out_specs=[any_spec] * 7,
        out_shape=[
            jax.ShapeDtypeStruct((4, n_exp, 2) + mine.shape, mine.dtype),
            jax.ShapeDtypeStruct((4, n_exp) + out.shape, out.dtype),
        ]
        + [jax.ShapeDtypeStruct((4, 2) + a.shape, a.dtype) for a in halves[:4:2]]
        + [jax.ShapeDtypeStruct((2,) + halves[4].shape, halves[4].dtype)]
        + [
            jax.ShapeDtypeStruct((n_exp, 2) + cot.shape, cot.dtype),
            jax.ShapeDtypeStruct((n_exp, 2, 2 * experts, cot.shape[0]), jnp.float32),
        ],
        scratch_shapes=[
            pltpu.SemaphoreType.DMA((6,)),
            pltpu.SemaphoreType.DMA((2, 4)),
            pair(2 * n_exp),
            pair(labels),
            pair(labels),
            pair(labels),
            pair(labels),
            column_sems(2, n_exp),
            pltpu.SemaphoreType.DMA((2, 4)),
            pltpu.SemaphoreType.DMA((2, 2, n_exp)),
            pltpu.VMEM((2 * experts, cot.shape[0]), jnp.float32),
        ],
        compiler_params=pltpu.CompilerParams(
            collective_id=1, has_side_effects=True, vmem_limit_bytes=32 * MIB
        ),
    )(mine, other, *halves, out, routes, gates, cot)


def exchange_kernel(n_exp, first_ref, second_ref, firsts_ref, seconds_ref, sems):
    column = Column(n_exp, (firsts_ref, seconds_ref), sems, (first_ref, second_ref))
    greet(column.z, n_exp, column.ids, (CORE, UP, DOWN))
    column.sends(1, START)
    column.pass_own(START)
    for hop in range(1, n_exp):
        column.arrivals(hop)
        if hop < n_exp - 1:
            column.sends(hop + 1, START)
        column.passes(hop, START)
    column.pass_own(WAIT)
    for hop in range(1, n_exp):
        column.sends(hop, WAIT_SEND)
        column.passes(hop, WAIT)


def exchange_column(tokens, table, n_exp):
    any_spec = pl.BlockSpec(memory_space=pl.ANY)
    return pl.pallas_call(
        functools.partial(exchange_kernel, n_exp),
        in_specs=[any_spec] * 2,
        out_specs=[any_spec] * 2,
        out_shape=[
            jax.ShapeDtypeStruct((n_exp, 2) + a.shape, a.dtype) for a in (tokens, table)
        ],
        scratch_shapes=[column_sems(2, n_exp)],
        compiler_params=pltpu.CompilerParams(collective_id=3, has_side_effects=True),
        cost_estimate=pl.CostEstimate(
            flops=0, bytes_accessed=16 * n_exp * tokens.size, transcendentals=0
        ),
    )(tokens, table)


def scatter_kernel(
    n_exp,
    turned,
    grad_ref,
    kv_grad_ref,
    extra_ref,
    stats_ref,
    mine_ref,
    theirs_ref,
    stats_sum_ref,
    part,
    from_x,
    from_y,
    second_x,
    second_y,
    total,
    from_z,
    from_core,
    x_sems,
    y_sems,
    x2_sems,
    y2_sems,
    z_sems,
    core_sems,
    held,
    arrived,
    stat_sems,
):
    bf16, f32 = jnp.bfloat16, jnp.float32
    x, y, z, core, ids = neighbours(n_exp)
    barrier = pltpu.get_barrier_semaphore()
    columns = [{EXP: (z + k) % n_exp} for k in range(1, n_exp)]
    for there in [ids[CORE], ids[X], ids[Y]] + columns:
        pl.semaphore_signal(barrier, inc=1, device_id=there, device_id_type=MESH)
    pl.semaphore_wait(barrier, 2 + n_exp)

    def remote(source, target, sems, slot, there):
        return pltpu.make_async_remote_copy(
            src_ref=source,
            dst_ref=target,
            send_sem=sems.at[0, slot],
            recv_sem=sems.at[1, slot],
            device_id=there,
            device_id_type=MESH,
        )

    rounds = [ids[CORE], ids[Y], ids[X]]
    rounds += [{EXP: xor_chip(z, 1 << i, n_exp)} for i in range(n_exp.bit_length() - 1)]
    held[0] = stats_ref[...]

    def stat_copy(i):
        return remote(held.at[i], arrived.at[i], stat_sems, i, rounds[i])

    def stat_round(i):
        if i:
            stat_copy(i - 1).wait()
            held[i] = held[i - 1] + arrived[i - 1]
        if i < len(rounds):
            stat_copy(i).start()

    stat_round(0)
    rows = mine_ref.shape[0]
    q_width, width = grad_ref.shape[1], grad_ref.shape[1] + kv_grad_ref.shape[1]
    steps = range(n_exp)

    def first_copies(k):
        return [
            remote(part.at[k, 1 - x, :, 0], from_x.at[k], x_sems, k, ids[X]),
            remote(part.at[k, :, 1 - y, 1], from_y.at[k], y_sems, k, ids[Y]),
        ]

    def second_copies(k):
        return [
            remote(part.at[k, x, 1 - y, 0], second_x.at[k], x2_sems, k, ids[Y]),
            remote(part.at[k, 1 - x, y, 1], second_y.at[k], y2_sems, k, ids[X]),
        ]

    def z_copy(k):
        return remote(
            total.at[k], from_z.at[k], z_sems, k, {EXP: (z + k + 1) % n_exp}
        )

    def produce(k):
        place = (z + k + 1) % n_exp
        blocks = []
        for px in range(2):
            for py in range(2):
                for c in range(2):
                    start = (((py * 2 + c) * 2 + px) * n_exp + place) * rows
                    blocks.append(turned[pl.ds(pl.multiple_of(start, rows), rows), :])
        block = jnp.concatenate(blocks, 0)
        grad = dot_plain(block, grad_ref[...]).astype(bf16)
        kv_grad = dot_plain(block, kv_grad_ref[...]).astype(bf16)
        i = 0
        for px in range(2):
            for py in range(2):
                for c in range(2):
                    part[k, px, py, c, :, :q_width] = grad[i * rows : (i + 1) * rows]
                    part[k, px, py, c, :, q_width:width] = kv_grad[i * rows : (i + 1) * rows]
                    part[k, px, py, c, :, width:] = extra_ref[py, c, px, place]
                    i += 1

    def launch(k):
        for copy in first_copies(k):
            copy.start()

    for k in steps:
        produce(k)
        if k < 2:
            launch(k)

    def second(k):
        along_x, along_y = first_copies(k)
        along_x.wait_recv()
        for py in range(2):
            part[k, x, py, 0] = (part[k, x, py, 0].astype(f32) + from_x[k, py].astype(f32)).astype(bf16)
        along_y.wait_recv()
        for px in range(2):
            part[k, px, y, 1] = (part[k, px, y, 1].astype(f32) + from_y[k, px].astype(f32)).astype(bf16)
        for copy in second_copies(k):
            copy.start()

    def third(k):
        along_y, along_x = second_copies(k)
        along_y.wait_recv()
        total[k, 0] = (part[k, x, y, 0].astype(f32) + second_x[k].astype(f32)).astype(bf16)
        along_x.wait_recv()
        total[k, 1] = (part[k, x, y, 1].astype(f32) + second_y[k].astype(f32)).astype(bf16)
        if k < n_exp - 1:
            z_copy(k).start()

    for k in steps:
        stat_round(k + 1)
        second(k)
        if k + 2 < n_exp:
            launch(k + 2)
        if k:
            third(k - 1)
    third(n_exp - 1)
    for i in range(n_exp + 1, len(rounds) + 1):
        stat_round(i)
    stats_sum_ref[...] = held[len(rounds)]
    result = total[n_exp - 1].astype(f32)
    for k in range(n_exp - 1):
        z_copy(k).wait_recv()
        result = result + from_z[k].astype(f32)
    total[n_exp - 1] = result.astype(bf16)
    to_core = remote(total.at[n_exp - 1, 1 - core], from_core, core_sems, 0, ids[CORE])
    to_core.start()
    for k in steps:
        for copy in first_copies(k) + second_copies(k) + ([z_copy(k)] if k < n_exp - 1 else []):
            copy.wait_send()
    to_core.wait()
    mine_ref[...] = total[n_exp - 1, core].astype(f32)
    theirs_ref[...] = from_core[...].astype(f32)


def dense_grad_scatter(turned, grad, kv_grad, extra, stats, n_exp):
    bf16 = jnp.bfloat16
    rows, model = extra.shape[4], turned.shape[0]
    width = grad.shape[1] + kv_grad.shape[1] + extra.shape[5]
    block = (rows, width)
    vmem = lambda *lead: pltpu.VMEM(lead + block, bf16)
    pair = lambda count: pltpu.SemaphoreType.DMA((2, count))
    spec = pl.BlockSpec(memory_space=pltpu.VMEM)
    return pl.pallas_call(
        functools.partial(scatter_kernel, n_exp),
        in_specs=[spec] * 5,
        out_specs=[spec] * 3,
        out_shape=[jax.ShapeDtypeStruct(block, jnp.float32)] * 2
        + [jax.ShapeDtypeStruct(stats.shape, stats.dtype)],
        scratch_shapes=[
            vmem(n_exp, 2, 2, 2),
            vmem(n_exp, 2),
            vmem(n_exp, 2),
            vmem(n_exp),
            vmem(n_exp),
            vmem(n_exp, 2),
            vmem(n_exp, 2),
            vmem(),
            pair(n_exp),
            pair(n_exp),
            pair(n_exp),
            pair(n_exp),
            pair(n_exp),
            pair(1),
            pltpu.VMEM((n_exp + 2,) + stats.shape, stats.dtype),
            pltpu.VMEM((n_exp + 2,) + stats.shape, stats.dtype),
            pair(n_exp + 2),
        ],
        compiler_params=pltpu.CompilerParams(
            collective_id=2, has_side_effects=True, vmem_limit_bytes=60 * MIB
        ),
        cost_estimate=pl.CostEstimate(
            flops=2 * turned.shape[1] * model * width, bytes_accessed=16 * MIB, transcendentals=0
        ),
    )(turned, grad, kv_grad, extra, stats)


def back_kernel(
    n_exp,
    jobs,
    query_grad_ref,
    key_grad_ref,
    value_grad_ref,
    raw_ref,
    w_query_ref,
    w_kv_ref,
    gain_ref,
    cos_ref,
    sin_ref,
    hidden_ref,
    row_gain_ref,
    middle_grad_ref,
    chip_ref,
    into_in_ref,
    kv_grad_ref,
    hidden_grad_ref,
    row_gain_grad_ref,
    gain_grad_ref,
    into_ref,
    kv_send,
    kv_got,
    sib_part,
    own_part,
    part_got,
    x_sems,
    core_sems,
    job_sems,
):
    bf16, f32 = jnp.bfloat16, jnp.float32
    x, _, z, _, ids = neighbours(n_exp)
    tokens, model = hidden_ref.shape
    keys_width = raw_ref.shape[1] // 2
    barrier = pltpu.get_barrier_semaphore()
    slots = sorted({job[2] for job in jobs})
    greeted = [ids[CORE], ids[X]] + [{EXP: xor_chip(z, slot, n_exp)} for slot in slots]
    for there in greeted:
        pl.semaphore_signal(barrier, inc=1, device_id=there, device_id_type=MESH)
    here, there = (pl.ds(pl.multiple_of(i * tokens, tokens), tokens) for i in (x, 1 - x))
    for s in range(2):
        kv_send[s, :, :keys_width] = key_grad_ref[s, there].astype(bf16)
        kv_send[s, :, keys_width:] = value_grad_ref[s, there].astype(bf16)
    pl.semaphore_wait(barrier, len(greeted))
    to_x = pltpu.make_async_remote_copy(
        src_ref=kv_send,
        dst_ref=kv_got,
        send_sem=x_sems.at[0],
        recv_sem=x_sems.at[1],
        device_id=ids[X],
        device_id_type=MESH,
    )
    to_x.start()
    sent = [sent_rows(chip_ref, into_ref, job, job_sems, i, n_exp) for i, job in enumerate(jobs)]
    for copy in sent:
        copy.start()
    tile = 256
    parts = ((1, sib_part), (0, own_part))

    def query_product(s, part):
        rows = query_grad_ref[s * tokens : (s + 1) * tokens]
        for start in range(0, model, tile):
            part[:, start : start + tile] = dot_cols(rows, w_query_ref[start : start + tile])

    for s, part in parts:
        query_product(s, part)
    to_x.wait()
    gain_grad = None
    for s in range(2):
        rows = slice(s * tokens, (s + 1) * tokens)
        for start in range(0, keys_width, HEAD_DIM):
            columns = slice(start, start + HEAD_DIM)
            grad = key_grad_ref[s, here, columns] + kv_got[s, :, columns].astype(f32)
            turned = rotate_rows_back(grad, cos_ref[...], sin_ref[...])
            raw = raw_ref[rows, columns]
            inverse = lax.rsqrt(jnp.mean(raw * raw, axis=-1, keepdims=True) + EPS)
            unit = raw * inverse
            total = jnp.sum(turned * unit, axis=0, keepdims=True)
            gain_grad = total if gain_grad is None else gain_grad + total
            scaled = turned * gain_ref[...]
            kv_grad_ref[rows, columns] = (
                inverse * (scaled - unit * jnp.mean(scaled * unit, axis=-1, keepdims=True))
            ).astype(bf16)
        value_grad = value_grad_ref[s, here] + kv_got[s, :, keys_width:].astype(f32)
        kv_grad_ref[rows, keys_width:] = value_grad.astype(bf16)
    gain_grad_ref[0:1] = gain_grad

    def kv_product(s, part):
        rows = kv_grad_ref[s * tokens : (s + 1) * tokens]
        for start in range(0, model, tile):
            part[:, start : start + tile] += dot_cols(rows, w_kv_ref[start : start + tile])

    kv_product(*parts[0])
    to_core = pltpu.make_async_remote_copy(
        src_ref=sib_part,
        dst_ref=part_got,
        send_sem=core_sems.at[0],
        recv_sem=core_sems.at[1],
        device_id=ids[CORE],
        device_id_type=MESH,
    )
    to_core.start()
    kv_product(*parts[1])
    to_core.wait()
    row_gain_grad_ref[...] = jnp.zeros_like(row_gain_grad_ref)
    count = min(tokens, 64)

    @pl.loop(0, tokens // count)
    def _(i):
        rows = pl.ds(pl.multiple_of(i * count, count), count)
        grad = own_part[rows] + part_got[rows]
        hidden = hidden_ref[rows].astype(f32)
        inverse = lax.rsqrt(jnp.mean(hidden * hidden, axis=-1, keepdims=True) + EPS)
        unit = hidden * inverse
        row_gain_grad_ref[...] += jnp.sum(grad * unit, axis=0, keepdims=True)
        scaled = grad * row_gain_ref[...]
        back = inverse * (scaled - unit * jnp.mean(scaled * unit, axis=-1, keepdims=True))
        hidden_grad_ref[rows] = (middle_grad_ref[rows] + back).astype(bf16)

    for copy in sent:
        copy.wait()


def back_to_input(
    query_grad, key_grad, value_grad, raw, weight, gain, cos, sin, hidden, row_gain, middle_grad,
    chip, into, jobs, n_exp
):
    bf16, f32 = jnp.bfloat16, jnp.float32
    tokens, model = hidden.shape
    total, q_width = query_grad.shape
    kv_width = raw.shape[1] - q_width
    once = dict(pipeline_mode=pl.Buffered(1))
    tail = lambda rows: pl.BlockSpec((rows, kv_width), lambda i: (0, q_width // kv_width), **once)
    vmem, any_spec = pl.BlockSpec(memory_space=pltpu.VMEM), pl.BlockSpec(memory_space=pl.ANY)
    return pl.pallas_call(
        functools.partial(back_kernel, n_exp, jobs),
        grid=(1,),
        in_specs=[vmem] * 3
        + [tail(total), pl.BlockSpec((model, q_width), lambda i: (0, 0), **once), tail(model)]
        + [vmem] * 6
        + [any_spec] * 2,
        out_specs=[vmem] * 4 + [any_spec],
        out_shape=[
            jax.ShapeDtypeStruct((total, kv_width), bf16),
            jax.ShapeDtypeStruct((tokens, model), bf16),
            jax.ShapeDtypeStruct((1, model), f32),
            jax.ShapeDtypeStruct((8, HEAD_DIM), f32),
            jax.ShapeDtypeStruct(into.shape, into.dtype),
        ],
        scratch_shapes=[
            pltpu.VMEM((2, tokens, kv_width), bf16),
            pltpu.VMEM((2, tokens, kv_width), bf16),
            pltpu.VMEM((tokens, model), f32),
            pltpu.VMEM((tokens, model), f32),
            pltpu.VMEM((tokens, model), f32),
            pltpu.SemaphoreType.DMA((2,)),
            pltpu.SemaphoreType.DMA((2,)),
            pltpu.SemaphoreType.DMA((2, len(jobs))),
        ],
        input_output_aliases={13: 4},
        compiler_params=pltpu.CompilerParams(
            vmem_limit_bytes=60 * MIB, collective_id=11, has_side_effects=True
        ),
        cost_estimate=pl.CostEstimate(
            flops=2 * total * model * (query_grad.shape[1] + kv_width),
            bytes_accessed=48 * MIB,
            transcendentals=0,
        ),
    )(
        query_grad, key_grad, value_grad, raw, weight, weight, gain, cos, sin, hidden, row_gain,
        middle_grad, chip, into
    )


def out_back_kernel(
    n_exp, jobs, mixed_ref, own_ref, sib_ref, weight_ref, valid_ref, chip_ref, into_in, weight_grad_ref, mixed_grad_ref, into_ref, grad_ref, sems
):
    bf16 = jnp.bfloat16
    sent = [sent_rows(chip_ref, into_ref, job, sems, i, n_exp) for i, job in enumerate(jobs)]
    step, tokens = pl.program_id(0), own_ref.shape[0]

    @pl.when(step == 0)
    def _():
        grad_ref[:tokens] = own_ref[...]
        grad_ref[tokens:] = sib_ref[...]
        greet_slots(sorted({job[2] for job in jobs}), n_exp)
        for copy in sent:
            copy.start()

    weight_grad_ref[...] = dot_plain(mixed_ref[...].T, grad_ref[...]).astype(bf16)
    mixed_grad = dot_cols(grad_ref[...], weight_ref[...]).astype(bf16)
    mixed_grad_ref[...] = mixed_grad * valid_ref[...].astype(bf16)

    @pl.when(step == pl.num_programs(0) - 1)
    def _():
        for copy in sent:
            copy.wait()


def out_back(mixed, own, sib, weight, valid, chip, into, jobs, n_exp):
    bf16 = jnp.bfloat16
    total, width = mixed.shape
    model = own.shape[1]
    block = 2 * HEAD_DIM
    any_spec = pl.BlockSpec(memory_space=pl.ANY)
    columns = pl.BlockSpec((total, block), lambda j: (0, j))
    rows = pl.BlockSpec((block, model), lambda j: (j, 0))
    return pl.pallas_call(
        functools.partial(out_back_kernel, n_exp, jobs),
        grid=(width // block,),
        in_specs=[
            columns,
            pl.BlockSpec(own.shape, lambda j: (0, 0)),
            pl.BlockSpec(own.shape, lambda j: (0, 0)),
            rows,
            pl.BlockSpec(valid.shape, lambda j: (0, 0)),
            any_spec,
            any_spec,
        ],
        out_specs=[rows, columns, any_spec],
        out_shape=[
            jax.ShapeDtypeStruct((width, model), bf16),
            jax.ShapeDtypeStruct((total, width), bf16),
            jax.ShapeDtypeStruct(into.shape, bf16),
        ],
        input_output_aliases={6: 2},
        scratch_shapes=[pltpu.VMEM((total, model), bf16), pltpu.SemaphoreType.DMA((2, len(jobs)))],
        compiler_params=pltpu.CompilerParams(
            vmem_limit_bytes=40 * MIB, collective_id=12, has_side_effects=True
        ),
        cost_estimate=pl.CostEstimate(
            flops=4 * total * model * width, bytes_accessed=24 * MIB, transcendentals=0
        ),
    )(mixed, own, sib, weight, valid, chip, into)


def pick(core, first, second):
    return jnp.where(core == 0, first, second)


def column_halves(weight, core):
    width = weight.shape[1] // KEY_VALUE_HEADS
    parts = [weight[:, i * width : (i + 1) * width] for i in range(KEY_VALUE_HEADS)]
    mine = [pick(core, parts[i], parts[i + 1]) for i in range(0, KEY_VALUE_HEADS, 2)]
    other = [pick(core, parts[i + 1], parts[i]) for i in range(0, KEY_VALUE_HEADS, 2)]
    return mine, other


LOG2E = 1.4426950408889634
MIB = 1 << 20


def rotate_rows(vectors, cosine_table, signed_sine):
    return vectors * cosine_table + pltpu.roll(vectors, HEAD_DIM // 2, 1) * signed_sine


def rotate_rows_back(gradient, cosine_table, signed_sine):
    return gradient * cosine_table - pltpu.roll(gradient, HEAD_DIM // 2, 1) * signed_sine


def dot_cols(first, second):
    return lax.dot_general(
        first, second, (((1,), (1,)), ((), ())), preferred_element_type=jnp.float32
    )


def dot_plain(first, second):
    return jnp.dot(first, second, preferred_element_type=jnp.float32)


def ordered_weight(n_y, weight_ref, ordered_ref):
    n_xz = weight_ref.shape[0] // n_y
    weight = jnp.concatenate(
        [weight_ref[y * n_xz + i, c] for y in range(n_y) for c in range(2) for i in range(n_xz)], 0
    )
    ordered_ref[...] = weight
    return weight


def store_rotated(raw, gain, cos_ref, sin_ref, low_ref):
    tokens = cos_ref.shape[0]
    for h in range(2):
        columns = slice(h * HEAD_DIM, (h + 1) * HEAD_DIM)
        head = raw[:, columns]
        inverse = lax.rsqrt(jnp.mean(head * head, axis=-1, keepdims=True) + EPS)
        scaled = head * inverse * gain
        for s in range(2):
            part = slice(s * tokens, (s + 1) * tokens)
            low_ref[part, columns] = rotate_rows(scaled[part], cos_ref[...], sin_ref[...]).astype(
                jnp.bfloat16
            )


def key_value_kernel(
    n_y,
    own_ref,
    sib_ref,
    row_gain_ref,
    weight_ref,
    gain_ref,
    cos_ref,
    sin_ref,
    raw_ref,
    low_ref,
    ordered_ref,
    normed_ref,
):
    tokens = own_ref.shape[0]

    @pl.when(pl.program_id(0) == 0)
    def _():
        for s, source in enumerate((own_ref, sib_ref)):
            hidden = source[...].astype(jnp.float32)
            inverse = lax.rsqrt(jnp.mean(hidden * hidden, axis=-1, keepdims=True) + EPS)
            normed_ref[s * tokens : (s + 1) * tokens] = (hidden * inverse * row_gain_ref[...]).astype(
                jnp.bfloat16
            )

    raw = dot_plain(normed_ref[...], ordered_weight(n_y, weight_ref, ordered_ref))
    raw_ref[...] = raw

    @pl.when(pl.program_id(0) == 0)
    def _():
        store_rotated(raw, gain_ref[...], cos_ref, sin_ref, low_ref)

    @pl.when(pl.program_id(0) == 1)
    def _():
        low_ref[...] = raw.astype(jnp.bfloat16)


def query_kernel(n_y, n_exp, normed_ref, weight_ref, gain_ref, cos_ref, sin_ref, *refs):
    if n_exp:
        raw_ref, low_ref, ordered_ref, gate_full_ref, up_full_ref, cots_ref, tables_ref = refs[4:11]
        plane = Plane(n_exp, (gate_full_ref, up_full_ref), refs[11])
        column = Column(n_exp, (cots_ref, tables_ref), refs[12])

        @pl.when(pl.program_id(0) == 0)
        def _():
            greet(column.z, n_exp, plane.ids, (CORE, X, Y, UP, DOWN))
            plane.each(START, False)
            column.sends(2, START)
            column.passes(1, START)
    else:
        raw_ref, low_ref, ordered_ref = refs
    raw = dot_plain(normed_ref[...], ordered_weight(n_y, weight_ref, ordered_ref))
    raw_ref[...] = raw
    store_rotated(raw, gain_ref[...], cos_ref, sin_ref, low_ref)
    if n_exp:

        @pl.when(pl.program_id(0) == pl.num_programs(0) - 1)
        def _():
            plane.each(WAIT, False)
            column.arrivals(2)
            column.sends(2, WAIT_SEND)
            column.passes(1, WAIT)


def project_kernel(
    n_y,
    n_exp,
    own_ref,
    sib_ref,
    row_gain_ref,
    weight_ref,
    key_gain_ref,
    gain_ref,
    cos_ref,
    sin_ref,
    *refs,
):
    raw_ref, low_ref, ordered_ref, turned_ref, kv_full_ref = refs[5:10]
    gate_full_ref, up_full_ref, cots_ref, tables_ref, kv_scr, normed_ref = refs[10:16]
    plane_sem, column_sem, kv_sems = refs[16:]
    plane = Plane(n_exp, (gate_full_ref, up_full_ref), plane_sem)
    column = Column(n_exp, (cots_ref, tables_ref), column_sem)
    column.own = (refs[0], tables_ref.at[column.z, column.core])
    j, tokens = pl.program_id(0), own_ref.shape[0]
    here = kv_full_ref.at[:, pl.ds(pl.multiple_of(column.x * tokens, tokens), tokens)]
    kv_copies = [
        pltpu.make_async_remote_copy(
            src_ref=kv_scr,
            dst_ref=here,
            send_sem=kv_sems.at[0],
            recv_sem=kv_sems.at[1],
            device_id=column.ids[X],
            device_id_type=MESH,
        ),
        pltpu.make_async_copy(kv_scr, here, kv_sems.at[2]),
    ]

    @pl.when(j == 0)
    def _():
        greet(column.z, n_exp, plane.ids, (CORE, X, Y, UP, DOWN))
        plane.each(START, False)
        column.sends(1, START)
        for s, source in enumerate((own_ref, sib_ref)):
            hidden = source[...].astype(jnp.float32)
            inverse = lax.rsqrt(jnp.mean(hidden * hidden, axis=-1, keepdims=True) + EPS)
            normed_ref[s * tokens : (s + 1) * tokens] = (hidden * inverse * row_gain_ref[...]).astype(
                jnp.bfloat16
            )

    @pl.when(j == pl.num_programs(0) // 2)
    def _():
        column.arrivals(1)
        column.sends(2, START)
        column.passes(1, START)

    raw = dot_plain(normed_ref[...], ordered_weight(n_y, weight_ref, ordered_ref))
    raw_ref[...] = raw

    @pl.when(j != 1)
    def _():
        gain = jnp.where(j == 0, key_gain_ref[...], gain_ref[...])
        store_rotated(raw, gain, cos_ref, sin_ref, low_ref)

    @pl.when(j == 1)
    def _():
        low_ref[...] = raw.astype(jnp.bfloat16)
        turned_ref[...] = normed_ref[...].T

    for which in range(2):

        @pl.when(j == which)
        def _(which=which):
            width = low_ref.shape[1]
            for s in range(2):
                kv_scr[s, :, which * width : (which + 1) * width] = low_ref[
                    s * tokens : (s + 1) * tokens
                ]
            if which:
                for copy in kv_copies:
                    copy.start()

    @pl.when(j == pl.num_programs(0) - 1)
    def _():
        for copy in kv_copies:
            copy.wait()
        plane.each(WAIT, False)
        column.arrivals(2)
        for hop in (1, 2):
            column.sends(hop, WAIT_SEND)
        column.passes(1, WAIT)


def project_all(own, sib, row_gain, gathered, blocks, key_gain, gain, cos, sin, cot, n_y, n_exp, moving):
    bf16 = jnp.bfloat16
    tokens, model = own.shape
    total, width = 2 * tokens, 2 * HEAD_DIM
    n_yxz, _, rows, _ = gathered.shape
    fixed = lambda j: (0, 0)
    block = lambda j: jnp.where(j < 2, blocks + j, j - 2)
    any_specs = [pl.BlockSpec(memory_space=pl.ANY)] * len(moving)
    columns = pl.BlockSpec((total, width), lambda j: (0, block(j)))
    return pl.pallas_call(
        functools.partial(project_kernel, n_y, n_exp),
        grid=(blocks + 2,),
        in_specs=[pl.BlockSpec(own.shape, fixed)] * 2
        + [
            pl.BlockSpec((1, model), fixed),
            pl.BlockSpec((n_yxz, 2, rows, width), lambda j: (0, 0, 0, block(j))),
            pl.BlockSpec((1, HEAD_DIM), fixed),
            pl.BlockSpec((1, HEAD_DIM), fixed),
            pl.BlockSpec(cos.shape, fixed),
            pl.BlockSpec(cos.shape, fixed),
            pl.BlockSpec(memory_space=pl.ANY),
        ]
        + any_specs,
        out_specs=[
            columns,
            columns,
            pl.BlockSpec((model, width), lambda j: (0, block(j))),
            pl.BlockSpec((model, total), fixed),
            pl.BlockSpec(memory_space=pl.ANY),
        ]
        + any_specs,
        out_shape=[
            jax.ShapeDtypeStruct((total, (blocks + 2) * width), jnp.float32),
            jax.ShapeDtypeStruct((total, (blocks + 2) * width), bf16),
            jax.ShapeDtypeStruct((model, (blocks + 2) * width), bf16),
            jax.ShapeDtypeStruct((model, total), bf16),
            jax.ShapeDtypeStruct((2, 2 * tokens, 2 * width), bf16),
        ]
        + [jax.ShapeDtypeStruct(a.shape, a.dtype) for a in moving],
        scratch_shapes=[
            pltpu.VMEM((2, tokens, 2 * width), bf16),
            pltpu.VMEM((total, model), bf16),
            plane_sems(2),
            column_sems(2, n_exp),
            pltpu.SemaphoreType.DMA((3,)),
        ],
        input_output_aliases={9 + i: 5 + i for i in range(len(moving))},
        compiler_params=pltpu.CompilerParams(
            vmem_limit_bytes=60 * MIB, collective_id=4, has_side_effects=True
        ),
        cost_estimate=pl.CostEstimate(
            flops=2 * total * model * (blocks + 2) * width, bytes_accessed=64 * MIB, transcendentals=0
        ),
    )(own, sib, row_gain, gathered, key_gain, gain, cos, sin, cot, *moving)


def projection_specs(normed_shape, gathered, first_block, blocks, cos):
    total, model = normed_shape
    n_yxz, _, rows, _ = gathered.shape
    width = 2 * HEAD_DIM
    fixed = lambda j: (0, 0)
    moving = lambda j: (0, j)
    weight = pl.BlockSpec((n_yxz, 2, rows, width), lambda j: (0, 0, 0, j + first_block))
    tail = [pl.BlockSpec((1, HEAD_DIM), fixed), pl.BlockSpec(cos.shape, fixed), pl.BlockSpec(cos.shape, fixed)]
    out_specs = [pl.BlockSpec((total, width), moving)] * 2 + [pl.BlockSpec((model, width), moving)]
    out_shape = [
        jax.ShapeDtypeStruct((total, blocks * width), jnp.float32),
        jax.ShapeDtypeStruct((total, blocks * width), jnp.bfloat16),
        jax.ShapeDtypeStruct((model, blocks * width), jnp.bfloat16),
    ]
    cost = pl.CostEstimate(
        flops=2 * total * model * blocks * width,
        bytes_accessed=total * model * 2 + blocks * width * (model * 4 + total * 6),
        transcendentals=0,
    )
    return weight, tail, out_specs, out_shape, cost


def project_keys(own, sib, row_gain, gathered, first_block, gain, cos, sin, n_y):
    tokens, model = own.shape
    normed_shape = (2 * tokens, model)
    weight, tail, out_specs, out_shape, cost = projection_specs(normed_shape, gathered, first_block, 2, cos)
    fixed = lambda j: (0, 0)
    return pl.pallas_call(
        functools.partial(key_value_kernel, n_y),
        grid=(2,),
        in_specs=[pl.BlockSpec(own.shape, fixed)] * 2
        + [pl.BlockSpec((1, model), fixed), weight]
        + tail,
        out_specs=out_specs + [pl.BlockSpec(normed_shape, fixed)],
        out_shape=out_shape + [jax.ShapeDtypeStruct(normed_shape, jnp.bfloat16)],
        compiler_params=pltpu.CompilerParams(vmem_limit_bytes=56 * MIB),
        cost_estimate=cost,
    )(own, sib, row_gain, gathered, gain, cos, sin)


def project_queries(normed, gathered, blocks, gain, cos, sin, n_y, n_exp, moving):
    weight, tail, out_specs, out_shape, cost = projection_specs(normed.shape, gathered, 0, blocks, cos)
    any_specs = [pl.BlockSpec(memory_space=pl.ANY)] * len(moving)
    return pl.pallas_call(
        functools.partial(query_kernel, n_y, n_exp if moving else 0),
        grid=(blocks,),
        in_specs=[pl.BlockSpec(normed.shape, lambda j: (0, 0)), weight] + tail + any_specs,
        out_specs=out_specs + any_specs,
        out_shape=out_shape + [jax.ShapeDtypeStruct(a.shape, a.dtype) for a in moving],
        scratch_shapes=[plane_sems(2), column_sems(2, n_exp)] if moving else [],
        input_output_aliases={5 + i: 3 + i for i in range(len(moving))},
        compiler_params=pltpu.CompilerParams(
            vmem_limit_bytes=56 * MIB,
            collective_id=4 if moving else None,
            has_side_effects=bool(moving),
        ),
        cost_estimate=cost,
    )(normed, gathered, gain, cos, sin, *moving)


def mask_bias(seg_key, info):
    keys, tokens = seg_key.shape[0], info.shape[1]
    key_pos = lax.broadcasted_iota(jnp.int32, (keys, tokens), 0)
    allowed = (seg_key == info[0:1]) & (key_pos <= info[1:2])
    return jnp.where(allowed, 0.0, MASKED)


def key_tile(keys):
    return min(keys, 256)


def attention_kernel(hops, info_ref, seg_ref, q_ref, k_ref, v_ref, *refs):
    if hops:
        mixed_ref, recip_ref, gate_ref, up_ref, cots_ref, tables_ref = refs[4:10]
        bias_ref, vt_ref, plane_sem, sems = refs[10:]
        column = Column(hops, (cots_ref, tables_ref), sems)
        plane = Plane(hops, (gate_ref, up_ref), plane_sem)
        places = [pl.program_id(i) for i in range(3)]
        ends = [pl.num_programs(i) - 1 for i in range(3)]

        @pl.when((places[0] == 0) & (places[1] == 0) & (places[2] == 0))
        def _():
            greet(column.z, hops, column.ids, (CORE, X, Y, UP, DOWN))
            plane.each(START, True)
            column.sends(hops - 1, START)
            column.passes(hops - 2, START)
    else:
        mixed_ref, recip_ref, bias_ref, vt_ref = refs
    keys = k_ref.shape[1]
    tile = key_tile(keys)

    @pl.when((pl.program_id(1) == 0) & (pl.program_id(2) == 0))
    def _():
        bias_ref[...] = mask_bias(seg_ref[0], info_ref[0])

    @pl.when(pl.program_id(2) == 0)
    def _():
        vt_ref[...] = v_ref[0].astype(jnp.float32).T.astype(jnp.bfloat16)

    queries = q_ref[...]
    total, mixed = None, None
    for start in range(0, keys, tile):
        part = slice(start, start + tile)
        scores = dot_cols(k_ref[0, part], queries) * (HEAD_DIM**-0.5 * LOG2E) + bias_ref[part]
        weights = jnp.exp2(scores)
        tile_total = jnp.sum(weights, axis=0, keepdims=True)
        tile_mixed = dot_plain(vt_ref[:, part], weights.astype(jnp.bfloat16))
        total = tile_total if total is None else total + tile_total
        mixed = tile_mixed if mixed is None else mixed + tile_mixed
    recip = 1.0 / total
    recip_ref[0] = recip
    valid = (info_ref[0, 0:1] > 0).astype(jnp.float32)
    mixed_ref[...] = (mixed * (recip * valid)).T.astype(jnp.bfloat16)
    if hops:

        @pl.when((places[0] == ends[0]) & (places[1] == ends[1]) & (places[2] == ends[2]))
        def _():
            plane.each(WAIT, True)
            column.arrivals(hops - 1)
            column.passes(hops - 1, START)
            column.sends(hops - 1, WAIT_SEND)
            column.passes(hops - 2, WAIT)
            column.passes(hops - 1, WAIT)


def attention_specs(tokens, keys, groups, per_group):
    head = pl.BlockSpec((tokens, HEAD_DIM), lambda s, g, h: (s, g * per_group + h))
    return dict(
        info=pl.BlockSpec((1, 8, tokens), lambda s, g, h: (s, 0, 0)),
        seg=pl.BlockSpec((1, keys, 1), lambda s, g, h: (s, 0, 0)),
        head=head,
        key=pl.BlockSpec((1, keys, HEAD_DIM), lambda s, g, h: (s, 0, g)),
        value=pl.BlockSpec((1, keys, HEAD_DIM), lambda s, g, h: (s, 0, groups + g)),
        recip=pl.BlockSpec((1, 1, tokens), lambda s, g, h: ((s * groups + g) * per_group + h, 0, 0)),
    )


def attend(info, seg_keys, queries, kv_full, groups, per_group, n_exp, moving):
    tokens, keys = info.shape[2], seg_keys.shape[1]
    specs = attention_specs(tokens, keys, groups, per_group)
    steps = 2 * groups * per_group
    return pl.pallas_call(
        functools.partial(attention_kernel, n_exp if moving else 0),
        grid=(2, groups, per_group),
        in_specs=[specs[INFO], specs[SEG], specs[HEAD], specs[KEY], specs[VALUE]]
        + [pl.BlockSpec(memory_space=pl.ANY)] * len(moving),
        out_specs=[specs[HEAD], specs[RECIP]]
        + [pl.BlockSpec(memory_space=pl.ANY)] * len(moving),
        out_shape=[
            jax.ShapeDtypeStruct((2 * tokens, groups * per_group * HEAD_DIM), jnp.bfloat16),
            jax.ShapeDtypeStruct((steps, 1, tokens), jnp.float32),
        ]
        + [jax.ShapeDtypeStruct(a.shape, a.dtype) for a in moving],
        scratch_shapes=[
            pltpu.VMEM((keys, tokens), jnp.float32),
            pltpu.VMEM((HEAD_DIM, keys), jnp.bfloat16),
        ]
        + ([plane_sems(2), column_sems(2, n_exp)] if moving else []),
        input_output_aliases={5 + i: 2 + i for i in range(len(moving))},
        compiler_params=pltpu.CompilerParams(
            vmem_limit_bytes=48 * MIB,
            collective_id=5 if moving else None,
            has_side_effects=bool(moving),
        ),
        cost_estimate=pl.CostEstimate(
            flops=steps * 8 * tokens * keys * HEAD_DIM,
            bytes_accessed=queries.size * 4 + kv_full.size * 2,
            transcendentals=steps * tokens * keys,
        ),
    )(info, seg_keys, queries, kv_full, kv_full, *moving)


def attention_back_kernel(
    info_ref,
    seg_ref,
    q_ref,
    k_ref,
    v_ref,
    mixed_ref,
    grad_ref,
    recip_ref,
    raw_ref,
    gain_ref,
    cos_ref,
    sin_ref,
    chip_ref,
    into_in_ref,
    raw_grad_ref,
    key_grad_ref,
    value_grad_ref,
    gain_grad_ref,
    into_ref,
    bias_ref,
    kt_ref,
    job_sems,
    *,
    n_exp,
    jobs,
):
    sent = [sent_rows(chip_ref, into_ref, job, job_sems, i, n_exp) for i, job in enumerate(jobs)]
    places = [pl.program_id(i) for i in range(3)]
    ends = [pl.num_programs(i) - 1 for i in range(3)]

    @pl.when((places[0] == 0) & (places[1] == 0) & (places[2] == 0))
    def _():
        greet_slots(sorted({job[2] for job in jobs}), n_exp)
        for copy in sent:
            copy.start()

    keys = k_ref.shape[1]
    tile = key_tile(keys)
    scale = HEAD_DIM**-0.5
    first = (pl.program_id(1) == 0) & (pl.program_id(2) == 0)

    @pl.when(first)
    def _():
        bias_ref[...] = mask_bias(seg_ref[0], info_ref[0])

    @pl.when(first & (pl.program_id(0) == 0))
    def _():
        gain_grad_ref[...] = jnp.zeros_like(gain_grad_ref)

    @pl.when(pl.program_id(2) == 0)
    def _():
        kt_ref[...] = k_ref[0].astype(jnp.float32).T.astype(jnp.bfloat16)
        key_grad_ref[...] = jnp.zeros_like(key_grad_ref)
        value_grad_ref[...] = jnp.zeros_like(value_grad_ref)

    queries, grad = q_ref[...], grad_ref[...]
    recip = recip_ref[0]
    overlap = grad.astype(jnp.float32) * mixed_ref[...].astype(jnp.float32)
    inner = jnp.sum(overlap.T, axis=0, keepdims=True)
    query_grad = None
    for start in range(0, keys, tile):
        part = slice(start, start + tile)
        scores = dot_cols(k_ref[0, part], queries) * (scale * LOG2E) + bias_ref[part]
        probs = jnp.exp2(scores) * recip
        grad_probs = dot_cols(v_ref[0, part], grad)
        grad_scores = (probs * (grad_probs - inner)).astype(jnp.bfloat16)
        value_grad_ref[0, part] += dot_plain(probs.astype(jnp.bfloat16), grad)
        key_grad_ref[0, part] += dot_plain(grad_scores, queries) * scale
        tile_grad = dot_plain(kt_ref[:, part], grad_scores)
        query_grad = tile_grad if query_grad is None else query_grad + tile_grad
    turned = rotate_rows_back((query_grad * scale).T, cos_ref[...], sin_ref[...])
    raw = raw_ref[...]
    inverse = lax.rsqrt(jnp.mean(raw * raw, axis=-1, keepdims=True) + EPS)
    unit = raw * inverse
    gain_grad_ref[0:1] += jnp.sum(turned * unit, axis=0, keepdims=True)
    scaled = turned * gain_ref[...]
    raw_grad_ref[...] = (
        inverse * (scaled - unit * jnp.mean(scaled * unit, axis=-1, keepdims=True))
    ).astype(jnp.bfloat16)

    @pl.when((places[0] == ends[0]) & (places[1] == ends[1]) & (places[2] == ends[2]))
    def _():
        for copy in sent:
            copy.wait()


def attend_back(
    info,
    seg_keys,
    queries,
    kv_full,
    mixed,
    grad_mixed,
    recip,
    raw,
    gain,
    cos,
    sin,
    groups,
    per_group,
    chip,
    into,
    jobs,
    n_exp,
):
    tokens, keys = info.shape[2], seg_keys.shape[1]
    specs = attention_specs(tokens, keys, groups, per_group)
    steps = 2 * groups * per_group
    fixed = lambda s, g, h: (0, 0)
    key_grad = jax.ShapeDtypeStruct((2, keys, groups * HEAD_DIM), jnp.float32)
    return pl.pallas_call(
        functools.partial(attention_back_kernel, n_exp=n_exp, jobs=jobs),
        grid=(2, groups, per_group),
        in_specs=[specs[INFO], specs[SEG], specs[HEAD], specs[KEY], specs[VALUE]]
        + [specs[HEAD], specs[HEAD], specs[RECIP], specs[HEAD]]
        + [pl.BlockSpec(a.shape, fixed) for a in (gain, cos, sin)]
        + [pl.BlockSpec(memory_space=pl.ANY)] * 2,
        out_specs=[specs[HEAD], specs[KEY], specs[KEY], pl.BlockSpec((8, HEAD_DIM), fixed)]
        + [pl.BlockSpec(memory_space=pl.ANY)],
        out_shape=[
            jax.ShapeDtypeStruct((2 * tokens, groups * per_group * HEAD_DIM), jnp.bfloat16),
            key_grad,
            key_grad,
            jax.ShapeDtypeStruct((8, HEAD_DIM), jnp.float32),
            jax.ShapeDtypeStruct(into.shape, into.dtype),
        ],
        scratch_shapes=[
            pltpu.VMEM((keys, tokens), jnp.float32),
            pltpu.VMEM((HEAD_DIM, keys), jnp.bfloat16),
            pltpu.SemaphoreType.DMA((2, len(jobs))),
        ],
        input_output_aliases={13: 4},
        compiler_params=pltpu.CompilerParams(
            vmem_limit_bytes=48 * MIB, collective_id=6, has_side_effects=True
        ),
        cost_estimate=pl.CostEstimate(
            flops=steps * 20 * tokens * keys * HEAD_DIM,
            bytes_accessed=queries.size * 12 + kv_full.size * 6,
            transcendentals=steps * tokens * keys,
        ),
    )(
        info, seg_keys, queries, kv_full, kv_full, mixed, grad_mixed, recip, raw, gain, cos, sin, chip, into
    )


def moe_kernel(
    n_exp,
    n_y,
    local_experts,
    table_ref,
    own_ref,
    own_cot_ref,
    cots_ref,
    gate_any,
    up_any,
    down_any,
    x_ref,
    val_ref,
    product_ref,
    gate_grad_ref,
    up_grad_ref,
    tokens_ref,
    partial_ref,
    grad_chip_ref,
    out_chip_ref,
    grad_into_ref,
    out_into_ref,
    gate_w,
    up_w,
    down_w,
    token_scr,
    cot_scr,
    held,
    send,
    got,
    weight_sems,
    load_sems,
    token_sems,
    core_sems,
    local_sems,
    grad_sems,
):
    bf16, f32 = jnp.bfloat16, jnp.float32
    column = Column(n_exp, (tokens_ref,), token_sems, (own_ref,))
    z, core = column.z, column.core
    c, q = pl.program_id(0), pl.program_id(1)
    e, s = q // 2, (q % 3 + 1) // 2
    owner = core + s * (1 - 2 * core)
    chip = xor_chip(z, c, n_exp)
    slots, tokens = x_ref.shape[1], token_scr.shape[1]

    def weight_copies(expert):
        for which, (source, target) in enumerate(
            ((gate_any, gate_w), (up_any, up_w), (down_any, down_w))
        ):
            chips, cores, _, depth, _ = source.shape
            n_x = chips // n_y
            for p in range(chips):
                for k in range(cores):
                    start = ((p // n_x * cores + k) * n_x + p % n_x) * depth
                    yield pltpu.make_async_copy(
                        source.at[p, k, expert],
                        target.at[expert, pl.ds(start, depth)],
                        weight_sems.at[which, expert, p * cores + k],
                    )

    def load(which, sources, methods):
        copies = [
            pltpu.make_async_copy(source, scratch.at[which], load_sems.at[which, i])
            for i, (source, scratch) in enumerate(zip(sources, (token_scr, cot_scr)))
        ]
        for method in methods:
            for copy in copies:
                getattr(copy, method)()

    def fetch(i):
        return pltpu.make_async_copy(partial_ref.at[c, i], got.at[i], local_sems.at[i])

    def store(chunk, i):
        target = (grad_chip_ref, out_chip_ref)[i].at[chunk]
        return pltpu.make_async_copy(got.at[i], target, local_sems.at[2 + i])

    other_parts = (tokens_ref.at[chip, 1 - core], cots_ref.at[chip, 1 - core])

    def core_copy(chunk, i):
        return pltpu.make_async_remote_copy(
            src_ref=send.at[i],
            dst_ref=partial_ref.at[chunk, i],
            send_sem=core_sems.at[0, chunk, i],
            recv_sem=core_sems.at[1, chunk, i],
            device_id=column.ids[CORE],
            device_id_type=MESH,
        )

    def grad_copy(chunk):
        return pltpu.make_async_remote_copy(
            src_ref=grad_chip_ref.at[chunk],
            dst_ref=grad_into_ref.at[chunk],
            send_sem=grad_sems.at[0, chunk],
            recv_sem=grad_sems.at[1, chunk],
            device_id={EXP: xor_chip(z, chunk, n_exp)},
            device_id_type=MESH,
        )

    @pl.when((c == 0) & (q == 0))
    def _():
        barrier = pltpu.get_barrier_semaphore()
        greeted = [column.ids[CORE]] + [{EXP: xor_chip(z, k, n_exp)} for k in range(1, n_exp)]
        for there in greeted:
            pl.semaphore_signal(barrier, inc=1, device_id=there, device_id_type=MESH)
        pl.semaphore_wait(barrier, n_exp)
        column.sends(1, START)
        column.pass_own(START)
        for expert in range(2):
            for copy in weight_copies(expert):
                copy.start()
        load(0, (own_ref, own_cot_ref), (START, WAIT))
        for copy in weight_copies(0):
            copy.wait()

    @pl.when((c > 0) & (q == 0))
    def _():
        column.arrivals(c)
        pl.when(c < n_exp - 1)(lambda: column.sends(c + 1, START))
        column.passes(c, START)
        load(0, (tokens_ref.at[chip, core], cots_ref.at[chip, core]), (START,))
        for i in range(2):
            store(c - 1, i).wait()
        pl.when(c == n_exp - 1)(lambda: grad_copy(1).start())
        pl.when(c > 2)(lambda: grad_copy(c - 1).start())
        load(0, (tokens_ref.at[chip, core], cots_ref.at[chip, core]), (WAIT,))

    @pl.when(q == 1)
    def _():
        for copy in column.copies(2, chip, False):
            copy.wait_recv()
        load(1, other_parts, (START, WAIT))

    @pl.when((c == 0) & (q == 2))
    def _():
        for copy in weight_copies(1):
            copy.wait()

    slot_ids = lax.broadcasted_iota(jnp.int32, (slots, tokens), 0).astype(f32)
    expert_rows = table_ref.shape[2] // 2
    first_row = z * local_experts + core * 2

    def hits_of(expert):
        return table_ref[chip, owner, pl.ds(first_row + expert, 1)] == slot_ids

    hits = hits_of(e)
    one_hot = hits.astype(f32).astype(bf16)
    gates = table_ref[chip, owner, pl.ds(expert_rows + first_row + e, 1)]
    gate_row = jnp.sum(jnp.where(hits, gates, 0.0), axis=1, keepdims=True)
    x_rows = dot_plain(one_hot, token_scr[s]).astype(bf16)
    x_ref[0] = x_rows
    grad_val = (gate_row * dot_plain(one_hot, cot_scr[s])).astype(bf16)
    val_ref[0] = grad_val
    gate_act = dot_plain(x_rows, gate_w[e])
    up_act = dot_plain(x_rows, up_w[e])
    sigmoid = 1.0 / (1.0 + jnp.exp(-gate_act))
    silu = gate_act * sigmoid
    product = (silu * up_act).astype(bf16)
    product_ref[0] = product
    grad_product = dot_cols(grad_val, down_w[e])
    grad_gate = (grad_product * up_act * (sigmoid * (1.0 + gate_act * (1.0 - sigmoid)))).astype(bf16)
    grad_up = (grad_product * silu).astype(bf16)
    gate_grad_ref[0] = grad_gate
    up_grad_ref[0] = grad_up
    grad_rows = (dot_cols(grad_gate, gate_w[e]) + dot_cols(grad_up, up_w[e])).astype(bf16)
    weighted = (gate_row * dot_plain(product, down_w[e])).astype(bf16)

    @pl.when(e == 0)
    def _():
        held[s, 0] = grad_rows
        held[s, 1] = weighted

    def combined(i, rows):
        before = hits_of(0).astype(f32).astype(bf16)
        return lax.dot_general(
            jnp.concatenate([before, one_hot], 0),
            jnp.concatenate([held[s, i], rows], 0),
            (((0,), (0,)), ((), ())),
            preferred_element_type=f32,
        )

    @pl.when(q == 2)
    def _():
        for i, rows in enumerate((grad_rows, weighted)):
            pl.when(c > 0)(lambda i=i: core_copy(c - 1, i).wait_send())
            send[i] = combined(i, rows).astype(bf16)
            core_copy(c, i).start()

    @pl.when(q == 3)
    def _():
        for i, rows in enumerate((grad_rows, weighted)):
            own = combined(i, rows)
            core_copy(c, i).wait_recv()
            fetch(i).start()
            fetch(i).wait()
            got[i] = (own + got[i].astype(f32)).astype(bf16)
            store(c, i).start()

    @pl.when((c == n_exp - 1) & (q == 3))
    def _():
        column.pass_own(WAIT_SEND)
        for hop in range(1, n_exp):
            column.sends(hop, WAIT_SEND)
            column.passes(hop, WAIT_SEND)
        for i in range(2):
            core_copy(n_exp - 1, i).wait_send()
            store(n_exp - 1, i).wait()
        for chunk in range(1, n_exp - 1):
            grad_copy(chunk).wait()


def run_experts(tables, own, own_cot, cots, weights, n_y, local_experts, slots, n_exp):
    bf16 = jnp.bfloat16
    tokens, model = own.shape
    ff = weights[0].shape[4]
    pieces = weights[0].shape[0] * weights[0].shape[1]
    any_spec = pl.BlockSpec(memory_space=pl.ANY)
    row_spec = lambda width: pl.BlockSpec(
        (1, slots, width), lambda c, q: (q // 2, 2 * c + (q % 3 + 1) // 2, 0)
    )
    widths = (model, model, ff, ff, ff)
    chip_shape = jax.ShapeDtypeStruct((n_exp, tokens, model), bf16)
    results = pl.pallas_call(
        functools.partial(moe_kernel, n_exp, n_y, local_experts),
        grid=(n_exp, 4),
        in_specs=[pl.BlockSpec(tables.shape, lambda c, q: (0, 0, 0, 0))] + [any_spec] * 6,
        out_specs=[row_spec(width) for width in widths] + [any_spec] * 6,
        out_shape=[jax.ShapeDtypeStruct((2, 2 * n_exp * slots, width), bf16) for width in widths]
        + [
            jax.ShapeDtypeStruct(cots.shape, bf16),
            jax.ShapeDtypeStruct((n_exp, 2, tokens, model), bf16),
            chip_shape,
            chip_shape,
            chip_shape,
            chip_shape,
        ],
        scratch_shapes=[
            pltpu.VMEM((2, model, ff), bf16),
            pltpu.VMEM((2, model, ff), bf16),
            pltpu.VMEM((2, ff, model), bf16),
            pltpu.VMEM((2, tokens, model), bf16),
            pltpu.VMEM((2, tokens, model), bf16),
            pltpu.VMEM((2, 2, slots, model), bf16),
            pltpu.VMEM((2, tokens, model), bf16),
            pltpu.VMEM((2, tokens, model), bf16),
            pltpu.SemaphoreType.DMA((3, 2, pieces)),
            pltpu.SemaphoreType.DMA((2, 2)),
            column_sems(1, n_exp),
            pltpu.SemaphoreType.DMA((2, n_exp, 2)),
            pltpu.SemaphoreType.DMA((4,)),
            pltpu.SemaphoreType.DMA((2, n_exp)),
        ],
        compiler_params=pltpu.CompilerParams(
            vmem_limit_bytes=63 * MIB, collective_id=7, has_side_effects=True
        ),
        cost_estimate=pl.CostEstimate(
            flops=4 * n_exp * (12 * slots * model * ff + 8 * slots * tokens * model),
            bytes_accessed=24 * model * ff + 4 * n_exp * slots * (2 * model + 3 * ff) * 2,
            transcendentals=4 * n_exp * slots * ff,
        ),
    )(tables, own, own_cot, cots, *weights)
    return results[:5], *results[7:]


def weight_grad_kernel(
    n_y,
    n_ctx,
    n_exp,
    merged,
    x_ref,
    val_ref,
    product_ref,
    gg_ref,
    gu_ref,
    chip_ref,
    into_in_ref,
    out_chip_ref,
    *refs,
):
    bf16 = jnp.bfloat16
    results, (into_ref, out_into_ref, pt_ref, ggt_ref, gut_ref, job_sems) = refs[:-6], refs[-6:]
    e, n = pl.program_id(0), pl.program_id(1)
    last, rows = n_exp - 1, chip_ref.shape[1]
    sent = [
        sent_rows(chip_ref, into_ref, (last, last, last, 0, rows), job_sems, 0, n_exp),
        sent_rows(out_chip_ref, out_into_ref, (last, last, 1, 0, rows), job_sems, 1, n_exp),
    ]

    @pl.when((e == 0) & (n == 0))
    def _():
        greet_slots([1, last], n_exp)
        for copy in sent:
            copy.start()

    @pl.when(n == 0)
    def _():
        for source, turned in ((product_ref, pt_ref), (gg_ref, ggt_ref), (gu_ref, gut_ref)):
            turned[...] = source[0].T

    gate, up = (dot_plain(turned[...], x_ref[0]).astype(bf16) for turned in (ggt_ref, gut_ref))
    down = dot_plain(pt_ref[...], val_ref[0]).astype(bf16)
    if merged:
        (result,) = results
        depth = result.shape[-2] // (2 * n_y * n_ctx)
        y, c, x = n // (2 * n_ctx), n // n_ctx % 2, n % n_ctx
        result[y, x, c, 0, 0] = gate
        result[y, x, c, 1, 0] = up
        rows = pl.ds(pl.multiple_of(n * depth, depth), depth)
        for shard in range(2 * n_y * n_ctx):
            place = (shard // (2 * n_ctx), shard % n_ctx, shard // n_ctx % 2, 2, 0, rows)
            result[place] = down[shard * depth : (shard + 1) * depth]
    else:
        for grad, result in zip((gate, up), results):
            depth = result.shape[-1]
            for i in range(result.shape[1]):
                result[0, i, 0, 0] = grad[:, i * depth : (i + 1) * depth]
        depth = results[2].shape[4]
        for shard in range(2 * n_y * n_ctx):
            place = (shard // (2 * n_ctx), shard % n_ctx, shard // n_ctx % 2, 0)
            results[2][place] = down[shard * depth : (shard + 1) * depth]

    @pl.when((e == 1) & (n == pl.num_programs(1) - 1))
    def _():
        for copy in sent:
            copy.wait()


def expert_weight_grads(rows, chip, into, out_chip, n_y, n_ctx, n_exp, merged):
    bf16 = jnp.bfloat16
    x_all, val_all, product_all, gg_all, gu_all = rows
    _, total, model = x_all.shape
    ff = gg_all.shape[2]
    shards = 2 * n_y * n_ctx
    col, depth, down_depth = 256, model // shards, ff // shards
    wide = pl.BlockSpec((1, total, col), lambda e, n: (e, 0, n))
    whole = pl.BlockSpec((1, total, ff), lambda e, n: (e, 0, 0))
    any_spec = pl.BlockSpec(memory_space=pl.ANY)
    if merged:
        out_specs = [
            pl.BlockSpec((n_y, n_ctx, 2, 3, 1, ff, depth), lambda e, n: (0, 0, 0, 0, e, 0, 0))
        ]
        out_shape = [jax.ShapeDtypeStruct((n_y, n_ctx, 2, 3, 2, ff, depth), bf16)]
    else:
        k = col // depth

        def place(e, n):
            shard = n * k
            return (shard // (2 * n_ctx), shard % n_ctx // k, shard // n_ctx % 2, e, 0, 0)

        out_specs = [pl.BlockSpec((1, k, 1, 1, ff, depth), place)] * 2
        out_specs.append(
            pl.BlockSpec((n_y, n_ctx, 2, 1, down_depth, col), lambda e, n: (0, 0, 0, e, 0, n))
        )
        out_shape = [jax.ShapeDtypeStruct((n_y, n_ctx, 2, 2, ff, depth), bf16)] * 2
        out_shape.append(jax.ShapeDtypeStruct((n_y, n_ctx, 2, 2, down_depth, model), bf16))
    *blocks, into, out_into = pl.pallas_call(
        functools.partial(weight_grad_kernel, n_y, n_ctx, n_exp, merged),
        grid=(2, model // col),
        in_specs=[wide, wide, whole, whole, whole] + [any_spec] * 3,
        out_specs=out_specs + [any_spec] * 2,
        out_shape=out_shape + [jax.ShapeDtypeStruct(a.shape, a.dtype) for a in (into, out_chip)],
        scratch_shapes=[pltpu.VMEM((ff, total), bf16)] * 3 + [pltpu.SemaphoreType.DMA((2, 2))],
        input_output_aliases={6: len(out_shape)},
        compiler_params=pltpu.CompilerParams(
            vmem_limit_bytes=63 * MIB, collective_id=8, has_side_effects=True
        ),
        cost_estimate=pl.CostEstimate(
            flops=2 * 6 * total * model * ff,
            bytes_accessed=2 * (2 * total * (2 * model + 3 * ff) + 6 * model * ff),
            transcendentals=0,
        ),
    )(x_all, val_all, product_all, gg_all, gu_all, chip, into, out_chip)
    return blocks, into, out_into


def part_grad_kernel(n_y, n_ctx, n_exp, jobs, wide_ref, *refs):
    bf16 = jnp.bfloat16
    sources, refs = (refs[:2], refs[2:]) if len(refs) == 12 else (refs[:1], refs[1:])
    chip_ref, _, out_chip_ref, _, result, into_ref, out_into_ref = refs[:7]
    turned_refs, job_sems = refs[7:-1], refs[-1]
    e, n = pl.program_id(0), pl.program_id(1)
    pairs = ((chip_ref, into_ref), (out_chip_ref, out_into_ref))
    sent = [
        sent_rows(*pairs[which], job, job_sems, i, n_exp) for i, (which, job) in enumerate(jobs)
    ]

    @pl.when((e == 0) & (n == 0))
    def _():
        greet_slots(sorted({job[2] for _, job in jobs}), n_exp)
        for copy in sent:
            copy.start()

    @pl.when(n == 0)
    def _():
        for source, turned in zip(sources, turned_refs):
            turned[...] = source[0].T

    grads = [dot_plain(turned[...], wide_ref[0]).astype(bf16) for turned in turned_refs]
    shards = 2 * n_y * n_ctx
    depth = result.shape[-2] // shards
    if len(grads) == 2:
        y, c, x = n // (2 * n_ctx), n // n_ctx % 2, n % n_ctx
        for i, grad in enumerate(grads):
            result[y, x, c, i, 0] = grad
    else:
        rows = pl.ds(pl.multiple_of(n * depth, depth), depth)
        for shard in range(shards):
            place = (shard // (2 * n_ctx), shard % n_ctx, shard // n_ctx % 2, 0, 0, rows)
            result[place] = grads[0][shard * depth : (shard + 1) * depth]

    @pl.when((e == 1) & (n == pl.num_programs(1) - 1))
    def _():
        for copy in sent:
            copy.wait()


def part_weight_grads(wide, sources, chip, into, out_chip, out_into, jobs, collective, n_y, n_ctx, n_exp):
    bf16 = jnp.bfloat16
    _, total, model = wide.shape
    ff, kinds, col = sources[0].shape[2], len(sources), 256
    whole = pl.BlockSpec((1, total, ff), lambda e, n: (e, 0, 0))
    any_spec = pl.BlockSpec(memory_space=pl.ANY)
    return pl.pallas_call(
        functools.partial(part_grad_kernel, n_y, n_ctx, n_exp, jobs),
        grid=(2, model // col),
        in_specs=[pl.BlockSpec((1, total, col), lambda e, n: (e, 0, n))]
        + [whole] * kinds
        + [any_spec] * 4,
        out_specs=[
            pl.BlockSpec((n_y, n_ctx, 2, kinds, 1, ff, col), lambda e, n: (0, 0, 0, 0, e, 0, 0))
        ]
        + [any_spec] * 2,
        out_shape=[jax.ShapeDtypeStruct((n_y, n_ctx, 2, kinds, 2, ff, col), bf16)]
        + [jax.ShapeDtypeStruct(a.shape, a.dtype) for a in (into, out_into)],
        scratch_shapes=[pltpu.VMEM((ff, total), bf16)] * kinds
        + [pltpu.SemaphoreType.DMA((2, len(jobs)))],
        input_output_aliases={kinds + 2: 1, kinds + 4: 2},
        compiler_params=pltpu.CompilerParams(
            vmem_limit_bytes=60 * MIB, collective_id=collective, has_side_effects=True
        ),
        cost_estimate=pl.CostEstimate(
            flops=4 * kinds * total * model * ff,
            bytes_accessed=4 * (total * (model + kinds * ff) + kinds * model * ff),
            transcendentals=0,
        ),
    )(wide, *sources, chip, into, out_chip, out_into)


def sum_kernel(plan, value_ref, total_ref, held, arrived, sems):
    partners = [{axis: xor_chip(lax.axis_index(axis), hop, size)} for axis, size, hop in plan]
    barrier = pltpu.get_barrier_semaphore()
    for there in partners:
        pl.semaphore_signal(barrier, inc=1, device_id=there, device_id_type=MESH)
    pl.semaphore_wait(barrier, len(plan))
    held[0] = value_ref[...]
    for i, there in enumerate(partners):
        copy = pltpu.make_async_remote_copy(
            src_ref=held.at[i],
            dst_ref=arrived.at[i],
            send_sem=sems.at[0, i],
            recv_sem=sems.at[1, i],
            device_id=there,
            device_id_type=MESH,
        )
        copy.start()
        copy.wait()
        held[i + 1] = held[i] + arrived[i]
    total_ref[...] = held[len(plan)]


def sum_devices(value, axes):
    plan = [(axis, size, 1 << i) for axis, size in axes for i in range(size.bit_length() - 1)]
    spec = pl.BlockSpec(memory_space=pltpu.VMEM)
    return pl.pallas_call(
        functools.partial(sum_kernel, plan),
        in_specs=[spec],
        out_specs=spec,
        out_shape=jax.ShapeDtypeStruct(value.shape, value.dtype),
        scratch_shapes=[
            pltpu.VMEM((len(plan) + 1,) + value.shape, value.dtype),
            pltpu.VMEM((len(plan),) + value.shape, value.dtype),
            pltpu.SemaphoreType.DMA((2, len(plan))),
        ],
        compiler_params=pltpu.CompilerParams(collective_id=9, has_side_effects=True),
    )(value)


def on_device(
    residual_in,
    segments,
    routes,
    gates,
    attn_gain,
    q_proj,
    key_projection,
    value_projection,
    q_gain,
    k_gain,
    o_proj,
    mlp_gain,
    gate_proj,
    up_proj,
    down_proj,
    out_grad,
):
    bf16, f32 = jnp.bfloat16, jnp.float32
    n_seq, n_ctx, n_exp = lax.axis_size(SEQ), lax.axis_size(CTX), lax.axis_size(EXP)
    n_y = n_seq // 2
    devices = n_seq * n_ctx * n_exp
    core = lax.axis_index(SEQ) % 2
    span_index = lax.axis_index(CTX)
    z_index = lax.axis_index(EXP)
    group_all = [
        [(s * n_ctx + x) * n_exp + z for s in range(c, n_seq, 2) for x in range(n_ctx) for z in range(n_exp)]
        for c in range(2)
    ]
    group_plane = [[s * n_ctx + x for s in range(c, n_seq, 2) for x in range(n_ctx)] for c in range(2)]

    def swap(value):
        return lax.ppermute(value, SEQ, [(i, i ^ 1) for i in range(n_seq)])

    def across(value, step):
        return lax.ppermute(value, EXP, [(i, i ^ step) for i in range(n_exp)])

    token_count = residual_in.shape[1]
    model_width = residual_in.shape[2]
    sequence_length = segments.shape[1]
    route_count = routes.shape[2]
    local_experts = gate_proj.shape[0]
    expert_count = local_experts * n_exp
    half_experts = local_experts // 2
    capacity = token_count * route_count * 9 // (expert_count * 8)
    slots = -(-capacity // 16) * 16
    groups = KEY_VALUE_HEADS // 2
    heads = QUERY_HEADS // 2
    heads_per_group = QUERY_HEADS // KEY_VALUE_HEADS
    score_scale = HEAD_DIM ** (-0.5)
    rows = q_proj.shape[0]
    gain_rows = q_gain.shape[0]
    q_width, kv_width = heads * HEAD_DIM, groups * HEAD_DIM
    width = q_width + 2 * kv_width

    route_ids = routes[0]
    route_hit = route_ids[:, :, None] == jnp.arange(expert_count, dtype=jnp.int32)[None, None, :]
    hit_counts = route_hit.astype(jnp.int32).sum(1)
    earlier = jnp.cumsum(hit_counts, axis=0) - hit_counts
    slot_of = jnp.where(hit_counts > 0, earlier, -1).astype(f32)
    gate_of = jnp.sum(jnp.where(route_hit, gates[0][:, :, None], 0.0), axis=1)
    table = jnp.concatenate([slot_of.T, gate_of.T], 0)
    def gain_block(model_parts, head_parts, dtype):
        lead = model_parts[0].shape[:-1]
        fill = lambda size: jnp.zeros(lead + (1, size), dtype)
        first = jnp.concatenate([p[..., None, :] for p in model_parts] + [fill(128 - 2 * rows)], -1)
        second = jnp.concatenate(
            [p[..., None, :] for p in head_parts] + [fill(128 - 2 * gain_rows)], -1
        )
        return jnp.concatenate([first, second, jnp.zeros(lead + (rows - 2, 128), dtype)], -2)

    extra = gain_block([attn_gain, mlp_gain], [q_gain, k_gain], bf16)
    mine_cols, other_cols = [], []
    for weight in (q_proj, key_projection, value_projection):
        mine, other = column_halves(weight, core)
        mine_cols += mine
        other_cols += other
    mine_block = jnp.concatenate(mine_cols + [extra], 1)
    other_block = jnp.concatenate(other_cols + [extra], 1)
    chips = n_y * n_ctx
    own_links = n_y == 2 and n_ctx == 2 and n_exp == 4
    if own_links:
        halves = []
        for weight in (gate_proj, up_proj, down_proj):
            low, high = weight[:half_experts], weight[half_experts:]
            halves += [pick(core, low, high), pick(core, high, low)]
        w_gathered, w_out, gate_full, up_full, down_pair, cots_all, tables_all = gather_chips(
            mine_block,
            other_block,
            halves,
            o_proj.reshape(4, -1, model_width),
            routes[0].T,
            gates[0].T,
            out_grad[0],
            expert_count,
            n_exp,
        )
        w_out = w_out.reshape(q_width, model_width)
        w_gathered = w_gathered.reshape(chips * n_exp, 2, rows, width + 128)
    else:
        theirs = swap(other_block)
        pair = jnp.stack([pick(core, mine_block, theirs), pick(core, theirs, mine_block)])
        w_gathered = lax.all_gather(
            pair, (SEQ, CTX, EXP), axis=0, tiled=False, axis_index_groups=group_all
        )
        cots_all, tables_all = exchange_column(out_grad[0], table, n_exp)
    w_extra = w_gathered[:, :, :2, width:].reshape(n_y, n_ctx * n_exp, 2, 2, 128)
    w_extra = w_extra.transpose(0, 2, 1, 3, 4).reshape(devices, 2, 128).astype(f32)
    gain_attn = w_extra[:, 0, :rows].reshape(model_width)
    gain_mlp_f = w_extra[:, 0, rows : 2 * rows].reshape(model_width)
    gain_query_f = w_extra[:, 1, :gain_rows].reshape(1, HEAD_DIM)
    gain_key_f = w_extra[:, 1, gain_rows : 2 * gain_rows].reshape(1, HEAD_DIM)

    if not own_links:
        w_out = lax.all_gather(
            o_proj, (SEQ, CTX, EXP), axis=0, tiled=True, axis_index_groups=group_all
        )

    def gather_expert(weight, after):
        if own_links:
            both = weight
        else:
            mine = pick(core, weight[:half_experts], weight[half_experts:])
            theirs = swap(pick(core, weight[half_experts:], weight[:half_experts]))
            both = jnp.stack([pick(core, mine, theirs), pick(core, theirs, mine)])
        both = lax.optimization_barrier((both, after))[0]
        full = lax.all_gather(
            both, (SEQ, CTX), axis=0, tiled=False, axis_index_groups=group_plane
        )
        full = full.reshape((n_y * n_ctx,) + both.shape)
        if own_links:
            return full
        full = full.reshape((n_y, n_ctx) + both.shape).transpose(3, 0, 2, 1, 4, 5)
        return full.reshape(1, 1, half_experts, -1, weight.shape[2])

    hidden = residual_in[0].astype(f32)
    seg_two = jnp.stack([segments[0], swap(segments)[0]])
    seg_here = lax.dynamic_slice_in_dim(seg_two, span_index * token_count, token_count, 1)
    valid_two = (seg_here > 0).astype(f32).reshape(2 * token_count, 1)
    valid_rows = valid_two[:token_count]
    positions = span_index * token_count + jnp.arange(token_count, dtype=jnp.int32)
    cos_one, sin_one = rope_tables(positions)
    half_dim = HEAD_DIM // 2
    signed_sine = jnp.concatenate([-sin_one[:, :half_dim], sin_one[:, half_dim:]], 1)
    info = jnp.zeros((2, 8, token_count), jnp.int32)
    info = info.at[:, 0].set(seg_here).at[:, 1].set(positions[None])
    seg_keys = seg_two[:, :, None]
    inv_attn = lax.rsqrt(jnp.mean(hidden * hidden, axis=-1, keepdims=True) + EPS)
    q_blocks = q_width // (2 * HEAD_DIM)
    if own_links:
        q_raw, query_rows, w_query, normed_turned, kv_full, *moving = project_all(
            residual_in[0],
            swap(residual_in[0]),
            gain_attn[None],
            w_gathered,
            q_blocks,
            gain_key_f,
            gain_query_f,
            cos_one,
            signed_sine,
            out_grad[0],
            n_y,
            n_exp,
            (gate_full, up_full, cots_all, tables_all),
        )
    else:
        kv_raw, kv_low, w_kv, normed_two = project_keys(
            residual_in[0],
            swap(residual_in[0]),
            gain_attn[None],
            w_gathered,
            q_blocks,
            gain_key_f,
            cos_one,
            signed_sine,
            n_y,
        )
        kv_here = kv_low.reshape(2, token_count, 2 * kv_width)
        kv_full = lax.all_gather(kv_here, CTX, axis=1, tiled=True)
        q_raw, query_rows, w_query, *moving = project_queries(
            normed_two, w_gathered, q_blocks, gain_query_f, cos_one, signed_sine, n_y, n_exp, ()
        )
    mixed_low, recip, *moving = attend(
        info, seg_keys, query_rows, kv_full, groups, heads_per_group, n_exp, moving
    )
    if own_links:
        gate_full, up_full, cots_all, tables_all = moving
    else:
        gate_full, up_full = gather_expert(gate_proj, gain_attn), gather_expert(up_proj, gain_attn)
    down_full = gather_expert(
        down_pair if own_links else down_proj, query_rows if own_links else gain_attn
    )
    if not own_links:
        tables_all = lax.dynamic_update_slice(
            tables_all, table[None, None], (z_index, core, jnp.int32(0), jnp.int32(0))
        )
    attn_partial = jnp.dot(mixed_low, w_out, preferred_element_type=f32)
    attn_out = attn_partial[:token_count] + swap(attn_partial[token_count:])
    middle = hidden + attn_out
    inv_mlp = lax.rsqrt(jnp.mean(middle * middle, axis=-1, keepdims=True) + EPS)
    normed_mlp = (middle * inv_mlp * gain_mlp_f).astype(bf16)

    rows_all, grad_chip, out_chip, grad_into, out_into = run_experts(
        tables_all,
        normed_mlp,
        out_grad[0],
        cots_all,
        (gate_full, up_full, down_full),
        n_y if own_links else 1,
        local_experts,
        slots,
        n_exp,
    )

    if own_links:
        x_rows, val_rows, product_rows, gate_rows, up_rows = rows_all
        last, first_rows = n_exp - 1, 5 * token_count // 16
        blocks = []
        for i, (wide, sources) in enumerate(
            ((val_rows, (product_rows,)), (x_rows, (gate_rows, up_rows)))
        ):
            span = ((0, first_rows), (first_rows, token_count))[i]
            jobs = [(0, (last, last, last, *span)), (1, (last, last, 1, *span))]
            block, grad_into, out_into = part_weight_grads(
                wide, sources, grad_chip, grad_into, out_chip, out_into, jobs, 13 + i, n_y, n_ctx, n_exp
            )
            blocks.append(block)
    else:
        weight_blocks, grad_into, out_into = expert_weight_grads(
            rows_all, grad_chip, grad_into, out_chip, n_y, n_ctx, n_exp, merged=False
        )
    out_far = (out_chip[2:3].astype(f32) + out_into[3:4].astype(f32)).astype(bf16)

    def scatter_plane(blocks):
        return lax.psum_scatter(
            blocks.reshape((n_y * n_ctx,) + blocks.shape[2:]),
            (SEQ, CTX),
            scatter_dimension=0,
            tiled=True,
            axis_index_groups=group_plane,
        )[0]

    def all_experts(part):
        mine = pick(core, part[0], part[1])
        theirs = swap(pick(core, part[1], part[0]))
        axis = mine.ndim - 3
        both = [pick(core, mine, theirs), pick(core, theirs, mine)]
        return jnp.concatenate(both, axis).astype(f32)

    if own_links:
        parts = []
        for block in blocks:
            part = scatter_plane(block.reshape(n_y, n_ctx, -1, block.shape[-1]))
            parts.append(lax.optimization_barrier(part).reshape(block.shape[2:]))
    else:
        parts = [scatter_plane(weight_blocks[0])]
        for blocks in weight_blocks[1:]:
            blocks, parts[-1] = lax.optimization_barrier((blocks, parts[-1]))
            parts.append(scatter_plane(blocks))

    grad_normed_mlp = grad_chip[0].astype(f32)
    for step in range(1, n_exp):
        grad_normed_mlp = grad_normed_mlp + grad_into[step].astype(f32)
    cotangent = out_grad[0].astype(f32)
    mlp_gain_grad = jnp.sum(grad_normed_mlp * middle * inv_mlp, axis=0)
    grad_middle = cotangent + norm_back(grad_normed_mlp, middle, inv_mlp, gain_mlp_f)
    grad_attn_own = grad_middle.astype(bf16)
    part_rows = token_count // 4
    out_jobs, back_jobs = [(0, 2, 2, 0, part_rows)], [(0, 2, 2, part_rows, token_count)]
    last_jobs = [(1, 1, 1, 0, token_count)]
    o_grad_part, mixture_gradient, out_into = out_back(
        mixed_low, grad_attn_own, swap(grad_attn_own), w_out, valid_two, out_far, out_into, out_jobs, n_exp
    )
    o_grad_plane = scatter_plane(o_grad_part.reshape(n_y, n_ctx, n_exp, -1, model_width))
    grad_q_raw, key_grad, value_grad, q_gain_rows, out_into = attend_back(
        info,
        seg_keys,
        query_rows,
        kv_full,
        mixed_low,
        mixture_gradient,
        recip,
        q_raw,
        gain_query_f,
        cos_one,
        signed_sine,
        groups,
        heads_per_group,
        out_far,
        out_into,
        back_jobs,
        n_exp,
    )
    q_gain_grad = q_gain_rows[0]
    if own_links:
        grad_kv, grad_hidden, attn_gain_grad, k_gain_rows, out_into = back_to_input(
            grad_q_raw,
            key_grad,
            value_grad,
            q_raw,
            w_query,
            gain_key_f,
            cos_one,
            signed_sine,
            residual_in[0],
            gain_attn[None],
            grad_middle,
            out_chip,
            out_into,
            last_jobs,
            n_exp,
        )
        k_gain_grad = k_gain_rows[0]
    else:
        kv_grad = jnp.concatenate([key_grad, value_grad], 2)
        query_part = contract_cols(grad_q_raw, w_query)
        kv_grad_here = lax.psum_scatter(
            kv_grad.astype(bf16), CTX, scatter_dimension=1, tiled=True
        ).astype(f32)
        kv_grad_here = kv_grad_here.reshape(2 * token_count, 2 * kv_width)
        cosine_table, sine_values = jnp.concatenate([cos_one] * 2, 0), jnp.concatenate([sin_one] * 2, 0)
        k_raw = kv_raw[:, :kv_width].reshape(-1, groups, HEAD_DIM)
        inv_key = lax.rsqrt(jnp.mean(k_raw * k_raw, axis=-1, keepdims=True) + EPS)
        grad_kn = inverse_rotation(
            kv_grad_here[:, :kv_width].reshape(-1, groups, HEAD_DIM), cosine_table, sine_values
        )
        k_gain_grad = jnp.sum(grad_kn * k_raw * inv_key, axis=(0, 1))
        grad_k_raw = norm_back(grad_kn, k_raw, inv_key, gain_key_f).astype(bf16)
        grad_kv = jnp.concatenate(
            [grad_k_raw.reshape(-1, kv_width), kv_grad_here[:, kv_width:].astype(bf16)], 1
        )
        normed_partial = query_part + contract_cols(grad_kv, w_kv)
        grad_normed = normed_partial[:token_count] + swap(normed_partial[token_count:])
        attn_gain_grad = jnp.sum(grad_normed * hidden * inv_attn, axis=0)
        grad_hidden = grad_middle + norm_back(grad_normed, hidden, inv_attn, gain_attn)

    extra_grad = gain_block(
        [attn_gain_grad.reshape(devices, rows), mlp_gain_grad.reshape(devices, rows)],
        [q_gain_grad.reshape(devices, gain_rows), k_gain_grad.reshape(devices, gain_rows)],
        f32,
    ).astype(bf16)
    if not own_links:
        near = across(out_chip[1], 1)
        out_into = lax.dynamic_update_slice(out_into, near[None], (1, 0, 0))
    expert_out = out_chip[0].astype(f32)
    for step in (1, 2):
        expert_out = expert_out + out_into[step].astype(f32)
    final_out = (middle + expert_out).astype(bf16)
    sums = [
        jnp.sum(value * value * valid_rows, keepdims=True) for value in (hidden, attn_out, expert_out)
    ]
    sums.append(jnp.sum(valid_rows, keepdims=True))
    stats = jnp.pad(jnp.concatenate(sums, 1), ((0, 7), (0, 124)))
    if not own_links:
        stats = sum_devices(stats, ((SEQ, n_seq), (CTX, n_ctx), (EXP, n_exp)))
    if own_links:
        extra_grad, o_grad_plane, _, stats, final_out = lax.optimization_barrier(
            (extra_grad, o_grad_plane, parts, stats, final_out)
        )
    o_proj_grad = lax.psum_scatter(o_grad_plane, EXP, scatter_dimension=0, tiled=True)
    o_proj_grad = o_proj_grad[0].astype(f32)
    if own_links:
        grad_mine, grad_theirs, stats = dense_grad_scatter(
            normed_turned,
            grad_q_raw,
            grad_kv,
            extra_grad.reshape(n_y, 2, n_ctx, n_exp, rows, 128),
            stats,
            n_exp,
        )
    else:
        w_grad = jnp.concatenate(
            [
                contract_rows(normed_two, grad_q_raw).astype(bf16),
                contract_rows(normed_two, grad_kv).astype(bf16),
                extra_grad.reshape(model_width, 128),
            ],
            1,
        )
        w_grad = w_grad.reshape(n_y, 2, n_ctx, n_exp, rows, width + 128).transpose(0, 2, 3, 1, 4, 5)
        w_grad = lax.psum_scatter(
            scatter_plane(w_grad), EXP, scatter_dimension=0, tiled=True
        )[0]
        grad_mine = pick(core, w_grad[0], w_grad[1])
        grad_theirs = swap(pick(core, w_grad[1], w_grad[0]))
    rms_stats = jnp.sqrt(stats[0, :3] / (stats[0, 3] * model_width))
    if own_links:
        part = all_experts(jnp.concatenate(parts[::-1], 1))
        gate_grad, up_grad = part[0].transpose(0, 2, 1), part[1].transpose(0, 2, 1)
        depth = part.shape[-1]
        down_grad = part[2].reshape(local_experts, model_width // depth, -1, depth)
        down_grad = down_grad.transpose(0, 2, 1, 3).reshape(local_experts, -1, model_width)
    else:
        gate_grad, up_grad = (all_experts(p).transpose(0, 2, 1) for p in parts[:2])
        down_grad = all_experts(parts[2])
    even = pick(core, grad_mine, grad_theirs).astype(f32)
    odd = pick(core, grad_theirs, grad_mine).astype(f32)

    def columns(start, size):
        step = size // groups
        parts = []
        for g in range(groups):
            parts += [half[:, start + g * step : start + (g + 1) * step] for half in (even, odd)]
        return jnp.concatenate(parts, 1)

    extra_total = even[:, width:] + odd[:, width:]
    return (
        final_out[None],
        grad_hidden.astype(bf16)[None],
        extra_total[0, :rows],
        columns(0, q_width),
        columns(q_width, kv_width),
        columns(q_width + kv_width, kv_width),
        extra_total[1, :gain_rows],
        extra_total[1, gain_rows : 2 * gain_rows],
        o_proj_grad,
        extra_total[0, rows : 2 * rows],
        gate_grad,
        up_grad,
        down_grad,
        rms_stats,
    )


def solution(mesh):
    in_specs = (
        P((SEQ, EXP), CTX, None),
        P((SEQ, EXP), None),
        P((SEQ, EXP), CTX, None),
        P((SEQ, EXP), CTX, None),
        P((SEQ, CTX, EXP)),
        P((SEQ, CTX, EXP), None),
        P((SEQ, CTX, EXP), None),
        P((SEQ, CTX, EXP), None),
        P((SEQ, CTX, EXP)),
        P((SEQ, CTX, EXP)),
        P((SEQ, CTX, EXP), None),
        P((SEQ, CTX, EXP)),
        P(EXP, (SEQ, CTX), None),
        P(EXP, (SEQ, CTX), None),
        P(EXP, (SEQ, CTX), None),
        P((SEQ, EXP), CTX, None),
    )
    out_specs = (
        P((SEQ, EXP), CTX, None),
        P((SEQ, EXP), CTX, None),
        P((SEQ, CTX, EXP)),
        P((SEQ, CTX, EXP), None),
        P((SEQ, CTX, EXP), None),
        P((SEQ, CTX, EXP), None),
        P((SEQ, CTX, EXP)),
        P((SEQ, CTX, EXP)),
        P((SEQ, CTX, EXP), None),
        P((SEQ, CTX, EXP)),
        P(EXP, (SEQ, CTX), None),
        P(EXP, (SEQ, CTX), None),
        P(EXP, (SEQ, CTX), None),
        P(),
    )
    return jax.shard_map(
        on_device, mesh=mesh, in_specs=in_specs, out_specs=out_specs, check_vma=False
    )
```

```python
import functools

import jax
import jax.numpy as jnp
from jax import lax
from jax.experimental import pallas as pl
from jax.experimental.pallas import tpu as pltpu
from jax.sharding import PartitionSpec as P

QUERY_HEADS = 32
KEY_VALUE_HEADS = 4
HEAD_DIM = 128


EPS = 1e-06
ROPE_BASE = 1000000.0
MASKED = -1e30
MESH = pl.DeviceIdType.MESH
SEQ = "seq"
CTX = "ctx"
EXP = "exp"
CORE = "core"
X = "x"
Y = "y"
UP = "up"
DOWN = "down"
START = "start"
WAIT = "wait"
WAIT_SEND = "wait_send"
WAIT_RECV = "wait_recv"
INFO = "info"
SEG = "seg"
HEAD = "head"
KEY = "key"
VALUE = "value"
RECIP = "recip"


def contract_rows(first_op, second_op):
    return lax.dot_general(
        first_op, second_op, (((0,), (0,)), ((), ())), preferred_element_type=jnp.float32
    )


def contract_cols(first_op, second_op):
    return lax.dot_general(
        first_op, second_op, (((1,), (1,)), ((), ())), preferred_element_type=jnp.float32
    )


def rope_tables(positions):
    half_dim = HEAD_DIM // 2
    inverse = ROPE_BASE ** (-jnp.arange(half_dim, dtype=jnp.float32) * 2.0 / HEAD_DIM)
    angles = positions.astype(jnp.float32)[:, None] * inverse[None, :]
    cosine_table = jnp.cos(angles)
    sine_values = jnp.sin(angles)
    return (
        jnp.concatenate([cosine_table, cosine_table], -1),
        jnp.concatenate([sine_values, sine_values], -1),
    )


def inverse_rotation(gradient, cosine_table, sine_values):
    half_dim = gradient.shape[-1] // 2
    scaled = gradient * sine_values[:, None, :]
    return gradient * cosine_table[:, None, :] + jnp.concatenate(
        [scaled[..., half_dim:], -scaled[..., :half_dim]], -1
    )


def norm_back(gradient, source, inverse, gain_vec):
    scaled = gradient * gain_vec
    return inverse * scaled - source * inverse**3 * jnp.mean(
        scaled * source, axis=-1, keepdims=True
    )


def neighbours(n_exp):
    seq, x, z = lax.axis_index(SEQ), lax.axis_index(CTX), lax.axis_index(EXP)
    y, core = seq // 2, seq % 2
    ids = {
        CORE: {SEQ: 2 * y + 1 - core},
        X: {CTX: 1 - x},
        Y: {SEQ: 2 * (1 - y) + core},
        UP: {EXP: z + 1},
        DOWN: {EXP: z - 1},
    }
    return x, y, z, core, ids


def greet(z, n_exp, ids, names):
    barrier = pltpu.get_barrier_semaphore()
    count = 0
    for name in names:
        if name in (UP, DOWN):
            there = (z < n_exp - 1) if name == UP else (z > 0)

            @pl.when(there)
            def _():
                pl.semaphore_signal(
                    barrier, inc=1, device_id=ids[name], device_id_type=MESH
                )

            count = count + there.astype(jnp.int32)
        else:
            pl.semaphore_signal(
                barrier, inc=1, device_id=ids[name], device_id_type=MESH
            )
            count = count + 1
    pl.semaphore_wait(barrier, count)


def xor_chip(z, step, n_exp):
    result, bit = 0, 1
    while bit < n_exp:
        result = result + bit * ((z // bit % 2 + step // bit % 2) % 2)
        bit *= 2
    return result


class Plane:
    def __init__(self, n_exp, fulls, sems):
        x, y, _, _, self.ids = neighbours(n_exp)
        self.here, self.beside, self.across = 2 * y + x, 2 * y + 1 - x, 2 * (1 - y) + x
        self.fulls, self.sems = fulls, sems

    def each(self, method, far):
        near = ((self.here,), X), ((self.here,), Y)
        cases = (((self.beside, 0), Y), ((self.across, 1), X)) if far else near
        for which, full in enumerate(self.fulls):
            for lane, (place, name) in enumerate(cases):
                part = full.at[place]
                copy = pltpu.make_async_remote_copy(
                    src_ref=part,
                    dst_ref=part,
                    send_sem=self.sems.at[0, which, lane],
                    recv_sem=self.sems.at[1, which, lane],
                    device_id=self.ids[name],
                    device_id_type=MESH,
                )
                getattr(copy, method)()


def plane_sems(arrays):
    return pltpu.SemaphoreType.DMA((2, arrays, 2))


class Column:
    def __init__(self, n_exp, everyone, sems, own=None):
        self.x, self.y, self.z, self.core, self.ids = neighbours(n_exp)
        self.n_exp, self.everyone, self.sems, self.own = n_exp, everyone, sems, own

    def copies(self, lane, part, first):
        for which, result in enumerate(self.everyone):
            there = result.at[part, self.core]
            yield pltpu.make_async_remote_copy(
                src_ref=self.own[which] if first else there,
                dst_ref=there,
                send_sem=self.sems.at[0, which, lane, part],
                recv_sem=self.sems.at[1, which, lane, part],
                device_id=self.ids[(UP, DOWN, CORE)[lane]],
                device_id_type=MESH,
            )

    def each(self, method, cases, first=False):
        for lane, part, there in cases:

            @pl.when(there)
            def _(lane=lane, part=part):
                for copy in self.copies(lane, part, first):
                    getattr(copy, method)()

    def sends(self, hop, method):
        z, n = self.z, self.n_exp
        cases = (
            (0, z - hop + 1, (z >= hop - 1) & (z < n - 1)),
            (1, z + hop - 1, (z + hop - 1 < n) & (z > 0)),
        )
        self.each(method, cases, first=isinstance(hop, int) and hop == 1)

    def arrivals(self, hop):
        z, n = self.z, self.n_exp
        self.each(WAIT_RECV, ((0, z - hop, z >= hop), (1, z + hop, z + hop < n)))

    def passes(self, hop, method):
        z, n = self.z, self.n_exp
        self.each(method, ((2, z - hop, z >= hop), (2, z + hop, z + hop < n)))

    def pass_own(self, method):
        for copy in self.copies(2, self.z, True):
            getattr(copy, method)()


def column_sems(arrays, n_exp):
    return pltpu.SemaphoreType.DMA((2, arrays, 3, n_exp))


def sent_rows(chip_ref, into_ref, job, sems, i, n_exp):
    slot, into, step, start, stop = job
    rows = pl.ds(start, stop - start)
    return pltpu.make_async_remote_copy(
        src_ref=chip_ref.at[slot, rows],
        dst_ref=into_ref.at[into, rows],
        send_sem=sems.at[0, i],
        recv_sem=sems.at[1, i],
        device_id={EXP: xor_chip(lax.axis_index(EXP), step, n_exp)},
        device_id_type=MESH,
    )


def greet_slots(slots, n_exp):
    barrier = pltpu.get_barrier_semaphore()
    for slot in slots:
        pl.semaphore_signal(
            barrier,
            inc=1,
            device_id={EXP: xor_chip(lax.axis_index(EXP), slot, n_exp)},
            device_id_type=MESH,
        )
    pl.semaphore_wait(barrier, len(slots))


def store_table(routes_ref, gates_ref, table_ref):
    f32, bf16 = jnp.float32, jnp.bfloat16
    experts, tokens = table_ref.shape[0] // 2, table_ref.shape[1]
    expert_ids = lax.broadcasted_iota(jnp.int32, (experts, tokens), 0)
    hits, gates = jnp.zeros((experts, tokens), f32), jnp.zeros((experts, tokens), f32)
    for k in range(routes_ref.shape[0]):
        named = routes_ref[k : k + 1] == expert_ids
        hits = hits + named.astype(f32)
        gates = gates + jnp.where(named, gates_ref[k : k + 1], 0.0)
    row = lax.broadcasted_iota(jnp.int32, (tokens, tokens), 0)
    before = (row < lax.broadcasted_iota(jnp.int32, (tokens, tokens), 1)).astype(f32).astype(bf16)
    table_ref[:experts] = jnp.where(hits > 0.0, dot_plain(hits.astype(bf16), before), -1.0)
    table_ref[experts:] = gates


def gather_kernel(
    n_exp,
    mine_ref,
    other_ref,
    gate_ref,
    other_gate_ref,
    up_ref,
    other_up_ref,
    down_ref,
    other_down_ref,
    out_ref,
    routes_ref,
    gates_ref,
    cot_ref,
    full_ref,
    out_full_ref,
    gate_full_ref,
    up_full_ref,
    down_pair_ref,
    cots_ref,
    tables_ref,
    local_sems,
    core_sems,
    z_sems,
    x_sems,
    y_sems,
    xf_sems,
    yf_sems,
    column_sem,
    first_sems,
    line_sems,
    table_ref,
):
    column = Column(n_exp, (cots_ref, tables_ref), column_sem, (cot_ref, table_ref))
    x, y, z, core, ids = neighbours(n_exp)
    greet(z, n_exp, ids, (CORE, X, Y, UP, DOWN))
    here, beside, across = 2 * y + x, 2 * y + 1 - x, 2 * (1 - y) + x

    fulls = (full_ref, out_full_ref)

    def act(method, place, sems, slot, name):
        for which, full in enumerate(fulls):
            if which and len(place) == 2:
                place = (*place, pl.ds(0, 2))
            part = full.at[place]
            copy = pltpu.make_async_remote_copy(
                src_ref=part,
                dst_ref=part,
                send_sem=sems.at[0, which, slot],
                recv_sem=sems.at[1, which, slot],
                device_id=ids[name],
                device_id_type=MESH,
            )
            getattr(copy, method)()

    def moved(method, place, sems, slot, name):
        part = out_full_ref.at[place]
        copy = pltpu.make_async_remote_copy(
            src_ref=part,
            dst_ref=part,
            send_sem=sems.at[(0, *slot)],
            recv_sem=sems.at[(1, *slot)],
            device_id=ids[name],
            device_id_type=MESH,
        )
        getattr(copy, method)()

    def first_near(method):
        for slot, name in enumerate((X, Y)):
            moved(method, (here, z, pl.ds(2, 2)), first_sems, (slot,), name)

    def first_far(method):
        moved(method, (beside, z, 2), first_sems, (2,), Y)
        moved(method, (across, z, 3), first_sems, (3,), X)

    def line(hop, method):
        for lane, name, part, there in (
            (0, UP, z - hop + 1, (z >= hop - 1) & (z < n_exp - 1)),
            (1, DOWN, z + hop - 1, (z + hop - 1 < n_exp) & (z > 0)),
        ):
            pl.when(there)(
                lambda lane=lane, name=name, part=part: moved(
                    method, (slice(None), part, pl.ds(2, 2)), line_sems, (lane, part), name
                )
            )

    def line_arrivals(hop):
        for lane, name, part, there in (
            (0, UP, z - hop, z >= hop),
            (1, DOWN, z + hop, z + hop < n_exp),
        ):
            pl.when(there)(
                lambda lane=lane, name=name, part=part: moved(
                    WAIT_RECV, (slice(None), part, pl.ds(2, 2)), line_sems, (lane, part), name
                )
            )

    places = (
        full_ref.at[here, z, core],
        gate_full_ref.at[here, core],
        up_full_ref.at[here, core],
        down_pair_ref.at[core],
    )
    kept = [
        pltpu.make_async_copy(source, place, local_sems.at[i])
        for i, (source, place) in enumerate(zip((mine_ref, gate_ref, up_ref, down_ref), places))
    ]
    kept.insert(1, pltpu.make_async_copy(out_ref, out_full_ref.at[here, z], local_sems.at[4]))
    to_core = [
        pltpu.make_async_remote_copy(
            src_ref=source,
            dst_ref=place,
            send_sem=core_sems.at[0, i],
            recv_sem=core_sems.at[1, i],
            device_id=ids[CORE],
            device_id_type=MESH,
        )
        for i, (source, place) in enumerate(zip((other_ref, other_gate_ref, other_up_ref, other_down_ref), places))
    ]
    for copy in kept + to_core:
        copy.start()
    store_table(routes_ref, gates_ref, table_ref)
    kept_table = pltpu.make_async_copy(table_ref, tables_ref.at[z, core], local_sems.at[5])
    kept_table.start()
    kept.append(kept_table)
    to_core[0].wait()
    kept[0].wait()
    kept[1].wait()
    column.pass_own(START)

    def source(label):
        hop = (label + 1) // 2
        if label == 0:
            return z, None
        return (z - hop, z >= hop) if label % 2 else (z + hop, z + hop < n_exp)

    labels = range(2 * n_exp - 1)

    def guarded(condition, action):
        if condition is None:
            action()
        else:
            pl.when(condition)(action)

    def z_slot(label, name):
        return label + 1 if label else (0 if name == UP else 1)

    def z_sends(label, method):
        part, there = source(label)
        for name in (UP, DOWN) if label == 0 else ((UP,) if label % 2 else (DOWN,)):
            room = (z < n_exp - 1) if name == UP else (z > 0)
            condition = room if there is None else there & room
            pl.when(condition)(
                lambda name=name: act(method, (here, part), z_sems, z_slot(label, name), name)
            )

    def z_arrival(label):
        hop = (label + 1) // 2
        name = UP if label % 2 else DOWN
        part, there = source(label)
        slot = z_slot(label - 2 if hop > 1 else 0, name)
        pl.when(there)(lambda: act(WAIT_RECV, (here, part), z_sems, slot, name))

    def spread(label):
        part, there = source(label)
        z_sends(label, START)

        def action():
            act(START, (here, part), x_sems, label, X)
            act(START, (here, part), y_sems, label, Y)

        guarded(there, action)

    def turn(label):
        part, there = source(label)

        def action():
            act(WAIT_RECV, (beside, part), x_sems, label, X)
            act(START, (beside, part, 0), xf_sems, label, Y)
            act(WAIT_RECV, (across, part), y_sems, label, Y)
            act(START, (across, part, 1), yf_sems, label, X)

        guarded(there, action)

    first_near(START)
    spread(0)
    for hop in range(1, n_exp):
        for label in (2 * hop - 1, 2 * hop):
            z_arrival(label)
            spread(label)
        if hop == 1:
            first_near(WAIT_RECV)
            first_far(START)
        if hop == n_exp - 1:
            first_far(WAIT_RECV)
            line(1, START)
        for label in (0,) if hop == 1 else (2 * hop - 3, 2 * hop - 2):
            turn(label)
    line_arrivals(1)
    line(2, START)
    for label in (2 * n_exp - 3, 2 * n_exp - 2):
        turn(label)
    for hop in range(2, n_exp):
        line_arrivals(hop)
        if hop < n_exp - 1:
            line(hop + 1, START)
    first_near(WAIT_SEND)
    first_far(WAIT_SEND)
    for hop in range(1, n_exp):
        line(hop, WAIT_SEND)
    opposite = 2 * (1 - y) + 1 - x
    for label in labels:
        part, there = source(label)

        def action(label=label, part=part):
            act(WAIT_SEND, (here, part), x_sems, label, X)
            act(WAIT_SEND, (here, part), y_sems, label, Y)
            act(WAIT_SEND, (beside, part, 0), xf_sems, label, Y)
            act(WAIT_SEND, (across, part, 1), yf_sems, label, X)
            act(WAIT_RECV, (opposite, part, 0), xf_sems, label, Y)
            act(WAIT_RECV, (opposite, part, 1), yf_sems, label, X)

        guarded(there, action)
        z_sends(label, WAIT_SEND)
    column.pass_own(WAIT)
    for copy in kept[2:] + to_core[1:]:
        copy.wait()


def gather_chips(mine, other, halves, out, routes, gates, cot, experts, n_exp):
    labels = 2 * n_exp - 1
    any_spec = pl.BlockSpec(memory_space=pl.ANY)
    vmem_spec = pl.BlockSpec(memory_space=pltpu.VMEM)
    pair = lambda count: pltpu.SemaphoreType.DMA((2, 2, count))
    return pl.pallas_call(
        functools.partial(gather_kernel, n_exp),
        in_specs=[vmem_spec] * 11 + [any_spec],
        out_specs=[any_spec] * 7,
        out_shape=[
            jax.ShapeDtypeStruct((4, n_exp, 2) + mine.shape, mine.dtype),
            jax.ShapeDtypeStruct((4, n_exp) + out.shape, out.dtype),
        ]
        + [jax.ShapeDtypeStruct((4, 2) + a.shape, a.dtype) for a in halves[:4:2]]
        + [jax.ShapeDtypeStruct((2,) + halves[4].shape, halves[4].dtype)]
        + [
            jax.ShapeDtypeStruct((n_exp, 2) + cot.shape, cot.dtype),
            jax.ShapeDtypeStruct((n_exp, 2, 2 * experts, cot.shape[0]), jnp.float32),
        ],
        scratch_shapes=[
            pltpu.SemaphoreType.DMA((6,)),
            pltpu.SemaphoreType.DMA((2, 4)),
            pair(2 * n_exp),
            pair(labels),
            pair(labels),
            pair(labels),
            pair(labels),
            column_sems(2, n_exp),
            pltpu.SemaphoreType.DMA((2, 4)),
            pltpu.SemaphoreType.DMA((2, 2, n_exp)),
            pltpu.VMEM((2 * experts, cot.shape[0]), jnp.float32),
        ],
        compiler_params=pltpu.CompilerParams(
            collective_id=1, has_side_effects=True, vmem_limit_bytes=32 * MIB
        ),
    )(mine, other, *halves, out, routes, gates, cot)


def exchange_kernel(n_exp, first_ref, second_ref, firsts_ref, seconds_ref, sems):
    column = Column(n_exp, (firsts_ref, seconds_ref), sems, (first_ref, second_ref))
    greet(column.z, n_exp, column.ids, (CORE, UP, DOWN))
    column.sends(1, START)
    column.pass_own(START)
    for hop in range(1, n_exp):
        column.arrivals(hop)
        if hop < n_exp - 1:
            column.sends(hop + 1, START)
        column.passes(hop, START)
    column.pass_own(WAIT)
    for hop in range(1, n_exp):
        column.sends(hop, WAIT_SEND)
        column.passes(hop, WAIT)


def exchange_column(tokens, table, n_exp):
    any_spec = pl.BlockSpec(memory_space=pl.ANY)
    return pl.pallas_call(
        functools.partial(exchange_kernel, n_exp),
        in_specs=[any_spec] * 2,
        out_specs=[any_spec] * 2,
        out_shape=[
            jax.ShapeDtypeStruct((n_exp, 2) + a.shape, a.dtype) for a in (tokens, table)
        ],
        scratch_shapes=[column_sems(2, n_exp)],
        compiler_params=pltpu.CompilerParams(collective_id=3, has_side_effects=True),
        cost_estimate=pl.CostEstimate(
            flops=0, bytes_accessed=16 * n_exp * tokens.size, transcendentals=0
        ),
    )(tokens, table)


def scatter_kernel(
    n_exp,
    turned,
    grad_ref,
    kv_grad_ref,
    extra_ref,
    stats_ref,
    mine_ref,
    theirs_ref,
    stats_sum_ref,
    part,
    from_x,
    from_y,
    second_x,
    second_y,
    total,
    from_z,
    from_core,
    x_sems,
    y_sems,
    x2_sems,
    y2_sems,
    z_sems,
    core_sems,
    held,
    arrived,
    stat_sems,
):
    bf16, f32 = jnp.bfloat16, jnp.float32
    x, y, z, core, ids = neighbours(n_exp)
    barrier = pltpu.get_barrier_semaphore()
    columns = [{EXP: (z + k) % n_exp} for k in range(1, n_exp)]
    for there in [ids[CORE], ids[X], ids[Y]] + columns:
        pl.semaphore_signal(barrier, inc=1, device_id=there, device_id_type=MESH)
    pl.semaphore_wait(barrier, 2 + n_exp)

    def remote(source, target, sems, slot, there):
        return pltpu.make_async_remote_copy(
            src_ref=source,
            dst_ref=target,
            send_sem=sems.at[0, slot],
            recv_sem=sems.at[1, slot],
            device_id=there,
            device_id_type=MESH,
        )

    rounds = [ids[CORE], ids[Y], ids[X]]
    rounds += [{EXP: xor_chip(z, 1 << i, n_exp)} for i in range(n_exp.bit_length() - 1)]
    held[0] = stats_ref[...]

    def stat_copy(i):
        return remote(held.at[i], arrived.at[i], stat_sems, i, rounds[i])

    def stat_round(i):
        if i:
            stat_copy(i - 1).wait()
            held[i] = held[i - 1] + arrived[i - 1]
        if i < len(rounds):
            stat_copy(i).start()

    stat_round(0)
    rows = mine_ref.shape[0]
    q_width, width = grad_ref.shape[1], grad_ref.shape[1] + kv_grad_ref.shape[1]
    steps = range(n_exp)

    def first_copies(k):
        return [
            remote(part.at[k, 1 - x, :, 0], from_x.at[k], x_sems, k, ids[X]),
            remote(part.at[k, :, 1 - y, 1], from_y.at[k], y_sems, k, ids[Y]),
        ]

    def second_copies(k):
        return [
            remote(part.at[k, x, 1 - y, 0], second_x.at[k], x2_sems, k, ids[Y]),
            remote(part.at[k, 1 - x, y, 1], second_y.at[k], y2_sems, k, ids[X]),
        ]

    def z_copy(k):
        return remote(
            total.at[k], from_z.at[k], z_sems, k, {EXP: (z + k + 1) % n_exp}
        )

    def produce(k):
        place = (z + k + 1) % n_exp
        blocks = []
        for px in range(2):
            for py in range(2):
                for c in range(2):
                    start = (((py * 2 + c) * 2 + px) * n_exp + place) * rows
                    blocks.append(turned[pl.ds(pl.multiple_of(start, rows), rows), :])
        block = jnp.concatenate(blocks, 0)
        grad = dot_plain(block, grad_ref[...]).astype(bf16)
        kv_grad = dot_plain(block, kv_grad_ref[...]).astype(bf16)
        i = 0
        for px in range(2):
            for py in range(2):
                for c in range(2):
                    part[k, px, py, c, :, :q_width] = grad[i * rows : (i + 1) * rows]
                    part[k, px, py, c, :, q_width:width] = kv_grad[i * rows : (i + 1) * rows]
                    part[k, px, py, c, :, width:] = extra_ref[py, c, px, place]
                    i += 1

    def launch(k):
        for copy in first_copies(k):
            copy.start()

    for k in steps:
        produce(k)
        if k < 2:
            launch(k)

    def second(k):
        along_x, along_y = first_copies(k)
        along_x.wait_recv()
        for py in range(2):
            part[k, x, py, 0] = (part[k, x, py, 0].astype(f32) + from_x[k, py].astype(f32)).astype(bf16)
        along_y.wait_recv()
        for px in range(2):
            part[k, px, y, 1] = (part[k, px, y, 1].astype(f32) + from_y[k, px].astype(f32)).astype(bf16)
        for copy in second_copies(k):
            copy.start()

    def third(k):
        along_y, along_x = second_copies(k)
        along_y.wait_recv()
        total[k, 0] = (part[k, x, y, 0].astype(f32) + second_x[k].astype(f32)).astype(bf16)
        along_x.wait_recv()
        total[k, 1] = (part[k, x, y, 1].astype(f32) + second_y[k].astype(f32)).astype(bf16)
        if k < n_exp - 1:
            z_copy(k).start()

    for k in steps:
        stat_round(k + 1)
        second(k)
        if k + 2 < n_exp:
            launch(k + 2)
        if k:
            third(k - 1)
    third(n_exp - 1)
    for i in range(n_exp + 1, len(rounds) + 1):
        stat_round(i)
    stats_sum_ref[...] = held[len(rounds)]
    result = total[n_exp - 1].astype(f32)
    for k in range(n_exp - 1):
        z_copy(k).wait_recv()
        result = result + from_z[k].astype(f32)
    total[n_exp - 1] = result.astype(bf16)
    to_core = remote(total.at[n_exp - 1, 1 - core], from_core, core_sems, 0, ids[CORE])
    to_core.start()
    for k in steps:
        for copy in first_copies(k) + second_copies(k) + ([z_copy(k)] if k < n_exp - 1 else []):
            copy.wait_send()
    to_core.wait()
    mine_ref[...] = total[n_exp - 1, core].astype(f32)
    theirs_ref[...] = from_core[...].astype(f32)


def dense_grad_scatter(turned, grad, kv_grad, extra, stats, n_exp):
    bf16 = jnp.bfloat16
    rows, model = extra.shape[4], turned.shape[0]
    width = grad.shape[1] + kv_grad.shape[1] + extra.shape[5]
    block = (rows, width)
    vmem = lambda *lead: pltpu.VMEM(lead + block, bf16)
    pair = lambda count: pltpu.SemaphoreType.DMA((2, count))
    spec = pl.BlockSpec(memory_space=pltpu.VMEM)
    return pl.pallas_call(
        functools.partial(scatter_kernel, n_exp),
        in_specs=[spec] * 5,
        out_specs=[spec] * 3,
        out_shape=[jax.ShapeDtypeStruct(block, jnp.float32)] * 2
        + [jax.ShapeDtypeStruct(stats.shape, stats.dtype)],
        scratch_shapes=[
            vmem(n_exp, 2, 2, 2),
            vmem(n_exp, 2),
            vmem(n_exp, 2),
            vmem(n_exp),
            vmem(n_exp),
            vmem(n_exp, 2),
            vmem(n_exp, 2),
            vmem(),
            pair(n_exp),
            pair(n_exp),
            pair(n_exp),
            pair(n_exp),
            pair(n_exp),
            pair(1),
            pltpu.VMEM((n_exp + 2,) + stats.shape, stats.dtype),
            pltpu.VMEM((n_exp + 2,) + stats.shape, stats.dtype),
            pair(n_exp + 2),
        ],
        compiler_params=pltpu.CompilerParams(
            collective_id=2, has_side_effects=True, vmem_limit_bytes=60 * MIB
        ),
        cost_estimate=pl.CostEstimate(
            flops=2 * turned.shape[1] * model * width, bytes_accessed=16 * MIB, transcendentals=0
        ),
    )(turned, grad, kv_grad, extra, stats)


def back_kernel(
    n_exp,
    jobs,
    query_grad_ref,
    key_grad_ref,
    value_grad_ref,
    raw_ref,
    w_query_ref,
    w_kv_ref,
    gain_ref,
    cos_ref,
    sin_ref,
    hidden_ref,
    row_gain_ref,
    middle_grad_ref,
    chip_ref,
    into_in_ref,
    kv_grad_ref,
    hidden_grad_ref,
    row_gain_grad_ref,
    gain_grad_ref,
    into_ref,
    kv_send,
    kv_got,
    sib_part,
    own_part,
    part_got,
    x_sems,
    core_sems,
    job_sems,
):
    bf16, f32 = jnp.bfloat16, jnp.float32
    x, _, z, _, ids = neighbours(n_exp)
    tokens, model = hidden_ref.shape
    keys_width = raw_ref.shape[1] // 2
    barrier = pltpu.get_barrier_semaphore()
    slots = sorted({job[2] for job in jobs})
    greeted = [ids[CORE], ids[X]] + [{EXP: xor_chip(z, slot, n_exp)} for slot in slots]
    for there in greeted:
        pl.semaphore_signal(barrier, inc=1, device_id=there, device_id_type=MESH)
    here, there = (pl.ds(pl.multiple_of(i * tokens, tokens), tokens) for i in (x, 1 - x))
    for s in range(2):
        kv_send[s, :, :keys_width] = key_grad_ref[s, there].astype(bf16)
        kv_send[s, :, keys_width:] = value_grad_ref[s, there].astype(bf16)
    pl.semaphore_wait(barrier, len(greeted))
    to_x = pltpu.make_async_remote_copy(
        src_ref=kv_send,
        dst_ref=kv_got,
        send_sem=x_sems.at[0],
        recv_sem=x_sems.at[1],
        device_id=ids[X],
        device_id_type=MESH,
    )
    to_x.start()
    sent = [sent_rows(chip_ref, into_ref, job, job_sems, i, n_exp) for i, job in enumerate(jobs)]
    for copy in sent:
        copy.start()
    tile = 256
    parts = ((1, sib_part), (0, own_part))

    def query_product(s, part):
        rows = query_grad_ref[s * tokens : (s + 1) * tokens]
        for start in range(0, model, tile):
            part[:, start : start + tile] = dot_cols(rows, w_query_ref[start : start + tile])

    for s, part in parts:
        query_product(s, part)
    to_x.wait()
    gain_grad = None
    for s in range(2):
        rows = slice(s * tokens, (s + 1) * tokens)
        for start in range(0, keys_width, HEAD_DIM):
            columns = slice(start, start + HEAD_DIM)
            grad = key_grad_ref[s, here, columns] + kv_got[s, :, columns].astype(f32)
            turned = rotate_rows_back(grad, cos_ref[...], sin_ref[...])
            raw = raw_ref[rows, columns]
            inverse = lax.rsqrt(jnp.mean(raw * raw, axis=-1, keepdims=True) + EPS)
            unit = raw * inverse
            total = jnp.sum(turned * unit, axis=0, keepdims=True)
            gain_grad = total if gain_grad is None else gain_grad + total
            scaled = turned * gain_ref[...]
            kv_grad_ref[rows, columns] = (
                inverse * (scaled - unit * jnp.mean(scaled * unit, axis=-1, keepdims=True))
            ).astype(bf16)
        value_grad = value_grad_ref[s, here] + kv_got[s, :, keys_width:].astype(f32)
        kv_grad_ref[rows, keys_width:] = value_grad.astype(bf16)
    gain_grad_ref[0:1] = gain_grad

    def kv_product(s, part):
        rows = kv_grad_ref[s * tokens : (s + 1) * tokens]
        for start in range(0, model, tile):
            part[:, start : start + tile] += dot_cols(rows, w_kv_ref[start : start + tile])

    kv_product(*parts[0])
    to_core = pltpu.make_async_remote_copy(
        src_ref=sib_part,
        dst_ref=part_got,
        send_sem=core_sems.at[0],
        recv_sem=core_sems.at[1],
        device_id=ids[CORE],
        device_id_type=MESH,
    )
    to_core.start()
    kv_product(*parts[1])
    to_core.wait()
    row_gain_grad_ref[...] = jnp.zeros_like(row_gain_grad_ref)
    count = min(tokens, 64)

    @pl.loop(0, tokens // count)
    def _(i):
        rows = pl.ds(pl.multiple_of(i * count, count), count)
        grad = own_part[rows] + part_got[rows]
        hidden = hidden_ref[rows].astype(f32)
        inverse = lax.rsqrt(jnp.mean(hidden * hidden, axis=-1, keepdims=True) + EPS)
        unit = hidden * inverse
        row_gain_grad_ref[...] += jnp.sum(grad * unit, axis=0, keepdims=True)
        scaled = grad * row_gain_ref[...]
        back = inverse * (scaled - unit * jnp.mean(scaled * unit, axis=-1, keepdims=True))
        hidden_grad_ref[rows] = (middle_grad_ref[rows] + back).astype(bf16)

    for copy in sent:
        copy.wait()


def back_to_input(
    query_grad, key_grad, value_grad, raw, weight, gain, cos, sin, hidden, row_gain, middle_grad,
    chip, into, jobs, n_exp
):
    bf16, f32 = jnp.bfloat16, jnp.float32
    tokens, model = hidden.shape
    total, q_width = query_grad.shape
    kv_width = raw.shape[1] - q_width
    once = dict(pipeline_mode=pl.Buffered(1))
    tail = lambda rows: pl.BlockSpec((rows, kv_width), lambda i: (0, q_width // kv_width), **once)
    vmem, any_spec = pl.BlockSpec(memory_space=pltpu.VMEM), pl.BlockSpec(memory_space=pl.ANY)
    return pl.pallas_call(
        functools.partial(back_kernel, n_exp, jobs),
        grid=(1,),
        in_specs=[vmem] * 3
        + [tail(total), pl.BlockSpec((model, q_width), lambda i: (0, 0), **once), tail(model)]
        + [vmem] * 6
        + [any_spec] * 2,
        out_specs=[vmem] * 4 + [any_spec],
        out_shape=[
            jax.ShapeDtypeStruct((total, kv_width), bf16),
            jax.ShapeDtypeStruct((tokens, model), bf16),
            jax.ShapeDtypeStruct((1, model), f32),
            jax.ShapeDtypeStruct((8, HEAD_DIM), f32),
            jax.ShapeDtypeStruct(into.shape, into.dtype),
        ],
        scratch_shapes=[
            pltpu.VMEM((2, tokens, kv_width), bf16),
            pltpu.VMEM((2, tokens, kv_width), bf16),
            pltpu.VMEM((tokens, model), f32),
            pltpu.VMEM((tokens, model), f32),
            pltpu.VMEM((tokens, model), f32),
            pltpu.SemaphoreType.DMA((2,)),
            pltpu.SemaphoreType.DMA((2,)),
            pltpu.SemaphoreType.DMA((2, len(jobs))),
        ],
        input_output_aliases={13: 4},
        compiler_params=pltpu.CompilerParams(
            vmem_limit_bytes=60 * MIB, collective_id=11, has_side_effects=True
        ),
        cost_estimate=pl.CostEstimate(
            flops=2 * total * model * (query_grad.shape[1] + kv_width),
            bytes_accessed=48 * MIB,
            transcendentals=0,
        ),
    )(
        query_grad, key_grad, value_grad, raw, weight, weight, gain, cos, sin, hidden, row_gain,
        middle_grad, chip, into
    )


def out_back_kernel(
    n_exp, jobs, mixed_ref, own_ref, sib_ref, weight_ref, valid_ref, chip_ref, into_in, weight_grad_ref, mixed_grad_ref, into_ref, grad_ref, sems
):
    bf16 = jnp.bfloat16
    sent = [sent_rows(chip_ref, into_ref, job, sems, i, n_exp) for i, job in enumerate(jobs)]
    step, tokens = pl.program_id(0), own_ref.shape[0]

    @pl.when(step == 0)
    def _():
        grad_ref[:tokens] = own_ref[...]
        grad_ref[tokens:] = sib_ref[...]
        greet_slots(sorted({job[2] for job in jobs}), n_exp)
        for copy in sent:
            copy.start()

    weight_grad_ref[...] = dot_plain(mixed_ref[...].T, grad_ref[...]).astype(bf16)
    mixed_grad = dot_cols(grad_ref[...], weight_ref[...]).astype(bf16)
    mixed_grad_ref[...] = mixed_grad * valid_ref[...].astype(bf16)

    @pl.when(step == pl.num_programs(0) - 1)
    def _():
        for copy in sent:
            copy.wait()


def out_back(mixed, own, sib, weight, valid, chip, into, jobs, n_exp):
    bf16 = jnp.bfloat16
    total, width = mixed.shape
    model = own.shape[1]
    block = 2 * HEAD_DIM
    any_spec = pl.BlockSpec(memory_space=pl.ANY)
    columns = pl.BlockSpec((total, block), lambda j: (0, j))
    rows = pl.BlockSpec((block, model), lambda j: (j, 0))
    return pl.pallas_call(
        functools.partial(out_back_kernel, n_exp, jobs),
        grid=(width // block,),
        in_specs=[
            columns,
            pl.BlockSpec(own.shape, lambda j: (0, 0)),
            pl.BlockSpec(own.shape, lambda j: (0, 0)),
            rows,
            pl.BlockSpec(valid.shape, lambda j: (0, 0)),
            any_spec,
            any_spec,
        ],
        out_specs=[rows, columns, any_spec],
        out_shape=[
            jax.ShapeDtypeStruct((width, model), bf16),
            jax.ShapeDtypeStruct((total, width), bf16),
            jax.ShapeDtypeStruct(into.shape, bf16),
        ],
        input_output_aliases={6: 2},
        scratch_shapes=[pltpu.VMEM((total, model), bf16), pltpu.SemaphoreType.DMA((2, len(jobs)))],
        compiler_params=pltpu.CompilerParams(
            vmem_limit_bytes=40 * MIB, collective_id=12, has_side_effects=True
        ),
        cost_estimate=pl.CostEstimate(
            flops=4 * total * model * width, bytes_accessed=24 * MIB, transcendentals=0
        ),
    )(mixed, own, sib, weight, valid, chip, into)


def pick(core, first, second):
    return jnp.where(core == 0, first, second)


def column_halves(weight, core):
    width = weight.shape[1] // KEY_VALUE_HEADS
    parts = [weight[:, i * width : (i + 1) * width] for i in range(KEY_VALUE_HEADS)]
    mine = [pick(core, parts[i], parts[i + 1]) for i in range(0, KEY_VALUE_HEADS, 2)]
    other = [pick(core, parts[i + 1], parts[i]) for i in range(0, KEY_VALUE_HEADS, 2)]
    return mine, other


LOG2E = 1.4426950408889634
MIB = 1 << 20


def rotate_rows(vectors, cosine_table, signed_sine):
    return vectors * cosine_table + pltpu.roll(vectors, HEAD_DIM // 2, 1) * signed_sine


def rotate_rows_back(gradient, cosine_table, signed_sine):
    return gradient * cosine_table - pltpu.roll(gradient, HEAD_DIM // 2, 1) * signed_sine


def dot_cols(first, second):
    return lax.dot_general(
        first, second, (((1,), (1,)), ((), ())), preferred_element_type=jnp.float32
    )


def dot_plain(first, second):
    return jnp.dot(first, second, preferred_element_type=jnp.float32)


def ordered_weight(n_y, weight_ref, ordered_ref):
    n_xz = weight_ref.shape[0] // n_y
    weight = jnp.concatenate(
        [weight_ref[y * n_xz + i, c] for y in range(n_y) for c in range(2) for i in range(n_xz)], 0
    )
    ordered_ref[...] = weight
    return weight


def store_rotated(raw, gain, cos_ref, sin_ref, low_ref):
    tokens = cos_ref.shape[0]
    for h in range(2):
        columns = slice(h * HEAD_DIM, (h + 1) * HEAD_DIM)
        head = raw[:, columns]
        inverse = lax.rsqrt(jnp.mean(head * head, axis=-1, keepdims=True) + EPS)
        scaled = head * inverse * gain
        for s in range(2):
            part = slice(s * tokens, (s + 1) * tokens)
            low_ref[part, columns] = rotate_rows(scaled[part], cos_ref[...], sin_ref[...]).astype(
                jnp.bfloat16
            )


def key_value_kernel(
    n_y,
    own_ref,
    sib_ref,
    row_gain_ref,
    weight_ref,
    gain_ref,
    cos_ref,
    sin_ref,
    raw_ref,
    low_ref,
    ordered_ref,
    normed_ref,
):
    tokens = own_ref.shape[0]

    @pl.when(pl.program_id(0) == 0)
    def _():
        for s, source in enumerate((own_ref, sib_ref)):
            hidden = source[...].astype(jnp.float32)
            inverse = lax.rsqrt(jnp.mean(hidden * hidden, axis=-1, keepdims=True) + EPS)
            normed_ref[s * tokens : (s + 1) * tokens] = (hidden * inverse * row_gain_ref[...]).astype(
                jnp.bfloat16
            )

    raw = dot_plain(normed_ref[...], ordered_weight(n_y, weight_ref, ordered_ref))
    raw_ref[...] = raw

    @pl.when(pl.program_id(0) == 0)
    def _():
        store_rotated(raw, gain_ref[...], cos_ref, sin_ref, low_ref)

    @pl.when(pl.program_id(0) == 1)
    def _():
        low_ref[...] = raw.astype(jnp.bfloat16)


def query_kernel(n_y, n_exp, normed_ref, weight_ref, gain_ref, cos_ref, sin_ref, *refs):
    if n_exp:
        raw_ref, low_ref, ordered_ref, gate_full_ref, up_full_ref, cots_ref, tables_ref = refs[4:11]
        plane = Plane(n_exp, (gate_full_ref, up_full_ref), refs[11])
        column = Column(n_exp, (cots_ref, tables_ref), refs[12])

        @pl.when(pl.program_id(0) == 0)
        def _():
            greet(column.z, n_exp, plane.ids, (CORE, X, Y, UP, DOWN))
            plane.each(START, False)
            column.sends(2, START)
            column.passes(1, START)
    else:
        raw_ref, low_ref, ordered_ref = refs
    raw = dot_plain(normed_ref[...], ordered_weight(n_y, weight_ref, ordered_ref))
    raw_ref[...] = raw
    store_rotated(raw, gain_ref[...], cos_ref, sin_ref, low_ref)
    if n_exp:

        @pl.when(pl.program_id(0) == pl.num_programs(0) - 1)
        def _():
            plane.each(WAIT, False)
            column.arrivals(2)
            column.sends(2, WAIT_SEND)
            column.passes(1, WAIT)


def project_kernel(
    n_y,
    n_exp,
    own_ref,
    sib_ref,
    row_gain_ref,
    weight_ref,
    key_gain_ref,
    gain_ref,
    cos_ref,
    sin_ref,
    *refs,
):
    raw_ref, low_ref, ordered_ref, turned_ref, kv_full_ref = refs[5:10]
    gate_full_ref, up_full_ref, cots_ref, tables_ref, kv_scr, normed_ref = refs[10:16]
    plane_sem, column_sem, kv_sems = refs[16:]
    plane = Plane(n_exp, (gate_full_ref, up_full_ref), plane_sem)
    column = Column(n_exp, (cots_ref, tables_ref), column_sem)
    column.own = (refs[0], tables_ref.at[column.z, column.core])
    j, tokens = pl.program_id(0), own_ref.shape[0]
    here = kv_full_ref.at[:, pl.ds(pl.multiple_of(column.x * tokens, tokens), tokens)]
    kv_copies = [
        pltpu.make_async_remote_copy(
            src_ref=kv_scr,
            dst_ref=here,
            send_sem=kv_sems.at[0],
            recv_sem=kv_sems.at[1],
            device_id=column.ids[X],
            device_id_type=MESH,
        ),
        pltpu.make_async_copy(kv_scr, here, kv_sems.at[2]),
    ]

    @pl.when(j == 0)
    def _():
        greet(column.z, n_exp, plane.ids, (CORE, X, Y, UP, DOWN))
        plane.each(START, False)
        column.sends(1, START)
        for s, source in enumerate((own_ref, sib_ref)):
            hidden = source[...].astype(jnp.float32)
            inverse = lax.rsqrt(jnp.mean(hidden * hidden, axis=-1, keepdims=True) + EPS)
            normed_ref[s * tokens : (s + 1) * tokens] = (hidden * inverse * row_gain_ref[...]).astype(
                jnp.bfloat16
            )

    @pl.when(j == pl.num_programs(0) // 2)
    def _():
        column.arrivals(1)
        column.sends(2, START)
        column.passes(1, START)

    raw = dot_plain(normed_ref[...], ordered_weight(n_y, weight_ref, ordered_ref))
    raw_ref[...] = raw

    @pl.when(j != 1)
    def _():
        gain = jnp.where(j == 0, key_gain_ref[...], gain_ref[...])
        store_rotated(raw, gain, cos_ref, sin_ref, low_ref)

    @pl.when(j == 1)
    def _():
        low_ref[...] = raw.astype(jnp.bfloat16)
        turned_ref[...] = normed_ref[...].T

    for which in range(2):

        @pl.when(j == which)
        def _(which=which):
            width = low_ref.shape[1]
            for s in range(2):
                kv_scr[s, :, which * width : (which + 1) * width] = low_ref[
                    s * tokens : (s + 1) * tokens
                ]
            if which:
                for copy in kv_copies:
                    copy.start()

    @pl.when(j == pl.num_programs(0) - 1)
    def _():
        for copy in kv_copies:
            copy.wait()
        plane.each(WAIT, False)
        column.arrivals(2)
        for hop in (1, 2):
            column.sends(hop, WAIT_SEND)
        column.passes(1, WAIT)


def project_all(own, sib, row_gain, gathered, blocks, key_gain, gain, cos, sin, cot, n_y, n_exp, moving):
    bf16 = jnp.bfloat16
    tokens, model = own.shape
    total, width = 2 * tokens, 2 * HEAD_DIM
    n_yxz, _, rows, _ = gathered.shape
    fixed = lambda j: (0, 0)
    block = lambda j: jnp.where(j < 2, blocks + j, j - 2)
    any_specs = [pl.BlockSpec(memory_space=pl.ANY)] * len(moving)
    columns = pl.BlockSpec((total, width), lambda j: (0, block(j)))
    return pl.pallas_call(
        functools.partial(project_kernel, n_y, n_exp),
        grid=(blocks + 2,),
        in_specs=[pl.BlockSpec(own.shape, fixed)] * 2
        + [
            pl.BlockSpec((1, model), fixed),
            pl.BlockSpec((n_yxz, 2, rows, width), lambda j: (0, 0, 0, block(j))),
            pl.BlockSpec((1, HEAD_DIM), fixed),
            pl.BlockSpec((1, HEAD_DIM), fixed),
            pl.BlockSpec(cos.shape, fixed),
            pl.BlockSpec(cos.shape, fixed),
            pl.BlockSpec(memory_space=pl.ANY),
        ]
        + any_specs,
        out_specs=[
            columns,
            columns,
            pl.BlockSpec((model, width), lambda j: (0, block(j))),
            pl.BlockSpec((model, total), fixed),
            pl.BlockSpec(memory_space=pl.ANY),
        ]
        + any_specs,
        out_shape=[
            jax.ShapeDtypeStruct((total, (blocks + 2) * width), jnp.float32),
            jax.ShapeDtypeStruct((total, (blocks + 2) * width), bf16),
            jax.ShapeDtypeStruct((model, (blocks + 2) * width), bf16),
            jax.ShapeDtypeStruct((model, total), bf16),
            jax.ShapeDtypeStruct((2, 2 * tokens, 2 * width), bf16),
        ]
        + [jax.ShapeDtypeStruct(a.shape, a.dtype) for a in moving],
        scratch_shapes=[
            pltpu.VMEM((2, tokens, 2 * width), bf16),
            pltpu.VMEM((total, model), bf16),
            plane_sems(2),
            column_sems(2, n_exp),
            pltpu.SemaphoreType.DMA((3,)),
        ],
        input_output_aliases={9 + i: 5 + i for i in range(len(moving))},
        compiler_params=pltpu.CompilerParams(
            vmem_limit_bytes=60 * MIB, collective_id=4, has_side_effects=True
        ),
        cost_estimate=pl.CostEstimate(
            flops=2 * total * model * (blocks + 2) * width, bytes_accessed=64 * MIB, transcendentals=0
        ),
    )(own, sib, row_gain, gathered, key_gain, gain, cos, sin, cot, *moving)


def projection_specs(normed_shape, gathered, first_block, blocks, cos):
    total, model = normed_shape
    n_yxz, _, rows, _ = gathered.shape
    width = 2 * HEAD_DIM
    fixed = lambda j: (0, 0)
    moving = lambda j: (0, j)
    weight = pl.BlockSpec((n_yxz, 2, rows, width), lambda j: (0, 0, 0, j + first_block))
    tail = [pl.BlockSpec((1, HEAD_DIM), fixed), pl.BlockSpec(cos.shape, fixed), pl.BlockSpec(cos.shape, fixed)]
    out_specs = [pl.BlockSpec((total, width), moving)] * 2 + [pl.BlockSpec((model, width), moving)]
    out_shape = [
        jax.ShapeDtypeStruct((total, blocks * width), jnp.float32),
        jax.ShapeDtypeStruct((total, blocks * width), jnp.bfloat16),
        jax.ShapeDtypeStruct((model, blocks * width), jnp.bfloat16),
    ]
    cost = pl.CostEstimate(
        flops=2 * total * model * blocks * width,
        bytes_accessed=total * model * 2 + blocks * width * (model * 4 + total * 6),
        transcendentals=0,
    )
    return weight, tail, out_specs, out_shape, cost


def project_keys(own, sib, row_gain, gathered, first_block, gain, cos, sin, n_y):
    tokens, model = own.shape
    normed_shape = (2 * tokens, model)
    weight, tail, out_specs, out_shape, cost = projection_specs(normed_shape, gathered, first_block, 2, cos)
    fixed = lambda j: (0, 0)
    return pl.pallas_call(
        functools.partial(key_value_kernel, n_y),
        grid=(2,),
        in_specs=[pl.BlockSpec(own.shape, fixed)] * 2
        + [pl.BlockSpec((1, model), fixed), weight]
        + tail,
        out_specs=out_specs + [pl.BlockSpec(normed_shape, fixed)],
        out_shape=out_shape + [jax.ShapeDtypeStruct(normed_shape, jnp.bfloat16)],
        compiler_params=pltpu.CompilerParams(vmem_limit_bytes=56 * MIB),
        cost_estimate=cost,
    )(own, sib, row_gain, gathered, gain, cos, sin)


def project_queries(normed, gathered, blocks, gain, cos, sin, n_y, n_exp, moving):
    weight, tail, out_specs, out_shape, cost = projection_specs(normed.shape, gathered, 0, blocks, cos)
    any_specs = [pl.BlockSpec(memory_space=pl.ANY)] * len(moving)
    return pl.pallas_call(
        functools.partial(query_kernel, n_y, n_exp if moving else 0),
        grid=(blocks,),
        in_specs=[pl.BlockSpec(normed.shape, lambda j: (0, 0)), weight] + tail + any_specs,
        out_specs=out_specs + any_specs,
        out_shape=out_shape + [jax.ShapeDtypeStruct(a.shape, a.dtype) for a in moving],
        scratch_shapes=[plane_sems(2), column_sems(2, n_exp)] if moving else [],
        input_output_aliases={5 + i: 3 + i for i in range(len(moving))},
        compiler_params=pltpu.CompilerParams(
            vmem_limit_bytes=56 * MIB,
            collective_id=4 if moving else None,
            has_side_effects=bool(moving),
        ),
        cost_estimate=cost,
    )(normed, gathered, gain, cos, sin, *moving)


def mask_bias(seg_key, info):
    keys, tokens = seg_key.shape[0], info.shape[1]
    key_pos = lax.broadcasted_iota(jnp.int32, (keys, tokens), 0)
    allowed = (seg_key == info[0:1]) & (key_pos <= info[1:2])
    return jnp.where(allowed, 0.0, MASKED)


def key_tile(keys):
    return min(keys, 256)


def attention_kernel(hops, info_ref, seg_ref, q_ref, k_ref, v_ref, *refs):
    if hops:
        mixed_ref, recip_ref, gate_ref, up_ref, cots_ref, tables_ref = refs[4:10]
        bias_ref, vt_ref, plane_sem, sems = refs[10:]
        column = Column(hops, (cots_ref, tables_ref), sems)
        plane = Plane(hops, (gate_ref, up_ref), plane_sem)
        places = [pl.program_id(i) for i in range(3)]
        ends = [pl.num_programs(i) - 1 for i in range(3)]

        @pl.when((places[0] == 0) & (places[1] == 0) & (places[2] == 0))
        def _():
            greet(column.z, hops, column.ids, (CORE, X, Y, UP, DOWN))
            plane.each(START, True)
            column.sends(hops - 1, START)
            column.passes(hops - 2, START)
    else:
        mixed_ref, recip_ref, bias_ref, vt_ref = refs
    keys = k_ref.shape[1]
    tile = key_tile(keys)

    @pl.when((pl.program_id(1) == 0) & (pl.program_id(2) == 0))
    def _():
        bias_ref[...] = mask_bias(seg_ref[0], info_ref[0])

    @pl.when(pl.program_id(2) == 0)
    def _():
        vt_ref[...] = v_ref[0].astype(jnp.float32).T.astype(jnp.bfloat16)

    queries = q_ref[...]
    total, mixed = None, None
    for start in range(0, keys, tile):
        part = slice(start, start + tile)
        scores = dot_cols(k_ref[0, part], queries) * (HEAD_DIM**-0.5 * LOG2E) + bias_ref[part]
        weights = jnp.exp2(scores)
        tile_total = jnp.sum(weights, axis=0, keepdims=True)
        tile_mixed = dot_plain(vt_ref[:, part], weights.astype(jnp.bfloat16))
        total = tile_total if total is None else total + tile_total
        mixed = tile_mixed if mixed is None else mixed + tile_mixed
    recip = 1.0 / total
    recip_ref[0] = recip
    valid = (info_ref[0, 0:1] > 0).astype(jnp.float32)
    mixed_ref[...] = (mixed * (recip * valid)).T.astype(jnp.bfloat16)
    if hops:

        @pl.when((places[0] == ends[0]) & (places[1] == ends[1]) & (places[2] == ends[2]))
        def _():
            plane.each(WAIT, True)
            column.arrivals(hops - 1)
            column.passes(hops - 1, START)
            column.sends(hops - 1, WAIT_SEND)
            column.passes(hops - 2, WAIT)
            column.passes(hops - 1, WAIT)


def attention_specs(tokens, keys, groups, per_group):
    head = pl.BlockSpec((tokens, HEAD_DIM), lambda s, g, h: (s, g * per_group + h))
    return dict(
        info=pl.BlockSpec((1, 8, tokens), lambda s, g, h: (s, 0, 0)),
        seg=pl.BlockSpec((1, keys, 1), lambda s, g, h: (s, 0, 0)),
        head=head,
        key=pl.BlockSpec((1, keys, HEAD_DIM), lambda s, g, h: (s, 0, g)),
        value=pl.BlockSpec((1, keys, HEAD_DIM), lambda s, g, h: (s, 0, groups + g)),
        recip=pl.BlockSpec((1, 1, tokens), lambda s, g, h: ((s * groups + g) * per_group + h, 0, 0)),
    )


def attend(info, seg_keys, queries, kv_full, groups, per_group, n_exp, moving):
    tokens, keys = info.shape[2], seg_keys.shape[1]
    specs = attention_specs(tokens, keys, groups, per_group)
    steps = 2 * groups * per_group
    return pl.pallas_call(
        functools.partial(attention_kernel, n_exp if moving else 0),
        grid=(2, groups, per_group),
        in_specs=[specs[INFO], specs[SEG], specs[HEAD], specs[KEY], specs[VALUE]]
        + [pl.BlockSpec(memory_space=pl.ANY)] * len(moving),
        out_specs=[specs[HEAD], specs[RECIP]]
        + [pl.BlockSpec(memory_space=pl.ANY)] * len(moving),
        out_shape=[
            jax.ShapeDtypeStruct((2 * tokens, groups * per_group * HEAD_DIM), jnp.bfloat16),
            jax.ShapeDtypeStruct((steps, 1, tokens), jnp.float32),
        ]
        + [jax.ShapeDtypeStruct(a.shape, a.dtype) for a in moving],
        scratch_shapes=[
            pltpu.VMEM((keys, tokens), jnp.float32),
            pltpu.VMEM((HEAD_DIM, keys), jnp.bfloat16),
        ]
        + ([plane_sems(2), column_sems(2, n_exp)] if moving else []),
        input_output_aliases={5 + i: 2 + i for i in range(len(moving))},
        compiler_params=pltpu.CompilerParams(
            vmem_limit_bytes=48 * MIB,
            collective_id=5 if moving else None,
            has_side_effects=bool(moving),
        ),
        cost_estimate=pl.CostEstimate(
            flops=steps * 8 * tokens * keys * HEAD_DIM,
            bytes_accessed=queries.size * 4 + kv_full.size * 2,
            transcendentals=steps * tokens * keys,
        ),
    )(info, seg_keys, queries, kv_full, kv_full, *moving)


def attention_back_kernel(
    info_ref,
    seg_ref,
    q_ref,
    k_ref,
    v_ref,
    mixed_ref,
    grad_ref,
    recip_ref,
    raw_ref,
    gain_ref,
    cos_ref,
    sin_ref,
    chip_ref,
    into_in_ref,
    raw_grad_ref,
    key_grad_ref,
    value_grad_ref,
    gain_grad_ref,
    into_ref,
    bias_ref,
    kt_ref,
    job_sems,
    *,
    n_exp,
    jobs,
):
    sent = [sent_rows(chip_ref, into_ref, job, job_sems, i, n_exp) for i, job in enumerate(jobs)]
    places = [pl.program_id(i) for i in range(3)]
    ends = [pl.num_programs(i) - 1 for i in range(3)]

    @pl.when((places[0] == 0) & (places[1] == 0) & (places[2] == 0))
    def _():
        greet_slots(sorted({job[2] for job in jobs}), n_exp)
        for copy in sent:
            copy.start()

    keys = k_ref.shape[1]
    tile = key_tile(keys)
    scale = HEAD_DIM**-0.5
    first = (pl.program_id(1) == 0) & (pl.program_id(2) == 0)

    @pl.when(first)
    def _():
        bias_ref[...] = mask_bias(seg_ref[0], info_ref[0])

    @pl.when(first & (pl.program_id(0) == 0))
    def _():
        gain_grad_ref[...] = jnp.zeros_like(gain_grad_ref)

    @pl.when(pl.program_id(2) == 0)
    def _():
        kt_ref[...] = k_ref[0].astype(jnp.float32).T.astype(jnp.bfloat16)
        key_grad_ref[...] = jnp.zeros_like(key_grad_ref)
        value_grad_ref[...] = jnp.zeros_like(value_grad_ref)

    queries, grad = q_ref[...], grad_ref[...]
    recip = recip_ref[0]
    overlap = grad.astype(jnp.float32) * mixed_ref[...].astype(jnp.float32)
    inner = jnp.sum(overlap.T, axis=0, keepdims=True)
    query_grad = None
    for start in range(0, keys, tile):
        part = slice(start, start + tile)
        scores = dot_cols(k_ref[0, part], queries) * (scale * LOG2E) + bias_ref[part]
        probs = jnp.exp2(scores) * recip
        grad_probs = dot_cols(v_ref[0, part], grad)
        grad_scores = (probs * (grad_probs - inner)).astype(jnp.bfloat16)
        value_grad_ref[0, part] += dot_plain(probs.astype(jnp.bfloat16), grad)
        key_grad_ref[0, part] += dot_plain(grad_scores, queries) * scale
        tile_grad = dot_plain(kt_ref[:, part], grad_scores)
        query_grad = tile_grad if query_grad is None else query_grad + tile_grad
    turned = rotate_rows_back((query_grad * scale).T, cos_ref[...], sin_ref[...])
    raw = raw_ref[...]
    inverse = lax.rsqrt(jnp.mean(raw * raw, axis=-1, keepdims=True) + EPS)
    unit = raw * inverse
    gain_grad_ref[0:1] += jnp.sum(turned * unit, axis=0, keepdims=True)
    scaled = turned * gain_ref[...]
    raw_grad_ref[...] = (
        inverse * (scaled - unit * jnp.mean(scaled * unit, axis=-1, keepdims=True))
    ).astype(jnp.bfloat16)

    @pl.when((places[0] == ends[0]) & (places[1] == ends[1]) & (places[2] == ends[2]))
    def _():
        for copy in sent:
            copy.wait()


def attend_back(
    info,
    seg_keys,
    queries,
    kv_full,
    mixed,
    grad_mixed,
    recip,
    raw,
    gain,
    cos,
    sin,
    groups,
    per_group,
    chip,
    into,
    jobs,
    n_exp,
):
    tokens, keys = info.shape[2], seg_keys.shape[1]
    specs = attention_specs(tokens, keys, groups, per_group)
    steps = 2 * groups * per_group
    fixed = lambda s, g, h: (0, 0)
    key_grad = jax.ShapeDtypeStruct((2, keys, groups * HEAD_DIM), jnp.float32)
    return pl.pallas_call(
        functools.partial(attention_back_kernel, n_exp=n_exp, jobs=jobs),
        grid=(2, groups, per_group),
        in_specs=[specs[INFO], specs[SEG], specs[HEAD], specs[KEY], specs[VALUE]]
        + [specs[HEAD], specs[HEAD], specs[RECIP], specs[HEAD]]
        + [pl.BlockSpec(a.shape, fixed) for a in (gain, cos, sin)]
        + [pl.BlockSpec(memory_space=pl.ANY)] * 2,
        out_specs=[specs[HEAD], specs[KEY], specs[KEY], pl.BlockSpec((8, HEAD_DIM), fixed)]
        + [pl.BlockSpec(memory_space=pl.ANY)],
        out_shape=[
            jax.ShapeDtypeStruct((2 * tokens, groups * per_group * HEAD_DIM), jnp.bfloat16),
            key_grad,
            key_grad,
            jax.ShapeDtypeStruct((8, HEAD_DIM), jnp.float32),
            jax.ShapeDtypeStruct(into.shape, into.dtype),
        ],
        scratch_shapes=[
            pltpu.VMEM((keys, tokens), jnp.float32),
            pltpu.VMEM((HEAD_DIM, keys), jnp.bfloat16),
            pltpu.SemaphoreType.DMA((2, len(jobs))),
        ],
        input_output_aliases={13: 4},
        compiler_params=pltpu.CompilerParams(
            vmem_limit_bytes=48 * MIB, collective_id=6, has_side_effects=True
        ),
        cost_estimate=pl.CostEstimate(
            flops=steps * 20 * tokens * keys * HEAD_DIM,
            bytes_accessed=queries.size * 12 + kv_full.size * 6,
            transcendentals=steps * tokens * keys,
        ),
    )(
        info, seg_keys, queries, kv_full, kv_full, mixed, grad_mixed, recip, raw, gain, cos, sin, chip, into
    )


def moe_kernel(
    n_exp,
    n_y,
    local_experts,
    table_ref,
    own_ref,
    own_cot_ref,
    cots_ref,
    gate_any,
    up_any,
    down_any,
    x_ref,
    val_ref,
    product_ref,
    gate_grad_ref,
    up_grad_ref,
    tokens_ref,
    partial_ref,
    grad_chip_ref,
    out_chip_ref,
    grad_into_ref,
    out_into_ref,
    gate_w,
    up_w,
    down_w,
    token_scr,
    cot_scr,
    held,
    send,
    got,
    weight_sems,
    load_sems,
    token_sems,
    core_sems,
    local_sems,
    grad_sems,
):
    bf16, f32 = jnp.bfloat16, jnp.float32
    column = Column(n_exp, (tokens_ref,), token_sems, (own_ref,))
    z, core = column.z, column.core
    c, q = pl.program_id(0), pl.program_id(1)
    e, s = q // 2, (q % 3 + 1) // 2
    owner = core + s * (1 - 2 * core)
    chip = xor_chip(z, c, n_exp)
    slots, tokens = x_ref.shape[1], token_scr.shape[1]

    def weight_copies(expert):
        for which, (source, target) in enumerate(
            ((gate_any, gate_w), (up_any, up_w), (down_any, down_w))
        ):
            chips, cores, _, depth, _ = source.shape
            n_x = chips // n_y
            for p in range(chips):
                for k in range(cores):
                    start = ((p // n_x * cores + k) * n_x + p % n_x) * depth
                    yield pltpu.make_async_copy(
                        source.at[p, k, expert],
                        target.at[expert, pl.ds(start, depth)],
                        weight_sems.at[which, expert, p * cores + k],
                    )

    def load(which, sources, methods):
        copies = [
            pltpu.make_async_copy(source, scratch.at[which], load_sems.at[which, i])
            for i, (source, scratch) in enumerate(zip(sources, (token_scr, cot_scr)))
        ]
        for method in methods:
            for copy in copies:
                getattr(copy, method)()

    def fetch(i):
        return pltpu.make_async_copy(partial_ref.at[c, i], got.at[i], local_sems.at[i])

    def store(chunk, i):
        target = (grad_chip_ref, out_chip_ref)[i].at[chunk]
        return pltpu.make_async_copy(got.at[i], target, local_sems.at[2 + i])

    other_parts = (tokens_ref.at[chip, 1 - core], cots_ref.at[chip, 1 - core])

    def core_copy(chunk, i):
        return pltpu.make_async_remote_copy(
            src_ref=send.at[i],
            dst_ref=partial_ref.at[chunk, i],
            send_sem=core_sems.at[0, chunk, i],
            recv_sem=core_sems.at[1, chunk, i],
            device_id=column.ids[CORE],
            device_id_type=MESH,
        )

    def grad_copy(chunk):
        return pltpu.make_async_remote_copy(
            src_ref=grad_chip_ref.at[chunk],
            dst_ref=grad_into_ref.at[chunk],
            send_sem=grad_sems.at[0, chunk],
            recv_sem=grad_sems.at[1, chunk],
            device_id={EXP: xor_chip(z, chunk, n_exp)},
            device_id_type=MESH,
        )

    @pl.when((c == 0) & (q == 0))
    def _():
        barrier = pltpu.get_barrier_semaphore()
        greeted = [column.ids[CORE]] + [{EXP: xor_chip(z, k, n_exp)} for k in range(1, n_exp)]
        for there in greeted:
            pl.semaphore_signal(barrier, inc=1, device_id=there, device_id_type=MESH)
        pl.semaphore_wait(barrier, n_exp)
        column.sends(1, START)
        column.pass_own(START)
        for expert in range(2):
            for copy in weight_copies(expert):
                copy.start()
        load(0, (own_ref, own_cot_ref), (START, WAIT))
        for copy in weight_copies(0):
            copy.wait()

    @pl.when((c > 0) & (q == 0))
    def _():
        column.arrivals(c)
        pl.when(c < n_exp - 1)(lambda: column.sends(c + 1, START))
        column.passes(c, START)
        load(0, (tokens_ref.at[chip, core], cots_ref.at[chip, core]), (START,))
        for i in range(2):
            store(c - 1, i).wait()
        pl.when(c == n_exp - 1)(lambda: grad_copy(1).start())
        pl.when(c > 2)(lambda: grad_copy(c - 1).start())
        load(0, (tokens_ref.at[chip, core], cots_ref.at[chip, core]), (WAIT,))

    @pl.when(q == 1)
    def _():
        for copy in column.copies(2, chip, False):
            copy.wait_recv()
        load(1, other_parts, (START, WAIT))

    @pl.when((c == 0) & (q == 2))
    def _():
        for copy in weight_copies(1):
            copy.wait()

    slot_ids = lax.broadcasted_iota(jnp.int32, (slots, tokens), 0).astype(f32)
    expert_rows = table_ref.shape[2] // 2
    first_row = z * local_experts + core * 2

    def hits_of(expert):
        return table_ref[chip, owner, pl.ds(first_row + expert, 1)] == slot_ids

    hits = hits_of(e)
    one_hot = hits.astype(f32).astype(bf16)
    gates = table_ref[chip, owner, pl.ds(expert_rows + first_row + e, 1)]
    gate_row = jnp.sum(jnp.where(hits, gates, 0.0), axis=1, keepdims=True)
    x_rows = dot_plain(one_hot, token_scr[s]).astype(bf16)
    x_ref[0] = x_rows
    grad_val = (gate_row * dot_plain(one_hot, cot_scr[s])).astype(bf16)
    val_ref[0] = grad_val
    gate_act = dot_plain(x_rows, gate_w[e])
    up_act = dot_plain(x_rows, up_w[e])
    sigmoid = 1.0 / (1.0 + jnp.exp(-gate_act))
    silu = gate_act * sigmoid
    product = (silu * up_act).astype(bf16)
    product_ref[0] = product
    grad_product = dot_cols(grad_val, down_w[e])
    grad_gate = (grad_product * up_act * (sigmoid * (1.0 + gate_act * (1.0 - sigmoid)))).astype(bf16)
    grad_up = (grad_product * silu).astype(bf16)
    gate_grad_ref[0] = grad_gate
    up_grad_ref[0] = grad_up
    grad_rows = (dot_cols(grad_gate, gate_w[e]) + dot_cols(grad_up, up_w[e])).astype(bf16)
    weighted = (gate_row * dot_plain(product, down_w[e])).astype(bf16)

    @pl.when(e == 0)
    def _():
        held[s, 0] = grad_rows
        held[s, 1] = weighted

    def combined(i, rows):
        before = hits_of(0).astype(f32).astype(bf16)
        return lax.dot_general(
            jnp.concatenate([before, one_hot], 0),
            jnp.concatenate([held[s, i], rows], 0),
            (((0,), (0,)), ((), ())),
            preferred_element_type=f32,
        )

    @pl.when(q == 2)
    def _():
        for i, rows in enumerate((grad_rows, weighted)):
            pl.when(c > 0)(lambda i=i: core_copy(c - 1, i).wait_send())
            send[i] = combined(i, rows).astype(bf16)
            core_copy(c, i).start()

    @pl.when(q == 3)
    def _():
        for i, rows in enumerate((grad_rows, weighted)):
            own = combined(i, rows)
            core_copy(c, i).wait_recv()
            fetch(i).start()
            fetch(i).wait()
            got[i] = (own + got[i].astype(f32)).astype(bf16)
            store(c, i).start()

    @pl.when((c == n_exp - 1) & (q == 3))
    def _():
        column.pass_own(WAIT_SEND)
        for hop in range(1, n_exp):
            column.sends(hop, WAIT_SEND)
            column.passes(hop, WAIT_SEND)
        for i in range(2):
            core_copy(n_exp - 1, i).wait_send()
            store(n_exp - 1, i).wait()
        for chunk in range(1, n_exp - 1):
            grad_copy(chunk).wait()


def run_experts(tables, own, own_cot, cots, weights, n_y, local_experts, slots, n_exp):
    bf16 = jnp.bfloat16
    tokens, model = own.shape
    ff = weights[0].shape[4]
    pieces = weights[0].shape[0] * weights[0].shape[1]
    any_spec = pl.BlockSpec(memory_space=pl.ANY)
    row_spec = lambda width: pl.BlockSpec(
        (1, slots, width), lambda c, q: (q // 2, 2 * c + (q % 3 + 1) // 2, 0)
    )
    widths = (model, model, ff, ff, ff)
    chip_shape = jax.ShapeDtypeStruct((n_exp, tokens, model), bf16)
    results = pl.pallas_call(
        functools.partial(moe_kernel, n_exp, n_y, local_experts),
        grid=(n_exp, 4),
        in_specs=[pl.BlockSpec(tables.shape, lambda c, q: (0, 0, 0, 0))] + [any_spec] * 6,
        out_specs=[row_spec(width) for width in widths] + [any_spec] * 6,
        out_shape=[jax.ShapeDtypeStruct((2, 2 * n_exp * slots, width), bf16) for width in widths]
        + [
            jax.ShapeDtypeStruct(cots.shape, bf16),
            jax.ShapeDtypeStruct((n_exp, 2, tokens, model), bf16),
            chip_shape,
            chip_shape,
            chip_shape,
            chip_shape,
        ],
        scratch_shapes=[
            pltpu.VMEM((2, model, ff), bf16),
            pltpu.VMEM((2, model, ff), bf16),
            pltpu.VMEM((2, ff, model), bf16),
            pltpu.VMEM((2, tokens, model), bf16),
            pltpu.VMEM((2, tokens, model), bf16),
            pltpu.VMEM((2, 2, slots, model), bf16),
            pltpu.VMEM((2, tokens, model), bf16),
            pltpu.VMEM((2, tokens, model), bf16),
            pltpu.SemaphoreType.DMA((3, 2, pieces)),
            pltpu.SemaphoreType.DMA((2, 2)),
            column_sems(1, n_exp),
            pltpu.SemaphoreType.DMA((2, n_exp, 2)),
            pltpu.SemaphoreType.DMA((4,)),
            pltpu.SemaphoreType.DMA((2, n_exp)),
        ],
        compiler_params=pltpu.CompilerParams(
            vmem_limit_bytes=63 * MIB, collective_id=7, has_side_effects=True
        ),
        cost_estimate=pl.CostEstimate(
            flops=4 * n_exp * (12 * slots * model * ff + 8 * slots * tokens * model),
            bytes_accessed=24 * model * ff + 4 * n_exp * slots * (2 * model + 3 * ff) * 2,
            transcendentals=4 * n_exp * slots * ff,
        ),
    )(tables, own, own_cot, cots, *weights)
    return results[:5], *results[7:]


def weight_grad_kernel(
    n_y,
    n_ctx,
    n_exp,
    merged,
    x_ref,
    val_ref,
    product_ref,
    gg_ref,
    gu_ref,
    chip_ref,
    into_in_ref,
    out_chip_ref,
    *refs,
):
    bf16 = jnp.bfloat16
    results, (into_ref, out_into_ref, pt_ref, ggt_ref, gut_ref, job_sems) = refs[:-6], refs[-6:]
    e, n = pl.program_id(0), pl.program_id(1)
    last, rows = n_exp - 1, chip_ref.shape[1]
    sent = [
        sent_rows(chip_ref, into_ref, (last, last, last, 0, rows), job_sems, 0, n_exp),
        sent_rows(out_chip_ref, out_into_ref, (last, last, 1, 0, rows), job_sems, 1, n_exp),
    ]

    @pl.when((e == 0) & (n == 0))
    def _():
        greet_slots([1, last], n_exp)
        for copy in sent:
            copy.start()

    @pl.when(n == 0)
    def _():
        for source, turned in ((product_ref, pt_ref), (gg_ref, ggt_ref), (gu_ref, gut_ref)):
            turned[...] = source[0].T

    gate, up = (dot_plain(turned[...], x_ref[0]).astype(bf16) for turned in (ggt_ref, gut_ref))
    down = dot_plain(pt_ref[...], val_ref[0]).astype(bf16)
    if merged:
        (result,) = results
        depth = result.shape[-2] // (2 * n_y * n_ctx)
        y, c, x = n // (2 * n_ctx), n // n_ctx % 2, n % n_ctx
        result[y, x, c, 0, 0] = gate
        result[y, x, c, 1, 0] = up
        rows = pl.ds(pl.multiple_of(n * depth, depth), depth)
        for shard in range(2 * n_y * n_ctx):
            place = (shard // (2 * n_ctx), shard % n_ctx, shard // n_ctx % 2, 2, 0, rows)
            result[place] = down[shard * depth : (shard + 1) * depth]
    else:
        for grad, result in zip((gate, up), results):
            depth = result.shape[-1]
            for i in range(result.shape[1]):
                result[0, i, 0, 0] = grad[:, i * depth : (i + 1) * depth]
        depth = results[2].shape[4]
        for shard in range(2 * n_y * n_ctx):
            place = (shard // (2 * n_ctx), shard % n_ctx, shard // n_ctx % 2, 0)
            results[2][place] = down[shard * depth : (shard + 1) * depth]

    @pl.when((e == 1) & (n == pl.num_programs(1) - 1))
    def _():
        for copy in sent:
            copy.wait()


def expert_weight_grads(rows, chip, into, out_chip, n_y, n_ctx, n_exp, merged):
    bf16 = jnp.bfloat16
    x_all, val_all, product_all, gg_all, gu_all = rows
    _, total, model = x_all.shape
    ff = gg_all.shape[2]
    shards = 2 * n_y * n_ctx
    col, depth, down_depth = 256, model // shards, ff // shards
    wide = pl.BlockSpec((1, total, col), lambda e, n: (e, 0, n))
    whole = pl.BlockSpec((1, total, ff), lambda e, n: (e, 0, 0))
    any_spec = pl.BlockSpec(memory_space=pl.ANY)
    if merged:
        out_specs = [
            pl.BlockSpec((n_y, n_ctx, 2, 3, 1, ff, depth), lambda e, n: (0, 0, 0, 0, e, 0, 0))
        ]
        out_shape = [jax.ShapeDtypeStruct((n_y, n_ctx, 2, 3, 2, ff, depth), bf16)]
    else:
        k = col // depth

        def place(e, n):
            shard = n * k
            return (shard // (2 * n_ctx), shard % n_ctx // k, shard // n_ctx % 2, e, 0, 0)

        out_specs = [pl.BlockSpec((1, k, 1, 1, ff, depth), place)] * 2
        out_specs.append(
            pl.BlockSpec((n_y, n_ctx, 2, 1, down_depth, col), lambda e, n: (0, 0, 0, e, 0, n))
        )
        out_shape = [jax.ShapeDtypeStruct((n_y, n_ctx, 2, 2, ff, depth), bf16)] * 2
        out_shape.append(jax.ShapeDtypeStruct((n_y, n_ctx, 2, 2, down_depth, model), bf16))
    *blocks, into, out_into = pl.pallas_call(
        functools.partial(weight_grad_kernel, n_y, n_ctx, n_exp, merged),
        grid=(2, model // col),
        in_specs=[wide, wide, whole, whole, whole] + [any_spec] * 3,
        out_specs=out_specs + [any_spec] * 2,
        out_shape=out_shape + [jax.ShapeDtypeStruct(a.shape, a.dtype) for a in (into, out_chip)],
        scratch_shapes=[pltpu.VMEM((ff, total), bf16)] * 3 + [pltpu.SemaphoreType.DMA((2, 2))],
        input_output_aliases={6: len(out_shape)},
        compiler_params=pltpu.CompilerParams(
            vmem_limit_bytes=63 * MIB, collective_id=8, has_side_effects=True
        ),
        cost_estimate=pl.CostEstimate(
            flops=2 * 6 * total * model * ff,
            bytes_accessed=2 * (2 * total * (2 * model + 3 * ff) + 6 * model * ff),
            transcendentals=0,
        ),
    )(x_all, val_all, product_all, gg_all, gu_all, chip, into, out_chip)
    return blocks, into, out_into


def part_grad_kernel(n_y, n_ctx, n_exp, jobs, wide_ref, *refs):
    bf16 = jnp.bfloat16
    sources, refs = (refs[:2], refs[2:]) if len(refs) == 12 else (refs[:1], refs[1:])
    chip_ref, _, out_chip_ref, _, result, into_ref, out_into_ref = refs[:7]
    turned_refs, job_sems = refs[7:-1], refs[-1]
    e, n = pl.program_id(0), pl.program_id(1)
    pairs = ((chip_ref, into_ref), (out_chip_ref, out_into_ref))
    sent = [
        sent_rows(*pairs[which], job, job_sems, i, n_exp) for i, (which, job) in enumerate(jobs)
    ]

    @pl.when((e == 0) & (n == 0))
    def _():
        greet_slots(sorted({job[2] for _, job in jobs}), n_exp)
        for copy in sent:
            copy.start()

    @pl.when(n == 0)
    def _():
        for source, turned in zip(sources, turned_refs):
            turned[...] = source[0].T

    grads = [dot_plain(turned[...], wide_ref[0]).astype(bf16) for turned in turned_refs]
    shards = 2 * n_y * n_ctx
    depth = result.shape[-2] // shards
    if len(grads) == 2:
        y, c, x = n // (2 * n_ctx), n // n_ctx % 2, n % n_ctx
        for i, grad in enumerate(grads):
            result[y, x, c, i, 0] = grad
    else:
        rows = pl.ds(pl.multiple_of(n * depth, depth), depth)
        for shard in range(shards):
            place = (shard // (2 * n_ctx), shard % n_ctx, shard // n_ctx % 2, 0, 0, rows)
            result[place] = grads[0][shard * depth : (shard + 1) * depth]

    @pl.when((e == 1) & (n == pl.num_programs(1) - 1))
    def _():
        for copy in sent:
            copy.wait()


def part_weight_grads(wide, sources, chip, into, out_chip, out_into, jobs, collective, n_y, n_ctx, n_exp):
    bf16 = jnp.bfloat16
    _, total, model = wide.shape
    ff, kinds, col = sources[0].shape[2], len(sources), 256
    whole = pl.BlockSpec((1, total, ff), lambda e, n: (e, 0, 0))
    any_spec = pl.BlockSpec(memory_space=pl.ANY)
    return pl.pallas_call(
        functools.partial(part_grad_kernel, n_y, n_ctx, n_exp, jobs),
        grid=(2, model // col),
        in_specs=[pl.BlockSpec((1, total, col), lambda e, n: (e, 0, n))]
        + [whole] * kinds
        + [any_spec] * 4,
        out_specs=[
            pl.BlockSpec((n_y, n_ctx, 2, kinds, 1, ff, col), lambda e, n: (0, 0, 0, 0, e, 0, 0))
        ]
        + [any_spec] * 2,
        out_shape=[jax.ShapeDtypeStruct((n_y, n_ctx, 2, kinds, 2, ff, col), bf16)]
        + [jax.ShapeDtypeStruct(a.shape, a.dtype) for a in (into, out_into)],
        scratch_shapes=[pltpu.VMEM((ff, total), bf16)] * kinds
        + [pltpu.SemaphoreType.DMA((2, len(jobs)))],
        input_output_aliases={kinds + 2: 1, kinds + 4: 2},
        compiler_params=pltpu.CompilerParams(
            vmem_limit_bytes=60 * MIB, collective_id=collective, has_side_effects=True
        ),
        cost_estimate=pl.CostEstimate(
            flops=4 * kinds * total * model * ff,
            bytes_accessed=4 * (total * (model + kinds * ff) + kinds * model * ff),
            transcendentals=0,
        ),
    )(wide, *sources, chip, into, out_chip, out_into)


def sum_kernel(plan, value_ref, total_ref, held, arrived, sems):
    partners = [{axis: xor_chip(lax.axis_index(axis), hop, size)} for axis, size, hop in plan]
    barrier = pltpu.get_barrier_semaphore()
    for there in partners:
        pl.semaphore_signal(barrier, inc=1, device_id=there, device_id_type=MESH)
    pl.semaphore_wait(barrier, len(plan))
    held[0] = value_ref[...]
    for i, there in enumerate(partners):
        copy = pltpu.make_async_remote_copy(
            src_ref=held.at[i],
            dst_ref=arrived.at[i],
            send_sem=sems.at[0, i],
            recv_sem=sems.at[1, i],
            device_id=there,
            device_id_type=MESH,
        )
        copy.start()
        copy.wait()
        held[i + 1] = held[i] + arrived[i]
    total_ref[...] = held[len(plan)]


def sum_devices(value, axes):
    plan = [(axis, size, 1 << i) for axis, size in axes for i in range(size.bit_length() - 1)]
    spec = pl.BlockSpec(memory_space=pltpu.VMEM)
    return pl.pallas_call(
        functools.partial(sum_kernel, plan),
        in_specs=[spec],
        out_specs=spec,
        out_shape=jax.ShapeDtypeStruct(value.shape, value.dtype),
        scratch_shapes=[
            pltpu.VMEM((len(plan) + 1,) + value.shape, value.dtype),
            pltpu.VMEM((len(plan),) + value.shape, value.dtype),
            pltpu.SemaphoreType.DMA((2, len(plan))),
        ],
        compiler_params=pltpu.CompilerParams(collective_id=9, has_side_effects=True),
    )(value)


def on_device(
    residual_in,
    segments,
    routes,
    gates,
    attn_gain,
    q_proj,
    key_projection,
    value_projection,
    q_gain,
    k_gain,
    o_proj,
    mlp_gain,
    gate_proj,
    up_proj,
    down_proj,
    out_grad,
):
    bf16, f32 = jnp.bfloat16, jnp.float32
    n_seq, n_ctx, n_exp = lax.axis_size(SEQ), lax.axis_size(CTX), lax.axis_size(EXP)
    n_y = n_seq // 2
    devices = n_seq * n_ctx * n_exp
    core = lax.axis_index(SEQ) % 2
    span_index = lax.axis_index(CTX)
    z_index = lax.axis_index(EXP)
    group_all = [
        [(s * n_ctx + x) * n_exp + z for s in range(c, n_seq, 2) for x in range(n_ctx) for z in range(n_exp)]
        for c in range(2)
    ]
    group_plane = [[s * n_ctx + x for s in range(c, n_seq, 2) for x in range(n_ctx)] for c in range(2)]

    def swap(value):
        return lax.ppermute(value, SEQ, [(i, i ^ 1) for i in range(n_seq)])

    def across(value, step):
        return lax.ppermute(value, EXP, [(i, i ^ step) for i in range(n_exp)])

    token_count = residual_in.shape[1]
    model_width = residual_in.shape[2]
    sequence_length = segments.shape[1]
    route_count = routes.shape[2]
    local_experts = gate_proj.shape[0]
    expert_count = local_experts * n_exp
    half_experts = local_experts // 2
    capacity = token_count * route_count * 9 // (expert_count * 8)
    slots = -(-capacity // 16) * 16
    groups = KEY_VALUE_HEADS // 2
    heads = QUERY_HEADS // 2
    heads_per_group = QUERY_HEADS // KEY_VALUE_HEADS
    score_scale = HEAD_DIM ** (-0.5)
    rows = q_proj.shape[0]
    gain_rows = q_gain.shape[0]
    q_width, kv_width = heads * HEAD_DIM, groups * HEAD_DIM
    width = q_width + 2 * kv_width

    route_ids = routes[0]
    route_hit = route_ids[:, :, None] == jnp.arange(expert_count, dtype=jnp.int32)[None, None, :]
    hit_counts = route_hit.astype(jnp.int32).sum(1)
    earlier = jnp.cumsum(hit_counts, axis=0) - hit_counts
    slot_of = jnp.where(hit_counts > 0, earlier, -1).astype(f32)
    gate_of = jnp.sum(jnp.where(route_hit, gates[0][:, :, None], 0.0), axis=1)
    table = jnp.concatenate([slot_of.T, gate_of.T], 0)
    def gain_block(model_parts, head_parts, dtype):
        lead = model_parts[0].shape[:-1]
        fill = lambda size: jnp.zeros(lead + (1, size), dtype)
        first = jnp.concatenate([p[..., None, :] for p in model_parts] + [fill(128 - 2 * rows)], -1)
        second = jnp.concatenate(
            [p[..., None, :] for p in head_parts] + [fill(128 - 2 * gain_rows)], -1
        )
        return jnp.concatenate([first, second, jnp.zeros(lead + (rows - 2, 128), dtype)], -2)

    extra = gain_block([attn_gain, mlp_gain], [q_gain, k_gain], bf16)
    mine_cols, other_cols = [], []
    for weight in (q_proj, key_projection, value_projection):
        mine, other = column_halves(weight, core)
        mine_cols += mine
        other_cols += other
    mine_block = jnp.concatenate(mine_cols + [extra], 1)
    other_block = jnp.concatenate(other_cols + [extra], 1)
    chips = n_y * n_ctx
    own_links = n_y == 2 and n_ctx == 2 and n_exp == 4
    if own_links:
        halves = []
        for weight in (gate_proj, up_proj, down_proj):
            low, high = weight[:half_experts], weight[half_experts:]
            halves += [pick(core, low, high), pick(core, high, low)]
        w_gathered, w_out, gate_full, up_full, down_pair, cots_all, tables_all = gather_chips(
            mine_block,
            other_block,
            halves,
            o_proj.reshape(4, -1, model_width),
            routes[0].T,
            gates[0].T,
            out_grad[0],
            expert_count,
            n_exp,
        )
        w_out = w_out.reshape(q_width, model_width)
        w_gathered = w_gathered.reshape(chips * n_exp, 2, rows, width + 128)
    else:
        theirs = swap(other_block)
        pair = jnp.stack([pick(core, mine_block, theirs), pick(core, theirs, mine_block)])
        w_gathered = lax.all_gather(
            pair, (SEQ, CTX, EXP), axis=0, tiled=False, axis_index_groups=group_all
        )
        cots_all, tables_all = exchange_column(out_grad[0], table, n_exp)
    w_extra = w_gathered[:, :, :2, width:].reshape(n_y, n_ctx * n_exp, 2, 2, 128)
    w_extra = w_extra.transpose(0, 2, 1, 3, 4).reshape(devices, 2, 128).astype(f32)
    gain_attn = w_extra[:, 0, :rows].reshape(model_width)
    gain_mlp_f = w_extra[:, 0, rows : 2 * rows].reshape(model_width)
    gain_query_f = w_extra[:, 1, :gain_rows].reshape(1, HEAD_DIM)
    gain_key_f = w_extra[:, 1, gain_rows : 2 * gain_rows].reshape(1, HEAD_DIM)

    if not own_links:
        w_out = lax.all_gather(
            o_proj, (SEQ, CTX, EXP), axis=0, tiled=True, axis_index_groups=group_all
        )

    def gather_expert(weight, after):
        if own_links:
            both = weight
        else:
            mine = pick(core, weight[:half_experts], weight[half_experts:])
            theirs = swap(pick(core, weight[half_experts:], weight[:half_experts]))
            both = jnp.stack([pick(core, mine, theirs), pick(core, theirs, mine)])
        both = lax.optimization_barrier((both, after))[0]
        full = lax.all_gather(
            both, (SEQ, CTX), axis=0, tiled=False, axis_index_groups=group_plane
        )
        full = full.reshape((n_y * n_ctx,) + both.shape)
        if own_links:
            return full
        full = full.reshape((n_y, n_ctx) + both.shape).transpose(3, 0, 2, 1, 4, 5)
        return full.reshape(1, 1, half_experts, -1, weight.shape[2])

    hidden = residual_in[0].astype(f32)
    seg_two = jnp.stack([segments[0], swap(segments)[0]])
    seg_here = lax.dynamic_slice_in_dim(seg_two, span_index * token_count, token_count, 1)
    valid_two = (seg_here > 0).astype(f32).reshape(2 * token_count, 1)
    valid_rows = valid_two[:token_count]
    positions = span_index * token_count + jnp.arange(token_count, dtype=jnp.int32)
    cos_one, sin_one = rope_tables(positions)
    half_dim = HEAD_DIM // 2
    signed_sine = jnp.concatenate([-sin_one[:, :half_dim], sin_one[:, half_dim:]], 1)
    info = jnp.zeros((2, 8, token_count), jnp.int32)
    info = info.at[:, 0].set(seg_here).at[:, 1].set(positions[None])
    seg_keys = seg_two[:, :, None]
    inv_attn = lax.rsqrt(jnp.mean(hidden * hidden, axis=-1, keepdims=True) + EPS)
    q_blocks = q_width // (2 * HEAD_DIM)
    if own_links:
        q_raw, query_rows, w_query, normed_turned, kv_full, *moving = project_all(
            residual_in[0],
            swap(residual_in[0]),
            gain_attn[None],
            w_gathered,
            q_blocks,
            gain_key_f,
            gain_query_f,
            cos_one,
            signed_sine,
            out_grad[0],
            n_y,
            n_exp,
            (gate_full, up_full, cots_all, tables_all),
        )
    else:
        kv_raw, kv_low, w_kv, normed_two = project_keys(
            residual_in[0],
            swap(residual_in[0]),
            gain_attn[None],
            w_gathered,
            q_blocks,
            gain_key_f,
            cos_one,
            signed_sine,
            n_y,
        )
        kv_here = kv_low.reshape(2, token_count, 2 * kv_width)
        kv_full = lax.all_gather(kv_here, CTX, axis=1, tiled=True)
        q_raw, query_rows, w_query, *moving = project_queries(
            normed_two, w_gathered, q_blocks, gain_query_f, cos_one, signed_sine, n_y, n_exp, ()
        )
    mixed_low, recip, *moving = attend(
        info, seg_keys, query_rows, kv_full, groups, heads_per_group, n_exp, moving
    )
    if own_links:
        gate_full, up_full, cots_all, tables_all = moving
    else:
        gate_full, up_full = gather_expert(gate_proj, gain_attn), gather_expert(up_proj, gain_attn)
    down_full = gather_expert(
        down_pair if own_links else down_proj, query_rows if own_links else gain_attn
    )
    if not own_links:
        tables_all = lax.dynamic_update_slice(
            tables_all, table[None, None], (z_index, core, jnp.int32(0), jnp.int32(0))
        )
    attn_partial = jnp.dot(mixed_low, w_out, preferred_element_type=f32)
    attn_out = attn_partial[:token_count] + swap(attn_partial[token_count:])
    middle = hidden + attn_out
    inv_mlp = lax.rsqrt(jnp.mean(middle * middle, axis=-1, keepdims=True) + EPS)
    normed_mlp = (middle * inv_mlp * gain_mlp_f).astype(bf16)

    rows_all, grad_chip, out_chip, grad_into, out_into = run_experts(
        tables_all,
        normed_mlp,
        out_grad[0],
        cots_all,
        (gate_full, up_full, down_full),
        n_y if own_links else 1,
        local_experts,
        slots,
        n_exp,
    )

    if own_links:
        x_rows, val_rows, product_rows, gate_rows, up_rows = rows_all
        last, first_rows = n_exp - 1, 5 * token_count // 16
        blocks = []
        for i, (wide, sources) in enumerate(
            ((val_rows, (product_rows,)), (x_rows, (gate_rows, up_rows)))
        ):
            span = ((0, first_rows), (first_rows, token_count))[i]
            jobs = [(0, (last, last, last, *span)), (1, (last, last, 1, *span))]
            block, grad_into, out_into = part_weight_grads(
                wide, sources, grad_chip, grad_into, out_chip, out_into, jobs, 13 + i, n_y, n_ctx, n_exp
            )
            blocks.append(block)
    else:
        weight_blocks, grad_into, out_into = expert_weight_grads(
            rows_all, grad_chip, grad_into, out_chip, n_y, n_ctx, n_exp, merged=False
        )
    out_far = (out_chip[2:3].astype(f32) + out_into[3:4].astype(f32)).astype(bf16)

    def scatter_plane(blocks):
        return lax.psum_scatter(
            blocks.reshape((n_y * n_ctx,) + blocks.shape[2:]),
            (SEQ, CTX),
            scatter_dimension=0,
            tiled=True,
            axis_index_groups=group_plane,
        )[0]

    def all_experts(part):
        mine = pick(core, part[0], part[1])
        theirs = swap(pick(core, part[1], part[0]))
        axis = mine.ndim - 3
        both = [pick(core, mine, theirs), pick(core, theirs, mine)]
        return jnp.concatenate(both, axis).astype(f32)

    if own_links:
        parts = []
        for block in blocks:
            part = scatter_plane(block.reshape(n_y, n_ctx, -1, block.shape[-1]))
            parts.append(lax.optimization_barrier(part).reshape(block.shape[2:]))
    else:
        parts = [scatter_plane(weight_blocks[0])]
        for blocks in weight_blocks[1:]:
            blocks, parts[-1] = lax.optimization_barrier((blocks, parts[-1]))
            parts.append(scatter_plane(blocks))

    grad_normed_mlp = grad_chip[0].astype(f32)
    for step in range(1, n_exp):
        grad_normed_mlp = grad_normed_mlp + grad_into[step].astype(f32)
    cotangent = out_grad[0].astype(f32)
    mlp_gain_grad = jnp.sum(grad_normed_mlp * middle * inv_mlp, axis=0)
    grad_middle = cotangent + norm_back(grad_normed_mlp, middle, inv_mlp, gain_mlp_f)
    grad_attn_own = grad_middle.astype(bf16)
    part_rows = token_count // 4
    out_jobs, back_jobs = [(0, 2, 2, 0, part_rows)], [(0, 2, 2, part_rows, token_count)]
    last_jobs = [(1, 1, 1, 0, token_count)]
    o_grad_part, mixture_gradient, out_into = out_back(
        mixed_low, grad_attn_own, swap(grad_attn_own), w_out, valid_two, out_far, out_into, out_jobs, n_exp
    )
    o_grad_plane = scatter_plane(o_grad_part.reshape(n_y, n_ctx, n_exp, -1, model_width))
    grad_q_raw, key_grad, value_grad, q_gain_rows, out_into = attend_back(
        info,
        seg_keys,
        query_rows,
        kv_full,
        mixed_low,
        mixture_gradient,
        recip,
        q_raw,
        gain_query_f,
        cos_one,
        signed_sine,
        groups,
        heads_per_group,
        out_far,
        out_into,
        back_jobs,
        n_exp,
    )
    q_gain_grad = q_gain_rows[0]
    if own_links:
        grad_kv, grad_hidden, attn_gain_grad, k_gain_rows, out_into = back_to_input(
            grad_q_raw,
            key_grad,
            value_grad,
            q_raw,
            w_query,
            gain_key_f,
            cos_one,
            signed_sine,
            residual_in[0],
            gain_attn[None],
            grad_middle,
            out_chip,
            out_into,
            last_jobs,
            n_exp,
        )
        k_gain_grad = k_gain_rows[0]
    else:
        kv_grad = jnp.concatenate([key_grad, value_grad], 2)
        query_part = contract_cols(grad_q_raw, w_query)
        kv_grad_here = lax.psum_scatter(
            kv_grad.astype(bf16), CTX, scatter_dimension=1, tiled=True
        ).astype(f32)
        kv_grad_here = kv_grad_here.reshape(2 * token_count, 2 * kv_width)
        cosine_table, sine_values = jnp.concatenate([cos_one] * 2, 0), jnp.concatenate([sin_one] * 2, 0)
        k_raw = kv_raw[:, :kv_width].reshape(-1, groups, HEAD_DIM)
        inv_key = lax.rsqrt(jnp.mean(k_raw * k_raw, axis=-1, keepdims=True) + EPS)
        grad_kn = inverse_rotation(
            kv_grad_here[:, :kv_width].reshape(-1, groups, HEAD_DIM), cosine_table, sine_values
        )
        k_gain_grad = jnp.sum(grad_kn * k_raw * inv_key, axis=(0, 1))
        grad_k_raw = norm_back(grad_kn, k_raw, inv_key, gain_key_f).astype(bf16)
        grad_kv = jnp.concatenate(
            [grad_k_raw.reshape(-1, kv_width), kv_grad_here[:, kv_width:].astype(bf16)], 1
        )
        normed_partial = query_part + contract_cols(grad_kv, w_kv)
        grad_normed = normed_partial[:token_count] + swap(normed_partial[token_count:])
        attn_gain_grad = jnp.sum(grad_normed * hidden * inv_attn, axis=0)
        grad_hidden = grad_middle + norm_back(grad_normed, hidden, inv_attn, gain_attn)

    extra_grad = gain_block(
        [attn_gain_grad.reshape(devices, rows), mlp_gain_grad.reshape(devices, rows)],
        [q_gain_grad.reshape(devices, gain_rows), k_gain_grad.reshape(devices, gain_rows)],
        f32,
    ).astype(bf16)
    if not own_links:
        near = across(out_chip[1], 1)
        out_into = lax.dynamic_update_slice(out_into, near[None], (1, 0, 0))
    expert_out = out_chip[0].astype(f32)
    for step in (1, 2):
        expert_out = expert_out + out_into[step].astype(f32)
    final_out = (middle + expert_out).astype(bf16)
    sums = [
        jnp.sum(value * value * valid_rows, keepdims=True) for value in (hidden, attn_out, expert_out)
    ]
    sums.append(jnp.sum(valid_rows, keepdims=True))
    stats = jnp.pad(jnp.concatenate(sums, 1), ((0, 7), (0, 124)))
    if not own_links:
        stats = sum_devices(stats, ((SEQ, n_seq), (CTX, n_ctx), (EXP, n_exp)))
    if own_links:
        part = all_experts(jnp.concatenate(parts[::-1], 1))
        gate_grad, up_grad = part[0].transpose(0, 2, 1), part[1].transpose(0, 2, 1)
        depth = part.shape[-1]
        down_grad = part[2].reshape(local_experts, model_width // depth, -1, depth)
        down_grad = down_grad.transpose(0, 2, 1, 3).reshape(local_experts, -1, model_width)
        extra_grad, o_grad_plane, gate_grad, up_grad, down_grad, stats, final_out = (
            lax.optimization_barrier(
                (extra_grad, o_grad_plane, gate_grad, up_grad, down_grad, stats, final_out)
            )
        )
    o_proj_grad = lax.psum_scatter(o_grad_plane, EXP, scatter_dimension=0, tiled=True)
    o_proj_grad = o_proj_grad[0].astype(f32)
    if own_links:
        grad_mine, grad_theirs, stats = dense_grad_scatter(
            normed_turned,
            grad_q_raw,
            grad_kv,
            extra_grad.reshape(n_y, 2, n_ctx, n_exp, rows, 128),
            stats,
            n_exp,
        )
    else:
        w_grad = jnp.concatenate(
            [
                contract_rows(normed_two, grad_q_raw).astype(bf16),
                contract_rows(normed_two, grad_kv).astype(bf16),
                extra_grad.reshape(model_width, 128),
            ],
            1,
        )
        w_grad = w_grad.reshape(n_y, 2, n_ctx, n_exp, rows, width + 128).transpose(0, 2, 3, 1, 4, 5)
        w_grad = lax.psum_scatter(
            scatter_plane(w_grad), EXP, scatter_dimension=0, tiled=True
        )[0]
        grad_mine = pick(core, w_grad[0], w_grad[1])
        grad_theirs = swap(pick(core, w_grad[1], w_grad[0]))
    rms_stats = jnp.sqrt(stats[0, :3] / (stats[0, 3] * model_width))
    if not own_links:
        gate_grad, up_grad = (all_experts(p).transpose(0, 2, 1) for p in parts[:2])
        down_grad = all_experts(parts[2])
    even = pick(core, grad_mine, grad_theirs).astype(f32)
    odd = pick(core, grad_theirs, grad_mine).astype(f32)

    def columns(start, size):
        step = size // groups
        parts = []
        for g in range(groups):
            parts += [half[:, start + g * step : start + (g + 1) * step] for half in (even, odd)]
        return jnp.concatenate(parts, 1)

    extra_total = even[:, width:] + odd[:, width:]
    return (
        final_out[None],
        grad_hidden.astype(bf16)[None],
        extra_total[0, :rows],
        columns(0, q_width),
        columns(q_width, kv_width),
        columns(q_width + kv_width, kv_width),
        extra_total[1, :gain_rows],
        extra_total[1, gain_rows : 2 * gain_rows],
        o_proj_grad,
        extra_total[0, rows : 2 * rows],
        gate_grad,
        up_grad,
        down_grad,
        rms_stats,
    )


def solution(mesh):
    in_specs = (
        P((SEQ, EXP), CTX, None),
        P((SEQ, EXP), None),
        P((SEQ, EXP), CTX, None),
        P((SEQ, EXP), CTX, None),
        P((SEQ, CTX, EXP)),
        P((SEQ, CTX, EXP), None),
        P((SEQ, CTX, EXP), None),
        P((SEQ, CTX, EXP), None),
        P((SEQ, CTX, EXP)),
        P((SEQ, CTX, EXP)),
        P((SEQ, CTX, EXP), None),
        P((SEQ, CTX, EXP)),
        P(EXP, (SEQ, CTX), None),
        P(EXP, (SEQ, CTX), None),
        P(EXP, (SEQ, CTX), None),
        P((SEQ, EXP), CTX, None),
    )
    out_specs = (
        P((SEQ, EXP), CTX, None),
        P((SEQ, EXP), CTX, None),
        P((SEQ, CTX, EXP)),
        P((SEQ, CTX, EXP), None),
        P((SEQ, CTX, EXP), None),
        P((SEQ, CTX, EXP), None),
        P((SEQ, CTX, EXP)),
        P((SEQ, CTX, EXP)),
        P((SEQ, CTX, EXP), None),
        P((SEQ, CTX, EXP)),
        P(EXP, (SEQ, CTX), None),
        P(EXP, (SEQ, CTX), None),
        P(EXP, (SEQ, CTX), None),
        P(),
    )
    return jax.shard_map(
        on_device, mesh=mesh, in_specs=in_specs, out_specs=out_specs, check_vma=False
    )
```

```python
import functools

import jax
import jax.numpy as jnp
from jax import lax
from jax.experimental import pallas as pl
from jax.experimental.pallas import tpu as pltpu
from jax.sharding import PartitionSpec as P

QUERY_HEADS = 32
KEY_VALUE_HEADS = 4
HEAD_DIM = 128


EPS = 1e-06
ROPE_BASE = 1000000.0
MASKED = -1e30
MESH = pl.DeviceIdType.MESH
SEQ = "seq"
CTX = "ctx"
EXP = "exp"
CORE = "core"
X = "x"
Y = "y"
UP = "up"
DOWN = "down"
START = "start"
WAIT = "wait"
WAIT_SEND = "wait_send"
WAIT_RECV = "wait_recv"
INFO = "info"
SEG = "seg"
HEAD = "head"
KEY = "key"
VALUE = "value"
RECIP = "recip"


def contract_rows(first_op, second_op):
    return lax.dot_general(
        first_op, second_op, (((0,), (0,)), ((), ())), preferred_element_type=jnp.float32
    )


def contract_cols(first_op, second_op):
    return lax.dot_general(
        first_op, second_op, (((1,), (1,)), ((), ())), preferred_element_type=jnp.float32
    )


def rope_tables(positions):
    half_dim = HEAD_DIM // 2
    inverse = ROPE_BASE ** (-jnp.arange(half_dim, dtype=jnp.float32) * 2.0 / HEAD_DIM)
    angles = positions.astype(jnp.float32)[:, None] * inverse[None, :]
    cosine_table = jnp.cos(angles)
    sine_values = jnp.sin(angles)
    return (
        jnp.concatenate([cosine_table, cosine_table], -1),
        jnp.concatenate([sine_values, sine_values], -1),
    )


def inverse_rotation(gradient, cosine_table, sine_values):
    half_dim = gradient.shape[-1] // 2
    scaled = gradient * sine_values[:, None, :]
    return gradient * cosine_table[:, None, :] + jnp.concatenate(
        [scaled[..., half_dim:], -scaled[..., :half_dim]], -1
    )


def norm_back(gradient, source, inverse, gain_vec):
    scaled = gradient * gain_vec
    return inverse * scaled - source * inverse**3 * jnp.mean(
        scaled * source, axis=-1, keepdims=True
    )


def neighbours(n_exp):
    seq, x, z = lax.axis_index(SEQ), lax.axis_index(CTX), lax.axis_index(EXP)
    y, core = seq // 2, seq % 2
    ids = {
        CORE: {SEQ: 2 * y + 1 - core},
        X: {CTX: 1 - x},
        Y: {SEQ: 2 * (1 - y) + core},
        UP: {EXP: z + 1},
        DOWN: {EXP: z - 1},
    }
    return x, y, z, core, ids


def greet(z, n_exp, ids, names):
    barrier = pltpu.get_barrier_semaphore()
    count = 0
    for name in names:
        if name in (UP, DOWN):
            there = (z < n_exp - 1) if name == UP else (z > 0)

            @pl.when(there)
            def _():
                pl.semaphore_signal(
                    barrier, inc=1, device_id=ids[name], device_id_type=MESH
                )

            count = count + there.astype(jnp.int32)
        else:
            pl.semaphore_signal(
                barrier, inc=1, device_id=ids[name], device_id_type=MESH
            )
            count = count + 1
    pl.semaphore_wait(barrier, count)


def xor_chip(z, step, n_exp):
    result, bit = 0, 1
    while bit < n_exp:
        result = result + bit * ((z // bit % 2 + step // bit % 2) % 2)
        bit *= 2
    return result


class Plane:
    def __init__(self, n_exp, fulls, sems):
        x, y, _, _, self.ids = neighbours(n_exp)
        self.here, self.beside, self.across = 2 * y + x, 2 * y + 1 - x, 2 * (1 - y) + x
        self.fulls, self.sems = fulls, sems

    def each(self, method, far):
        near = ((self.here,), X), ((self.here,), Y)
        cases = (((self.beside, 0), Y), ((self.across, 1), X)) if far else near
        for which, full in enumerate(self.fulls):
            for lane, (place, name) in enumerate(cases):
                part = full.at[place]
                copy = pltpu.make_async_remote_copy(
                    src_ref=part,
                    dst_ref=part,
                    send_sem=self.sems.at[0, which, lane],
                    recv_sem=self.sems.at[1, which, lane],
                    device_id=self.ids[name],
                    device_id_type=MESH,
                )
                getattr(copy, method)()


def plane_sems(arrays):
    return pltpu.SemaphoreType.DMA((2, arrays, 2))


class Column:
    def __init__(self, n_exp, everyone, sems, own=None):
        self.x, self.y, self.z, self.core, self.ids = neighbours(n_exp)
        self.n_exp, self.everyone, self.sems, self.own = n_exp, everyone, sems, own

    def copies(self, lane, part, first):
        for which, result in enumerate(self.everyone):
            there = result.at[part, self.core]
            yield pltpu.make_async_remote_copy(
                src_ref=self.own[which] if first else there,
                dst_ref=there,
                send_sem=self.sems.at[0, which, lane, part],
                recv_sem=self.sems.at[1, which, lane, part],
                device_id=self.ids[(UP, DOWN, CORE)[lane]],
                device_id_type=MESH,
            )

    def each(self, method, cases, first=False):
        for lane, part, there in cases:

            @pl.when(there)
            def _(lane=lane, part=part):
                for copy in self.copies(lane, part, first):
                    getattr(copy, method)()

    def sends(self, hop, method):
        z, n = self.z, self.n_exp
        cases = (
            (0, z - hop + 1, (z >= hop - 1) & (z < n - 1)),
            (1, z + hop - 1, (z + hop - 1 < n) & (z > 0)),
        )
        self.each(method, cases, first=isinstance(hop, int) and hop == 1)

    def arrivals(self, hop):
        z, n = self.z, self.n_exp
        self.each(WAIT_RECV, ((0, z - hop, z >= hop), (1, z + hop, z + hop < n)))

    def passes(self, hop, method):
        z, n = self.z, self.n_exp
        self.each(method, ((2, z - hop, z >= hop), (2, z + hop, z + hop < n)))

    def pass_own(self, method):
        for copy in self.copies(2, self.z, True):
            getattr(copy, method)()


def column_sems(arrays, n_exp):
    return pltpu.SemaphoreType.DMA((2, arrays, 3, n_exp))


def sent_rows(chip_ref, into_ref, job, sems, i, n_exp):
    slot, into, step, start, stop = job
    rows = pl.ds(start, stop - start)
    return pltpu.make_async_remote_copy(
        src_ref=chip_ref.at[slot, rows],
        dst_ref=into_ref.at[into, rows],
        send_sem=sems.at[0, i],
        recv_sem=sems.at[1, i],
        device_id={EXP: xor_chip(lax.axis_index(EXP), step, n_exp)},
        device_id_type=MESH,
    )


def greet_slots(slots, n_exp):
    barrier = pltpu.get_barrier_semaphore()
    for slot in slots:
        pl.semaphore_signal(
            barrier,
            inc=1,
            device_id={EXP: xor_chip(lax.axis_index(EXP), slot, n_exp)},
            device_id_type=MESH,
        )
    pl.semaphore_wait(barrier, len(slots))


def store_table(routes_ref, gates_ref, table_ref):
    f32, bf16 = jnp.float32, jnp.bfloat16
    experts, tokens = table_ref.shape[0] // 2, table_ref.shape[1]
    expert_ids = lax.broadcasted_iota(jnp.int32, (experts, tokens), 0)
    hits, gates = jnp.zeros((experts, tokens), f32), jnp.zeros((experts, tokens), f32)
    for k in range(routes_ref.shape[0]):
        named = routes_ref[k : k + 1] == expert_ids
        hits = hits + named.astype(f32)
        gates = gates + jnp.where(named, gates_ref[k : k + 1], 0.0)
    row = lax.broadcasted_iota(jnp.int32, (tokens, tokens), 0)
    before = (row < lax.broadcasted_iota(jnp.int32, (tokens, tokens), 1)).astype(f32).astype(bf16)
    table_ref[:experts] = jnp.where(hits > 0.0, dot_plain(hits.astype(bf16), before), -1.0)
    table_ref[experts:] = gates


def gather_kernel(
    n_exp,
    mine_ref,
    other_ref,
    gate_ref,
    other_gate_ref,
    up_ref,
    other_up_ref,
    down_ref,
    other_down_ref,
    out_ref,
    routes_ref,
    gates_ref,
    cot_ref,
    full_ref,
    out_full_ref,
    gate_full_ref,
    up_full_ref,
    down_pair_ref,
    cots_ref,
    tables_ref,
    local_sems,
    core_sems,
    z_sems,
    x_sems,
    y_sems,
    xf_sems,
    yf_sems,
    column_sem,
    first_sems,
    line_sems,
    table_ref,
):
    column = Column(n_exp, (cots_ref, tables_ref), column_sem, (cot_ref, table_ref))
    x, y, z, core, ids = neighbours(n_exp)
    greet(z, n_exp, ids, (CORE, X, Y, UP, DOWN))
    here, beside, across = 2 * y + x, 2 * y + 1 - x, 2 * (1 - y) + x

    fulls = (full_ref, out_full_ref)

    def act(method, place, sems, slot, name):
        for which, full in enumerate(fulls):
            if which and len(place) == 2:
                place = (*place, pl.ds(0, 2))
            part = full.at[place]
            copy = pltpu.make_async_remote_copy(
                src_ref=part,
                dst_ref=part,
                send_sem=sems.at[0, which, slot],
                recv_sem=sems.at[1, which, slot],
                device_id=ids[name],
                device_id_type=MESH,
            )
            getattr(copy, method)()

    def moved(method, place, sems, slot, name):
        part = out_full_ref.at[place]
        copy = pltpu.make_async_remote_copy(
            src_ref=part,
            dst_ref=part,
            send_sem=sems.at[(0, *slot)],
            recv_sem=sems.at[(1, *slot)],
            device_id=ids[name],
            device_id_type=MESH,
        )
        getattr(copy, method)()

    def first_near(method):
        for slot, name in enumerate((X, Y)):
            moved(method, (here, z, pl.ds(2, 2)), first_sems, (slot,), name)

    def first_far(method):
        moved(method, (beside, z, 2), first_sems, (2,), Y)
        moved(method, (across, z, 3), first_sems, (3,), X)

    def line(hop, method):
        for lane, name, part, there in (
            (0, UP, z - hop + 1, (z >= hop - 1) & (z < n_exp - 1)),
            (1, DOWN, z + hop - 1, (z + hop - 1 < n_exp) & (z > 0)),
        ):
            pl.when(there)(
                lambda lane=lane, name=name, part=part: moved(
                    method, (slice(None), part, pl.ds(2, 2)), line_sems, (lane, part), name
                )
            )

    def line_arrivals(hop):
        for lane, name, part, there in (
            (0, UP, z - hop, z >= hop),
            (1, DOWN, z + hop, z + hop < n_exp),
        ):
            pl.when(there)(
                lambda lane=lane, name=name, part=part: moved(
                    WAIT_RECV, (slice(None), part, pl.ds(2, 2)), line_sems, (lane, part), name
                )
            )

    places = (
        full_ref.at[here, z, core],
        gate_full_ref.at[here, core],
        up_full_ref.at[here, core],
        down_pair_ref.at[core],
    )
    kept = [
        pltpu.make_async_copy(source, place, local_sems.at[i])
        for i, (source, place) in enumerate(zip((mine_ref, gate_ref, up_ref, down_ref), places))
    ]
    kept.insert(1, pltpu.make_async_copy(out_ref, out_full_ref.at[here, z], local_sems.at[4]))
    to_core = [
        pltpu.make_async_remote_copy(
            src_ref=source,
            dst_ref=place,
            send_sem=core_sems.at[0, i],
            recv_sem=core_sems.at[1, i],
            device_id=ids[CORE],
            device_id_type=MESH,
        )
        for i, (source, place) in enumerate(zip((other_ref, other_gate_ref, other_up_ref, other_down_ref), places))
    ]
    for copy in kept + to_core:
        copy.start()
    store_table(routes_ref, gates_ref, table_ref)
    kept_table = pltpu.make_async_copy(table_ref, tables_ref.at[z, core], local_sems.at[5])
    kept_table.start()
    kept.append(kept_table)
    to_core[0].wait()
    kept[0].wait()
    kept[1].wait()
    column.pass_own(START)

    def source(label):
        hop = (label + 1) // 2
        if label == 0:
            return z, None
        return (z - hop, z >= hop) if label % 2 else (z + hop, z + hop < n_exp)

    labels = range(2 * n_exp - 1)

    def guarded(condition, action):
        if condition is None:
            action()
        else:
            pl.when(condition)(action)

    def z_slot(label, name):
        return label + 1 if label else (0 if name == UP else 1)

    def z_sends(label, method):
        part, there = source(label)
        for name in (UP, DOWN) if label == 0 else ((UP,) if label % 2 else (DOWN,)):
            room = (z < n_exp - 1) if name == UP else (z > 0)
            condition = room if there is None else there & room
            pl.when(condition)(
                lambda name=name: act(method, (here, part), z_sems, z_slot(label, name), name)
            )

    def z_arrival(label):
        hop = (label + 1) // 2
        name = UP if label % 2 else DOWN
        part, there = source(label)
        slot = z_slot(label - 2 if hop > 1 else 0, name)
        pl.when(there)(lambda: act(WAIT_RECV, (here, part), z_sems, slot, name))

    def spread(label):
        part, there = source(label)
        z_sends(label, START)

        def action():
            act(START, (here, part), x_sems, label, X)
            act(START, (here, part), y_sems, label, Y)

        guarded(there, action)

    def turn(label):
        part, there = source(label)

        def action():
            act(WAIT_RECV, (beside, part), x_sems, label, X)
            act(START, (beside, part, 0), xf_sems, label, Y)
            act(WAIT_RECV, (across, part), y_sems, label, Y)
            act(START, (across, part, 1), yf_sems, label, X)

        guarded(there, action)

    first_near(START)
    spread(0)
    for hop in range(1, n_exp):
        for label in (2 * hop - 1, 2 * hop):
            z_arrival(label)
            spread(label)
        if hop == 1:
            first_near(WAIT_RECV)
            first_far(START)
        if hop == n_exp - 1:
            first_far(WAIT_RECV)
            line(1, START)
        for label in (0,) if hop == 1 else (2 * hop - 3, 2 * hop - 2):
            turn(label)
    line_arrivals(1)
    line(2, START)
    for label in (2 * n_exp - 3, 2 * n_exp - 2):
        turn(label)
    for hop in range(2, n_exp):
        line_arrivals(hop)
        if hop < n_exp - 1:
            line(hop + 1, START)
    first_near(WAIT_SEND)
    first_far(WAIT_SEND)
    for hop in range(1, n_exp):
        line(hop, WAIT_SEND)
    opposite = 2 * (1 - y) + 1 - x
    for label in labels:
        part, there = source(label)

        def action(label=label, part=part):
            act(WAIT_SEND, (here, part), x_sems, label, X)
            act(WAIT_SEND, (here, part), y_sems, label, Y)
            act(WAIT_SEND, (beside, part, 0), xf_sems, label, Y)
            act(WAIT_SEND, (across, part, 1), yf_sems, label, X)
            act(WAIT_RECV, (opposite, part, 0), xf_sems, label, Y)
            act(WAIT_RECV, (opposite, part, 1), yf_sems, label, X)

        guarded(there, action)
        z_sends(label, WAIT_SEND)
    column.pass_own(WAIT)
    for copy in kept[2:] + to_core[1:]:
        copy.wait()


def gather_chips(mine, other, halves, out, routes, gates, cot, experts, n_exp):
    labels = 2 * n_exp - 1
    any_spec = pl.BlockSpec(memory_space=pl.ANY)
    vmem_spec = pl.BlockSpec(memory_space=pltpu.VMEM)
    pair = lambda count: pltpu.SemaphoreType.DMA((2, 2, count))
    return pl.pallas_call(
        functools.partial(gather_kernel, n_exp),
        in_specs=[vmem_spec] * 11 + [any_spec],
        out_specs=[any_spec] * 7,
        out_shape=[
            jax.ShapeDtypeStruct((4, n_exp, 2) + mine.shape, mine.dtype),
            jax.ShapeDtypeStruct((4, n_exp) + out.shape, out.dtype),
        ]
        + [jax.ShapeDtypeStruct((4, 2) + a.shape, a.dtype) for a in halves[:4:2]]
        + [jax.ShapeDtypeStruct((2,) + halves[4].shape, halves[4].dtype)]
        + [
            jax.ShapeDtypeStruct((n_exp, 2) + cot.shape, cot.dtype),
            jax.ShapeDtypeStruct((n_exp, 2, 2 * experts, cot.shape[0]), jnp.float32),
        ],
        scratch_shapes=[
            pltpu.SemaphoreType.DMA((6,)),
            pltpu.SemaphoreType.DMA((2, 4)),
            pair(2 * n_exp),
            pair(labels),
            pair(labels),
            pair(labels),
            pair(labels),
            column_sems(2, n_exp),
            pltpu.SemaphoreType.DMA((2, 4)),
            pltpu.SemaphoreType.DMA((2, 2, n_exp)),
            pltpu.VMEM((2 * experts, cot.shape[0]), jnp.float32),
        ],
        compiler_params=pltpu.CompilerParams(
            collective_id=1, has_side_effects=True, vmem_limit_bytes=32 * MIB
        ),
    )(mine, other, *halves, out, routes, gates, cot)


def exchange_kernel(n_exp, first_ref, second_ref, firsts_ref, seconds_ref, sems):
    column = Column(n_exp, (firsts_ref, seconds_ref), sems, (first_ref, second_ref))
    greet(column.z, n_exp, column.ids, (CORE, UP, DOWN))
    column.sends(1, START)
    column.pass_own(START)
    for hop in range(1, n_exp):
        column.arrivals(hop)
        if hop < n_exp - 1:
            column.sends(hop + 1, START)
        column.passes(hop, START)
    column.pass_own(WAIT)
    for hop in range(1, n_exp):
        column.sends(hop, WAIT_SEND)
        column.passes(hop, WAIT)


def exchange_column(tokens, table, n_exp):
    any_spec = pl.BlockSpec(memory_space=pl.ANY)
    return pl.pallas_call(
        functools.partial(exchange_kernel, n_exp),
        in_specs=[any_spec] * 2,
        out_specs=[any_spec] * 2,
        out_shape=[
            jax.ShapeDtypeStruct((n_exp, 2) + a.shape, a.dtype) for a in (tokens, table)
        ],
        scratch_shapes=[column_sems(2, n_exp)],
        compiler_params=pltpu.CompilerParams(collective_id=3, has_side_effects=True),
        cost_estimate=pl.CostEstimate(
            flops=0, bytes_accessed=16 * n_exp * tokens.size, transcendentals=0
        ),
    )(tokens, table)


def scatter_kernel(
    n_exp,
    turned,
    grad_ref,
    kv_grad_ref,
    extra_ref,
    stats_ref,
    mine_ref,
    theirs_ref,
    stats_sum_ref,
    part,
    from_x,
    from_y,
    second_x,
    second_y,
    total,
    from_z,
    from_core,
    x_sems,
    y_sems,
    x2_sems,
    y2_sems,
    z_sems,
    core_sems,
    held,
    arrived,
    stat_sems,
):
    bf16, f32 = jnp.bfloat16, jnp.float32
    x, y, z, core, ids = neighbours(n_exp)
    barrier = pltpu.get_barrier_semaphore()
    columns = [{EXP: (z + k) % n_exp} for k in range(1, n_exp)]
    for there in [ids[CORE], ids[X], ids[Y]] + columns:
        pl.semaphore_signal(barrier, inc=1, device_id=there, device_id_type=MESH)
    pl.semaphore_wait(barrier, 2 + n_exp)

    def remote(source, target, sems, slot, there):
        return pltpu.make_async_remote_copy(
            src_ref=source,
            dst_ref=target,
            send_sem=sems.at[0, slot],
            recv_sem=sems.at[1, slot],
            device_id=there,
            device_id_type=MESH,
        )

    rounds = [ids[CORE], ids[Y], ids[X]]
    rounds += [{EXP: xor_chip(z, 1 << i, n_exp)} for i in range(n_exp.bit_length() - 1)]
    held[0] = stats_ref[...]

    def stat_copy(i):
        return remote(held.at[i], arrived.at[i], stat_sems, i, rounds[i])

    def stat_round(i):
        if i:
            stat_copy(i - 1).wait()
            held[i] = held[i - 1] + arrived[i - 1]
        if i < len(rounds):
            stat_copy(i).start()

    stat_round(0)
    rows = mine_ref.shape[0]
    q_width, width = grad_ref.shape[1], grad_ref.shape[1] + kv_grad_ref.shape[1]
    steps = range(n_exp)

    def first_copies(k):
        return [
            remote(part.at[k, 1 - x, :, 0], from_x.at[k], x_sems, k, ids[X]),
            remote(part.at[k, :, 1 - y, 1], from_y.at[k], y_sems, k, ids[Y]),
        ]

    def second_copies(k):
        return [
            remote(part.at[k, x, 1 - y, 0], second_x.at[k], x2_sems, k, ids[Y]),
            remote(part.at[k, 1 - x, y, 1], second_y.at[k], y2_sems, k, ids[X]),
        ]

    def z_copy(k):
        return remote(
            total.at[k], from_z.at[k], z_sems, k, {EXP: (z + k + 1) % n_exp}
        )

    def produce(k):
        place = (z + k + 1) % n_exp
        blocks = []
        for px in range(2):
            for py in range(2):
                for c in range(2):
                    start = (((py * 2 + c) * 2 + px) * n_exp + place) * rows
                    blocks.append(turned[pl.ds(pl.multiple_of(start, rows), rows), :])
        block = jnp.concatenate(blocks, 0)
        grad = dot_plain(block, grad_ref[...]).astype(bf16)
        kv_grad = dot_plain(block, kv_grad_ref[...]).astype(bf16)
        i = 0
        for px in range(2):
            for py in range(2):
                for c in range(2):
                    part[k, px, py, c, :, :q_width] = grad[i * rows : (i + 1) * rows]
                    part[k, px, py, c, :, q_width:width] = kv_grad[i * rows : (i + 1) * rows]
                    part[k, px, py, c, :, width:] = extra_ref[py, c, px, place]
                    i += 1

    def launch(k):
        for copy in first_copies(k):
            copy.start()

    for k in steps:
        produce(k)
        if k < 2:
            launch(k)

    def second(k):
        along_x, along_y = first_copies(k)
        along_x.wait_recv()
        for py in range(2):
            part[k, x, py, 0] = (part[k, x, py, 0].astype(f32) + from_x[k, py].astype(f32)).astype(bf16)
        along_y.wait_recv()
        for px in range(2):
            part[k, px, y, 1] = (part[k, px, y, 1].astype(f32) + from_y[k, px].astype(f32)).astype(bf16)
        for copy in second_copies(k):
            copy.start()

    def third(k):
        along_y, along_x = second_copies(k)
        along_y.wait_recv()
        total[k, 0] = (part[k, x, y, 0].astype(f32) + second_x[k].astype(f32)).astype(bf16)
        along_x.wait_recv()
        total[k, 1] = (part[k, x, y, 1].astype(f32) + second_y[k].astype(f32)).astype(bf16)
        if k < n_exp - 1:
            z_copy(k).start()

    for k in steps:
        stat_round(k + 1)
        second(k)
        if k + 2 < n_exp:
            launch(k + 2)
        if k:
            third(k - 1)
    third(n_exp - 1)
    for i in range(n_exp + 1, len(rounds) + 1):
        stat_round(i)
    stats_sum_ref[...] = held[len(rounds)]
    result = total[n_exp - 1].astype(f32)
    for k in range(n_exp - 1):
        z_copy(k).wait_recv()
        result = result + from_z[k].astype(f32)
    total[n_exp - 1] = result.astype(bf16)
    to_core = remote(total.at[n_exp - 1, 1 - core], from_core, core_sems, 0, ids[CORE])
    to_core.start()
    for k in steps:
        for copy in first_copies(k) + second_copies(k) + ([z_copy(k)] if k < n_exp - 1 else []):
            copy.wait_send()
    to_core.wait()
    mine_ref[...] = total[n_exp - 1, core].astype(f32)
    theirs_ref[...] = from_core[...].astype(f32)


def dense_grad_scatter(turned, grad, kv_grad, extra, stats, n_exp):
    bf16 = jnp.bfloat16
    rows, model = extra.shape[4], turned.shape[0]
    width = grad.shape[1] + kv_grad.shape[1] + extra.shape[5]
    block = (rows, width)
    vmem = lambda *lead: pltpu.VMEM(lead + block, bf16)
    pair = lambda count: pltpu.SemaphoreType.DMA((2, count))
    spec = pl.BlockSpec(memory_space=pltpu.VMEM)
    return pl.pallas_call(
        functools.partial(scatter_kernel, n_exp),
        in_specs=[spec] * 5,
        out_specs=[spec] * 3,
        out_shape=[jax.ShapeDtypeStruct(block, jnp.float32)] * 2
        + [jax.ShapeDtypeStruct(stats.shape, stats.dtype)],
        scratch_shapes=[
            vmem(n_exp, 2, 2, 2),
            vmem(n_exp, 2),
            vmem(n_exp, 2),
            vmem(n_exp),
            vmem(n_exp),
            vmem(n_exp, 2),
            vmem(n_exp, 2),
            vmem(),
            pair(n_exp),
            pair(n_exp),
            pair(n_exp),
            pair(n_exp),
            pair(n_exp),
            pair(1),
            pltpu.VMEM((n_exp + 2,) + stats.shape, stats.dtype),
            pltpu.VMEM((n_exp + 2,) + stats.shape, stats.dtype),
            pair(n_exp + 2),
        ],
        compiler_params=pltpu.CompilerParams(
            collective_id=2, has_side_effects=True, vmem_limit_bytes=60 * MIB
        ),
        cost_estimate=pl.CostEstimate(
            flops=2 * turned.shape[1] * model * width, bytes_accessed=16 * MIB, transcendentals=0
        ),
    )(turned, grad, kv_grad, extra, stats)


def back_kernel(
    n_exp,
    jobs,
    query_grad_ref,
    key_grad_ref,
    value_grad_ref,
    raw_ref,
    w_query_ref,
    w_kv_ref,
    gain_ref,
    cos_ref,
    sin_ref,
    hidden_ref,
    row_gain_ref,
    middle_grad_ref,
    chip_ref,
    into_in_ref,
    kv_grad_ref,
    hidden_grad_ref,
    row_gain_grad_ref,
    gain_grad_ref,
    into_ref,
    kv_send,
    kv_got,
    sib_part,
    own_part,
    part_got,
    x_sems,
    core_sems,
    job_sems,
):
    bf16, f32 = jnp.bfloat16, jnp.float32
    x, _, z, _, ids = neighbours(n_exp)
    tokens, model = hidden_ref.shape
    keys_width = raw_ref.shape[1] // 2
    barrier = pltpu.get_barrier_semaphore()
    slots = sorted({job[2] for job in jobs})
    greeted = [ids[CORE], ids[X]] + [{EXP: xor_chip(z, slot, n_exp)} for slot in slots]
    for there in greeted:
        pl.semaphore_signal(barrier, inc=1, device_id=there, device_id_type=MESH)
    here, there = (pl.ds(pl.multiple_of(i * tokens, tokens), tokens) for i in (x, 1 - x))
    for s in range(2):
        kv_send[s, :, :keys_width] = key_grad_ref[s, there].astype(bf16)
        kv_send[s, :, keys_width:] = value_grad_ref[s, there].astype(bf16)
    pl.semaphore_wait(barrier, len(greeted))
    to_x = pltpu.make_async_remote_copy(
        src_ref=kv_send,
        dst_ref=kv_got,
        send_sem=x_sems.at[0],
        recv_sem=x_sems.at[1],
        device_id=ids[X],
        device_id_type=MESH,
    )
    to_x.start()
    sent = [sent_rows(chip_ref, into_ref, job, job_sems, i, n_exp) for i, job in enumerate(jobs)]
    for copy in sent:
        copy.start()
    tile = 256
    parts = ((1, sib_part), (0, own_part))

    def query_product(s, part):
        rows = query_grad_ref[s * tokens : (s + 1) * tokens]
        for start in range(0, model, tile):
            part[:, start : start + tile] = dot_cols(rows, w_query_ref[start : start + tile])

    for s, part in parts:
        query_product(s, part)
    to_x.wait()
    gain_grad = None
    for s in range(2):
        rows = slice(s * tokens, (s + 1) * tokens)
        for start in range(0, keys_width, HEAD_DIM):
            columns = slice(start, start + HEAD_DIM)
            grad = key_grad_ref[s, here, columns] + kv_got[s, :, columns].astype(f32)
            turned = rotate_rows_back(grad, cos_ref[...], sin_ref[...])
            raw = raw_ref[rows, columns]
            inverse = lax.rsqrt(jnp.mean(raw * raw, axis=-1, keepdims=True) + EPS)
            unit = raw * inverse
            total = jnp.sum(turned * unit, axis=0, keepdims=True)
            gain_grad = total if gain_grad is None else gain_grad + total
            scaled = turned * gain_ref[...]
            kv_grad_ref[rows, columns] = (
                inverse * (scaled - unit * jnp.mean(scaled * unit, axis=-1, keepdims=True))
            ).astype(bf16)
        value_grad = value_grad_ref[s, here] + kv_got[s, :, keys_width:].astype(f32)
        kv_grad_ref[rows, keys_width:] = value_grad.astype(bf16)
    gain_grad_ref[0:1] = gain_grad

    def kv_product(s, part):
        rows = kv_grad_ref[s * tokens : (s + 1) * tokens]
        for start in range(0, model, tile):
            part[:, start : start + tile] += dot_cols(rows, w_kv_ref[start : start + tile])

    kv_product(*parts[0])
    to_core = pltpu.make_async_remote_copy(
        src_ref=sib_part,
        dst_ref=part_got,
        send_sem=core_sems.at[0],
        recv_sem=core_sems.at[1],
        device_id=ids[CORE],
        device_id_type=MESH,
    )
    to_core.start()
    kv_product(*parts[1])
    to_core.wait()
    row_gain_grad_ref[...] = jnp.zeros_like(row_gain_grad_ref)
    count = min(tokens, 64)

    @pl.loop(0, tokens // count)
    def _(i):
        rows = pl.ds(pl.multiple_of(i * count, count), count)
        grad = own_part[rows] + part_got[rows]
        hidden = hidden_ref[rows].astype(f32)
        inverse = lax.rsqrt(jnp.mean(hidden * hidden, axis=-1, keepdims=True) + EPS)
        unit = hidden * inverse
        row_gain_grad_ref[...] += jnp.sum(grad * unit, axis=0, keepdims=True)
        scaled = grad * row_gain_ref[...]
        back = inverse * (scaled - unit * jnp.mean(scaled * unit, axis=-1, keepdims=True))
        hidden_grad_ref[rows] = (middle_grad_ref[rows] + back).astype(bf16)

    for copy in sent:
        copy.wait()


def back_to_input(
    query_grad, key_grad, value_grad, raw, weight, gain, cos, sin, hidden, row_gain, middle_grad,
    chip, into, jobs, n_exp
):
    bf16, f32 = jnp.bfloat16, jnp.float32
    tokens, model = hidden.shape
    total, q_width = query_grad.shape
    kv_width = raw.shape[1] - q_width
    once = dict(pipeline_mode=pl.Buffered(1))
    tail = lambda rows: pl.BlockSpec((rows, kv_width), lambda i: (0, q_width // kv_width), **once)
    vmem, any_spec = pl.BlockSpec(memory_space=pltpu.VMEM), pl.BlockSpec(memory_space=pl.ANY)
    return pl.pallas_call(
        functools.partial(back_kernel, n_exp, jobs),
        grid=(1,),
        in_specs=[vmem] * 3
        + [tail(total), pl.BlockSpec((model, q_width), lambda i: (0, 0), **once), tail(model)]
        + [vmem] * 6
        + [any_spec] * 2,
        out_specs=[vmem] * 4 + [any_spec],
        out_shape=[
            jax.ShapeDtypeStruct((total, kv_width), bf16),
            jax.ShapeDtypeStruct((tokens, model), bf16),
            jax.ShapeDtypeStruct((1, model), f32),
            jax.ShapeDtypeStruct((8, HEAD_DIM), f32),
            jax.ShapeDtypeStruct(into.shape, into.dtype),
        ],
        scratch_shapes=[
            pltpu.VMEM((2, tokens, kv_width), bf16),
            pltpu.VMEM((2, tokens, kv_width), bf16),
            pltpu.VMEM((tokens, model), f32),
            pltpu.VMEM((tokens, model), f32),
            pltpu.VMEM((tokens, model), f32),
            pltpu.SemaphoreType.DMA((2,)),
            pltpu.SemaphoreType.DMA((2,)),
            pltpu.SemaphoreType.DMA((2, len(jobs))),
        ],
        input_output_aliases={13: 4},
        compiler_params=pltpu.CompilerParams(
            vmem_limit_bytes=60 * MIB, collective_id=11, has_side_effects=True
        ),
        cost_estimate=pl.CostEstimate(
            flops=2 * total * model * (query_grad.shape[1] + kv_width),
            bytes_accessed=48 * MIB,
            transcendentals=0,
        ),
    )(
        query_grad, key_grad, value_grad, raw, weight, weight, gain, cos, sin, hidden, row_gain,
        middle_grad, chip, into
    )


def out_back_kernel(
    n_exp, jobs, mixed_ref, own_ref, sib_ref, weight_ref, valid_ref, chip_ref, into_in, weight_grad_ref, mixed_grad_ref, into_ref, grad_ref, sems
):
    bf16 = jnp.bfloat16
    sent = [sent_rows(chip_ref, into_ref, job, sems, i, n_exp) for i, job in enumerate(jobs)]
    step, tokens = pl.program_id(0), own_ref.shape[0]

    @pl.when(step == 0)
    def _():
        grad_ref[:tokens] = own_ref[...]
        grad_ref[tokens:] = sib_ref[...]
        greet_slots(sorted({job[2] for job in jobs}), n_exp)
        for copy in sent:
            copy.start()

    weight_grad_ref[...] = dot_plain(mixed_ref[...].T, grad_ref[...]).astype(bf16)
    mixed_grad = dot_cols(grad_ref[...], weight_ref[...]).astype(bf16)
    mixed_grad_ref[...] = mixed_grad * valid_ref[...].astype(bf16)

    @pl.when(step == pl.num_programs(0) - 1)
    def _():
        for copy in sent:
            copy.wait()


def out_back(mixed, own, sib, weight, valid, chip, into, jobs, n_exp):
    bf16 = jnp.bfloat16
    total, width = mixed.shape
    model = own.shape[1]
    block = 2 * HEAD_DIM
    any_spec = pl.BlockSpec(memory_space=pl.ANY)
    columns = pl.BlockSpec((total, block), lambda j: (0, j))
    rows = pl.BlockSpec((block, model), lambda j: (j, 0))
    return pl.pallas_call(
        functools.partial(out_back_kernel, n_exp, jobs),
        grid=(width // block,),
        in_specs=[
            columns,
            pl.BlockSpec(own.shape, lambda j: (0, 0)),
            pl.BlockSpec(own.shape, lambda j: (0, 0)),
            rows,
            pl.BlockSpec(valid.shape, lambda j: (0, 0)),
            any_spec,
            any_spec,
        ],
        out_specs=[rows, columns, any_spec],
        out_shape=[
            jax.ShapeDtypeStruct((width, model), bf16),
            jax.ShapeDtypeStruct((total, width), bf16),
            jax.ShapeDtypeStruct(into.shape, bf16),
        ],
        input_output_aliases={6: 2},
        scratch_shapes=[pltpu.VMEM((total, model), bf16), pltpu.SemaphoreType.DMA((2, len(jobs)))],
        compiler_params=pltpu.CompilerParams(
            vmem_limit_bytes=40 * MIB, collective_id=12, has_side_effects=True
        ),
        cost_estimate=pl.CostEstimate(
            flops=4 * total * model * width, bytes_accessed=24 * MIB, transcendentals=0
        ),
    )(mixed, own, sib, weight, valid, chip, into)


def pick(core, first, second):
    return jnp.where(core == 0, first, second)


def column_halves(weight, core):
    width = weight.shape[1] // KEY_VALUE_HEADS
    parts = [weight[:, i * width : (i + 1) * width] for i in range(KEY_VALUE_HEADS)]
    mine = [pick(core, parts[i], parts[i + 1]) for i in range(0, KEY_VALUE_HEADS, 2)]
    other = [pick(core, parts[i + 1], parts[i]) for i in range(0, KEY_VALUE_HEADS, 2)]
    return mine, other


LOG2E = 1.4426950408889634
MIB = 1 << 20


def rotate_rows(vectors, cosine_table, signed_sine):
    return vectors * cosine_table + pltpu.roll(vectors, HEAD_DIM // 2, 1) * signed_sine


def rotate_rows_back(gradient, cosine_table, signed_sine):
    return gradient * cosine_table - pltpu.roll(gradient, HEAD_DIM // 2, 1) * signed_sine


def dot_cols(first, second):
    return lax.dot_general(
        first, second, (((1,), (1,)), ((), ())), preferred_element_type=jnp.float32
    )


def dot_plain(first, second):
    return jnp.dot(first, second, preferred_element_type=jnp.float32)


def ordered_weight(n_y, weight_ref, ordered_ref):
    n_xz = weight_ref.shape[0] // n_y
    weight = jnp.concatenate(
        [weight_ref[y * n_xz + i, c] for y in range(n_y) for c in range(2) for i in range(n_xz)], 0
    )
    ordered_ref[...] = weight
    return weight


def store_rotated(raw, gain, cos_ref, sin_ref, low_ref):
    tokens = cos_ref.shape[0]
    for h in range(2):
        columns = slice(h * HEAD_DIM, (h + 1) * HEAD_DIM)
        head = raw[:, columns]
        inverse = lax.rsqrt(jnp.mean(head * head, axis=-1, keepdims=True) + EPS)
        scaled = head * inverse * gain
        for s in range(2):
            part = slice(s * tokens, (s + 1) * tokens)
            low_ref[part, columns] = rotate_rows(scaled[part], cos_ref[...], sin_ref[...]).astype(
                jnp.bfloat16
            )


def key_value_kernel(
    n_y,
    own_ref,
    sib_ref,
    row_gain_ref,
    weight_ref,
    gain_ref,
    cos_ref,
    sin_ref,
    raw_ref,
    low_ref,
    ordered_ref,
    normed_ref,
):
    tokens = own_ref.shape[0]

    @pl.when(pl.program_id(0) == 0)
    def _():
        for s, source in enumerate((own_ref, sib_ref)):
            hidden = source[...].astype(jnp.float32)
            inverse = lax.rsqrt(jnp.mean(hidden * hidden, axis=-1, keepdims=True) + EPS)
            normed_ref[s * tokens : (s + 1) * tokens] = (hidden * inverse * row_gain_ref[...]).astype(
                jnp.bfloat16
            )

    raw = dot_plain(normed_ref[...], ordered_weight(n_y, weight_ref, ordered_ref))
    raw_ref[...] = raw

    @pl.when(pl.program_id(0) == 0)
    def _():
        store_rotated(raw, gain_ref[...], cos_ref, sin_ref, low_ref)

    @pl.when(pl.program_id(0) == 1)
    def _():
        low_ref[...] = raw.astype(jnp.bfloat16)


def query_kernel(n_y, n_exp, normed_ref, weight_ref, gain_ref, cos_ref, sin_ref, *refs):
    if n_exp:
        raw_ref, low_ref, ordered_ref, gate_full_ref, up_full_ref, cots_ref, tables_ref = refs[4:11]
        plane = Plane(n_exp, (gate_full_ref, up_full_ref), refs[11])
        column = Column(n_exp, (cots_ref, tables_ref), refs[12])

        @pl.when(pl.program_id(0) == 0)
        def _():
            greet(column.z, n_exp, plane.ids, (CORE, X, Y, UP, DOWN))
            plane.each(START, False)
            column.sends(2, START)
            column.passes(1, START)
    else:
        raw_ref, low_ref, ordered_ref = refs
    raw = dot_plain(normed_ref[...], ordered_weight(n_y, weight_ref, ordered_ref))
    raw_ref[...] = raw
    store_rotated(raw, gain_ref[...], cos_ref, sin_ref, low_ref)
    if n_exp:

        @pl.when(pl.program_id(0) == pl.num_programs(0) - 1)
        def _():
            plane.each(WAIT, False)
            column.arrivals(2)
            column.sends(2, WAIT_SEND)
            column.passes(1, WAIT)


def project_kernel(
    n_y,
    n_exp,
    own_ref,
    sib_ref,
    row_gain_ref,
    weight_ref,
    key_gain_ref,
    gain_ref,
    cos_ref,
    sin_ref,
    *refs,
):
    raw_ref, low_ref, ordered_ref, turned_ref, kv_full_ref = refs[5:10]
    gate_full_ref, up_full_ref, cots_ref, tables_ref, kv_scr, normed_ref = refs[10:16]
    plane_sem, column_sem, kv_sems = refs[16:]
    plane = Plane(n_exp, (gate_full_ref, up_full_ref), plane_sem)
    column = Column(n_exp, (cots_ref, tables_ref), column_sem)
    column.own = (refs[0], tables_ref.at[column.z, column.core])
    j, tokens = pl.program_id(0), own_ref.shape[0]
    here = kv_full_ref.at[:, pl.ds(pl.multiple_of(column.x * tokens, tokens), tokens)]
    kv_copies = [
        pltpu.make_async_remote_copy(
            src_ref=kv_scr,
            dst_ref=here,
            send_sem=kv_sems.at[0],
            recv_sem=kv_sems.at[1],
            device_id=column.ids[X],
            device_id_type=MESH,
        ),
        pltpu.make_async_copy(kv_scr, here, kv_sems.at[2]),
    ]

    @pl.when(j == 0)
    def _():
        greet(column.z, n_exp, plane.ids, (CORE, X, Y, UP, DOWN))
        plane.each(START, False)
        column.sends(1, START)
        for s, source in enumerate((own_ref, sib_ref)):
            hidden = source[...].astype(jnp.float32)
            inverse = lax.rsqrt(jnp.mean(hidden * hidden, axis=-1, keepdims=True) + EPS)
            normed_ref[s * tokens : (s + 1) * tokens] = (hidden * inverse * row_gain_ref[...]).astype(
                jnp.bfloat16
            )

    @pl.when(j == pl.num_programs(0) // 2)
    def _():
        column.arrivals(1)
        column.sends(2, START)
        column.passes(1, START)

    raw = dot_plain(normed_ref[...], ordered_weight(n_y, weight_ref, ordered_ref))
    raw_ref[...] = raw

    @pl.when(j != 1)
    def _():
        gain = jnp.where(j == 0, key_gain_ref[...], gain_ref[...])
        store_rotated(raw, gain, cos_ref, sin_ref, low_ref)

    @pl.when(j == 1)
    def _():
        low_ref[...] = raw.astype(jnp.bfloat16)
        turned_ref[...] = normed_ref[...].T

    for which in range(2):

        @pl.when(j == which)
        def _(which=which):
            width = low_ref.shape[1]
            for s in range(2):
                kv_scr[s, :, which * width : (which + 1) * width] = low_ref[
                    s * tokens : (s + 1) * tokens
                ]
            if which:
                for copy in kv_copies:
                    copy.start()

    @pl.when(j == pl.num_programs(0) - 1)
    def _():
        for copy in kv_copies:
            copy.wait()
        plane.each(WAIT, False)
        column.arrivals(2)
        for hop in (1, 2):
            column.sends(hop, WAIT_SEND)
        column.passes(1, WAIT)


def project_all(own, sib, row_gain, gathered, blocks, key_gain, gain, cos, sin, cot, n_y, n_exp, moving):
    bf16 = jnp.bfloat16
    tokens, model = own.shape
    total, width = 2 * tokens, 2 * HEAD_DIM
    n_yxz, _, rows, _ = gathered.shape
    fixed = lambda j: (0, 0)
    block = lambda j: jnp.where(j < 2, blocks + j, j - 2)
    any_specs = [pl.BlockSpec(memory_space=pl.ANY)] * len(moving)
    columns = pl.BlockSpec((total, width), lambda j: (0, block(j)))
    return pl.pallas_call(
        functools.partial(project_kernel, n_y, n_exp),
        grid=(blocks + 2,),
        in_specs=[pl.BlockSpec(own.shape, fixed)] * 2
        + [
            pl.BlockSpec((1, model), fixed),
            pl.BlockSpec((n_yxz, 2, rows, width), lambda j: (0, 0, 0, block(j))),
            pl.BlockSpec((1, HEAD_DIM), fixed),
            pl.BlockSpec((1, HEAD_DIM), fixed),
            pl.BlockSpec(cos.shape, fixed),
            pl.BlockSpec(cos.shape, fixed),
            pl.BlockSpec(memory_space=pl.ANY),
        ]
        + any_specs,
        out_specs=[
            columns,
            columns,
            pl.BlockSpec((model, width), lambda j: (0, block(j))),
            pl.BlockSpec((model, total), fixed),
            pl.BlockSpec(memory_space=pl.ANY),
        ]
        + any_specs,
        out_shape=[
            jax.ShapeDtypeStruct((total, (blocks + 2) * width), jnp.float32),
            jax.ShapeDtypeStruct((total, (blocks + 2) * width), bf16),
            jax.ShapeDtypeStruct((model, (blocks + 2) * width), bf16),
            jax.ShapeDtypeStruct((model, total), bf16),
            jax.ShapeDtypeStruct((2, 2 * tokens, 2 * width), bf16),
        ]
        + [jax.ShapeDtypeStruct(a.shape, a.dtype) for a in moving],
        scratch_shapes=[
            pltpu.VMEM((2, tokens, 2 * width), bf16),
            pltpu.VMEM((total, model), bf16),
            plane_sems(2),
            column_sems(2, n_exp),
            pltpu.SemaphoreType.DMA((3,)),
        ],
        input_output_aliases={9 + i: 5 + i for i in range(len(moving))},
        compiler_params=pltpu.CompilerParams(
            vmem_limit_bytes=60 * MIB, collective_id=4, has_side_effects=True
        ),
        cost_estimate=pl.CostEstimate(
            flops=2 * total * model * (blocks + 2) * width, bytes_accessed=64 * MIB, transcendentals=0
        ),
    )(own, sib, row_gain, gathered, key_gain, gain, cos, sin, cot, *moving)


def projection_specs(normed_shape, gathered, first_block, blocks, cos):
    total, model = normed_shape
    n_yxz, _, rows, _ = gathered.shape
    width = 2 * HEAD_DIM
    fixed = lambda j: (0, 0)
    moving = lambda j: (0, j)
    weight = pl.BlockSpec((n_yxz, 2, rows, width), lambda j: (0, 0, 0, j + first_block))
    tail = [pl.BlockSpec((1, HEAD_DIM), fixed), pl.BlockSpec(cos.shape, fixed), pl.BlockSpec(cos.shape, fixed)]
    out_specs = [pl.BlockSpec((total, width), moving)] * 2 + [pl.BlockSpec((model, width), moving)]
    out_shape = [
        jax.ShapeDtypeStruct((total, blocks * width), jnp.float32),
        jax.ShapeDtypeStruct((total, blocks * width), jnp.bfloat16),
        jax.ShapeDtypeStruct((model, blocks * width), jnp.bfloat16),
    ]
    cost = pl.CostEstimate(
        flops=2 * total * model * blocks * width,
        bytes_accessed=total * model * 2 + blocks * width * (model * 4 + total * 6),
        transcendentals=0,
    )
    return weight, tail, out_specs, out_shape, cost


def project_keys(own, sib, row_gain, gathered, first_block, gain, cos, sin, n_y):
    tokens, model = own.shape
    normed_shape = (2 * tokens, model)
    weight, tail, out_specs, out_shape, cost = projection_specs(normed_shape, gathered, first_block, 2, cos)
    fixed = lambda j: (0, 0)
    return pl.pallas_call(
        functools.partial(key_value_kernel, n_y),
        grid=(2,),
        in_specs=[pl.BlockSpec(own.shape, fixed)] * 2
        + [pl.BlockSpec((1, model), fixed), weight]
        + tail,
        out_specs=out_specs + [pl.BlockSpec(normed_shape, fixed)],
        out_shape=out_shape + [jax.ShapeDtypeStruct(normed_shape, jnp.bfloat16)],
        compiler_params=pltpu.CompilerParams(vmem_limit_bytes=56 * MIB),
        cost_estimate=cost,
    )(own, sib, row_gain, gathered, gain, cos, sin)


def project_queries(normed, gathered, blocks, gain, cos, sin, n_y, n_exp, moving):
    weight, tail, out_specs, out_shape, cost = projection_specs(normed.shape, gathered, 0, blocks, cos)
    any_specs = [pl.BlockSpec(memory_space=pl.ANY)] * len(moving)
    return pl.pallas_call(
        functools.partial(query_kernel, n_y, n_exp if moving else 0),
        grid=(blocks,),
        in_specs=[pl.BlockSpec(normed.shape, lambda j: (0, 0)), weight] + tail + any_specs,
        out_specs=out_specs + any_specs,
        out_shape=out_shape + [jax.ShapeDtypeStruct(a.shape, a.dtype) for a in moving],
        scratch_shapes=[plane_sems(2), column_sems(2, n_exp)] if moving else [],
        input_output_aliases={5 + i: 3 + i for i in range(len(moving))},
        compiler_params=pltpu.CompilerParams(
            vmem_limit_bytes=56 * MIB,
            collective_id=4 if moving else None,
            has_side_effects=bool(moving),
        ),
        cost_estimate=cost,
    )(normed, gathered, gain, cos, sin, *moving)


def mask_bias(seg_key, info):
    keys, tokens = seg_key.shape[0], info.shape[1]
    key_pos = lax.broadcasted_iota(jnp.int32, (keys, tokens), 0)
    allowed = (seg_key == info[0:1]) & (key_pos <= info[1:2])
    return jnp.where(allowed, 0.0, MASKED)


def key_tile(keys):
    return min(keys, 256)


def attention_kernel(hops, info_ref, seg_ref, q_ref, k_ref, v_ref, *refs):
    if hops:
        mixed_ref, recip_ref, gate_ref, up_ref, cots_ref, tables_ref = refs[4:10]
        bias_ref, vt_ref, plane_sem, sems = refs[10:]
        column = Column(hops, (cots_ref, tables_ref), sems)
        plane = Plane(hops, (gate_ref, up_ref), plane_sem)
        places = [pl.program_id(i) for i in range(3)]
        ends = [pl.num_programs(i) - 1 for i in range(3)]

        @pl.when((places[0] == 0) & (places[1] == 0) & (places[2] == 0))
        def _():
            greet(column.z, hops, column.ids, (CORE, X, Y, UP, DOWN))
            plane.each(START, True)
            column.sends(hops - 1, START)
            column.passes(hops - 2, START)
    else:
        mixed_ref, recip_ref, bias_ref, vt_ref = refs
    keys = k_ref.shape[1]
    tile = key_tile(keys)

    @pl.when((pl.program_id(1) == 0) & (pl.program_id(2) == 0))
    def _():
        bias_ref[...] = mask_bias(seg_ref[0], info_ref[0])

    @pl.when(pl.program_id(2) == 0)
    def _():
        vt_ref[...] = v_ref[0].astype(jnp.float32).T.astype(jnp.bfloat16)

    queries = q_ref[...]
    total, mixed = None, None
    for start in range(0, keys, tile):
        part = slice(start, start + tile)
        scores = dot_cols(k_ref[0, part], queries) * (HEAD_DIM**-0.5 * LOG2E) + bias_ref[part]
        weights = jnp.exp2(scores)
        tile_total = jnp.sum(weights, axis=0, keepdims=True)
        tile_mixed = dot_plain(vt_ref[:, part], weights.astype(jnp.bfloat16))
        total = tile_total if total is None else total + tile_total
        mixed = tile_mixed if mixed is None else mixed + tile_mixed
    recip = 1.0 / total
    recip_ref[0] = recip
    valid = (info_ref[0, 0:1] > 0).astype(jnp.float32)
    mixed_ref[...] = (mixed * (recip * valid)).T.astype(jnp.bfloat16)
    if hops:

        @pl.when((places[0] == ends[0]) & (places[1] == ends[1]) & (places[2] == ends[2]))
        def _():
            plane.each(WAIT, True)
            column.arrivals(hops - 1)
            column.passes(hops - 1, START)
            column.sends(hops - 1, WAIT_SEND)
            column.passes(hops - 2, WAIT)
            column.passes(hops - 1, WAIT)


def attention_specs(tokens, keys, groups, per_group):
    head = pl.BlockSpec((tokens, HEAD_DIM), lambda s, g, h: (s, g * per_group + h))
    return dict(
        info=pl.BlockSpec((1, 8, tokens), lambda s, g, h: (s, 0, 0)),
        seg=pl.BlockSpec((1, keys, 1), lambda s, g, h: (s, 0, 0)),
        head=head,
        key=pl.BlockSpec((1, keys, HEAD_DIM), lambda s, g, h: (s, 0, g)),
        value=pl.BlockSpec((1, keys, HEAD_DIM), lambda s, g, h: (s, 0, groups + g)),
        recip=pl.BlockSpec((1, 1, tokens), lambda s, g, h: ((s * groups + g) * per_group + h, 0, 0)),
    )


def attend(info, seg_keys, queries, kv_full, groups, per_group, n_exp, moving):
    tokens, keys = info.shape[2], seg_keys.shape[1]
    specs = attention_specs(tokens, keys, groups, per_group)
    steps = 2 * groups * per_group
    return pl.pallas_call(
        functools.partial(attention_kernel, n_exp if moving else 0),
        grid=(2, groups, per_group),
        in_specs=[specs[INFO], specs[SEG], specs[HEAD], specs[KEY], specs[VALUE]]
        + [pl.BlockSpec(memory_space=pl.ANY)] * len(moving),
        out_specs=[specs[HEAD], specs[RECIP]]
        + [pl.BlockSpec(memory_space=pl.ANY)] * len(moving),
        out_shape=[
            jax.ShapeDtypeStruct((2 * tokens, groups * per_group * HEAD_DIM), jnp.bfloat16),
            jax.ShapeDtypeStruct((steps, 1, tokens), jnp.float32),
        ]
        + [jax.ShapeDtypeStruct(a.shape, a.dtype) for a in moving],
        scratch_shapes=[
            pltpu.VMEM((keys, tokens), jnp.float32),
            pltpu.VMEM((HEAD_DIM, keys), jnp.bfloat16),
        ]
        + ([plane_sems(2), column_sems(2, n_exp)] if moving else []),
        input_output_aliases={5 + i: 2 + i for i in range(len(moving))},
        compiler_params=pltpu.CompilerParams(
            vmem_limit_bytes=48 * MIB,
            collective_id=5 if moving else None,
            has_side_effects=bool(moving),
        ),
        cost_estimate=pl.CostEstimate(
            flops=steps * 8 * tokens * keys * HEAD_DIM,
            bytes_accessed=queries.size * 4 + kv_full.size * 2,
            transcendentals=steps * tokens * keys,
        ),
    )(info, seg_keys, queries, kv_full, kv_full, *moving)


def attention_back_kernel(
    info_ref,
    seg_ref,
    q_ref,
    k_ref,
    v_ref,
    mixed_ref,
    grad_ref,
    recip_ref,
    raw_ref,
    gain_ref,
    cos_ref,
    sin_ref,
    chip_ref,
    into_in_ref,
    raw_grad_ref,
    key_grad_ref,
    value_grad_ref,
    gain_grad_ref,
    into_ref,
    bias_ref,
    kt_ref,
    job_sems,
    *,
    n_exp,
    jobs,
):
    sent = [sent_rows(chip_ref, into_ref, job, job_sems, i, n_exp) for i, job in enumerate(jobs)]
    places = [pl.program_id(i) for i in range(3)]
    ends = [pl.num_programs(i) - 1 for i in range(3)]

    @pl.when((places[0] == 0) & (places[1] == 0) & (places[2] == 0))
    def _():
        greet_slots(sorted({job[2] for job in jobs}), n_exp)
        for copy in sent:
            copy.start()

    keys = k_ref.shape[1]
    tile = key_tile(keys)
    scale = HEAD_DIM**-0.5
    first = (pl.program_id(1) == 0) & (pl.program_id(2) == 0)

    @pl.when(first)
    def _():
        bias_ref[...] = mask_bias(seg_ref[0], info_ref[0])

    @pl.when(first & (pl.program_id(0) == 0))
    def _():
        gain_grad_ref[...] = jnp.zeros_like(gain_grad_ref)

    @pl.when(pl.program_id(2) == 0)
    def _():
        kt_ref[...] = k_ref[0].astype(jnp.float32).T.astype(jnp.bfloat16)
        key_grad_ref[...] = jnp.zeros_like(key_grad_ref)
        value_grad_ref[...] = jnp.zeros_like(value_grad_ref)

    queries, grad = q_ref[...], grad_ref[...]
    recip = recip_ref[0]
    overlap = grad.astype(jnp.float32) * mixed_ref[...].astype(jnp.float32)
    inner = jnp.sum(overlap.T, axis=0, keepdims=True)
    query_grad = None
    for start in range(0, keys, tile):
        part = slice(start, start + tile)
        scores = dot_cols(k_ref[0, part], queries) * (scale * LOG2E) + bias_ref[part]
        probs = jnp.exp2(scores) * recip
        grad_probs = dot_cols(v_ref[0, part], grad)
        grad_scores = (probs * (grad_probs - inner)).astype(jnp.bfloat16)
        value_grad_ref[0, part] += dot_plain(probs.astype(jnp.bfloat16), grad)
        key_grad_ref[0, part] += dot_plain(grad_scores, queries) * scale
        tile_grad = dot_plain(kt_ref[:, part], grad_scores)
        query_grad = tile_grad if query_grad is None else query_grad + tile_grad
    turned = rotate_rows_back((query_grad * scale).T, cos_ref[...], sin_ref[...])
    raw = raw_ref[...]
    inverse = lax.rsqrt(jnp.mean(raw * raw, axis=-1, keepdims=True) + EPS)
    unit = raw * inverse
    gain_grad_ref[0:1] += jnp.sum(turned * unit, axis=0, keepdims=True)
    scaled = turned * gain_ref[...]
    raw_grad_ref[...] = (
        inverse * (scaled - unit * jnp.mean(scaled * unit, axis=-1, keepdims=True))
    ).astype(jnp.bfloat16)

    @pl.when((places[0] == ends[0]) & (places[1] == ends[1]) & (places[2] == ends[2]))
    def _():
        for copy in sent:
            copy.wait()


def attend_back(
    info,
    seg_keys,
    queries,
    kv_full,
    mixed,
    grad_mixed,
    recip,
    raw,
    gain,
    cos,
    sin,
    groups,
    per_group,
    chip,
    into,
    jobs,
    n_exp,
):
    tokens, keys = info.shape[2], seg_keys.shape[1]
    specs = attention_specs(tokens, keys, groups, per_group)
    steps = 2 * groups * per_group
    fixed = lambda s, g, h: (0, 0)
    key_grad = jax.ShapeDtypeStruct((2, keys, groups * HEAD_DIM), jnp.float32)
    return pl.pallas_call(
        functools.partial(attention_back_kernel, n_exp=n_exp, jobs=jobs),
        grid=(2, groups, per_group),
        in_specs=[specs[INFO], specs[SEG], specs[HEAD], specs[KEY], specs[VALUE]]
        + [specs[HEAD], specs[HEAD], specs[RECIP], specs[HEAD]]
        + [pl.BlockSpec(a.shape, fixed) for a in (gain, cos, sin)]
        + [pl.BlockSpec(memory_space=pl.ANY)] * 2,
        out_specs=[specs[HEAD], specs[KEY], specs[KEY], pl.BlockSpec((8, HEAD_DIM), fixed)]
        + [pl.BlockSpec(memory_space=pl.ANY)],
        out_shape=[
            jax.ShapeDtypeStruct((2 * tokens, groups * per_group * HEAD_DIM), jnp.bfloat16),
            key_grad,
            key_grad,
            jax.ShapeDtypeStruct((8, HEAD_DIM), jnp.float32),
            jax.ShapeDtypeStruct(into.shape, into.dtype),
        ],
        scratch_shapes=[
            pltpu.VMEM((keys, tokens), jnp.float32),
            pltpu.VMEM((HEAD_DIM, keys), jnp.bfloat16),
            pltpu.SemaphoreType.DMA((2, len(jobs))),
        ],
        input_output_aliases={13: 4},
        compiler_params=pltpu.CompilerParams(
            vmem_limit_bytes=48 * MIB, collective_id=6, has_side_effects=True
        ),
        cost_estimate=pl.CostEstimate(
            flops=steps * 20 * tokens * keys * HEAD_DIM,
            bytes_accessed=queries.size * 12 + kv_full.size * 6,
            transcendentals=steps * tokens * keys,
        ),
    )(
        info, seg_keys, queries, kv_full, kv_full, mixed, grad_mixed, recip, raw, gain, cos, sin, chip, into
    )


def moe_kernel(
    n_exp,
    n_y,
    local_experts,
    table_ref,
    own_ref,
    own_cot_ref,
    cots_ref,
    gate_any,
    up_any,
    down_any,
    x_ref,
    val_ref,
    product_ref,
    gate_grad_ref,
    up_grad_ref,
    tokens_ref,
    partial_ref,
    grad_chip_ref,
    out_chip_ref,
    grad_into_ref,
    out_into_ref,
    gate_w,
    up_w,
    down_w,
    token_scr,
    cot_scr,
    held,
    send,
    got,
    weight_sems,
    load_sems,
    token_sems,
    core_sems,
    local_sems,
    grad_sems,
):
    bf16, f32 = jnp.bfloat16, jnp.float32
    column = Column(n_exp, (tokens_ref,), token_sems, (own_ref,))
    z, core = column.z, column.core
    c, q = pl.program_id(0), pl.program_id(1)
    e, s = q // 2, (q % 3 + 1) // 2
    owner = core + s * (1 - 2 * core)
    chip = xor_chip(z, c, n_exp)
    slots, tokens = x_ref.shape[1], token_scr.shape[1]

    def weight_copies(expert):
        for which, (source, target) in enumerate(
            ((gate_any, gate_w), (up_any, up_w), (down_any, down_w))
        ):
            chips, cores, _, depth, _ = source.shape
            n_x = chips // n_y
            for p in range(chips):
                for k in range(cores):
                    start = ((p // n_x * cores + k) * n_x + p % n_x) * depth
                    yield pltpu.make_async_copy(
                        source.at[p, k, expert],
                        target.at[expert, pl.ds(start, depth)],
                        weight_sems.at[which, expert, p * cores + k],
                    )

    def load(which, sources, methods):
        copies = [
            pltpu.make_async_copy(source, scratch.at[which], load_sems.at[which, i])
            for i, (source, scratch) in enumerate(zip(sources, (token_scr, cot_scr)))
        ]
        for method in methods:
            for copy in copies:
                getattr(copy, method)()

    def fetch(i):
        return pltpu.make_async_copy(partial_ref.at[c, i], got.at[i], local_sems.at[i])

    def store(chunk, i):
        target = (grad_chip_ref, out_chip_ref)[i].at[chunk]
        return pltpu.make_async_copy(got.at[i], target, local_sems.at[2 + i])

    other_parts = (tokens_ref.at[chip, 1 - core], cots_ref.at[chip, 1 - core])

    def core_copy(chunk, i):
        return pltpu.make_async_remote_copy(
            src_ref=send.at[i],
            dst_ref=partial_ref.at[chunk, i],
            send_sem=core_sems.at[0, chunk, i],
            recv_sem=core_sems.at[1, chunk, i],
            device_id=column.ids[CORE],
            device_id_type=MESH,
        )

    def grad_copy(chunk):
        return pltpu.make_async_remote_copy(
            src_ref=grad_chip_ref.at[chunk],
            dst_ref=grad_into_ref.at[chunk],
            send_sem=grad_sems.at[0, chunk],
            recv_sem=grad_sems.at[1, chunk],
            device_id={EXP: xor_chip(z, chunk, n_exp)},
            device_id_type=MESH,
        )

    @pl.when((c == 0) & (q == 0))
    def _():
        barrier = pltpu.get_barrier_semaphore()
        greeted = [column.ids[CORE]] + [{EXP: xor_chip(z, k, n_exp)} for k in range(1, n_exp)]
        for there in greeted:
            pl.semaphore_signal(barrier, inc=1, device_id=there, device_id_type=MESH)
        pl.semaphore_wait(barrier, n_exp)
        column.sends(1, START)
        column.pass_own(START)
        for expert in range(2):
            for copy in weight_copies(expert):
                copy.start()
        load(0, (own_ref, own_cot_ref), (START, WAIT))
        for copy in weight_copies(0):
            copy.wait()

    @pl.when((c > 0) & (q == 0))
    def _():
        column.arrivals(c)
        pl.when(c < n_exp - 1)(lambda: column.sends(c + 1, START))
        column.passes(c, START)
        load(0, (tokens_ref.at[chip, core], cots_ref.at[chip, core]), (START,))
        for i in range(2):
            store(c - 1, i).wait()
        pl.when(c == n_exp - 1)(lambda: grad_copy(1).start())
        pl.when(c > 2)(lambda: grad_copy(c - 1).start())
        load(0, (tokens_ref.at[chip, core], cots_ref.at[chip, core]), (WAIT,))

    @pl.when(q == 1)
    def _():
        for copy in column.copies(2, chip, False):
            copy.wait_recv()
        load(1, other_parts, (START, WAIT))

    @pl.when((c == 0) & (q == 2))
    def _():
        for copy in weight_copies(1):
            copy.wait()

    slot_ids = lax.broadcasted_iota(jnp.int32, (slots, tokens), 0).astype(f32)
    expert_rows = table_ref.shape[2] // 2
    first_row = z * local_experts + core * 2

    def hits_of(expert):
        return table_ref[chip, owner, pl.ds(first_row + expert, 1)] == slot_ids

    hits = hits_of(e)
    one_hot = hits.astype(f32).astype(bf16)
    gates = table_ref[chip, owner, pl.ds(expert_rows + first_row + e, 1)]
    gate_row = jnp.sum(jnp.where(hits, gates, 0.0), axis=1, keepdims=True)
    x_rows = dot_plain(one_hot, token_scr[s]).astype(bf16)
    x_ref[0] = x_rows
    grad_val = (gate_row * dot_plain(one_hot, cot_scr[s])).astype(bf16)
    val_ref[0] = grad_val
    gate_act = dot_plain(x_rows, gate_w[e])
    up_act = dot_plain(x_rows, up_w[e])
    sigmoid = 1.0 / (1.0 + jnp.exp(-gate_act))
    silu = gate_act * sigmoid
    product = (silu * up_act).astype(bf16)
    product_ref[0] = product
    grad_product = dot_cols(grad_val, down_w[e])
    grad_gate = (grad_product * up_act * (sigmoid * (1.0 + gate_act * (1.0 - sigmoid)))).astype(bf16)
    grad_up = (grad_product * silu).astype(bf16)
    gate_grad_ref[0] = grad_gate
    up_grad_ref[0] = grad_up
    grad_rows = (dot_cols(grad_gate, gate_w[e]) + dot_cols(grad_up, up_w[e])).astype(bf16)
    weighted = (gate_row * dot_plain(product, down_w[e])).astype(bf16)

    @pl.when(e == 0)
    def _():
        held[s, 0] = grad_rows
        held[s, 1] = weighted

    def combined(i, rows):
        before = hits_of(0).astype(f32).astype(bf16)
        return lax.dot_general(
            jnp.concatenate([before, one_hot], 0),
            jnp.concatenate([held[s, i], rows], 0),
            (((0,), (0,)), ((), ())),
            preferred_element_type=f32,
        )

    @pl.when(q == 2)
    def _():
        for i, rows in enumerate((grad_rows, weighted)):
            pl.when(c > 0)(lambda i=i: core_copy(c - 1, i).wait_send())
            send[i] = combined(i, rows).astype(bf16)
            core_copy(c, i).start()

    @pl.when(q == 3)
    def _():
        for i, rows in enumerate((grad_rows, weighted)):
            own = combined(i, rows)
            core_copy(c, i).wait_recv()
            fetch(i).start()
            fetch(i).wait()
            got[i] = (own + got[i].astype(f32)).astype(bf16)
            store(c, i).start()

    @pl.when((c == n_exp - 1) & (q == 3))
    def _():
        column.pass_own(WAIT_SEND)
        for hop in range(1, n_exp):
            column.sends(hop, WAIT_SEND)
            column.passes(hop, WAIT_SEND)
        for i in range(2):
            core_copy(n_exp - 1, i).wait_send()
            store(n_exp - 1, i).wait()
        for chunk in range(1, n_exp - 1):
            grad_copy(chunk).wait()


def run_experts(tables, own, own_cot, cots, weights, n_y, local_experts, slots, n_exp):
    bf16 = jnp.bfloat16
    tokens, model = own.shape
    ff = weights[0].shape[4]
    pieces = weights[0].shape[0] * weights[0].shape[1]
    any_spec = pl.BlockSpec(memory_space=pl.ANY)
    row_spec = lambda width: pl.BlockSpec(
        (1, slots, width), lambda c, q: (q // 2, 2 * c + (q % 3 + 1) // 2, 0)
    )
    widths = (model, model, ff, ff, ff)
    chip_shape = jax.ShapeDtypeStruct((n_exp, tokens, model), bf16)
    results = pl.pallas_call(
        functools.partial(moe_kernel, n_exp, n_y, local_experts),
        grid=(n_exp, 4),
        in_specs=[pl.BlockSpec(tables.shape, lambda c, q: (0, 0, 0, 0))] + [any_spec] * 6,
        out_specs=[row_spec(width) for width in widths] + [any_spec] * 6,
        out_shape=[jax.ShapeDtypeStruct((2, 2 * n_exp * slots, width), bf16) for width in widths]
        + [
            jax.ShapeDtypeStruct(cots.shape, bf16),
            jax.ShapeDtypeStruct((n_exp, 2, tokens, model), bf16),
            chip_shape,
            chip_shape,
            chip_shape,
            chip_shape,
        ],
        scratch_shapes=[
            pltpu.VMEM((2, model, ff), bf16),
            pltpu.VMEM((2, model, ff), bf16),
            pltpu.VMEM((2, ff, model), bf16),
            pltpu.VMEM((2, tokens, model), bf16),
            pltpu.VMEM((2, tokens, model), bf16),
            pltpu.VMEM((2, 2, slots, model), bf16),
            pltpu.VMEM((2, tokens, model), bf16),
            pltpu.VMEM((2, tokens, model), bf16),
            pltpu.SemaphoreType.DMA((3, 2, pieces)),
            pltpu.SemaphoreType.DMA((2, 2)),
            column_sems(1, n_exp),
            pltpu.SemaphoreType.DMA((2, n_exp, 2)),
            pltpu.SemaphoreType.DMA((4,)),
            pltpu.SemaphoreType.DMA((2, n_exp)),
        ],
        compiler_params=pltpu.CompilerParams(
            vmem_limit_bytes=63 * MIB, collective_id=7, has_side_effects=True
        ),
        cost_estimate=pl.CostEstimate(
            flops=4 * n_exp * (12 * slots * model * ff + 8 * slots * tokens * model),
            bytes_accessed=24 * model * ff + 4 * n_exp * slots * (2 * model + 3 * ff) * 2,
            transcendentals=4 * n_exp * slots * ff,
        ),
    )(tables, own, own_cot, cots, *weights)
    return results[:5], *results[7:]


def weight_grad_kernel(
    n_y,
    n_ctx,
    n_exp,
    merged,
    x_ref,
    val_ref,
    product_ref,
    gg_ref,
    gu_ref,
    chip_ref,
    into_in_ref,
    out_chip_ref,
    *refs,
):
    bf16 = jnp.bfloat16
    results, (into_ref, out_into_ref, pt_ref, ggt_ref, gut_ref, job_sems) = refs[:-6], refs[-6:]
    e, n = pl.program_id(0), pl.program_id(1)
    last, rows = n_exp - 1, chip_ref.shape[1]
    sent = [
        sent_rows(chip_ref, into_ref, (last, last, last, 0, rows), job_sems, 0, n_exp),
        sent_rows(out_chip_ref, out_into_ref, (last, last, 1, 0, rows), job_sems, 1, n_exp),
    ]

    @pl.when((e == 0) & (n == 0))
    def _():
        greet_slots([1, last], n_exp)
        for copy in sent:
            copy.start()

    @pl.when(n == 0)
    def _():
        for source, turned in ((product_ref, pt_ref), (gg_ref, ggt_ref), (gu_ref, gut_ref)):
            turned[...] = source[0].T

    gate, up = (dot_plain(turned[...], x_ref[0]).astype(bf16) for turned in (ggt_ref, gut_ref))
    down = dot_plain(pt_ref[...], val_ref[0]).astype(bf16)
    if merged:
        (result,) = results
        depth = result.shape[-2] // (2 * n_y * n_ctx)
        y, c, x = n // (2 * n_ctx), n // n_ctx % 2, n % n_ctx
        result[y, x, c, 0, 0] = gate
        result[y, x, c, 1, 0] = up
        rows = pl.ds(pl.multiple_of(n * depth, depth), depth)
        for shard in range(2 * n_y * n_ctx):
            place = (shard // (2 * n_ctx), shard % n_ctx, shard // n_ctx % 2, 2, 0, rows)
            result[place] = down[shard * depth : (shard + 1) * depth]
    else:
        for grad, result in zip((gate, up), results):
            depth = result.shape[-1]
            for i in range(result.shape[1]):
                result[0, i, 0, 0] = grad[:, i * depth : (i + 1) * depth]
        depth = results[2].shape[4]
        for shard in range(2 * n_y * n_ctx):
            place = (shard // (2 * n_ctx), shard % n_ctx, shard // n_ctx % 2, 0)
            results[2][place] = down[shard * depth : (shard + 1) * depth]

    @pl.when((e == 1) & (n == pl.num_programs(1) - 1))
    def _():
        for copy in sent:
            copy.wait()


def expert_weight_grads(rows, chip, into, out_chip, n_y, n_ctx, n_exp, merged):
    bf16 = jnp.bfloat16
    x_all, val_all, product_all, gg_all, gu_all = rows
    _, total, model = x_all.shape
    ff = gg_all.shape[2]
    shards = 2 * n_y * n_ctx
    col, depth, down_depth = 256, model // shards, ff // shards
    wide = pl.BlockSpec((1, total, col), lambda e, n: (e, 0, n))
    whole = pl.BlockSpec((1, total, ff), lambda e, n: (e, 0, 0))
    any_spec = pl.BlockSpec(memory_space=pl.ANY)
    if merged:
        out_specs = [
            pl.BlockSpec((n_y, n_ctx, 2, 3, 1, ff, depth), lambda e, n: (0, 0, 0, 0, e, 0, 0))
        ]
        out_shape = [jax.ShapeDtypeStruct((n_y, n_ctx, 2, 3, 2, ff, depth), bf16)]
    else:
        k = col // depth

        def place(e, n):
            shard = n * k
            return (shard // (2 * n_ctx), shard % n_ctx // k, shard // n_ctx % 2, e, 0, 0)

        out_specs = [pl.BlockSpec((1, k, 1, 1, ff, depth), place)] * 2
        out_specs.append(
            pl.BlockSpec((n_y, n_ctx, 2, 1, down_depth, col), lambda e, n: (0, 0, 0, e, 0, n))
        )
        out_shape = [jax.ShapeDtypeStruct((n_y, n_ctx, 2, 2, ff, depth), bf16)] * 2
        out_shape.append(jax.ShapeDtypeStruct((n_y, n_ctx, 2, 2, down_depth, model), bf16))
    *blocks, into, out_into = pl.pallas_call(
        functools.partial(weight_grad_kernel, n_y, n_ctx, n_exp, merged),
        grid=(2, model // col),
        in_specs=[wide, wide, whole, whole, whole] + [any_spec] * 3,
        out_specs=out_specs + [any_spec] * 2,
        out_shape=out_shape + [jax.ShapeDtypeStruct(a.shape, a.dtype) for a in (into, out_chip)],
        scratch_shapes=[pltpu.VMEM((ff, total), bf16)] * 3 + [pltpu.SemaphoreType.DMA((2, 2))],
        input_output_aliases={6: len(out_shape)},
        compiler_params=pltpu.CompilerParams(
            vmem_limit_bytes=63 * MIB, collective_id=8, has_side_effects=True
        ),
        cost_estimate=pl.CostEstimate(
            flops=2 * 6 * total * model * ff,
            bytes_accessed=2 * (2 * total * (2 * model + 3 * ff) + 6 * model * ff),
            transcendentals=0,
        ),
    )(x_all, val_all, product_all, gg_all, gu_all, chip, into, out_chip)
    return blocks, into, out_into


def part_grad_kernel(n_y, n_ctx, n_exp, jobs, wide_ref, *refs):
    bf16 = jnp.bfloat16
    sources, refs = (refs[:2], refs[2:]) if len(refs) == 12 else (refs[:1], refs[1:])
    chip_ref, _, out_chip_ref, _, result, into_ref, out_into_ref = refs[:7]
    turned_refs, job_sems = refs[7:-1], refs[-1]
    e, n = pl.program_id(0), pl.program_id(1)
    pairs = ((chip_ref, into_ref), (out_chip_ref, out_into_ref))
    sent = [
        sent_rows(*pairs[which], job, job_sems, i, n_exp) for i, (which, job) in enumerate(jobs)
    ]

    @pl.when((e == 0) & (n == 0))
    def _():
        greet_slots(sorted({job[2] for _, job in jobs}), n_exp)
        for copy in sent:
            copy.start()

    @pl.when(n == 0)
    def _():
        for source, turned in zip(sources, turned_refs):
            turned[...] = source[0].T

    grads = [dot_plain(turned[...], wide_ref[0]).astype(bf16) for turned in turned_refs]
    shards = 2 * n_y * n_ctx
    depth = result.shape[-2] // shards
    if len(grads) == 2:
        y, c, x = n // (2 * n_ctx), n // n_ctx % 2, n % n_ctx
        for i, grad in enumerate(grads):
            result[y, x, c, i, 0] = grad
    else:
        rows = pl.ds(pl.multiple_of(n * depth, depth), depth)
        for shard in range(shards):
            place = (shard // (2 * n_ctx), shard % n_ctx, shard // n_ctx % 2, 0, 0, rows)
            result[place] = grads[0][shard * depth : (shard + 1) * depth]

    @pl.when((e == 1) & (n == pl.num_programs(1) - 1))
    def _():
        for copy in sent:
            copy.wait()


def part_weight_grads(wide, sources, chip, into, out_chip, out_into, jobs, collective, n_y, n_ctx, n_exp):
    bf16 = jnp.bfloat16
    _, total, model = wide.shape
    ff, kinds, col = sources[0].shape[2], len(sources), 256
    whole = pl.BlockSpec((1, total, ff), lambda e, n: (e, 0, 0))
    any_spec = pl.BlockSpec(memory_space=pl.ANY)
    return pl.pallas_call(
        functools.partial(part_grad_kernel, n_y, n_ctx, n_exp, jobs),
        grid=(2, model // col),
        in_specs=[pl.BlockSpec((1, total, col), lambda e, n: (e, 0, n))]
        + [whole] * kinds
        + [any_spec] * 4,
        out_specs=[
            pl.BlockSpec((n_y, n_ctx, 2, kinds, 1, ff, col), lambda e, n: (0, 0, 0, 0, e, 0, 0))
        ]
        + [any_spec] * 2,
        out_shape=[jax.ShapeDtypeStruct((n_y, n_ctx, 2, kinds, 2, ff, col), bf16)]
        + [jax.ShapeDtypeStruct(a.shape, a.dtype) for a in (into, out_into)],
        scratch_shapes=[pltpu.VMEM((ff, total), bf16)] * kinds
        + [pltpu.SemaphoreType.DMA((2, len(jobs)))],
        input_output_aliases={kinds + 2: 1, kinds + 4: 2},
        compiler_params=pltpu.CompilerParams(
            vmem_limit_bytes=60 * MIB, collective_id=collective, has_side_effects=True
        ),
        cost_estimate=pl.CostEstimate(
            flops=4 * kinds * total * model * ff,
            bytes_accessed=4 * (total * (model + kinds * ff) + kinds * model * ff),
            transcendentals=0,
        ),
    )(wide, *sources, chip, into, out_chip, out_into)


def sum_kernel(plan, value_ref, total_ref, held, arrived, sems):
    partners = [{axis: xor_chip(lax.axis_index(axis), hop, size)} for axis, size, hop in plan]
    barrier = pltpu.get_barrier_semaphore()
    for there in partners:
        pl.semaphore_signal(barrier, inc=1, device_id=there, device_id_type=MESH)
    pl.semaphore_wait(barrier, len(plan))
    held[0] = value_ref[...]
    for i, there in enumerate(partners):
        copy = pltpu.make_async_remote_copy(
            src_ref=held.at[i],
            dst_ref=arrived.at[i],
            send_sem=sems.at[0, i],
            recv_sem=sems.at[1, i],
            device_id=there,
            device_id_type=MESH,
        )
        copy.start()
        copy.wait()
        held[i + 1] = held[i] + arrived[i]
    total_ref[...] = held[len(plan)]


def sum_devices(value, axes):
    plan = [(axis, size, 1 << i) for axis, size in axes for i in range(size.bit_length() - 1)]
    spec = pl.BlockSpec(memory_space=pltpu.VMEM)
    return pl.pallas_call(
        functools.partial(sum_kernel, plan),
        in_specs=[spec],
        out_specs=spec,
        out_shape=jax.ShapeDtypeStruct(value.shape, value.dtype),
        scratch_shapes=[
            pltpu.VMEM((len(plan) + 1,) + value.shape, value.dtype),
            pltpu.VMEM((len(plan),) + value.shape, value.dtype),
            pltpu.SemaphoreType.DMA((2, len(plan))),
        ],
        compiler_params=pltpu.CompilerParams(collective_id=9, has_side_effects=True),
    )(value)


def on_device(
    residual_in,
    segments,
    routes,
    gates,
    attn_gain,
    q_proj,
    key_projection,
    value_projection,
    q_gain,
    k_gain,
    o_proj,
    mlp_gain,
    gate_proj,
    up_proj,
    down_proj,
    out_grad,
):
    bf16, f32 = jnp.bfloat16, jnp.float32
    n_seq, n_ctx, n_exp = lax.axis_size(SEQ), lax.axis_size(CTX), lax.axis_size(EXP)
    n_y = n_seq // 2
    devices = n_seq * n_ctx * n_exp
    core = lax.axis_index(SEQ) % 2
    span_index = lax.axis_index(CTX)
    z_index = lax.axis_index(EXP)
    group_all = [
        [(s * n_ctx + x) * n_exp + z for s in range(c, n_seq, 2) for x in range(n_ctx) for z in range(n_exp)]
        for c in range(2)
    ]
    group_plane = [[s * n_ctx + x for s in range(c, n_seq, 2) for x in range(n_ctx)] for c in range(2)]

    def swap(value):
        return lax.ppermute(value, SEQ, [(i, i ^ 1) for i in range(n_seq)])

    def across(value, step):
        return lax.ppermute(value, EXP, [(i, i ^ step) for i in range(n_exp)])

    token_count = residual_in.shape[1]
    model_width = residual_in.shape[2]
    sequence_length = segments.shape[1]
    route_count = routes.shape[2]
    local_experts = gate_proj.shape[0]
    expert_count = local_experts * n_exp
    half_experts = local_experts // 2
    capacity = token_count * route_count * 9 // (expert_count * 8)
    slots = -(-capacity // 16) * 16
    groups = KEY_VALUE_HEADS // 2
    heads = QUERY_HEADS // 2
    heads_per_group = QUERY_HEADS // KEY_VALUE_HEADS
    score_scale = HEAD_DIM ** (-0.5)
    rows = q_proj.shape[0]
    gain_rows = q_gain.shape[0]
    q_width, kv_width = heads * HEAD_DIM, groups * HEAD_DIM
    width = q_width + 2 * kv_width

    route_ids = routes[0]
    route_hit = route_ids[:, :, None] == jnp.arange(expert_count, dtype=jnp.int32)[None, None, :]
    hit_counts = route_hit.astype(jnp.int32).sum(1)
    earlier = jnp.cumsum(hit_counts, axis=0) - hit_counts
    slot_of = jnp.where(hit_counts > 0, earlier, -1).astype(f32)
    gate_of = jnp.sum(jnp.where(route_hit, gates[0][:, :, None], 0.0), axis=1)
    table = jnp.concatenate([slot_of.T, gate_of.T], 0)
    def gain_block(model_parts, head_parts, dtype):
        lead = model_parts[0].shape[:-1]
        fill = lambda size: jnp.zeros(lead + (1, size), dtype)
        first = jnp.concatenate([p[..., None, :] for p in model_parts] + [fill(128 - 2 * rows)], -1)
        second = jnp.concatenate(
            [p[..., None, :] for p in head_parts] + [fill(128 - 2 * gain_rows)], -1
        )
        return jnp.concatenate([first, second, jnp.zeros(lead + (rows - 2, 128), dtype)], -2)

    extra = gain_block([attn_gain, mlp_gain], [q_gain, k_gain], bf16)
    mine_cols, other_cols = [], []
    for weight in (q_proj, key_projection, value_projection):
        mine, other = column_halves(weight, core)
        mine_cols += mine
        other_cols += other
    mine_block = jnp.concatenate(mine_cols + [extra], 1)
    other_block = jnp.concatenate(other_cols + [extra], 1)
    chips = n_y * n_ctx
    own_links = n_y == 2 and n_ctx == 2 and n_exp == 4
    if own_links:
        halves = []
        for weight in (gate_proj, up_proj, down_proj):
            low, high = weight[:half_experts], weight[half_experts:]
            halves += [pick(core, low, high), pick(core, high, low)]
        w_gathered, w_out, gate_full, up_full, down_pair, cots_all, tables_all = gather_chips(
            mine_block,
            other_block,
            halves,
            o_proj.reshape(4, -1, model_width),
            routes[0].T,
            gates[0].T,
            out_grad[0],
            expert_count,
            n_exp,
        )
        w_out = w_out.reshape(q_width, model_width)
        w_gathered = w_gathered.reshape(chips * n_exp, 2, rows, width + 128)
    else:
        theirs = swap(other_block)
        pair = jnp.stack([pick(core, mine_block, theirs), pick(core, theirs, mine_block)])
        w_gathered = lax.all_gather(
            pair, (SEQ, CTX, EXP), axis=0, tiled=False, axis_index_groups=group_all
        )
        cots_all, tables_all = exchange_column(out_grad[0], table, n_exp)
    w_extra = w_gathered[:, :, :2, width:].reshape(n_y, n_ctx * n_exp, 2, 2, 128)
    w_extra = w_extra.transpose(0, 2, 1, 3, 4).reshape(devices, 2, 128).astype(f32)
    gain_attn = w_extra[:, 0, :rows].reshape(model_width)
    gain_mlp_f = w_extra[:, 0, rows : 2 * rows].reshape(model_width)
    gain_query_f = w_extra[:, 1, :gain_rows].reshape(1, HEAD_DIM)
    gain_key_f = w_extra[:, 1, gain_rows : 2 * gain_rows].reshape(1, HEAD_DIM)

    if not own_links:
        w_out = lax.all_gather(
            o_proj, (SEQ, CTX, EXP), axis=0, tiled=True, axis_index_groups=group_all
        )

    def gather_expert(weight, after):
        if own_links:
            both = weight
        else:
            mine = pick(core, weight[:half_experts], weight[half_experts:])
            theirs = swap(pick(core, weight[half_experts:], weight[:half_experts]))
            both = jnp.stack([pick(core, mine, theirs), pick(core, theirs, mine)])
        both = lax.optimization_barrier((both, after))[0]
        full = lax.all_gather(
            both, (SEQ, CTX), axis=0, tiled=False, axis_index_groups=group_plane
        )
        full = full.reshape((n_y * n_ctx,) + both.shape)
        if own_links:
            return full
        full = full.reshape((n_y, n_ctx) + both.shape).transpose(3, 0, 2, 1, 4, 5)
        return full.reshape(1, 1, half_experts, -1, weight.shape[2])

    hidden = residual_in[0].astype(f32)
    seg_two = jnp.stack([segments[0], swap(segments)[0]])
    seg_here = lax.dynamic_slice_in_dim(seg_two, span_index * token_count, token_count, 1)
    valid_two = (seg_here > 0).astype(f32).reshape(2 * token_count, 1)
    valid_rows = valid_two[:token_count]
    positions = span_index * token_count + jnp.arange(token_count, dtype=jnp.int32)
    cos_one, sin_one = rope_tables(positions)
    half_dim = HEAD_DIM // 2
    signed_sine = jnp.concatenate([-sin_one[:, :half_dim], sin_one[:, half_dim:]], 1)
    info = jnp.zeros((2, 8, token_count), jnp.int32)
    info = info.at[:, 0].set(seg_here).at[:, 1].set(positions[None])
    seg_keys = seg_two[:, :, None]
    inv_attn = lax.rsqrt(jnp.mean(hidden * hidden, axis=-1, keepdims=True) + EPS)
    q_blocks = q_width // (2 * HEAD_DIM)
    if own_links:
        q_raw, query_rows, w_query, normed_turned, kv_full, *moving = project_all(
            residual_in[0],
            swap(residual_in[0]),
            gain_attn[None],
            w_gathered,
            q_blocks,
            gain_key_f,
            gain_query_f,
            cos_one,
            signed_sine,
            out_grad[0],
            n_y,
            n_exp,
            (gate_full, up_full, cots_all, tables_all),
        )
    else:
        kv_raw, kv_low, w_kv, normed_two = project_keys(
            residual_in[0],
            swap(residual_in[0]),
            gain_attn[None],
            w_gathered,
            q_blocks,
            gain_key_f,
            cos_one,
            signed_sine,
            n_y,
        )
        kv_here = kv_low.reshape(2, token_count, 2 * kv_width)
        kv_full = lax.all_gather(kv_here, CTX, axis=1, tiled=True)
        q_raw, query_rows, w_query, *moving = project_queries(
            normed_two, w_gathered, q_blocks, gain_query_f, cos_one, signed_sine, n_y, n_exp, ()
        )
    mixed_low, recip, *moving = attend(
        info, seg_keys, query_rows, kv_full, groups, heads_per_group, n_exp, moving
    )
    if own_links:
        gate_full, up_full, cots_all, tables_all = moving
    else:
        gate_full, up_full = gather_expert(gate_proj, gain_attn), gather_expert(up_proj, gain_attn)
    down_full = gather_expert(
        down_pair if own_links else down_proj, query_rows if own_links else gain_attn
    )
    if not own_links:
        tables_all = lax.dynamic_update_slice(
            tables_all, table[None, None], (z_index, core, jnp.int32(0), jnp.int32(0))
        )
    attn_theirs = swap(jnp.dot(mixed_low[token_count:], w_out, preferred_element_type=f32))
    attn_out = jnp.dot(mixed_low[:token_count], w_out, preferred_element_type=f32) + attn_theirs
    middle = hidden + attn_out
    inv_mlp = lax.rsqrt(jnp.mean(middle * middle, axis=-1, keepdims=True) + EPS)
    normed_mlp = (middle * inv_mlp * gain_mlp_f).astype(bf16)

    rows_all, grad_chip, out_chip, grad_into, out_into = run_experts(
        tables_all,
        normed_mlp,
        out_grad[0],
        cots_all,
        (gate_full, up_full, down_full),
        n_y if own_links else 1,
        local_experts,
        slots,
        n_exp,
    )

    if own_links:
        x_rows, val_rows, product_rows, gate_rows, up_rows = rows_all
        last, first_rows = n_exp - 1, 5 * token_count // 16
        blocks = []
        for i, (wide, sources) in enumerate(
            ((val_rows, (product_rows,)), (x_rows, (gate_rows, up_rows)))
        ):
            span = ((0, first_rows), (first_rows, token_count))[i]
            jobs = [(0, (last, last, last, *span)), (1, (last, last, 1, *span))]
            block, grad_into, out_into = part_weight_grads(
                wide, sources, grad_chip, grad_into, out_chip, out_into, jobs, 13 + i, n_y, n_ctx, n_exp
            )
            blocks.append(block)
    else:
        weight_blocks, grad_into, out_into = expert_weight_grads(
            rows_all, grad_chip, grad_into, out_chip, n_y, n_ctx, n_exp, merged=False
        )
    out_far = (out_chip[2:3].astype(f32) + out_into[3:4].astype(f32)).astype(bf16)

    def scatter_plane(blocks):
        return lax.psum_scatter(
            blocks.reshape((n_y * n_ctx,) + blocks.shape[2:]),
            (SEQ, CTX),
            scatter_dimension=0,
            tiled=True,
            axis_index_groups=group_plane,
        )[0]

    def all_experts(part):
        mine = pick(core, part[0], part[1])
        theirs = swap(pick(core, part[1], part[0]))
        axis = mine.ndim - 3
        both = [pick(core, mine, theirs), pick(core, theirs, mine)]
        return jnp.concatenate(both, axis).astype(f32)

    if own_links:
        parts = []
        for block in blocks:
            part = scatter_plane(block.reshape(n_y, n_ctx, -1, block.shape[-1]))
            parts.append(lax.optimization_barrier(part).reshape(block.shape[2:]))
    else:
        parts = [scatter_plane(weight_blocks[0])]
        for blocks in weight_blocks[1:]:
            blocks, parts[-1] = lax.optimization_barrier((blocks, parts[-1]))
            parts.append(scatter_plane(blocks))

    grad_normed_mlp = grad_chip[0].astype(f32)
    for step in range(1, n_exp):
        grad_normed_mlp = grad_normed_mlp + grad_into[step].astype(f32)
    cotangent = out_grad[0].astype(f32)
    mlp_gain_grad = jnp.sum(grad_normed_mlp * middle * inv_mlp, axis=0)
    grad_middle = cotangent + norm_back(grad_normed_mlp, middle, inv_mlp, gain_mlp_f)
    grad_attn_own = grad_middle.astype(bf16)
    part_rows = token_count // 4
    out_jobs, back_jobs = [(0, 2, 2, 0, part_rows)], [(0, 2, 2, part_rows, token_count)]
    last_jobs = [(1, 1, 1, 0, token_count)]
    o_grad_part, mixture_gradient, out_into = out_back(
        mixed_low, grad_attn_own, swap(grad_attn_own), w_out, valid_two, out_far, out_into, out_jobs, n_exp
    )
    o_grad_plane = scatter_plane(o_grad_part.reshape(n_y, n_ctx, n_exp, -1, model_width))
    grad_q_raw, key_grad, value_grad, q_gain_rows, out_into = attend_back(
        info,
        seg_keys,
        query_rows,
        kv_full,
        mixed_low,
        mixture_gradient,
        recip,
        q_raw,
        gain_query_f,
        cos_one,
        signed_sine,
        groups,
        heads_per_group,
        out_far,
        out_into,
        back_jobs,
        n_exp,
    )
    q_gain_grad = q_gain_rows[0]
    if own_links:
        grad_kv, grad_hidden, attn_gain_grad, k_gain_rows, out_into = back_to_input(
            grad_q_raw,
            key_grad,
            value_grad,
            q_raw,
            w_query,
            gain_key_f,
            cos_one,
            signed_sine,
            residual_in[0],
            gain_attn[None],
            grad_middle,
            out_chip,
            out_into,
            last_jobs,
            n_exp,
        )
        k_gain_grad = k_gain_rows[0]
    else:
        kv_grad = jnp.concatenate([key_grad, value_grad], 2)
        query_part = contract_cols(grad_q_raw, w_query)
        kv_grad_here = lax.psum_scatter(
            kv_grad.astype(bf16), CTX, scatter_dimension=1, tiled=True
        ).astype(f32)
        kv_grad_here = kv_grad_here.reshape(2 * token_count, 2 * kv_width)
        cosine_table, sine_values = jnp.concatenate([cos_one] * 2, 0), jnp.concatenate([sin_one] * 2, 0)
        k_raw = kv_raw[:, :kv_width].reshape(-1, groups, HEAD_DIM)
        inv_key = lax.rsqrt(jnp.mean(k_raw * k_raw, axis=-1, keepdims=True) + EPS)
        grad_kn = inverse_rotation(
            kv_grad_here[:, :kv_width].reshape(-1, groups, HEAD_DIM), cosine_table, sine_values
        )
        k_gain_grad = jnp.sum(grad_kn * k_raw * inv_key, axis=(0, 1))
        grad_k_raw = norm_back(grad_kn, k_raw, inv_key, gain_key_f).astype(bf16)
        grad_kv = jnp.concatenate(
            [grad_k_raw.reshape(-1, kv_width), kv_grad_here[:, kv_width:].astype(bf16)], 1
        )
        normed_partial = query_part + contract_cols(grad_kv, w_kv)
        grad_normed = normed_partial[:token_count] + swap(normed_partial[token_count:])
        attn_gain_grad = jnp.sum(grad_normed * hidden * inv_attn, axis=0)
        grad_hidden = grad_middle + norm_back(grad_normed, hidden, inv_attn, gain_attn)

    extra_grad = gain_block(
        [attn_gain_grad.reshape(devices, rows), mlp_gain_grad.reshape(devices, rows)],
        [q_gain_grad.reshape(devices, gain_rows), k_gain_grad.reshape(devices, gain_rows)],
        f32,
    ).astype(bf16)
    if not own_links:
        near = across(out_chip[1], 1)
        out_into = lax.dynamic_update_slice(out_into, near[None], (1, 0, 0))
    expert_out = out_chip[0].astype(f32)
    for step in (1, 2):
        expert_out = expert_out + out_into[step].astype(f32)
    final_out = (middle + expert_out).astype(bf16)
    sums = [
        jnp.sum(value * value * valid_rows, keepdims=True) for value in (hidden, attn_out, expert_out)
    ]
    sums.append(jnp.sum(valid_rows, keepdims=True))
    stats = jnp.pad(jnp.concatenate(sums, 1), ((0, 7), (0, 124)))
    if not own_links:
        stats = sum_devices(stats, ((SEQ, n_seq), (CTX, n_ctx), (EXP, n_exp)))
    if own_links:
        part = all_experts(jnp.concatenate(parts[::-1], 1))
        gate_grad, up_grad = part[0].transpose(0, 2, 1), part[1].transpose(0, 2, 1)
        depth = part.shape[-1]
        down_grad = part[2].reshape(local_experts, model_width // depth, -1, depth)
        down_grad = down_grad.transpose(0, 2, 1, 3).reshape(local_experts, -1, model_width)
        extra_grad, o_grad_plane, gate_grad, up_grad, down_grad, stats, final_out = (
            lax.optimization_barrier(
                (extra_grad, o_grad_plane, gate_grad, up_grad, down_grad, stats, final_out)
            )
        )
    o_proj_grad = lax.psum_scatter(o_grad_plane, EXP, scatter_dimension=0, tiled=True)
    o_proj_grad = o_proj_grad[0].astype(f32)
    if own_links:
        grad_mine, grad_theirs, stats = dense_grad_scatter(
            normed_turned,
            grad_q_raw,
            grad_kv,
            extra_grad.reshape(n_y, 2, n_ctx, n_exp, rows, 128),
            stats,
            n_exp,
        )
    else:
        w_grad = jnp.concatenate(
            [
                contract_rows(normed_two, grad_q_raw).astype(bf16),
                contract_rows(normed_two, grad_kv).astype(bf16),
                extra_grad.reshape(model_width, 128),
            ],
            1,
        )
        w_grad = w_grad.reshape(n_y, 2, n_ctx, n_exp, rows, width + 128).transpose(0, 2, 3, 1, 4, 5)
        w_grad = lax.psum_scatter(
            scatter_plane(w_grad), EXP, scatter_dimension=0, tiled=True
        )[0]
        grad_mine = pick(core, w_grad[0], w_grad[1])
        grad_theirs = swap(pick(core, w_grad[1], w_grad[0]))
    rms_stats = jnp.sqrt(stats[0, :3] / (stats[0, 3] * model_width))
    if not own_links:
        gate_grad, up_grad = (all_experts(p).transpose(0, 2, 1) for p in parts[:2])
        down_grad = all_experts(parts[2])
    even = pick(core, grad_mine, grad_theirs).astype(f32)
    odd = pick(core, grad_theirs, grad_mine).astype(f32)

    def columns(start, size):
        step = size // groups
        parts = []
        for g in range(groups):
            parts += [half[:, start + g * step : start + (g + 1) * step] for half in (even, odd)]
        return jnp.concatenate(parts, 1)

    extra_total = even[:, width:] + odd[:, width:]
    return (
        final_out[None],
        grad_hidden.astype(bf16)[None],
        extra_total[0, :rows],
        columns(0, q_width),
        columns(q_width, kv_width),
        columns(q_width + kv_width, kv_width),
        extra_total[1, :gain_rows],
        extra_total[1, gain_rows : 2 * gain_rows],
        o_proj_grad,
        extra_total[0, rows : 2 * rows],
        gate_grad,
        up_grad,
        down_grad,
        rms_stats,
    )


def solution(mesh):
    in_specs = (
        P((SEQ, EXP), CTX, None),
        P((SEQ, EXP), None),
        P((SEQ, EXP), CTX, None),
        P((SEQ, EXP), CTX, None),
        P((SEQ, CTX, EXP)),
        P((SEQ, CTX, EXP), None),
        P((SEQ, CTX, EXP), None),
        P((SEQ, CTX, EXP), None),
        P((SEQ, CTX, EXP)),
        P((SEQ, CTX, EXP)),
        P((SEQ, CTX, EXP), None),
        P((SEQ, CTX, EXP)),
        P(EXP, (SEQ, CTX), None),
        P(EXP, (SEQ, CTX), None),
        P(EXP, (SEQ, CTX), None),
        P((SEQ, EXP), CTX, None),
    )
    out_specs = (
        P((SEQ, EXP), CTX, None),
        P((SEQ, EXP), CTX, None),
        P((SEQ, CTX, EXP)),
        P((SEQ, CTX, EXP), None),
        P((SEQ, CTX, EXP), None),
        P((SEQ, CTX, EXP), None),
        P((SEQ, CTX, EXP)),
        P((SEQ, CTX, EXP)),
        P((SEQ, CTX, EXP), None),
        P((SEQ, CTX, EXP)),
        P(EXP, (SEQ, CTX), None),
        P(EXP, (SEQ, CTX), None),
        P(EXP, (SEQ, CTX), None),
        P(),
    )
    return jax.shard_map(
        on_device, mesh=mesh, in_specs=in_specs, out_specs=out_specs, check_vma=False
    )
```
